32 devices in a mesh: unit: 8 (over z, x), day: 4 (over y, core).
Axes of the slice: x: 2, y: 2, z: 4, core: 2. Of those that a mesh axis runs over, the one named last changes fastest.
Arguments:
- outcomes: float32 [32768, 1024], P('unit', 'day'), may hold values from -6 to 6
- cohort: int32 [32768], P('unit'), may hold values from 0 to 8
- pre_end: int32 [8], replicated, may hold values from 256 to 511
- post_start: int32 [8], replicated, may hold values from 512 to 767
- unit_logit: float32 [8, 32768], P(None, 'unit'), may hold values from -4 to 4
- time_logit: float32 [8, 1024], P(None, 'day'), may hold values from -4 to 4
Outputs:
- unit_weights: float32 [8, 32768], P(None, 'unit')
- time_weights: float32 [8, 1024], P(None, 'day')
The draws below stay inside these ranges and needn't reach their ends.
All inputs are finite; a program needn't handle non-finite values.
Results may differ from the reference program's by a relative error of at most 0.0003.
Values sent between devices are 32-bit elements; how exact they have to be, the bound alone decides.
No kernel may reach another device: no remote copies, remote signals or barrier semaphores. Data moves between devices by JAX's collectives and lax.ppermute only.
A program may use at most 64 MiB of HBM per device.

```python
import jax
import jax.numpy as jnp
from jax import lax

COHORTS = 8
UNITS = 32768
DAYS = 1024


def draw_outcomes(key, part):
    value_key = jax.random.fold_in(key, 11)
    values = jax.random.normal(value_key, (UNITS, DAYS), jnp.float32)
    return jnp.clip(values, -6.0, 6.0).astype(jnp.float32)


def place_ends(result, own_key, low, largest):
    index_at = [jax.random.randint(jax.random.fold_in(own_key, axis), (), 0, length) for axis, length in enumerate(result.shape)]
    longest = result.shape.index(max(result.shape))
    beside = index_at[:longest] + [(index_at[longest] + 1) % result.shape[longest]] + index_at[longest + 1:]
    return result.at[tuple(index_at)].set(low).at[tuple(beside)].set(largest)


def levels(key, shape, cuts, low, top_value):
    factor_of, own = 1.0, jax.random.fold_in(key, 6)
    for dim, shards_of in cuts:
        draws = jnp.exp(jax.random.uniform(jax.random.fold_in(own, dim), (shards_of,), jnp.float32, low / len(cuts), top_value / len(cuts)))
        factor_of = factor_of * jnp.repeat(draws, shape[dim] // shards_of).reshape([-1 if axis == dim else 1 for axis in range(len(shape))])
    return factor_of


def bell_draw(key, extent, width, most, cuts=(), kind=jnp.bfloat16):
    factor_of = levels(key, extent, cuts, -0.22, 0.18) if cuts else 1.0
    entries = jax.random.normal(key, extent, jnp.float32) * width * factor_of
    return jnp.minimum(jnp.maximum(entries, -most), most).astype(kind)


def setup_inputs(seed: int = 0) -> dict:
    key_list = jax.random.split(jax.random.key(seed), 7)
    return {
        "outcomes": draw_outcomes(jax.random.fold_in(key_list[6], 71), 0),
        "cohort": place_ends(jax.random.randint(key_list[1], (UNITS,), 0, COHORTS + 1), jax.random.fold_in(key_list[1], 1), 0, COHORTS).astype(jnp.int32),
        "pre_end": place_ends(jax.random.randint(key_list[2], (COHORTS,), DAYS // 4, DAYS // 2), jax.random.fold_in(key_list[2], 1), DAYS // 4, (DAYS // 2) - 1).astype(jnp.int32),
        "post_start": place_ends(jax.random.randint(key_list[3], (COHORTS,), DAYS // 2, 3 * DAYS // 4), jax.random.fold_in(key_list[3], 1), DAYS // 2, (3 * DAYS // 4) - 1).astype(jnp.int32),
        "unit_logit": bell_draw(key_list[4], (COHORTS, UNITS), 0.7, 4.0, ((1, 8),), jnp.float32),
        "time_logit": bell_draw(key_list[5], (COHORTS, DAYS), 0.7, 4.0, ((1, 4),), jnp.float32),
    }


highest = lax.Precision.HIGHEST
step_rate = 16.0

def weigh_days(left, outcomes):
    return lax.dot_general(left, outcomes, (((1,), (1,)), ((), ())), precision=highest, preferred_element_type=jnp.float32)

def reference(outcomes, cohort, pre_end, post_start, unit_logit, time_logit):
    labels = jnp.arange(COHORTS, dtype=jnp.int32)[:, None]
    treated = (cohort[None, :] == labels).astype(jnp.float32)
    control = (cohort[None, :] > labels).astype(jnp.float32)
    day_index = jnp.arange(DAYS, dtype=jnp.int32)[None, :]
    before = (day_index < pre_end[:, None]).astype(jnp.float32)
    after_mask = (day_index >= post_start[:, None]).astype(jnp.float32)
    before_len = pre_end.astype(jnp.float32)
    after_len = (DAYS - post_start).astype(jnp.float32)
    raised = jnp.exp(unit_logit) * control
    unit_norm = lax.optimization_barrier(jnp.sum(raised, axis=1))
    treat_count = jnp.maximum(lax.optimization_barrier(jnp.sum(treated, axis=1)), 1.0)
    ctrl_count = lax.optimization_barrier(jnp.sum(control, axis=1))
    weights = raised / unit_norm[:, None]
    fitted = jnp.dot(weights, outcomes, precision=highest, preferred_element_type=jnp.float32)
    treat_sum = jnp.dot(treated, outcomes, precision=highest, preferred_element_type=jnp.float32)
    residual = (fitted - treat_sum / treat_count[:, None]) * before
    unit_grad = weigh_days(residual, outcomes)
    updated = weights * jnp.exp(-step_rate * unit_grad / jnp.sqrt(before_len)[:, None])
    unit_weights = updated / lax.optimization_barrier(jnp.sum(updated, axis=1))[:, None] * ctrl_count[:, None]
    time_raised = jnp.exp(time_logit) * before
    time_lam = time_raised / lax.optimization_barrier(jnp.sum(time_raised, axis=1))[:, None]
    time_fit = weigh_days(time_lam, outcomes)
    post_sum = weigh_days(after_mask, outcomes)
    shortfall = (time_fit - post_sum / after_len[:, None]) * control
    time_grad = jnp.dot(shortfall, outcomes, precision=highest, preferred_element_type=jnp.float32)
    moved = time_lam * jnp.exp(-step_rate * time_grad / jnp.sqrt(jnp.maximum(ctrl_count, 1.0))[:, None])
    time_weights = moved / lax.optimization_barrier(jnp.sum(moved, axis=1))[:, None] * before_len[:, None]
    return (unit_weights, time_weights)
```

```python
import functools

import jax
import jax.numpy as jnp
from jax import lax
from jax.experimental import pallas as pl
from jax.experimental.pallas import tpu as pltpu
from jax.sharding import PartitionSpec as P

step_rate = 16.0
f32 = jnp.float32
bf16 = jnp.bfloat16
lanes = 128


def split_left(value):
    first = value.astype(bf16).astype(f32)
    rest = value - first
    second = rest.astype(bf16).astype(f32)
    return [first, second, rest - second]


def split_panel(value):
    high = value.astype(bf16)
    return high, (value - high.astype(f32)).astype(bf16)


def rows_dot(left, high, low):
    return jnp.dot(left, high, preferred_element_type=f32) + jnp.dot(left, low, preferred_element_type=f32)


def days_dot(left, high, low):
    dims = (((1,), (1,)), ((), ()))
    return lax.dot_general(left, high, dims, preferred_element_type=f32) + lax.dot_general(
        left, low, dims, preferred_element_type=f32
    )


def add_terms(stack, groups):
    return stack[:groups] + stack[groups : 2 * groups] + stack[2 * groups : 3 * groups]


def day_masks(day_axis, pre_end, post_start, groups, day_cols):
    start = lax.axis_index(day_axis) * day_cols
    days = start + lax.broadcasted_iota(jnp.int32, (groups, day_cols), 1)
    return days < pre_end, days >= post_start


def first_kernel(all_count, panel, cohort, pre_end, post_start, unit_logit, time_logit, sums, cross, raised_days):
    groups, day_cols = time_logit.shape
    before, after = day_masks("day", pre_end[...], post_start[...], groups, day_cols)
    raised_time = jnp.where(before, jnp.exp(time_logit[...]), 0.0)
    after_len = (all_count - post_start[...]).astype(f32)
    coef = raised_time - jnp.where(after, 1.0, 0.0) / after_len

    @pl.when(pl.program_id(0) == 0)
    def _():
        sums[...] = jnp.zeros_like(sums)
        raised_days[...] = raised_time

    rows = cohort.shape[1]
    label = lax.broadcasted_iota(jnp.int32, (groups, rows), 0)
    treated = jnp.where(cohort[...] == label, 1.0, 0.0)
    control = jnp.where(cohort[...] > label, 1.0, 0.0)
    raised = jnp.exp(unit_logit[...]) * control
    high, low = split_panel(panel[...])
    left = jnp.concatenate(split_left(raised) + [treated], axis=0).astype(bf16)
    product = rows_dot(left, high, low)
    sums[:groups, :] += add_terms(product, groups)
    sums[groups : 2 * groups, :] += product[3 * groups :]
    lane = lax.broadcasted_iota(jnp.int32, (groups, day_cols), 1)
    sums[2 * groups :, :] += jnp.where(
        lane == 0,
        jnp.sum(raised, axis=1, keepdims=True),
        jnp.where(
            lane == 1,
            jnp.sum(treated, axis=1, keepdims=True),
            jnp.where(lane == 2, jnp.sum(control, axis=1, keepdims=True), 0.0),
        ),
    )
    coef_terms = split_left(coef)
    left = jnp.concatenate(coef_terms + [jnp.zeros_like(coef)], axis=0).astype(bf16)
    cross[...] = add_terms(days_dot(left, high, low), groups)


def second_kernel(unit_devices, panel, sums, pre_end, post_start, cross, raised_days, pack, norms):
    groups, day_cols = raised_days.shape
    rows = panel.shape[0]
    unit_rows = cross.shape[1]
    step = pl.program_id(0)
    total = sums[pl.ds(0, 3 * groups), :]
    for other in range(1, unit_devices):
        total = total + sums[pl.ds(other * 3 * groups, 3 * groups), :]
    unit_norm = total[2 * groups :, 0:1]
    treat_count = jnp.maximum(total[2 * groups :, 1:2], 1.0)
    before, _ = day_masks("day", pre_end[...], post_start[...], groups, day_cols)
    gap = total[:groups] / unit_norm - total[groups : 2 * groups] / treat_count
    residual = jnp.where(before, gap, 0.0)

    @pl.when(step == 0)
    def _():
        norms[...] = total[2 * groups :, :lanes]
        pack[groups:, :unit_rows] = cross[...]
        pack[groups:, unit_rows:] = raised_days[...]
        pack[:groups, unit_rows:] = jnp.zeros_like(raised_days)

    high, low = split_panel(panel[...])
    left = jnp.concatenate(split_left(residual) + [jnp.zeros_like(residual)], axis=0).astype(bf16)
    here = pl.ds(pl.multiple_of(step * rows, rows), rows)
    pack[:groups, here] = add_terms(days_dot(left, high, low), groups)


def third_kernel(day_devices, panel, pack, norms, cohort, unit_logit, pre_end, updated, out):
    groups = unit_logit.shape[0]
    rows = panel.shape[0]
    day_cols = panel.shape[1]
    unit_rows = pack.shape[1] - day_cols
    step = pl.program_id(0)
    half = day_devices // 2
    here = pl.ds(pl.multiple_of(step * rows, rows), rows)

    def part(index, lower, where):
        return pack[pl.ds((2 * index + lower) * groups, groups), where]

    time_norm = jnp.zeros((groups, 1), f32)
    for index in range(half):
        time_norm += jnp.sum(part(index, 1, pl.ds(unit_rows, day_cols)), axis=1, keepdims=True)
    unit_grad = part(0, 0, here)
    time_fit = part(0, 1, here)
    post_mean = part(half, 1, here)
    for index in range(1, half):
        unit_grad = unit_grad + part(index, 0, here)
        time_fit = time_fit + part(index, 1, here)
        post_mean = post_mean + part(half + index, 1, here)
    label = lax.broadcasted_iota(jnp.int32, (groups, rows), 0)
    control = cohort[...] > label
    weights = jnp.where(control, jnp.exp(unit_logit[...]), 0.0) / norms[:, 0:1]
    root = jnp.sqrt(pre_end[...].astype(f32))
    new = weights * jnp.exp(unit_grad * (-step_rate / root))
    updated[...] = new
    shortfall = jnp.where(control, time_fit / time_norm + post_mean, 0.0)
    high, low = split_panel(panel[...])
    left = jnp.concatenate(split_left(shortfall) + [jnp.zeros_like(shortfall)], axis=0).astype(bf16)

    @pl.when(step == 0)
    def _():
        out[...] = jnp.zeros_like(out)

    out[:groups, :] += add_terms(rows_dot(left, high, low), groups)
    out[groups:, :] += jnp.broadcast_to(jnp.sum(new, axis=1, keepdims=True), (groups, day_cols))


def fourth_kernel(unit_devices, day_devices, gathered, updated, norms, pack, pre_end, unit_weights, time_weights):
    groups, unit_rows = updated.shape
    day_cols = time_weights.shape[1]
    own_day = lax.axis_index("day")
    half = day_devices // 2
    ctrl_count = norms[:, 2:3]
    root = jnp.sqrt(jnp.maximum(ctrl_count, 1.0))
    length = pre_end[...].astype(f32)

    def part(unit, day, lower):
        return gathered[pl.ds(((unit * day_devices + day) * 2 + lower) * groups, groups), :]

    unit_total = part(0, 0, 1)[:, 0:1]
    for unit in range(1, unit_devices):
        unit_total = unit_total + part(unit, 0, 1)[:, 0:1]
    unit_weights[...] = updated[...] * (ctrl_count / unit_total)
    time_norm = jnp.zeros((groups, 1), f32)
    raised = []
    for day in range(half):
        raised.append(pack[pl.ds((2 * day + 1) * groups, groups), pl.ds(unit_rows, day_cols)])
        time_norm += jnp.sum(raised[-1], axis=1, keepdims=True)
    moved_total = jnp.zeros((groups, 1), f32)
    own = jnp.zeros((groups, day_cols), f32)
    for day in range(half):
        grad = part(0, day, 0)
        for unit in range(1, unit_devices):
            grad = grad + part(unit, day, 0)
        moved = raised[day] / time_norm * jnp.exp(grad * (-step_rate / root))
        moved_total += jnp.sum(moved, axis=1, keepdims=True)
        own = jnp.where(own_day == day, moved, own)
    time_weights[...] = own * (length / moved_total)


def local(outcomes, cohort, pre_end, post_start, unit_logit, time_logit):
    groups = pre_end.shape[0]
    unit_rows, day_cols = outcomes.shape
    day_devices = lax.axis_size("day")
    unit_devices = lax.axis_size("unit")
    steps = 4
    rows = unit_rows // steps
    cohort = cohort[None, :]
    pre_end = pre_end[:, None]
    post_start = post_start[:, None]

    def whole(*shape):
        return pl.BlockSpec(shape, lambda i: (0,) * len(shape))

    panel_spec = pl.BlockSpec((rows, day_cols), lambda i: (i, 0))
    group_spec = pl.BlockSpec((groups, rows), lambda i: (0, i))
    label_spec = pl.BlockSpec((1, rows), lambda i: (0, i))
    end_spec = whole(groups, 1)
    days_spec = whole(groups, day_cols)
    params = pltpu.CompilerParams(vmem_limit_bytes=32 * 1024 * 1024)

    sums, cross, raised_days = pl.pallas_call(
        functools.partial(first_kernel, day_devices * day_cols),
        grid=(steps,),
        in_specs=[panel_spec, label_spec, end_spec, end_spec, group_spec, days_spec],
        out_specs=[whole(3 * groups, day_cols), group_spec, days_spec],
        out_shape=[
            jax.ShapeDtypeStruct((3 * groups, day_cols), f32),
            jax.ShapeDtypeStruct((groups, unit_rows), f32),
            jax.ShapeDtypeStruct((groups, day_cols), f32),
        ],
        compiler_params=params,
        name="first_products",
    )(outcomes, cohort, pre_end, post_start, unit_logit, time_logit)
    all_sums = lax.all_gather(sums, "unit", axis=0, tiled=True)
    width = unit_rows + day_cols
    pack, norms = pl.pallas_call(
        functools.partial(second_kernel, unit_devices),
        grid=(steps,),
        in_specs=[
            panel_spec,
            whole(unit_devices * 3 * groups, day_cols),
            end_spec,
            end_spec,
            whole(groups, unit_rows),
            days_spec,
        ],
        out_specs=[whole(2 * groups, width), whole(groups, lanes)],
        out_shape=[
            jax.ShapeDtypeStruct((2 * groups, width), f32),
            jax.ShapeDtypeStruct((groups, lanes), f32),
        ],
        compiler_params=params,
        name="unit_gradient",
    )(outcomes, all_sums, pre_end, post_start, cross, raised_days)
    all_pack = lax.all_gather(pack, "day", axis=0, tiled=True)
    updated, grads = pl.pallas_call(
        functools.partial(third_kernel, day_devices),
        grid=(steps,),
        in_specs=[
            panel_spec,
            whole(day_devices * 2 * groups, width),
            whole(groups, lanes),
            label_spec,
            group_spec,
            end_spec,
        ],
        out_specs=[group_spec, whole(2 * groups, day_cols)],
        out_shape=[
            jax.ShapeDtypeStruct((groups, unit_rows), f32),
            jax.ShapeDtypeStruct((2 * groups, day_cols), f32),
        ],
        compiler_params=params,
        name="time_gradient",
    )(outcomes, all_pack, norms, cohort, unit_logit, pre_end)
    all_grads = lax.all_gather(grads, ("unit", "day"), axis=0, tiled=True)
    return pl.pallas_call(
        functools.partial(fourth_kernel, unit_devices, day_devices),
        out_shape=[
            jax.ShapeDtypeStruct((groups, unit_rows), f32),
            jax.ShapeDtypeStruct((groups, day_cols), f32),
        ],
        compiler_params=params,
        name="new_weights",
    )(all_grads, updated, norms, all_pack, pre_end)


def solution(mesh):
    return jax.shard_map(
        local,
        mesh=mesh,
        in_specs=(P("unit", "day"), P("unit"), P(), P(), P(None, "unit"), P(None, "day")),
        out_specs=(P(None, "unit"), P(None, "day")),
        check_vma=False,
    )
```

```python
import functools

import jax
import jax.numpy as jnp
from jax import lax
from jax.experimental import pallas as pl
from jax.experimental.pallas import tpu as pltpu
from jax.sharding import PartitionSpec as P

step_rate = 16.0
f32 = jnp.float32
bf16 = jnp.bfloat16
lanes = 128
params = pltpu.CompilerParams(vmem_limit_bytes=24 * 1024 * 1024)


def split_left(value):
    first = value.astype(bf16).astype(f32)
    rest = value - first
    second = rest.astype(bf16).astype(f32)
    return [first, second, rest - second]


def left_of(value, other=None):
    other = jnp.zeros_like(value) if other is None else other
    return jnp.concatenate(split_left(value) + [other], axis=0).astype(bf16)


def split_panel(value):
    high = value.astype(bf16)
    return high, (value - high.astype(f32)).astype(bf16)


def rows_dot(left, high, low):
    return jnp.dot(left, high, preferred_element_type=f32) + jnp.dot(left, low, preferred_element_type=f32)


def days_dot(left, high, low):
    dims = (((1,), (1,)), ((), ()))
    return lax.dot_general(left, high, dims, preferred_element_type=f32) + lax.dot_general(
        left, low, dims, preferred_element_type=f32
    )


def add_terms(stack, groups):
    return stack[:groups] + stack[groups : 2 * groups] + stack[2 * groups : 3 * groups]


def tree_sum(values):
    values = list(values)
    while len(values) > 1:
        values = [values[i] + values[i + 1] for i in range(0, len(values), 2)]
    return values[0]


def column(row_ref):
    count = row_ref.shape[1]
    wide = jnp.broadcast_to(row_ref[...].astype(f32), (count, count))
    row = lax.broadcasted_iota(jnp.int32, (count, count), 0)
    lane = lax.broadcasted_iota(jnp.int32, (count, count), 1)
    return jnp.sum(jnp.where(row == lane, wide, 0.0), axis=1, keepdims=True).astype(jnp.int32)


def days_of(device, shape):
    return device * shape[1] + lax.broadcasted_iota(jnp.int32, shape, 1)


def first_kernel(
    all_count, chunks, panel, cohort, pre_row, post_row, unit_logit, time_logit, sums, cross, high_ref, low_ref, held, sems
):
    groups, day_cols = time_logit.shape
    unit_rows = panel.shape[0]
    rows = unit_rows // chunks
    copies = []
    for chunk in range(chunks):
        here = pl.ds(chunk * rows, rows)
        copies.append(pltpu.make_async_copy(panel.at[here], held.at[here], sems.at[chunk]))
        copies[-1].start()
    pre_end, post_start = column(pre_row), column(post_row)
    days = days_of(lax.axis_index("day"), (groups, day_cols))
    raised_time = jnp.where(days < pre_end, jnp.exp(time_logit[...]), 0.0)
    after_len = (all_count - post_start).astype(f32)
    coef = left_of(raised_time - jnp.where(days >= post_start, 1.0, 0.0) / after_len)
    fitted = jnp.zeros((groups, day_cols), f32)
    treat_sum = jnp.zeros((groups, day_cols), f32)
    norm = jnp.zeros((groups, 1), f32)
    treat_count = jnp.zeros((groups, 1), f32)
    ctrl_count = jnp.zeros((groups, 1), f32)
    label = lax.broadcasted_iota(jnp.int32, (groups, rows), 0)
    for chunk in range(chunks):
        here = pl.ds(chunk * rows, rows)
        treated = jnp.where(cohort[:, here] == label, 1.0, 0.0)
        control = jnp.where(cohort[:, here] > label, 1.0, 0.0)
        raised = jnp.exp(unit_logit[:, here]) * control
        left = left_of(raised, treated)
        norm += jnp.sum(raised, axis=1, keepdims=True)
        treat_count += jnp.sum(treated, axis=1, keepdims=True)
        ctrl_count += jnp.sum(control, axis=1, keepdims=True)
        copies[chunk].wait()
        high, low = split_panel(held[here, :])
        high_ref[here, :] = high
        low_ref[here, :] = low
        product = rows_dot(left, high, low)
        fitted += add_terms(product, groups)
        treat_sum += product[3 * groups :]
        cross[:, here] = add_terms(days_dot(coef, high, low), groups)
    sums[:, :day_cols] = fitted
    sums[:, day_cols : 2 * day_cols] = treat_sum
    lane = lax.broadcasted_iota(jnp.int32, (groups, lanes), 1)
    sums[:, 2 * day_cols :] = jnp.where(lane == 0, norm, jnp.where(lane == 1, treat_count, ctrl_count))


def second_kernel(unit_devices, half, chunks, *refs):
    sums, refs = refs[:unit_devices], refs[unit_devices:]
    logits, refs = refs[:half], refs[half:]
    high_ref, low_ref, cross, post, pre_row, part, lam, norms = refs
    groups, day_cols = lam.shape
    unit_rows = cross.shape[1]
    rows = unit_rows // chunks
    total = tree_sum(ref[...] for ref in sums)
    unit_norm = total[:, 2 * day_cols : 2 * day_cols + 1]
    treat_count = jnp.maximum(total[:, 2 * day_cols + 1 : 2 * day_cols + 2], 1.0)
    norms[...] = total[:, 2 * day_cols :]
    pre_end = column(pre_row)
    me = lax.axis_index("day")
    raised = []
    for k in range(half):
        days = days_of(jnp.bitwise_xor(me, k), (groups, day_cols))
        raised.append(jnp.where(days < pre_end, jnp.exp(logits[k][...]), 0.0))
    time_norm = tree_sum(jnp.sum(value, axis=1, keepdims=True) for value in raised)
    lam[...] = raised[0] / time_norm
    gap = total[:, :day_cols] / unit_norm - total[:, day_cols : 2 * day_cols] / treat_count
    left = left_of(jnp.where(days_of(me, (groups, day_cols)) < pre_end, gap, 0.0))
    for chunk in range(chunks):
        here = pl.ds(chunk * rows, rows)
        part[:groups, here] = add_terms(days_dot(left, high_ref[here, :], low_ref[here, :]), groups)
        part[groups:, here] = cross[:, here] / time_norm + post[:, here]


def third_kernel(half, chunks, *refs):
    parts, refs = refs[:half], refs[half:]
    high_ref, low_ref, norms, cohort, unit_logit, pre_row, scaled, grads, unit_sum = refs
    groups, unit_rows = unit_logit.shape
    rows = unit_rows // chunks
    unit_norm, ctrl_count = norms[:, 0:1], norms[:, 2:3]
    factor = -step_rate / jnp.sqrt(column(pre_row).astype(f32))
    label = lax.broadcasted_iota(jnp.int32, (groups, rows), 0)
    time_grad = jnp.zeros(grads.shape, f32)
    new_sum = jnp.zeros((groups, 1), f32)
    for chunk in range(chunks):
        here = pl.ds(chunk * rows, rows)
        whole = tree_sum(ref[:, here] for ref in parts)
        control = cohort[:, here] > label
        weights = jnp.where(control, jnp.exp(unit_logit[:, here]), 0.0) / unit_norm
        new = weights * jnp.exp(whole[:groups] * factor)
        new_sum += jnp.sum(new, axis=1, keepdims=True)
        scaled[:, here] = new * ctrl_count
        left = left_of(jnp.where(control, whole[groups:], 0.0))
        time_grad += add_terms(rows_dot(left, high_ref[here, :], low_ref[here, :]), groups)
    grads[...] = time_grad
    unit_sum[...] = jnp.broadcast_to(new_sum, unit_sum.shape)


def fourth_kernel(unit_devices, half, *refs):
    grads, refs = refs[:unit_devices], refs[unit_devices:]
    own_sums, refs = refs[:unit_devices], refs[unit_devices:]
    sent_sums, refs = refs[:unit_devices], refs[unit_devices:]
    lam, norms, moved, moved_sum, unit_total = refs
    first = lax.axis_index("day") < half
    own = tree_sum(ref[...] for ref in own_sums)
    sent = tree_sum(ref[...] for ref in sent_sums)
    unit_total[...] = jnp.where(first, own, sent)
    root = jnp.sqrt(jnp.maximum(norms[:, 2:3], 1.0))
    time_grad = tree_sum(ref[...] for ref in grads)
    new = lam[...] * jnp.exp(time_grad * (-step_rate / root))
    moved[...] = new
    moved_sum[...] = jnp.broadcast_to(jnp.sum(new, axis=1, keepdims=True), moved_sum.shape)


def local(outcomes, cohort, pre_end, post_start, unit_logit, time_logit):
    groups = pre_end.shape[0]
    unit_rows, day_cols = outcomes.shape
    day_devices = lax.axis_size("day")
    unit_devices = lax.axis_size("unit")
    half = day_devices // 2
    assert half * 2 == day_devices and half & (half - 1) == 0
    assert unit_devices & (unit_devices - 1) == 0
    chunks = 8
    labels = cohort[None, :]
    pre_row = pre_end[None, :]
    post_row = post_start[None, :]
    vmem = pl.BlockSpec(memory_space=pltpu.VMEM)

    def spread(value, unit_xor, day_xor, up):
        pairs = [
            (u * day_devices + d, (u ^ unit_xor) * day_devices + (d ^ day_xor) + up)
            for u in range(unit_devices)
            for d in range(half)
        ]
        return lax.ppermute(value, ("unit", "day"), pairs)

    def over_units(value):
        return [value] + [spread(value, k, 0, 0) for k in range(1, unit_devices)]

    def over_days(value):
        return [value] + [spread(value, 0, k, 0) for k in range(1, half)]

    def call(kernel, count, shapes, name, args, specs=None, **more):
        return pl.pallas_call(
            kernel,
            in_specs=specs or [vmem] * count,
            out_specs=[vmem] * len(shapes),
            out_shape=[jax.ShapeDtypeStruct(shape, kind) for shape, kind in shapes],
            compiler_params=params,
            name=name,
            **more,
        )(*args)

    logits = over_days(time_logit)
    sums, cross, high, low = call(
        functools.partial(first_kernel, day_devices * day_cols, chunks),
        6,
        [
            ((groups, 2 * day_cols + lanes), f32),
            ((groups, unit_rows), f32),
            ((unit_rows, day_cols), bf16),
            ((unit_rows, day_cols), bf16),
        ],
        "first_products",
        (outcomes, labels, pre_row, post_row, unit_logit, time_logit),
        specs=[pl.BlockSpec(memory_space=pltpu.HBM)] + [vmem] * 5,
        scratch_shapes=[pltpu.VMEM((unit_rows, day_cols), f32), pltpu.SemaphoreType.DMA((chunks,))],
    )
    all_sums = over_units(sums)
    downward = [
        (u * day_devices + d + half, u * day_devices + d) for u in range(unit_devices) for d in range(half)
    ]
    post = lax.ppermute(cross, ("unit", "day"), downward)
    args = (*all_sums, *logits, high, low, cross, post, pre_row)
    part, lam, norms = call(
        functools.partial(second_kernel, unit_devices, half, chunks),
        len(args),
        [((2 * groups, unit_rows), f32), ((groups, day_cols), f32), ((groups, lanes), f32)],
        "unit_gradient",
        args,
    )
    args = (*over_days(part), high, low, norms, labels, unit_logit, pre_row)
    scaled, grads, unit_sum = call(
        functools.partial(third_kernel, half, chunks),
        len(args),
        [((groups, unit_rows), f32), ((groups, day_cols), f32), ((groups, lanes), f32)],
        "time_gradient",
        args,
    )
    all_grads = over_units(grads)
    own_sums = over_units(unit_sum)
    sent_sums = [spread(unit_sum, k, 0, half) for k in range(unit_devices)]
    sent_scaled = spread(scaled, 0, 0, half)
    args = (*all_grads, *own_sums, *sent_sums, lam, norms)
    moved, moved_sum, unit_total = call(
        functools.partial(fourth_kernel, unit_devices, half),
        len(args),
        [((groups, day_cols), f32), ((groups, lanes), f32), ((groups, lanes), f32)],
        "new_time_weights",
        args,
    )
    first = lax.axis_index("day") < half
    unit_weights = jnp.where(first, scaled, sent_scaled) / unit_total[:, :1]
    day_total = tree_sum(value[:, :1] for value in over_days(moved_sum))
    time_weights = moved / day_total * pre_end.astype(f32)[:, None]
    return unit_weights, jnp.where(first, time_weights, 0.0)


def solution(mesh):
    return jax.shard_map(
        local,
        mesh=mesh,
        in_specs=(P("unit", "day"), P("unit"), P(), P(), P(None, "unit"), P(None, "day")),
        out_specs=(P(None, "unit"), P(None, "day")),
        check_vma=False,
    )
```

```python
import functools

import jax
import jax.numpy as jnp
from jax import lax
from jax.experimental import pallas as pl
from jax.experimental.pallas import tpu as pltpu
from jax.sharding import PartitionSpec as P

step_rate = 16.0
f32 = jnp.float32
bf16 = jnp.bfloat16
lanes = 128
params = pltpu.CompilerParams(vmem_limit_bytes=24 * 1024 * 1024)


def split_left(value):
    first = value.astype(bf16).astype(f32)
    rest = value - first
    second = rest.astype(bf16).astype(f32)
    return [first, second, rest - second]


def left_of(value, other=None):
    other = jnp.zeros_like(value) if other is None else other
    return jnp.concatenate(split_left(value) + [other], axis=0).astype(bf16)


def split_panel(value):
    high = value.astype(bf16)
    return high, (value - high.astype(f32)).astype(bf16)


def rows_dot(left, high, low):
    return jnp.dot(left, high, preferred_element_type=f32) + jnp.dot(left, low, preferred_element_type=f32)


def days_dot(left, high, low):
    dims = (((1,), (1,)), ((), ()))
    return lax.dot_general(left, high, dims, preferred_element_type=f32) + lax.dot_general(
        left, low, dims, preferred_element_type=f32
    )


def add_terms(stack, groups):
    return stack[:groups] + stack[groups : 2 * groups] + stack[2 * groups : 3 * groups]


def tree_sum(values):
    values = list(values)
    while len(values) > 1:
        values = [values[i] + values[i + 1] for i in range(0, len(values), 2)]
    return values[0]


def column(row_ref):
    count = row_ref.shape[1]
    wide = jnp.broadcast_to(row_ref[...].astype(f32), (count, count))
    row = lax.broadcasted_iota(jnp.int32, (count, count), 0)
    lane = lax.broadcasted_iota(jnp.int32, (count, count), 1)
    return jnp.sum(jnp.where(row == lane, wide, 0.0), axis=1, keepdims=True).astype(jnp.int32)


def days_of(device, shape):
    return device * shape[1] + lax.broadcasted_iota(jnp.int32, shape, 1)


def first_kernel(all_count, copies_out, chunks, *refs):
    arguments, refs = refs[:6], refs[6:]
    sums, cross, raised_units, raised_days, ends, high_ref, low_ref, *held, small_sems, sems = refs
    panel, held_panel = arguments[0], held[0]
    groups, day_cols = held[5].shape
    unit_rows = panel.shape[0]
    rows = unit_rows // chunks
    small = [
        pltpu.make_async_copy(source, target, small_sems.at[i])
        for i, (source, target) in enumerate(zip(arguments[1:], held[1:]))
    ]
    for copy in small:
        copy.start()
    copies = []
    for chunk in range(chunks):
        here = pl.ds(chunk * rows, rows)
        copies.append(pltpu.make_async_copy(panel.at[here], held_panel.at[here], sems.at[chunk]))
        copies[-1].start()
    for copy in small:
        copy.wait()
    cohort, pre_row, post_row, unit_logit, time_logit = held[1:]
    pre_end, post_start = column(pre_row), column(post_row)
    ends[...] = jnp.broadcast_to(pre_end.astype(f32), ends.shape)
    days = days_of(lax.axis_index("day"), (groups, day_cols))
    raised_time = jnp.where(days < pre_end, jnp.exp(time_logit[...]), 0.0)
    raised_days[...] = raised_time
    after_len = (all_count - post_start).astype(f32)
    coef = left_of(raised_time - jnp.where(days >= post_start, 1.0, 0.0) / after_len)
    fitted = jnp.zeros((groups, day_cols), f32)
    treat_sum = jnp.zeros((groups, day_cols), f32)
    norm = jnp.zeros((groups, 1), f32)
    treat_count = jnp.zeros((groups, 1), f32)
    ctrl_count = jnp.zeros((groups, 1), f32)
    label = lax.broadcasted_iota(jnp.int32, (groups, rows), 0)
    for chunk in range(chunks):
        here = pl.ds(chunk * rows, rows)
        treated = jnp.where(cohort[:, here] == label, 1.0, 0.0)
        control = jnp.where(cohort[:, here] > label, 1.0, 0.0)
        raised = jnp.exp(unit_logit[:, here]) * control
        raised_units[:, here] = raised
        left = left_of(raised, treated)
        norm += jnp.sum(raised, axis=1, keepdims=True)
        treat_count += jnp.sum(treated, axis=1, keepdims=True)
        ctrl_count += jnp.sum(control, axis=1, keepdims=True)
        copies[chunk].wait()
        high, low = split_panel(held_panel[here, :])
        high_ref[here, :] = high
        low_ref[here, :] = low
        product = rows_dot(left, high, low)
        fitted += add_terms(product, groups)
        treat_sum += product[3 * groups :]
        cross[:, here] = add_terms(days_dot(coef, high, low), groups)
    lane = lax.broadcasted_iota(jnp.int32, (groups, lanes), 1)
    norms = jnp.where(lane == 0, norm, jnp.where(lane == 1, treat_count, ctrl_count))
    for i in range(copies_out):
        here = pl.ds(i * groups, groups)
        sums[here, :day_cols] = fitted
        sums[here, day_cols : 2 * day_cols] = treat_sum
        sums[here, 2 * day_cols :] = norms


def second_kernel(unit_devices, chunks, sums, high_ref, low_ref, cross, post, raised_days, ends, pack, norms):
    groups, day_cols = raised_days.shape
    unit_rows = cross.shape[1]
    rows = unit_rows // chunks
    total = tree_sum(sums[pl.ds(u * groups, groups), :] for u in range(unit_devices))
    unit_norm = total[:, 2 * day_cols : 2 * day_cols + 1]
    treat_count = jnp.maximum(total[:, 2 * day_cols + 1 : 2 * day_cols + 2], 1.0)
    norms[...] = total[:, 2 * day_cols :]
    gap = total[:, :day_cols] / unit_norm - total[:, day_cols : 2 * day_cols] / treat_count
    days = days_of(lax.axis_index("day"), (groups, day_cols)).astype(f32)
    left = left_of(jnp.where(days < ends[:, 0:1], gap, 0.0))
    for chunk in range(chunks):
        here = pl.ds(chunk * rows, rows)
        pack[:groups, here] = add_terms(days_dot(left, high_ref[here, :], low_ref[here, :]), groups)
    pack[groups : 2 * groups, :unit_rows] = cross[...]
    pack[2 * groups :, :unit_rows] = post[...]
    time_norm = jnp.sum(raised_days[...], axis=1, keepdims=True)
    pack[:, unit_rows:] = jnp.broadcast_to(jnp.concatenate([time_norm] * 3, axis=0), (3 * groups, lanes))


def third_kernel(half, copies_out, chunks, *refs):
    parts, refs = refs[:half], refs[half:]
    high_ref, low_ref, norms, raised_units, raised_days, ends, scaled, lam, grads = refs
    groups, unit_rows = raised_units.shape
    day_cols = raised_days.shape[1]
    rows = unit_rows // chunks
    unit_norm, ctrl_count = norms[:, 0:1], norms[:, 2:3]
    factor = -step_rate / jnp.sqrt(ends[:, 0:1])
    time_norm = tree_sum(ref[:groups, unit_rows : unit_rows + 1] for ref in parts)
    lam[...] = raised_days[...] / time_norm
    time_grad = jnp.zeros((groups, day_cols), f32)
    new_sum = jnp.zeros((groups, 1), f32)
    for chunk in range(chunks):
        here = pl.ds(chunk * rows, rows)
        whole = tree_sum(ref[:, here] for ref in parts)
        raised = raised_units[:, here]
        new = raised / unit_norm * jnp.exp(whole[:groups] * factor)
        new_sum += jnp.sum(new, axis=1, keepdims=True)
        scaled[:, here] = new * ctrl_count
        shortfall = whole[groups : 2 * groups] / time_norm + whole[2 * groups :]
        left = left_of(jnp.where(raised > 0.0, shortfall, 0.0))
        time_grad += add_terms(rows_dot(left, high_ref[here, :], low_ref[here, :]), groups)
    for i in range(copies_out):
        here = pl.ds(i * groups, groups)
        grads[here, :day_cols] = time_grad
        grads[here, day_cols:] = jnp.broadcast_to(new_sum, (groups, lanes))


def fourth_kernel(unit_devices, grads, lam, norms, moved, totals):
    groups, day_cols = lam.shape
    total = tree_sum(grads[pl.ds(u * groups, groups), :] for u in range(unit_devices))
    root = jnp.sqrt(jnp.maximum(norms[:, 2:3], 1.0))
    new = lam[...] * jnp.exp(total[:, :day_cols] * (-step_rate / root))
    moved[...] = new
    lane = lax.broadcasted_iota(jnp.int32, (groups, lanes), 1)
    totals[...] = jnp.where(lane == 0, total[:, day_cols:], jnp.sum(new, axis=1, keepdims=True))


def fifth_kernel(half, *refs):
    totals, refs = refs[:half], refs[half:]
    sent_totals, scaled, sent_scaled, moved, ends, unit_weights, time_weights = refs
    first = lax.axis_index("day") < half
    own = jnp.where(first, totals[0][:, 0:1], sent_totals[:, 0:1])
    unit_weights[...] = jnp.where(first, scaled[...], sent_scaled[...]) / own
    day_total = tree_sum(ref[:, 1:2] for ref in totals)
    time_weights[...] = jnp.where(first, moved[...] / day_total * ends[:, 0:1], 0.0)


def local(outcomes, cohort, pre_end, post_start, unit_logit, time_logit):
    groups = pre_end.shape[0]
    unit_rows, day_cols = outcomes.shape
    day_devices = lax.axis_size("day")
    unit_devices = lax.axis_size("unit")
    half = day_devices // 2
    assert half * 2 == day_devices and half & (half - 1) == 0
    assert unit_devices & (unit_devices - 1) == 0
    chunks = 8
    vmem = pl.BlockSpec(memory_space=pltpu.VMEM)
    hbm = pl.BlockSpec(memory_space=pltpu.HBM)

    def spread(value, day_xor, up):
        pairs = [
            (u * day_devices + d, u * day_devices + (d ^ day_xor) + up) for u in range(unit_devices) for d in range(half)
        ]
        return lax.ppermute(value, ("unit", "day"), pairs)

    def over_days(value):
        return [value] + [spread(value, k, 0) for k in range(1, half)]

    def over_units(value):
        return lax.all_to_all(value, "unit", split_axis=0, concat_axis=0, tiled=True)

    def call(kernel, shapes, name, args, in_spec=vmem, **more):
        return pl.pallas_call(
            kernel,
            in_specs=[in_spec] * len(args),
            out_specs=[vmem] * len(shapes),
            out_shape=[jax.ShapeDtypeStruct(shape, kind) for shape, kind in shapes],
            compiler_params=params,
            name=name,
            **more,
        )(*args)

    arguments = (outcomes, cohort[None, :], pre_end[None, :], post_start[None, :], unit_logit, time_logit)
    sums, cross, raised_units, raised_days, ends, high, low = call(
        functools.partial(first_kernel, day_devices * day_cols, unit_devices, chunks),
        [
            ((unit_devices * groups, 2 * day_cols + lanes), f32),
            ((groups, unit_rows), f32),
            ((groups, unit_rows), f32),
            ((groups, day_cols), f32),
            ((groups, lanes), f32),
            ((unit_rows, day_cols), bf16),
            ((unit_rows, day_cols), bf16),
        ],
        "first_products",
        [pltpu.with_memory_space_constraint(argument, pltpu.HBM) for argument in arguments],
        in_spec=hbm,
        scratch_shapes=[pltpu.VMEM(argument.shape, argument.dtype) for argument in arguments]
        + [pltpu.SemaphoreType.DMA((5,)), pltpu.SemaphoreType.DMA((chunks,))],
    )
    downward = [
        (u * day_devices + d + half, u * day_devices + d) for u in range(unit_devices) for d in range(half)
    ]
    post = lax.ppermute(cross, ("unit", "day"), downward)
    all_sums = over_units(sums)
    pack, norms = call(
        functools.partial(second_kernel, unit_devices, chunks),
        [((3 * groups, unit_rows + lanes), f32), ((groups, lanes), f32)],
        "unit_gradient",
        (all_sums, high, low, cross, post, raised_days, ends),
    )
    scaled, lam, grads = call(
        functools.partial(third_kernel, half, unit_devices, chunks),
        [
            ((groups, unit_rows), f32),
            ((groups, day_cols), f32),
            ((unit_devices * groups, day_cols + lanes), f32),
        ],
        "time_gradient",
        (*over_days(pack), high, low, norms, raised_units, raised_days, ends),
    )
    sent_scaled = spread(scaled, 0, half)
    moved, totals = call(
        functools.partial(fourth_kernel, unit_devices),
        [((groups, day_cols), f32), ((groups, lanes), f32)],
        "new_time_weights",
        (over_units(grads), lam, norms),
    )
    sent_totals = spread(totals, 0, half)
    return call(
        functools.partial(fifth_kernel, half),
        [((groups, unit_rows), f32), ((groups, day_cols), f32)],
        "scale_weights",
        (*over_days(totals), sent_totals, scaled, sent_scaled, moved, ends),
    )


def solution(mesh):
    return jax.shard_map(
        local,
        mesh=mesh,
        in_specs=(P("unit", "day"), P("unit"), P(), P(), P(None, "unit"), P(None, "day")),
        out_specs=(P(None, "unit"), P(None, "day")),
        check_vma=False,
    )
```

```python
import functools

import jax
import jax.numpy as jnp
from jax import lax
from jax.experimental import pallas as pl
from jax.experimental.pallas import tpu as pltpu
from jax.sharding import PartitionSpec as P

step_rate = 16.0
f32 = jnp.float32
bf16 = jnp.bfloat16
lanes = 128
params = pltpu.CompilerParams(vmem_limit_bytes=24 * 1024 * 1024)


def split_left(value):
    first = value.astype(bf16).astype(f32)
    rest = value - first
    second = rest.astype(bf16).astype(f32)
    return [first, second, rest - second]


def left_of(value, other=None):
    other = jnp.zeros_like(value) if other is None else other
    return jnp.concatenate(split_left(value) + [other], axis=0).astype(bf16)


def split_panel(value):
    high = value.astype(bf16)
    return high, (value - high.astype(f32)).astype(bf16)


def rows_dot(left, high, low):
    return jnp.dot(left, high, preferred_element_type=f32) + jnp.dot(left, low, preferred_element_type=f32)


def days_dot(left, high, low):
    dims = (((1,), (1,)), ((), ()))
    return lax.dot_general(left, high, dims, preferred_element_type=f32) + lax.dot_general(
        left, low, dims, preferred_element_type=f32
    )


def add_terms(stack, groups):
    return stack[:groups] + stack[groups : 2 * groups] + stack[2 * groups : 3 * groups]


def tree_sum(values):
    values = list(values)
    while len(values) > 1:
        values = [values[i] + values[i + 1] for i in range(0, len(values), 2)]
    return values[0]


def column(row_ref):
    count = row_ref.shape[1]
    wide = jnp.broadcast_to(row_ref[...].astype(f32), (count, count))
    row = lax.broadcasted_iota(jnp.int32, (count, count), 0)
    lane = lax.broadcasted_iota(jnp.int32, (count, count), 1)
    return jnp.sum(jnp.where(row == lane, wide, 0.0), axis=1, keepdims=True).astype(jnp.int32)


def days_of(device, shape):
    return device * shape[1] + lax.broadcasted_iota(jnp.int32, shape, 1)


def first_kernel(all_count, chunks, *refs):
    arguments, refs = refs[:6], refs[6:]
    sums, cross, raised_units, raised_days, ends, high_ref, low_ref, *held, small_sems, sems = refs
    panel, held_panel = arguments[0], held[0]
    groups, day_cols = held[5].shape
    unit_rows = panel.shape[0]
    rows = unit_rows // chunks
    small = [
        pltpu.make_async_copy(source, target, small_sems.at[i])
        for i, (source, target) in enumerate(zip(arguments[1:], held[1:]))
    ]
    for copy in small:
        copy.start()
    copies = []
    for chunk in range(chunks):
        here = pl.ds(chunk * rows, rows)
        copies.append(pltpu.make_async_copy(panel.at[here], held_panel.at[here], sems.at[chunk]))
        copies[-1].start()
    for copy in small:
        copy.wait()
    cohort, pre_row, post_row, unit_logit, time_logit = held[1:]
    pre_end, post_start = column(pre_row), column(post_row)
    ends[...] = jnp.broadcast_to(pre_end.astype(f32), ends.shape)
    days = days_of(lax.axis_index("day"), (groups, day_cols))
    raised_time = jnp.where(days < pre_end, jnp.exp(time_logit[...]), 0.0)
    raised_days[...] = raised_time
    after_len = (all_count - post_start).astype(f32)
    coef = left_of(raised_time - jnp.where(days >= post_start, 1.0, 0.0) / after_len)
    fitted = jnp.zeros((groups, day_cols), f32)
    treat_sum = jnp.zeros((groups, day_cols), f32)
    norm = jnp.zeros((groups, 1), f32)
    treat_count = jnp.zeros((groups, 1), f32)
    ctrl_count = jnp.zeros((groups, 1), f32)
    label = lax.broadcasted_iota(jnp.int32, (groups, rows), 0)
    for chunk in range(chunks):
        here = pl.ds(chunk * rows, rows)
        treated = jnp.where(cohort[:, here] == label, 1.0, 0.0)
        control = jnp.where(cohort[:, here] > label, 1.0, 0.0)
        raised = jnp.exp(unit_logit[:, here]) * control
        raised_units[:, here] = raised
        left = left_of(raised, treated)
        norm += jnp.sum(raised, axis=1, keepdims=True)
        treat_count += jnp.sum(treated, axis=1, keepdims=True)
        ctrl_count += jnp.sum(control, axis=1, keepdims=True)
        copies[chunk].wait()
        high, low = split_panel(held_panel[here, :])
        high_ref[here, :] = high
        low_ref[here, :] = low
        product = rows_dot(left, high, low)
        fitted += add_terms(product, groups)
        treat_sum += product[3 * groups :]
        cross[:, here] = add_terms(days_dot(coef, high, low), groups)
    lane = lax.broadcasted_iota(jnp.int32, (groups, lanes), 1)
    norms = jnp.where(lane == 0, norm, jnp.where(lane == 1, treat_count, ctrl_count))
    sums[:, :day_cols] = fitted
    sums[:, day_cols : 2 * day_cols] = treat_sum
    sums[:, 2 * day_cols :] = norms


def second_kernel(chunks, sums, high_ref, low_ref, cross, post, raised_days, ends, pack, norms):
    groups, day_cols = raised_days.shape
    unit_rows = cross.shape[1]
    rows = unit_rows // chunks
    total = sums[0]
    for other in range(1, sums.shape[0]):
        total = total + sums[other]
    unit_norm = total[:, 2 * day_cols : 2 * day_cols + 1]
    treat_count = jnp.maximum(total[:, 2 * day_cols + 1 : 2 * day_cols + 2], 1.0)
    norms[...] = total[:, 2 * day_cols :]
    gap = total[:, :day_cols] / unit_norm - total[:, day_cols : 2 * day_cols] / treat_count
    days = days_of(lax.axis_index("day"), (groups, day_cols)).astype(f32)
    left = left_of(jnp.where(days < ends[:, 0:1], gap, 0.0))
    for chunk in range(chunks):
        here = pl.ds(chunk * rows, rows)
        pack[:groups, here] = add_terms(days_dot(left, high_ref[here, :], low_ref[here, :]), groups)
    pack[groups : 2 * groups, :unit_rows] = cross[...]
    pack[2 * groups :, :unit_rows] = post[...]
    time_norm = jnp.sum(raised_days[...], axis=1, keepdims=True)
    pack[:, unit_rows:] = jnp.broadcast_to(jnp.concatenate([time_norm] * 3, axis=0), (3 * groups, lanes))


def third_kernel(half, chunks, *refs):
    parts, refs = refs[:half], refs[half:]
    high_ref, low_ref, norms, raised_units, raised_days, ends, scaled, lam, grads = refs
    groups, unit_rows = raised_units.shape
    day_cols = raised_days.shape[1]
    rows = unit_rows // chunks
    unit_norm, ctrl_count = norms[:, 0:1], norms[:, 2:3]
    factor = -step_rate / jnp.sqrt(ends[:, 0:1])
    time_norm = tree_sum(ref[:groups, unit_rows : unit_rows + 1] for ref in parts)
    lam[...] = raised_days[...] / time_norm
    time_grad = jnp.zeros((groups, day_cols), f32)
    new_sum = jnp.zeros((groups, 1), f32)
    for chunk in range(chunks):
        here = pl.ds(chunk * rows, rows)
        whole = tree_sum(ref[:, here] for ref in parts)
        raised = raised_units[:, here]
        new = raised / unit_norm * jnp.exp(whole[:groups] * factor)
        new_sum += jnp.sum(new, axis=1, keepdims=True)
        scaled[:, here] = new * ctrl_count
        shortfall = whole[groups : 2 * groups] / time_norm + whole[2 * groups :]
        left = left_of(jnp.where(raised > 0.0, shortfall, 0.0))
        time_grad += add_terms(rows_dot(left, high_ref[here, :], low_ref[here, :]), groups)
    grads[:, :day_cols] = time_grad
    grads[:, day_cols:] = jnp.broadcast_to(new_sum, (groups, lanes))


def fourth_kernel(grads, lam, norms, moved, totals):
    groups, day_cols = lam.shape
    total = grads[0]
    for other in range(1, grads.shape[0]):
        total = total + grads[other]
    root = jnp.sqrt(jnp.maximum(norms[:, 2:3], 1.0))
    new = lam[...] * jnp.exp(total[:, :day_cols] * (-step_rate / root))
    moved[...] = new
    lane = lax.broadcasted_iota(jnp.int32, (groups, lanes), 1)
    totals[...] = jnp.where(lane == 0, total[:, day_cols:], jnp.sum(new, axis=1, keepdims=True))


def fifth_kernel(half, *refs):
    totals, refs = refs[:half], refs[half:]
    sent_totals, scaled, sent_scaled, moved, ends, unit_weights, time_weights = refs
    first = lax.axis_index("day") < half
    own = jnp.where(first, totals[0][:, 0:1], sent_totals[:, 0:1])
    unit_weights[...] = jnp.where(first, scaled[...], sent_scaled[...]) / own
    day_total = tree_sum(ref[:, 1:2] for ref in totals)
    time_weights[...] = jnp.where(first, moved[...] / day_total * ends[:, 0:1], 0.0)


def local(outcomes, cohort, pre_end, post_start, unit_logit, time_logit):
    groups = pre_end.shape[0]
    unit_rows, day_cols = outcomes.shape
    day_devices = lax.axis_size("day")
    unit_devices = lax.axis_size("unit")
    half = day_devices // 2
    assert half * 2 == day_devices and half & (half - 1) == 0
    assert unit_devices & (unit_devices - 1) == 0
    chunks = 8
    vmem = pl.BlockSpec(memory_space=pltpu.VMEM)
    hbm = pl.BlockSpec(memory_space=pltpu.HBM)

    def spread(value, day_xor, up):
        pairs = [
            (u * day_devices + d, u * day_devices + (d ^ day_xor) + up) for u in range(unit_devices) for d in range(half)
        ]
        return lax.ppermute(value, ("unit", "day"), pairs)

    def over_days(value):
        return [value] + [spread(value, k, 0) for k in range(1, half)]

    def gather_step(value, low, count):
        starts = [u for u in range(unit_devices) if u // low % count == 0]
        members = [[u + low * i for i in range(count)] for u in starts]
        return lax.all_gather(value, "unit", axis_index_groups=members)

    def over_units(value, digits):
        low = 1
        for count in digits:
            if low > 1:
                value = jnp.sum(value, axis=0)
            value = gather_step(value, low, count)
            low *= count
        return value

    def call(kernel, shapes, name, args, in_spec=vmem, **more):
        return pl.pallas_call(
            kernel,
            in_specs=[in_spec] * len(args),
            out_specs=[vmem] * len(shapes),
            out_shape=[jax.ShapeDtypeStruct(shape, kind) for shape, kind in shapes],
            compiler_params=params,
            name=name,
            **more,
        )(*args)

    arguments = (outcomes, cohort[None, :], pre_end[None, :], post_start[None, :], unit_logit, time_logit)
    sums, cross, raised_units, raised_days, ends, high, low = call(
        functools.partial(first_kernel, day_devices * day_cols, chunks),
        [
            ((groups, 2 * day_cols + lanes), f32),
            ((groups, unit_rows), f32),
            ((groups, unit_rows), f32),
            ((groups, day_cols), f32),
            ((groups, lanes), f32),
            ((unit_rows, day_cols), bf16),
            ((unit_rows, day_cols), bf16),
        ],
        "first_products",
        [pltpu.with_memory_space_constraint(argument, pltpu.HBM) for argument in arguments],
        in_spec=hbm,
        scratch_shapes=[pltpu.VMEM(argument.shape, argument.dtype) for argument in arguments]
        + [pltpu.SemaphoreType.DMA((5,)), pltpu.SemaphoreType.DMA((chunks,))],
    )
    downward = [
        (u * day_devices + d + half, u * day_devices + d) for u in range(unit_devices) for d in range(half)
    ]
    post = lax.ppermute(cross, ("unit", "day"), downward)
    all_sums = over_units(sums, [2] * (unit_devices.bit_length() - 1))
    pack, norms = call(
        functools.partial(second_kernel, chunks),
        [((3 * groups, unit_rows + lanes), f32), ((groups, lanes), f32)],
        "unit_gradient",
        (all_sums, high, low, cross, post, raised_days, ends),
    )
    scaled, lam, grads = call(
        functools.partial(third_kernel, half, chunks),
        [
            ((groups, unit_rows), f32),
            ((groups, day_cols), f32),
            ((groups, day_cols + lanes), f32),
        ],
        "time_gradient",
        (*over_days(pack), high, low, norms, raised_units, raised_days, ends),
    )
    sent_scaled = spread(scaled, 0, half)
    moved, totals = call(
        fourth_kernel,
        [((groups, day_cols), f32), ((groups, lanes), f32)],
        "new_time_weights",
        (over_units(grads, [2, unit_devices // 2]), lam, norms),
    )
    sent_totals = spread(totals, 0, half)
    return call(
        functools.partial(fifth_kernel, half),
        [((groups, unit_rows), f32), ((groups, day_cols), f32)],
        "scale_weights",
        (*over_days(totals), sent_totals, scaled, sent_scaled, moved, ends),
    )


def solution(mesh):
    return jax.shard_map(
        local,
        mesh=mesh,
        in_specs=(P("unit", "day"), P("unit"), P(), P(), P(None, "unit"), P(None, "day")),
        out_specs=(P(None, "unit"), P(None, "day")),
        check_vma=False,
    )
```

```python
import functools

import jax
import jax.numpy as jnp
from jax import lax
from jax.experimental import pallas as pl
from jax.experimental.pallas import tpu as pltpu
from jax.sharding import PartitionSpec as P

step_rate = 16.0
f32 = jnp.float32
bf16 = jnp.bfloat16
lanes = 128
params = pltpu.CompilerParams(vmem_limit_bytes=24 * 1024 * 1024)


def split_left(value):
    first = value.astype(bf16).astype(f32)
    rest = value - first
    second = rest.astype(bf16).astype(f32)
    return [first, second, rest - second]


def left_of(value, other=None):
    other = jnp.zeros_like(value) if other is None else other
    return jnp.concatenate(split_left(value) + [other], axis=0).astype(bf16)


def split_panel(value):
    high = value.astype(bf16)
    return high, (value - high.astype(f32)).astype(bf16)


def rows_dot(left, high, low):
    return jnp.dot(left, high, preferred_element_type=f32) + jnp.dot(left, low, preferred_element_type=f32)


def days_dot(left, high, low):
    dims = (((1,), (1,)), ((), ()))
    return lax.dot_general(left, high, dims, preferred_element_type=f32) + lax.dot_general(
        left, low, dims, preferred_element_type=f32
    )


def add_terms(stack, groups):
    return stack[:groups] + stack[groups : 2 * groups] + stack[2 * groups : 3 * groups]


def tree_sum(values):
    values = list(values)
    while len(values) > 1:
        values = [values[i] + values[i + 1] for i in range(0, len(values), 2)]
    return values[0]


def column(row_ref):
    count = row_ref.shape[1]
    wide = jnp.broadcast_to(row_ref[...].astype(f32), (count, count))
    row = lax.broadcasted_iota(jnp.int32, (count, count), 0)
    lane = lax.broadcasted_iota(jnp.int32, (count, count), 1)
    return jnp.sum(jnp.where(row == lane, wide, 0.0), axis=1, keepdims=True).astype(jnp.int32)


def days_of(device, shape):
    return device * shape[1] + lax.broadcasted_iota(jnp.int32, shape, 1)


def first_kernel(all_count, chunks, *refs):
    arguments, refs = refs[:6], refs[6:]
    sums, raised_units, raised_days, coef, ends, high_ref, low_ref, *held, left_ref, small_sems, sems = refs
    panel, held_panel = arguments[0], held[0]
    groups, day_cols = held[5].shape
    unit_rows = panel.shape[0]
    rows = unit_rows // chunks
    small = [
        pltpu.make_async_copy(source, target, small_sems.at[i])
        for i, (source, target) in enumerate(zip(arguments[1:], held[1:]))
    ]
    for copy in small:
        copy.start()
    copies = []
    for chunk in range(chunks):
        here = pl.ds(chunk * rows, rows)
        copies.append(pltpu.make_async_copy(panel.at[here], held_panel.at[here], sems.at[chunk]))
        copies[-1].start()
    for copy in small:
        copy.wait()
    cohort, pre_row, post_row, unit_logit, time_logit = held[1:]
    label = lax.broadcasted_iota(jnp.int32, (groups, unit_rows), 0)
    treated = jnp.where(cohort[...] == label, 1.0, 0.0)
    control = jnp.where(cohort[...] > label, 1.0, 0.0)
    raised = jnp.exp(unit_logit[...]) * control
    raised_units[...] = raised
    left_ref[...] = left_of(raised, treated)
    lane = lax.broadcasted_iota(jnp.int32, (groups, lanes), 1)
    sums[:, 2 * day_cols :] = jnp.where(
        lane == 0,
        jnp.sum(raised, axis=1, keepdims=True),
        jnp.where(
            lane == 1, jnp.sum(treated, axis=1, keepdims=True), jnp.sum(control, axis=1, keepdims=True)
        ),
    )
    pre_end, post_start = column(pre_row), column(post_row)
    ends[...] = jnp.broadcast_to(pre_end.astype(f32), ends.shape)
    days = days_of(lax.axis_index("day"), (groups, day_cols))
    raised_time = jnp.where(days < pre_end, jnp.exp(time_logit[...]), 0.0)
    raised_days[...] = raised_time
    after_len = (all_count - post_start).astype(f32)
    coef[...] = left_of(raised_time - jnp.where(days >= post_start, 1.0, 0.0) / after_len)
    product = jnp.zeros((4 * groups, day_cols), f32)
    for chunk in range(chunks):
        here = pl.ds(chunk * rows, rows)
        copies[chunk].wait()
        high, low = split_panel(held_panel[here, :])
        high_ref[here, :] = high
        low_ref[here, :] = low
        product += rows_dot(left_ref[:, here], high, low)
    sums[:, :day_cols] = add_terms(product, groups)
    sums[:, day_cols : 2 * day_cols] = product[3 * groups :]


def cross_kernel(chunks, coef, high_ref, low_ref, cross):
    groups, unit_rows = cross.shape
    rows = unit_rows // chunks
    for chunk in range(chunks):
        here = pl.ds(chunk * rows, rows)
        cross[:, here] = add_terms(days_dot(coef[...], high_ref[here, :], low_ref[here, :]), groups)


def add_kernel(left, right, *refs):
    refs[-1][...] = left[...] + right[...]


def second_kernel(chunks, sums, other_sums, high_ref, low_ref, cross, post, raised_days, ends, pack, norms):
    groups, day_cols = raised_days.shape
    unit_rows = cross.shape[1]
    rows = unit_rows // chunks
    total = sums[...] + other_sums[...]
    unit_norm = total[:, 2 * day_cols : 2 * day_cols + 1]
    treat_count = jnp.maximum(total[:, 2 * day_cols + 1 : 2 * day_cols + 2], 1.0)
    norms[...] = total[:, 2 * day_cols :]
    gap = total[:, :day_cols] / unit_norm - total[:, day_cols : 2 * day_cols] / treat_count
    days = days_of(lax.axis_index("day"), (groups, day_cols)).astype(f32)
    left = left_of(jnp.where(days < ends[:, 0:1], gap, 0.0))
    for chunk in range(chunks):
        here = pl.ds(chunk * rows, rows)
        pack[:groups, here] = add_terms(days_dot(left, high_ref[here, :], low_ref[here, :]), groups)
    pack[groups : 2 * groups, :unit_rows] = cross[...]
    pack[2 * groups :, :unit_rows] = post[...]
    time_norm = jnp.sum(raised_days[...], axis=1, keepdims=True)
    pack[:, unit_rows:] = jnp.broadcast_to(jnp.concatenate([time_norm] * 3, axis=0), (3 * groups, lanes))


def third_kernel(half, chunks, *refs):
    parts, refs = refs[:half], refs[half:]
    high_ref, low_ref, norms, raised_units, raised_days, ends, scaled, lam, grads = refs
    groups, unit_rows = raised_units.shape
    day_cols = raised_days.shape[1]
    rows = unit_rows // chunks
    unit_norm, ctrl_count = norms[:, 0:1], norms[:, 2:3]
    factor = -step_rate / jnp.sqrt(ends[:, 0:1])
    time_norm = tree_sum(ref[:groups, unit_rows : unit_rows + 1] for ref in parts)
    lam[...] = raised_days[...] / time_norm
    time_grad = jnp.zeros((groups, day_cols), f32)
    new_sum = jnp.zeros((groups, 1), f32)
    for chunk in range(chunks):
        here = pl.ds(chunk * rows, rows)
        whole = tree_sum(ref[:, here] for ref in parts)
        raised = raised_units[:, here]
        new = raised / unit_norm * jnp.exp(whole[:groups] * factor)
        new_sum += jnp.sum(new, axis=1, keepdims=True)
        scaled[:, here] = new * ctrl_count
        shortfall = whole[groups : 2 * groups] / time_norm + whole[2 * groups :]
        left = left_of(jnp.where(raised > 0.0, shortfall, 0.0))
        time_grad += add_terms(rows_dot(left, high_ref[here, :], low_ref[here, :]), groups)
    grads[:, :day_cols] = time_grad
    grads[:, day_cols:] = jnp.broadcast_to(new_sum, (groups, lanes))


def fourth_kernel(grads, other_grads, lam, norms, moved, totals):
    groups, day_cols = lam.shape
    total = grads[...] + other_grads[...]
    root = jnp.sqrt(jnp.maximum(norms[:, 2:3], 1.0))
    new = lam[...] * jnp.exp(total[:, :day_cols] * (-step_rate / root))
    moved[...] = new
    lane = lax.broadcasted_iota(jnp.int32, (groups, lanes), 1)
    totals[...] = jnp.where(lane == 0, total[:, day_cols:], jnp.sum(new, axis=1, keepdims=True))


def fifth_kernel(half, *refs):
    totals, refs = refs[:half], refs[half:]
    sent_totals, scaled, sent_scaled, moved, ends, unit_weights, time_weights = refs
    first = lax.axis_index("day") < half
    own = jnp.where(first, totals[0][:, 0:1], sent_totals[:, 0:1])
    unit_weights[...] = jnp.where(first, scaled[...], sent_scaled[...]) / own
    day_total = tree_sum(ref[:, 1:2] for ref in totals)
    time_weights[...] = jnp.where(first, moved[...] / day_total * ends[:, 0:1], 0.0)


def local(outcomes, cohort, pre_end, post_start, unit_logit, time_logit):
    groups = pre_end.shape[0]
    unit_rows, day_cols = outcomes.shape
    day_devices = lax.axis_size("day")
    unit_devices = lax.axis_size("unit")
    half = day_devices // 2
    assert half * 2 == day_devices and half & (half - 1) == 0
    assert unit_devices & (unit_devices - 1) == 0
    chunks = 8
    beside = pl.CostEstimate(flops=10**10, bytes_accessed=0, transcendentals=0)
    vmem = pl.BlockSpec(memory_space=pltpu.VMEM)
    hbm = pl.BlockSpec(memory_space=pltpu.HBM)

    def spread(value, unit_xor, day_xor, up):
        pairs = [
            (u * day_devices + d, (u ^ unit_xor) * day_devices + (d ^ day_xor) + up)
            for u in range(unit_devices)
            for d in range(half)
        ]
        return lax.ppermute(value, ("unit", "day"), pairs)

    def over_days(value):
        return [value] + [spread(value, 0, k, 0) for k in range(1, half)]

    def over_units(value, after=()):
        weight = 1
        while 2 * weight < unit_devices:
            args = (value, spread(value, weight, 0, 0), *after)
            (value,) = call(
                add_kernel,
                [(value.shape, f32)],
                "add_halves",
                args,
                in_specs=[vmem, vmem] + [pl.BlockSpec(memory_space=pl.ANY)] * len(after),
                cost_estimate=beside,
            )
            weight, after = 2 * weight, ()
        return value, spread(value, weight, 0, 0)

    def call(kernel, shapes, name, args, in_specs=None, **more):
        return pl.pallas_call(
            kernel,
            in_specs=in_specs or [vmem] * len(args),
            out_specs=[vmem] * len(shapes),
            out_shape=[jax.ShapeDtypeStruct(shape, kind) for shape, kind in shapes],
            compiler_params=params,
            name=name,
            **more,
        )(*args)

    arguments = (outcomes, cohort[None, :], pre_end[None, :], post_start[None, :], unit_logit, time_logit)
    sums, raised_units, raised_days, coef, ends, high, low = call(
        functools.partial(first_kernel, day_devices * day_cols, 4),
        [
            ((groups, 2 * day_cols + lanes), f32),
            ((groups, unit_rows), f32),
            ((groups, day_cols), f32),
            ((4 * groups, day_cols), bf16),
            ((groups, lanes), f32),
            ((unit_rows, day_cols), bf16),
            ((unit_rows, day_cols), bf16),
        ],
        "first_product",
        [pltpu.with_memory_space_constraint(argument, pltpu.HBM) for argument in arguments],
        in_specs=[hbm] * len(arguments),
        scratch_shapes=[pltpu.VMEM(argument.shape, argument.dtype) for argument in arguments]
        + [
            pltpu.VMEM((4 * groups, unit_rows), bf16),
            pltpu.SemaphoreType.DMA((5,)),
            pltpu.SemaphoreType.DMA((4,)),
        ],
    )
    (cross,) = call(
        functools.partial(cross_kernel, chunks),
        [((groups, unit_rows), f32)],
        "time_product",
        (coef, high, low),
        cost_estimate=pl.CostEstimate(
            flops=4 * 32 * unit_rows * day_cols, bytes_accessed=4 * unit_rows * day_cols, transcendentals=0
        ),
    )
    downward = [
        (u * day_devices + d + half, u * day_devices + d) for u in range(unit_devices) for d in range(half)
    ]
    post = lax.ppermute(cross, ("unit", "day"), downward)
    all_sums = over_units(sums, (cross,))
    pack, norms = call(
        functools.partial(second_kernel, chunks),
        [((3 * groups, unit_rows + lanes), f32), ((groups, lanes), f32)],
        "unit_gradient",
        (*all_sums, high, low, cross, post, raised_days, ends),
    )
    scaled, lam, grads = call(
        functools.partial(third_kernel, half, chunks),
        [
            ((groups, unit_rows), f32),
            ((groups, day_cols), f32),
            ((groups, day_cols + lanes), f32),
        ],
        "time_gradient",
        (*over_days(pack), high, low, norms, raised_units, raised_days, ends),
    )
    sent_scaled = spread(scaled, 0, 0, half)
    moved, totals = call(
        fourth_kernel,
        [((groups, day_cols), f32), ((groups, lanes), f32)],
        "new_time_weights",
        (*over_units(grads), lam, norms),
    )
    all_totals = over_days(totals)
    sent_totals = spread(totals, 0, 0, half)
    return call(
        functools.partial(fifth_kernel, half),
        [((groups, unit_rows), f32), ((groups, day_cols), f32)],
        "scale_weights",
        (*all_totals, sent_totals, scaled, sent_scaled, moved, ends),
    )


def solution(mesh):
    return jax.shard_map(
        local,
        mesh=mesh,
        in_specs=(P("unit", "day"), P("unit"), P(), P(), P(None, "unit"), P(None, "day")),
        out_specs=(P(None, "unit"), P(None, "day")),
        check_vma=False,
    )
```

```python
import functools

import jax
import jax.numpy as jnp
from jax import lax
from jax.experimental import pallas as pl
from jax.experimental.pallas import tpu as pltpu
from jax.sharding import PartitionSpec as P

step_rate = 16.0
f32 = jnp.float32
bf16 = jnp.bfloat16
lanes = 128
params = pltpu.CompilerParams(vmem_limit_bytes=24 * 1024 * 1024)
vmem = pl.BlockSpec(memory_space=pltpu.VMEM)
hbm = pl.BlockSpec(memory_space=pltpu.HBM)
any_space = pl.BlockSpec(memory_space=pl.ANY)


def split_left(value):
    first = value.astype(bf16).astype(f32)
    rest = value - first
    second = rest.astype(bf16).astype(f32)
    return [first, second, rest - second]


def left_of(value, other=None):
    other = jnp.zeros_like(value) if other is None else other
    return jnp.concatenate(split_left(value) + [other], axis=0).astype(bf16)


def split_panel(value):
    high = value.astype(bf16)
    return high, (value - high.astype(f32)).astype(bf16)


def rows_dot(left, high, low):
    return jnp.dot(left, high, preferred_element_type=f32) + jnp.dot(left, low, preferred_element_type=f32)


def days_dot(left, high, low):
    dims = (((1,), (1,)), ((), ()))
    return lax.dot_general(left, high, dims, preferred_element_type=f32) + lax.dot_general(
        left, low, dims, preferred_element_type=f32
    )


def add_terms(stack, groups):
    return stack[:groups] + stack[groups : 2 * groups] + stack[2 * groups : 3 * groups]


def tree_sum(values):
    values = list(values)
    while len(values) > 1:
        values = [values[i] + values[i + 1] for i in range(0, len(values), 2)]
    return values[0]


def column(row_ref):
    count = row_ref.shape[1]
    wide = jnp.broadcast_to(row_ref[...].astype(f32), (count, count))
    row = lax.broadcasted_iota(jnp.int32, (count, count), 0)
    lane = lax.broadcasted_iota(jnp.int32, (count, count), 1)
    return jnp.sum(jnp.where(row == lane, wide, 0.0), axis=1, keepdims=True).astype(jnp.int32)


def days_of(device, shape):
    return device * shape[1] + lax.broadcasted_iota(jnp.int32, shape, 1)


def fetch(sources, targets, sems):
    copies = [pltpu.make_async_copy(*pair, sems.at[i]) for i, pair in enumerate(zip(sources, targets))]
    for copy in copies:
        copy.start()
    return copies


def fetch_rows(source, target, sems, chunks):
    rows = source.shape[0] // chunks
    parts = [pl.ds(chunk * rows, rows) for chunk in range(chunks)]
    copies = fetch([source.at[here] for here in parts], [target.at[here] for here in parts], sems)
    return list(zip(parts, copies))


def wait_all(copies):
    for copy in copies:
        copy.wait()


def repeat_out(block, out, sems):
    rows = block.shape[0]
    places = [out.at[pl.ds(i * rows, rows)] for i in range(out.shape[0] // rows)]
    wait_all(fetch([block] * len(places), places, sems))


def first_kernel(all_count, half, chunks, *refs):
    arguments, refs = refs[:6], refs[6:]
    out, cross, *held, block, left_ref, small_sems, panel_sems, out_sems = refs
    groups, day_cols = held[5].shape
    unit_rows = held[0].shape[0]
    small = fetch(arguments[1:], held[1:], small_sems)
    parts = fetch_rows(arguments[0], held[0], panel_sems, chunks)
    panel, cohort, _, post_row, unit_logit, _ = held
    wait_all(small)
    me = lax.axis_index("day")

    @pl.when(me < half)
    def _():
        label = lax.broadcasted_iota(jnp.int32, (groups, unit_rows), 0)
        treated = jnp.where(cohort[...] == label, 1.0, 0.0)
        control = jnp.where(cohort[...] > label, 1.0, 0.0)
        raised = jnp.exp(unit_logit[...]) * control
        left_ref[...] = left_of(raised, treated)
        lane = lax.broadcasted_iota(jnp.int32, (groups, lanes), 1)
        block[:, 2 * day_cols :] = jnp.where(
            lane == 0,
            jnp.sum(raised, axis=1, keepdims=True),
            jnp.where(
                lane == 1, jnp.sum(treated, axis=1, keepdims=True), jnp.sum(control, axis=1, keepdims=True)
            ),
        )
        product = jnp.zeros((4 * groups, day_cols), f32)
        for here, copy in parts:
            copy.wait()
            product += rows_dot(left_ref[:, here], *split_panel(panel[here, :]))
        block[:, :day_cols] = add_terms(product, groups)
        block[:, day_cols : 2 * day_cols] = product[3 * groups :]
        repeat_out(block, out, out_sems)

    @pl.when(me >= half)
    def _():
        post_start = column(post_row)
        after = jnp.where(days_of(me, (groups, day_cols)) >= post_start, 1.0, 0.0)
        left = left_of(after / (all_count - post_start).astype(f32))
        for here, copy in parts:
            copy.wait()
            cross[:, here] = add_terms(days_dot(left, *split_panel(panel[here, :])), groups)


def token_kernel(value, token):
    token[...] = value[:, : token.shape[1]]


def second_kernel(chunks, unit_devices, half, *refs):
    arguments, refs = refs[:6], refs[6:]
    sums, post, _, pack, norms, raised_units, raised_days, ends, high_ref, low_ref, *refs = refs
    held, small_sems, panel_sems = refs[:6], refs[6], refs[7]
    groups, day_cols = raised_days.shape
    unit_rows = raised_units.shape[1]
    small = fetch(arguments[1:], held[1:], small_sems)
    parts = fetch_rows(arguments[0], held[0], panel_sems, chunks)
    panel, cohort, pre_row, _, unit_logit, time_logit = held
    total = tree_sum(sums[pl.ds(u * groups, groups), :] for u in range(unit_devices))
    unit_norm = total[:, 2 * day_cols : 2 * day_cols + 1]
    treat_count = jnp.maximum(total[:, 2 * day_cols + 1 : 2 * day_cols + 2], 1.0)
    norms[...] = total[:, 2 * day_cols :]
    pack[2 * groups :, :unit_rows] = post[...]
    wait_all(small)
    pre_end = column(pre_row)
    ends[...] = jnp.broadcast_to(pre_end.astype(f32), ends.shape)
    before = days_of(lax.axis_index("day"), (groups, day_cols)) < pre_end
    gap = total[:, :day_cols] / unit_norm - total[:, day_cols : 2 * day_cols] / treat_count
    raised_time = jnp.where(before, jnp.exp(time_logit[...]), 0.0)
    raised_days[...] = raised_time
    time_norm = jnp.sum(raised_time, axis=1, keepdims=True)
    pack[:, unit_rows:] = jnp.broadcast_to(jnp.concatenate([time_norm] * 3, axis=0), (3 * groups, lanes))
    left = split_left(jnp.where(before, gap, 0.0)) + split_left(raised_time)
    left = jnp.concatenate(left, axis=0).astype(bf16)
    label = lax.broadcasted_iota(jnp.int32, (groups, unit_rows), 0)
    raised_units[...] = jnp.where(cohort[...] > label, jnp.exp(unit_logit[...]), 0.0)
    for here, copy in parts:
        copy.wait()
        high, low = split_panel(panel[here, :])
        high_ref[here, :] = high
        low_ref[here, :] = low
        product = days_dot(left, high, low)
        pack[:groups, here] = add_terms(product, groups)
        pack[groups : 2 * groups, here] = add_terms(product[3 * groups :], groups)


def third_kernel(half, chunks, *refs):
    parts, refs = refs[:half], refs[half:]
    high_ref, low_ref, norms, raised_units, raised_days, ends, scaled, lam, out, block, out_sems = refs
    groups, unit_rows = raised_units.shape
    day_cols = raised_days.shape[1]
    rows = unit_rows // chunks
    unit_norm, ctrl_count = norms[:, 0:1], norms[:, 2:3]
    factor = -step_rate / jnp.sqrt(ends[:, 0:1])
    time_norm = tree_sum(ref[:groups, unit_rows : unit_rows + 1] for ref in parts)
    lam[...] = raised_days[...] / time_norm
    time_grad = jnp.zeros((groups, day_cols), f32)
    new_sum = jnp.zeros((groups, 1), f32)
    for chunk in range(chunks):
        here = pl.ds(chunk * rows, rows)
        whole = tree_sum(ref[:, here] for ref in parts)
        raised = raised_units[:, here]
        new = raised / unit_norm * jnp.exp(whole[:groups] * factor)
        new_sum += jnp.sum(new, axis=1, keepdims=True)
        scaled[:, here] = new * ctrl_count
        shortfall = whole[groups : 2 * groups] / time_norm - whole[2 * groups :]
        left = left_of(jnp.where(raised > 0.0, shortfall, 0.0))
        time_grad += add_terms(rows_dot(left, high_ref[here, :], low_ref[here, :]), groups)
    block[:, :day_cols] = time_grad
    block[:, day_cols:] = jnp.broadcast_to(new_sum, (groups, lanes))
    repeat_out(block, out, out_sems)


def fourth_kernel(unit_devices, grads, lam, norms, moved, totals):
    groups, day_cols = lam.shape
    total = tree_sum(grads[pl.ds(u * groups, groups), :] for u in range(unit_devices))
    root = jnp.sqrt(jnp.maximum(norms[:, 2:3], 1.0))
    new = lam[...] * jnp.exp(total[:, :day_cols] * (-step_rate / root))
    moved[...] = new
    lane = lax.broadcasted_iota(jnp.int32, (groups, lanes), 1)
    totals[...] = jnp.where(lane == 0, total[:, day_cols:], jnp.sum(new, axis=1, keepdims=True))


def fifth_kernel(half, *refs):
    totals, refs = refs[:half], refs[half:]
    sent_totals, scaled, sent_scaled, moved, ends, unit_weights, time_weights = refs
    first = lax.axis_index("day") < half
    own = jnp.where(first, totals[0][:, 0:1], sent_totals[:, 0:1])
    unit_weights[...] = jnp.where(first, scaled[...], sent_scaled[...]) / own
    day_total = tree_sum(ref[:, 1:2] for ref in totals)
    time_weights[...] = jnp.where(first, moved[...] / day_total * ends[:, 0:1], 0.0)


def local(outcomes, cohort, pre_end, post_start, unit_logit, time_logit):
    groups = pre_end.shape[0]
    unit_rows, day_cols = outcomes.shape
    day_devices = lax.axis_size("day")
    unit_devices = lax.axis_size("unit")
    half = day_devices // 2
    assert half * 2 == day_devices and half & (half - 1) == 0
    assert unit_devices & (unit_devices - 1) == 0
    chunks = 4
    beside = pl.CostEstimate(flops=10**10, bytes_accessed=0, transcendentals=0)

    def spread(value, day_xor, up):
        pairs = [
            (u * day_devices + d, u * day_devices + (d ^ day_xor) + up) for u in range(unit_devices) for d in range(half)
        ]
        return lax.ppermute(value, ("unit", "day"), pairs)

    def over_days(value):
        return [value] + [spread(value, k, 0) for k in range(1, half)]

    def over_units(value):
        return lax.all_to_all(value, "unit", split_axis=0, concat_axis=0, tiled=True)

    def call(kernel, shapes, name, args, in_specs=None, out_specs=None, **more):
        return pl.pallas_call(
            kernel,
            in_specs=in_specs or [vmem] * len(args),
            out_specs=out_specs or [vmem] * len(shapes),
            out_shape=[
                shape if isinstance(shape, type(in_hbm)) else jax.ShapeDtypeStruct(*shape) for shape in shapes
            ],
            compiler_params=params,
            name=name,
            **more,
        )(*args)

    arguments = (outcomes, cohort[None, :], pre_end[None, :], post_start[None, :], unit_logit, time_logit)
    fixed = [pltpu.with_memory_space_constraint(argument, pltpu.HBM) for argument in arguments]
    held = [pltpu.VMEM(argument.shape, argument.dtype) for argument in arguments]
    small_sems, panel_sems = pltpu.SemaphoreType.DMA((5,)), pltpu.SemaphoreType.DMA((chunks,))
    out_sems = pltpu.SemaphoreType.DMA((unit_devices,))
    width = 2 * day_cols + lanes
    in_hbm = pltpu.HBM((unit_devices * groups, width), f32)
    sums, cross = call(
        functools.partial(first_kernel, day_devices * day_cols, half, chunks),
        [in_hbm, ((groups, unit_rows), f32)],
        "first_product",
        fixed,
        in_specs=[hbm] * 6,
        out_specs=[hbm, vmem],
        scratch_shapes=held
        + [
            pltpu.VMEM((groups, width), f32),
            pltpu.VMEM((4 * groups, unit_rows), bf16),
            small_sems,
            panel_sems,
            out_sems,
        ],
    )
    downward = [
        (u * day_devices + d + half, u * day_devices + d) for u in range(unit_devices) for d in range(half)
    ]
    post = lax.ppermute(cross, ("unit", "day"), downward)
    (token,) = call(token_kernel, [((groups, lanes), f32)], "post_here", (post,), cost_estimate=beside)
    pack, norms, raised_units, raised_days, ends, high, low = call(
        functools.partial(second_kernel, chunks, unit_devices, half),
        [
            ((3 * groups, unit_rows + lanes), f32),
            ((groups, lanes), f32),
            ((groups, unit_rows), f32),
            ((groups, day_cols), f32),
            ((groups, lanes), f32),
            ((unit_rows, day_cols), bf16),
            ((unit_rows, day_cols), bf16),
        ],
        "unit_gradient",
        (*fixed, over_units(sums), post, token),
        in_specs=[hbm] * 6 + [vmem, vmem, any_space],
        scratch_shapes=held + [small_sems, panel_sems],
    )
    width = day_cols + lanes
    scaled, lam, grads = call(
        functools.partial(third_kernel, half, 8),
        [
            ((groups, unit_rows), f32),
            ((groups, day_cols), f32),
            pltpu.HBM((unit_devices * groups, width), f32),
        ],
        "time_gradient",
        (*over_days(pack), high, low, norms, raised_units, raised_days, ends),
        out_specs=[vmem, vmem, hbm],
        scratch_shapes=[pltpu.VMEM((groups, width), f32), out_sems],
    )
    sent_scaled = spread(scaled, 0, half)
    moved, totals = call(
        functools.partial(fourth_kernel, unit_devices),
        [((groups, day_cols), f32), ((groups, lanes), f32)],
        "new_time_weights",
        (over_units(grads), lam, norms),
    )
    sent_totals = spread(totals, 0, half)
    return call(
        functools.partial(fifth_kernel, half),
        [((groups, unit_rows), f32), ((groups, day_cols), f32)],
        "scale_weights",
        (*over_days(totals), sent_totals, scaled, sent_scaled, moved, ends),
    )


def solution(mesh):
    return jax.shard_map(
        local,
        mesh=mesh,
        in_specs=(P("unit", "day"), P("unit"), P(), P(), P(None, "unit"), P(None, "day")),
        out_specs=(P(None, "unit"), P(None, "day")),
        check_vma=False,
    )
```

```python
import functools

import jax
import jax.numpy as jnp
from jax import lax
from jax.experimental import pallas as pl
from jax.experimental.pallas import tpu as pltpu
from jax.sharding import PartitionSpec as P

step_rate = 16.0
f32 = jnp.float32
bf16 = jnp.bfloat16
lanes = 128
params = pltpu.CompilerParams(vmem_limit_bytes=24 * 1024 * 1024)
vmem = pl.BlockSpec(memory_space=pltpu.VMEM)
hbm = pl.BlockSpec(memory_space=pltpu.HBM)
any_space = pl.BlockSpec(memory_space=pl.ANY)


def split_left(value):
    first = value.astype(bf16).astype(f32)
    rest = value - first
    second = rest.astype(bf16).astype(f32)
    return [first, second, rest - second]


def left_of(value, other=None):
    other = jnp.zeros_like(value) if other is None else other
    return jnp.concatenate(split_left(value) + [other], axis=0).astype(bf16)


def split_panel(value):
    high = value.astype(bf16)
    return high, (value - high.astype(f32)).astype(bf16)


def rows_dot(left, high, low):
    return jnp.dot(left, high, preferred_element_type=f32) + jnp.dot(left, low, preferred_element_type=f32)


def days_dot(left, high, low):
    dims = (((1,), (1,)), ((), ()))
    return lax.dot_general(left, high, dims, preferred_element_type=f32) + lax.dot_general(
        left, low, dims, preferred_element_type=f32
    )


def add_terms(stack, groups):
    return stack[:groups] + stack[groups : 2 * groups] + stack[2 * groups : 3 * groups]


def tree_sum(values):
    values = list(values)
    while len(values) > 1:
        values = [values[i] + values[i + 1] for i in range(0, len(values), 2)]
    return values[0]


def column(row_ref):
    count = row_ref.shape[1]
    wide = jnp.broadcast_to(row_ref[...].astype(f32), (count, count))
    row = lax.broadcasted_iota(jnp.int32, (count, count), 0)
    lane = lax.broadcasted_iota(jnp.int32, (count, count), 1)
    return jnp.sum(jnp.where(row == lane, wide, 0.0), axis=1, keepdims=True).astype(jnp.int32)


def days_of(device, shape):
    return device * shape[1] + lax.broadcasted_iota(jnp.int32, shape, 1)


def fetch(sources, targets, sems):
    copies = [pltpu.make_async_copy(*pair, sems.at[i]) for i, pair in enumerate(zip(sources, targets))]
    for copy in copies:
        copy.start()
    return copies


def fetch_rows(source, target, sems, chunks):
    rows = source.shape[0] // chunks
    parts = [pl.ds(chunk * rows, rows) for chunk in range(chunks)]
    copies = fetch([source.at[here] for here in parts], [target.at[here] for here in parts], sems)
    return list(zip(parts, copies))


def wait_all(copies):
    for copy in copies:
        copy.wait()


def repeat_out(block, out, sems):
    rows = block.shape[0]
    places = [out.at[pl.ds(i * rows, rows)] for i in range(out.shape[0] // rows)]
    wait_all(fetch([block] * len(places), places, sems))


def first_kernel(all_count, half, chunks, *refs):
    arguments, refs = refs[:6], refs[6:]
    block, cross, *held, left_ref, small_sems, panel_sems = refs
    groups, day_cols = held[5].shape
    unit_rows = held[0].shape[0]
    small = fetch(arguments[1:], held[1:], small_sems)
    parts = fetch_rows(arguments[0], held[0], panel_sems, chunks)
    panel, cohort, _, post_row, unit_logit, _ = held
    wait_all(small)
    me = lax.axis_index("day")

    @pl.when(me < half)
    def _():
        label = lax.broadcasted_iota(jnp.int32, (groups, unit_rows), 0)
        treated = jnp.where(cohort[...] == label, 1.0, 0.0)
        control = jnp.where(cohort[...] > label, 1.0, 0.0)
        raised = jnp.exp(unit_logit[...]) * control
        left_ref[...] = left_of(raised, treated)
        lane = lax.broadcasted_iota(jnp.int32, (groups, lanes), 1)
        block[:, 2 * day_cols :] = jnp.where(
            lane == 0,
            jnp.sum(raised, axis=1, keepdims=True),
            jnp.where(
                lane == 1, jnp.sum(treated, axis=1, keepdims=True), jnp.sum(control, axis=1, keepdims=True)
            ),
        )
        product = jnp.zeros((4 * groups, day_cols), f32)
        for here, copy in parts:
            copy.wait()
            product += rows_dot(left_ref[:, here], *split_panel(panel[here, :]))
        block[:, :day_cols] = add_terms(product, groups)
        block[:, day_cols : 2 * day_cols] = product[3 * groups :]

    @pl.when(me >= half)
    def _():
        post_start = column(post_row)
        after = jnp.where(days_of(me, (groups, day_cols)) >= post_start, 1.0, 0.0)
        left = left_of(after / (all_count - post_start).astype(f32))
        for here, copy in parts:
            copy.wait()
            cross[:, here] = add_terms(days_dot(left, *split_panel(panel[here, :])), groups)


def pair_kernel(gathered, out, block, out_sems):
    block[...] = gathered[0] + gathered[1]
    repeat_out(block, out, out_sems)


def corner_kernel(half, day_cols, gathered, _, out, carried, block, out_sems):
    for day in range(half):
        block[:, day * day_cols : (day + 1) * day_cols] = (
            gathered[day, :, :day_cols] + gathered[half + day, :, :day_cols]
        )
    block[:, half * day_cols :] = gathered[0, :, day_cols:] + gathered[half, :, day_cols:]
    repeat_out(block, out, out_sems)


def second_kernel(chunks, lines, *refs):
    arguments, refs = refs[:6], refs[6:]
    sums, post, pack, norms, raised_units, ends, high_ref, low_ref, *refs = refs
    held, small_sems, panel_sems = refs[:6], refs[6], refs[7]
    groups, unit_rows = raised_units.shape
    day_cols = held[5].shape[1]
    small = fetch(arguments[1:], held[1:], small_sems)
    parts = fetch_rows(arguments[0], held[0], panel_sems, chunks)
    panel, cohort, pre_row, _, unit_logit, time_logit = held
    total = tree_sum(sums[pl.ds(u * groups, groups), :] for u in range(lines))
    unit_norm = total[:, 2 * day_cols : 2 * day_cols + 1]
    treat_count = jnp.maximum(total[:, 2 * day_cols + 1 : 2 * day_cols + 2], 1.0)
    norms[...] = total[:, 2 * day_cols :]
    pack[2 * groups :, :unit_rows] = post[...]
    wait_all(small)
    pre_end = column(pre_row)
    ends[...] = jnp.broadcast_to(pre_end.astype(f32), ends.shape)
    before = days_of(lax.axis_index("day"), (groups, day_cols)) < pre_end
    gap = total[:, :day_cols] / unit_norm - total[:, day_cols : 2 * day_cols] / treat_count
    raised_time = jnp.where(before, jnp.exp(time_logit[...]), 0.0)
    pack[:groups, unit_rows:] = raised_time
    pack[groups:, unit_rows:] = jnp.zeros((2 * groups, day_cols), f32)
    left = split_left(jnp.where(before, gap, 0.0)) + split_left(raised_time)
    left = jnp.concatenate(left, axis=0).astype(bf16)
    label = lax.broadcasted_iota(jnp.int32, (groups, unit_rows), 0)
    raised_units[...] = jnp.where(cohort[...] > label, jnp.exp(unit_logit[...]), 0.0)
    for here, copy in parts:
        copy.wait()
        high, low = split_panel(panel[here, :])
        high_ref[here, :] = high
        low_ref[here, :] = low
        product = days_dot(left, high, low)
        pack[:groups, here] = add_terms(product, groups)
        pack[groups : 2 * groups, here] = add_terms(product[3 * groups :], groups)


def third_kernel(half, chunks, *refs):
    parts, refs = refs[:half], refs[half:]
    high_ref, low_ref, norms, raised_units, ends, scaled, lam, block = refs
    groups, unit_rows = raised_units.shape
    day_cols = high_ref.shape[1]
    rows = unit_rows // chunks
    unit_norm, ctrl_count = norms[:, 0:1], norms[:, 2:3]
    factor = -step_rate / jnp.sqrt(ends[:, 0:1])
    raised_days = [ref[:groups, unit_rows:] for ref in parts]
    time_norm = tree_sum(jnp.sum(value, axis=1, keepdims=True) for value in raised_days)
    me = lax.rem(lax.axis_index("day"), half)
    for day in range(half):
        here = raised_days[0]
        for k in range(1, half):
            here = jnp.where(jnp.bitwise_xor(me, k) == day, raised_days[k], here)
        lam[:, day * day_cols : (day + 1) * day_cols] = here / time_norm
    time_grad = jnp.zeros((groups, day_cols), f32)
    new_sum = jnp.zeros((groups, 1), f32)
    for chunk in range(chunks):
        here = pl.ds(chunk * rows, rows)
        whole = tree_sum(ref[:, here] for ref in parts)
        raised = raised_units[:, here]
        new = raised / unit_norm * jnp.exp(whole[:groups] * factor)
        new_sum += jnp.sum(new, axis=1, keepdims=True)
        scaled[:, here] = new * ctrl_count
        shortfall = whole[groups : 2 * groups] / time_norm - whole[2 * groups :]
        left = left_of(jnp.where(raised > 0.0, shortfall, 0.0))
        time_grad += add_terms(rows_dot(left, high_ref[here, :], low_ref[here, :]), groups)
    block[:, :day_cols] = time_grad
    block[:, day_cols:] = jnp.broadcast_to(new_sum, (groups, lanes))


def fourth_kernel(lines, half, grads, lam, norms, ends, own_days, totals):
    groups, day_cols = own_days.shape
    total = tree_sum(grads[pl.ds(u * groups, groups), :] for u in range(lines))
    root = jnp.sqrt(jnp.maximum(norms[:, 2:3], 1.0))
    moved = lam[...] * jnp.exp(total[:, : half * day_cols] * (-step_rate / root))
    scale = ends[:, 0:1] / jnp.sum(moved, axis=1, keepdims=True)
    me = lax.axis_index("day")
    own = jnp.zeros((groups, day_cols), f32)
    for day in range(half):
        own = jnp.where(me == day, moved[:, day * day_cols : (day + 1) * day_cols], own)
    own_days[...] = jnp.where(me < half, own * scale, 0.0)
    totals[...] = total[:, half * day_cols :]


def fifth_kernel(half, totals, sent_totals, scaled, sent_scaled, own_days, unit_weights, time_weights):
    first = lax.axis_index("day") < half
    total = jnp.where(first, totals[:, 0:1], sent_totals[:, 0:1])
    unit_weights[...] = jnp.where(first, scaled[...], sent_scaled[...]) / total
    time_weights[...] = own_days[...]


def local(outcomes, cohort, pre_end, post_start, unit_logit, time_logit):
    groups = pre_end.shape[0]
    unit_rows, day_cols = outcomes.shape
    day_devices = lax.axis_size("day")
    unit_devices = lax.axis_size("unit")
    half = day_devices // 2
    assert half * 2 == day_devices and half & (half - 1) == 0
    assert unit_devices & (unit_devices - 1) == 0
    chunks = 8
    lines = unit_devices // 2

    def spread(value, day_xor, up):
        pairs = [
            (u * day_devices + d, u * day_devices + (d ^ day_xor) + up) for u in range(unit_devices) for d in range(half)
        ]
        return lax.ppermute(value, ("unit", "day"), pairs)

    def over_days(value):
        return [value] + [spread(value, k, 0) for k in range(1, half)]

    def over_lines(value):
        members = [[2 * line + side for line in range(lines)] for side in range(2)]
        return lax.all_to_all(value, "unit", split_axis=0, concat_axis=0, axis_index_groups=members, tiled=True)

    def call(kernel, shapes, name, args, in_specs=None, out_specs=None, **more):
        return pl.pallas_call(
            kernel,
            in_specs=in_specs or [vmem] * len(args),
            out_specs=out_specs or [vmem] * len(shapes),
            out_shape=[
                shape if isinstance(shape, type(in_hbm)) else jax.ShapeDtypeStruct(*shape) for shape in shapes
            ],
            compiler_params=params,
            name=name,
            **more,
        )(*args)

    arguments = (outcomes, cohort[None, :], pre_end[None, :], post_start[None, :], unit_logit, time_logit)
    fixed = [pltpu.with_memory_space_constraint(argument, pltpu.HBM) for argument in arguments]
    held = [pltpu.VMEM(argument.shape, argument.dtype) for argument in arguments]
    small_sems, panel_sems = pltpu.SemaphoreType.DMA((5,)), pltpu.SemaphoreType.DMA((chunks,))
    out_sems = pltpu.SemaphoreType.DMA((lines,))
    width = 2 * day_cols + lanes
    in_hbm = pltpu.HBM((lines * groups, width), f32)
    sums, cross = call(
        functools.partial(first_kernel, day_devices * day_cols, half, chunks // 2),
        [((groups, width), f32), ((groups, unit_rows), f32)],
        "first_product",
        fixed,
        in_specs=[hbm] * 6,
        scratch_shapes=held
        + [
            pltpu.VMEM((4 * groups, unit_rows), bf16),
            small_sems,
            panel_sems,
        ],
    )
    pairs = [[2 * line, 2 * line + 1] for line in range(lines)]
    downward = [
        (u * day_devices + d + half, u * day_devices + d) for u in range(unit_devices) for d in range(half)
    ]
    post = lax.ppermute(cross, ("unit", "day"), downward)
    (sums,) = call(
        pair_kernel,
        [in_hbm],
        "pair_sums",
        (lax.all_gather(sums, "unit", axis_index_groups=pairs),),
        out_specs=[hbm],
        scratch_shapes=[pltpu.VMEM((groups, width), f32), out_sems],
    )
    all_sums = over_lines(sums)
    pack, norms, raised_units, ends, high, low = call(
        functools.partial(second_kernel, chunks, lines),
        [
            ((3 * groups, unit_rows + day_cols), f32),
            ((groups, lanes), f32),
            ((groups, unit_rows), f32),
            ((groups, lanes), f32),
            ((unit_rows, day_cols), bf16),
            ((unit_rows, day_cols), bf16),
        ],
        "unit_gradient",
        (*fixed, all_sums, post),
        in_specs=[hbm] * 6 + [vmem] * 2,
        scratch_shapes=held + [small_sems, panel_sems],
    )
    width = day_cols + lanes
    scaled, lam, grads = call(
        functools.partial(third_kernel, half, 8),
        [((groups, unit_rows), f32), ((groups, half * day_cols), f32), ((groups, width), f32)],
        "time_gradient",
        (*over_days(pack), high, low, norms, raised_units, ends),
    )
    corners = [
        [unit * day_devices + day for unit in pair for day in range(start, start + half)]
        for pair in pairs
        for start in (0, half)
    ]
    width = half * day_cols + lanes
    grads, scaled = call(
        functools.partial(corner_kernel, half, day_cols),
        [pltpu.HBM((lines * groups, width), f32), ((groups, unit_rows), f32)],
        "corner_sums",
        (lax.all_gather(grads, ("unit", "day"), axis_index_groups=corners), scaled),
        in_specs=[vmem, any_space],
        out_specs=[hbm, any_space],
        input_output_aliases={1: 1},
        scratch_shapes=[pltpu.VMEM((groups, width), f32), out_sems],
    )
    all_grads = over_lines(grads)
    sent_scaled = spread(scaled, 0, half)
    own_days, totals = call(
        functools.partial(fourth_kernel, lines, half),
        [((groups, day_cols), f32), ((groups, lanes), f32)],
        "new_time_weights",
        (all_grads, lam, norms, ends),
    )
    return call(
        functools.partial(fifth_kernel, half),
        [((groups, unit_rows), f32), ((groups, day_cols), f32)],
        "scale_weights",
        (totals, spread(totals, 0, half), scaled, sent_scaled, own_days),
    )


def solution(mesh):
    return jax.shard_map(
        local,
        mesh=mesh,
        in_specs=(P("unit", "day"), P("unit"), P(), P(), P(None, "unit"), P(None, "day")),
        out_specs=(P(None, "unit"), P(None, "day")),
        check_vma=False,
    )
```

```python
import functools

import jax
import jax.numpy as jnp
from jax import lax
from jax.experimental import pallas as pl
from jax.experimental.pallas import tpu as pltpu
from jax.sharding import PartitionSpec as P

step_rate = 16.0
f32 = jnp.float32
bf16 = jnp.bfloat16
lanes = 128
block_rows = 256
params = pltpu.CompilerParams(vmem_limit_bytes=24 * 1024 * 1024)
vmem = pl.BlockSpec(memory_space=pltpu.VMEM)
hbm = pl.BlockSpec(memory_space=pltpu.HBM)


def split_left(value):
    first = value.astype(bf16).astype(f32)
    rest = value - first
    second = rest.astype(bf16).astype(f32)
    return [first, second, rest - second]


def left_of(value, other=None):
    other = jnp.zeros_like(value) if other is None else other
    return jnp.concatenate(split_left(value) + [other], axis=0).astype(bf16)


def split_panel(value):
    high = value.astype(bf16)
    return high, (value - high.astype(f32)).astype(bf16)


def rows_dot(left, high, low):
    return jnp.dot(left, high, preferred_element_type=f32) + jnp.dot(left, low, preferred_element_type=f32)


def days_dot(left, high, low):
    dims = (((1,), (1,)), ((), ()))
    return lax.dot_general(left, high, dims, preferred_element_type=f32) + lax.dot_general(
        left, low, dims, preferred_element_type=f32
    )


def add_terms(stack, groups):
    return stack[:groups] + stack[groups : 2 * groups] + stack[2 * groups : 3 * groups]


def tree_sum(values):
    values = list(values)
    while len(values) > 1:
        values = [values[i] + values[i + 1] for i in range(0, len(values), 2)]
    return values[0]


def column(row_ref):
    count = row_ref.shape[1]
    wide = jnp.broadcast_to(row_ref[...].astype(f32), (count, count))
    row = lax.broadcasted_iota(jnp.int32, (count, count), 0)
    lane = lax.broadcasted_iota(jnp.int32, (count, count), 1)
    return jnp.sum(jnp.where(row == lane, wide, 0.0), axis=1, keepdims=True).astype(jnp.int32)


def days_of(device, shape):
    return device * shape[1] + lax.broadcasted_iota(jnp.int32, shape, 1)


def fetch(sources, targets, sems):
    copies = [pltpu.make_async_copy(*pair, sems.at[i]) for i, pair in enumerate(zip(sources, targets))]
    for copy in copies:
        copy.start()
    return copies


def fetch_rows(source, target, sems, chunks):
    rows = source.shape[0] // chunks
    parts = [pl.ds(chunk * rows, rows) for chunk in range(chunks)]
    copies = fetch([source.at[here] for here in parts], [target.at[here] for here in parts], sems)
    blocks = [[pl.ds(part.start + i, block_rows) for i in range(0, rows, block_rows)] for part in parts]
    return list(zip(blocks, copies))


def wait_all(copies):
    for copy in copies:
        copy.wait()


def repeat_out(block, out, sems):
    rows = block.shape[0]
    places = [out.at[pl.ds(i * rows, rows)] for i in range(out.shape[0] // rows)]
    wait_all(fetch([block] * len(places), places, sems))


def first_kernel(all_count, half, chunks, *refs):
    arguments, refs = refs[:6], refs[6:]
    out, cross, *held, block, left_ref, small_sems, panel_sems, out_sems = refs
    groups, day_cols = held[5].shape
    unit_rows = held[0].shape[0]
    small = fetch(arguments[1:], held[1:], small_sems)
    parts = fetch_rows(arguments[0], held[0], panel_sems, chunks)
    panel, cohort, _, post_row, unit_logit, _ = held
    wait_all(small)
    me = lax.axis_index("day")

    @pl.when(me < half)
    def _():
        label = lax.broadcasted_iota(jnp.int32, (groups, unit_rows), 0)
        treated = jnp.where(cohort[...] == label, 1.0, 0.0)
        control = jnp.where(cohort[...] > label, 1.0, 0.0)
        raised = jnp.exp(unit_logit[...]) * control
        left_ref[...] = left_of(raised, treated)
        lane = lax.broadcasted_iota(jnp.int32, (groups, lanes), 1)
        block[:, 2 * day_cols :] = jnp.where(
            lane == 0,
            jnp.sum(raised, axis=1, keepdims=True),
            jnp.where(
                lane == 1, jnp.sum(treated, axis=1, keepdims=True), jnp.sum(control, axis=1, keepdims=True)
            ),
        )
        product = jnp.zeros((4 * groups, day_cols), f32)
        for blocks, copy in parts:
            copy.wait()
            for here in blocks:
                product += rows_dot(left_ref[:, here], *split_panel(panel[here, :]))
        block[:, :day_cols] = add_terms(product, groups)
        block[:, day_cols : 2 * day_cols] = product[3 * groups :]
        repeat_out(block, out, out_sems)

    @pl.when(me >= half)
    def _():
        post_start = column(post_row)
        after = jnp.where(days_of(me, (groups, day_cols)) >= post_start, 1.0, 0.0)
        left = left_of(after / (all_count - post_start).astype(f32))
        for blocks, copy in parts:
            copy.wait()
            for here in blocks:
                cross[:, here] = add_terms(days_dot(left, *split_panel(panel[here, :])), groups)


def second_kernel(chunks, unit_devices, half, *refs):
    arguments, refs = refs[:6], refs[6:]
    sums, post, pack, norms, raised_units, raised_days, ends, high_ref, low_ref, *refs = refs
    held, small_sems, panel_sems = refs[:6], refs[6], refs[7]
    groups, day_cols = raised_days.shape
    unit_rows = raised_units.shape[1]
    small = fetch(arguments[1:], held[1:], small_sems)
    parts = fetch_rows(arguments[0], held[0], panel_sems, chunks)
    panel, cohort, pre_row, _, unit_logit, time_logit = held
    total = tree_sum(sums[pl.ds(u * groups, groups), :] for u in range(unit_devices))
    unit_norm = total[:, 2 * day_cols : 2 * day_cols + 1]
    treat_count = jnp.maximum(total[:, 2 * day_cols + 1 : 2 * day_cols + 2], 1.0)
    norms[...] = total[:, 2 * day_cols :]
    pack[2 * groups :, :unit_rows] = post[...]
    wait_all(small)
    pre_end = column(pre_row)
    ends[...] = jnp.broadcast_to(pre_end.astype(f32), ends.shape)
    before = days_of(lax.axis_index("day"), (groups, day_cols)) < pre_end
    gap = total[:, :day_cols] / unit_norm - total[:, day_cols : 2 * day_cols] / treat_count
    raised_time = jnp.where(before, jnp.exp(time_logit[...]), 0.0)
    raised_days[...] = raised_time
    time_norm = jnp.sum(raised_time, axis=1, keepdims=True)
    pack[:, unit_rows:] = jnp.broadcast_to(jnp.concatenate([time_norm] * 3, axis=0), (3 * groups, lanes))
    left = split_left(jnp.where(before, gap, 0.0)) + split_left(raised_time)
    left = jnp.concatenate(left, axis=0).astype(bf16)
    label = lax.broadcasted_iota(jnp.int32, (groups, unit_rows), 0)
    raised_units[...] = jnp.where(cohort[...] > label, jnp.exp(unit_logit[...]), 0.0)
    for blocks, copy in parts:
        copy.wait()
        for here in blocks:
            high, low = split_panel(panel[here, :])
            high_ref[here, :] = high
            low_ref[here, :] = low
            product = days_dot(left, high, low)
            pack[:groups, here] = add_terms(product, groups)
            pack[groups : 2 * groups, here] = add_terms(product[3 * groups :], groups)


def third_kernel(half, chunks, *refs):
    parts, refs = refs[:half], refs[half:]
    high_ref, low_ref, norms, raised_units, raised_days, ends, scaled, lam, out, block, out_sems = refs
    groups, unit_rows = raised_units.shape
    day_cols = raised_days.shape[1]
    rows = unit_rows // chunks
    unit_norm, ctrl_count = norms[:, 0:1], norms[:, 2:3]
    factor = -step_rate / jnp.sqrt(ends[:, 0:1])
    time_norm = tree_sum(ref[:groups, unit_rows : unit_rows + 1] for ref in parts)
    lam[...] = raised_days[...] / time_norm
    time_grad = jnp.zeros((groups, day_cols), f32)
    new_sum = jnp.zeros((groups, 1), f32)
    for chunk in range(chunks):
        here = pl.ds(chunk * rows, rows)
        whole = tree_sum(ref[:, here] for ref in parts)
        raised = raised_units[:, here]
        new = raised / unit_norm * jnp.exp(whole[:groups] * factor)
        new_sum += jnp.sum(new, axis=1, keepdims=True)
        scaled[:, here] = new * ctrl_count
        shortfall = whole[groups : 2 * groups] / time_norm - whole[2 * groups :]
        left = left_of(jnp.where(raised > 0.0, shortfall, 0.0))
        time_grad += add_terms(rows_dot(left, high_ref[here, :], low_ref[here, :]), groups)
    block[:, :day_cols] = time_grad
    block[:, day_cols:] = jnp.broadcast_to(new_sum, (groups, lanes))
    repeat_out(block, out, out_sems)


def fourth_kernel(unit_devices, grads, lam, norms, moved, moved_sum, totals):
    groups, day_cols = lam.shape
    total = tree_sum(grads[pl.ds(u * groups, groups), :] for u in range(unit_devices))
    root = jnp.sqrt(jnp.maximum(norms[:, 2:3], 1.0))
    new = lam[...] * jnp.exp(total[:, :day_cols] * (-step_rate / root))
    moved[...] = new
    totals[...] = total[:, day_cols:]
    moved_sum[...] = jnp.broadcast_to(jnp.sum(new, axis=1, keepdims=True), moved_sum.shape)


def fifth_kernel(half, *refs):
    moved_sums, refs = refs[:half], refs[half:]
    totals, sent_totals, scaled, sent_scaled, moved, ends, unit_weights, time_weights = refs
    first = lax.axis_index("day") < half
    own = jnp.where(first, totals[:, 0:1], sent_totals[:, 0:1])
    unit_weights[...] = jnp.where(first, scaled[...], sent_scaled[...]) / own
    day_total = tree_sum(ref[:, 0:1] for ref in moved_sums)
    time_weights[...] = jnp.where(first, moved[...] / day_total * ends[:, 0:1], 0.0)


def local(outcomes, cohort, pre_end, post_start, unit_logit, time_logit):
    groups = pre_end.shape[0]
    unit_rows, day_cols = outcomes.shape
    day_devices = lax.axis_size("day")
    unit_devices = lax.axis_size("unit")
    half = day_devices // 2
    assert half * 2 == day_devices and half & (half - 1) == 0
    assert unit_devices & (unit_devices - 1) == 0
    chunks = 4
    def spread(value, day_xor, up):
        pairs = [
            (u * day_devices + d, u * day_devices + (d ^ day_xor) + up) for u in range(unit_devices) for d in range(half)
        ]
        return lax.ppermute(value, ("unit", "day"), pairs)

    def over_days(value):
        return [value] + [spread(value, k, 0) for k in range(1, half)]

    def over_units(value):
        return lax.all_to_all(value, "unit", split_axis=0, concat_axis=0, tiled=True)

    def call(kernel, shapes, name, args, in_specs=None, out_specs=None, **more):
        return pl.pallas_call(
            kernel,
            in_specs=in_specs or [vmem] * len(args),
            out_specs=out_specs or [vmem] * len(shapes),
            out_shape=[
                shape if isinstance(shape, type(in_hbm)) else jax.ShapeDtypeStruct(*shape) for shape in shapes
            ],
            compiler_params=params,
            name=name,
            **more,
        )(*args)

    arguments = (outcomes, cohort[None, :], pre_end[None, :], post_start[None, :], unit_logit, time_logit)
    fixed = [pltpu.with_memory_space_constraint(argument, pltpu.HBM) for argument in arguments]
    held = [pltpu.VMEM(argument.shape, argument.dtype) for argument in arguments]
    small_sems, panel_sems = pltpu.SemaphoreType.DMA((5,)), pltpu.SemaphoreType.DMA((chunks,))
    out_sems = pltpu.SemaphoreType.DMA((unit_devices,))
    width = 2 * day_cols + lanes
    in_hbm = pltpu.HBM((unit_devices * groups, width), f32)
    sums, cross = call(
        functools.partial(first_kernel, day_devices * day_cols, half, chunks),
        [in_hbm, ((groups, unit_rows), f32)],
        "first_product",
        fixed,
        in_specs=[hbm] * 6,
        out_specs=[hbm, vmem],
        scratch_shapes=held
        + [
            pltpu.VMEM((groups, width), f32),
            pltpu.VMEM((4 * groups, unit_rows), bf16),
            small_sems,
            panel_sems,
            out_sems,
        ],
    )
    downward = [
        (u * day_devices + d + half, u * day_devices + d) for u in range(unit_devices) for d in range(half)
    ]
    post = lax.ppermute(cross, ("unit", "day"), downward)
    pack, norms, raised_units, raised_days, ends, high, low = call(
        functools.partial(second_kernel, chunks, unit_devices, half),
        [
            ((3 * groups, unit_rows + lanes), f32),
            ((groups, lanes), f32),
            ((groups, unit_rows), f32),
            ((groups, day_cols), f32),
            ((groups, lanes), f32),
            ((unit_rows, day_cols), bf16),
            ((unit_rows, day_cols), bf16),
        ],
        "unit_gradient",
        (*fixed, over_units(sums), post),
        in_specs=[hbm] * 6 + [vmem] * 2,
        scratch_shapes=held + [small_sems, panel_sems],
    )
    width = day_cols + lanes
    scaled, lam, grads = call(
        functools.partial(third_kernel, half, 8),
        [
            ((groups, unit_rows), f32),
            ((groups, day_cols), f32),
            pltpu.HBM((unit_devices * groups, width), f32),
        ],
        "time_gradient",
        (*over_days(pack), high, low, norms, raised_units, raised_days, ends),
        out_specs=[vmem, vmem, hbm],
        scratch_shapes=[pltpu.VMEM((groups, width), f32), out_sems],
    )
    sent_scaled = spread(scaled, 0, half)
    moved, moved_sum, totals = call(
        functools.partial(fourth_kernel, unit_devices),
        [((groups, day_cols), f32), ((groups, lanes), f32), ((groups, lanes), f32)],
        "new_time_weights",
        (over_units(grads), lam, norms),
    )
    return call(
        functools.partial(fifth_kernel, half),
        [((groups, unit_rows), f32), ((groups, day_cols), f32)],
        "scale_weights",
        (*over_days(moved_sum), totals, spread(totals, 0, half), scaled, sent_scaled, moved, ends),
    )


def solution(mesh):
    return jax.shard_map(
        local,
        mesh=mesh,
        in_specs=(P("unit", "day"), P("unit"), P(), P(), P(None, "unit"), P(None, "day")),
        out_specs=(P(None, "unit"), P(None, "day")),
        check_vma=False,
    )
```

```python
import functools

import jax
import jax.numpy as jnp
from jax import lax
from jax.experimental import pallas as pl
from jax.experimental.pallas import tpu as pltpu
from jax.sharding import PartitionSpec as P

step_rate = 16.0
f32 = jnp.float32
bf16 = jnp.bfloat16
lanes = 128
block_rows = 256
params = pltpu.CompilerParams(vmem_limit_bytes=24 * 1024 * 1024)
vmem = pl.BlockSpec(memory_space=pltpu.VMEM)
hbm = pl.BlockSpec(memory_space=pltpu.HBM)


def split_left(value):
    first = value.astype(bf16).astype(f32)
    rest = value - first
    second = rest.astype(bf16).astype(f32)
    return [first, second, rest - second]


def left_of(value, other=None):
    other = jnp.zeros_like(value) if other is None else other
    return jnp.concatenate(split_left(value) + [other], axis=0).astype(bf16)


def split_panel(value):
    high = value.astype(bf16)
    return high, (value - high.astype(f32)).astype(bf16)


def rows_dot(left, high, low):
    return jnp.dot(left, high, preferred_element_type=f32) + jnp.dot(left, low, preferred_element_type=f32)


def days_dot(left, high, low):
    dims = (((1,), (1,)), ((), ()))
    return lax.dot_general(left, high, dims, preferred_element_type=f32) + lax.dot_general(
        left, low, dims, preferred_element_type=f32
    )


def add_terms(stack, groups):
    return stack[:groups] + stack[groups : 2 * groups] + stack[2 * groups : 3 * groups]


def tree_sum(values):
    values = list(values)
    while len(values) > 1:
        values = [values[i] + values[i + 1] for i in range(0, len(values), 2)]
    return values[0]


def column(row_ref):
    count = row_ref.shape[1]
    wide = jnp.broadcast_to(row_ref[...].astype(f32), (count, count))
    row = lax.broadcasted_iota(jnp.int32, (count, count), 0)
    lane = lax.broadcasted_iota(jnp.int32, (count, count), 1)
    return jnp.sum(jnp.where(row == lane, wide, 0.0), axis=1, keepdims=True).astype(jnp.int32)


def days_of(device, shape):
    return device * shape[1] + lax.broadcasted_iota(jnp.int32, shape, 1)


def fetch(sources, targets, sems):
    copies = [pltpu.make_async_copy(*pair, sems.at[i]) for i, pair in enumerate(zip(sources, targets))]
    for copy in copies:
        copy.start()
    return copies


def fetch_rows(source, target, sems, chunks, first=0):
    rows = (source.shape[0] - first) // chunks
    parts = [pl.ds(first + chunk * rows, rows) for chunk in range(chunks)]
    copies = fetch([source.at[here] for here in parts], [target.at[here] for here in parts], sems)
    blocks = [[pl.ds(part.start + i, block_rows) for i in range(0, rows, block_rows)] for part in parts]
    return list(zip(blocks, copies))


def wait_all(copies):
    for copy in copies:
        copy.wait()


def repeat_out(block, out, sems):
    rows = block.shape[0]
    places = [out.at[pl.ds(i * rows, rows)] for i in range(out.shape[0] // rows)]
    wait_all(fetch([block] * len(places), places, sems))


def first_kernel(all_count, half, chunks, *refs):
    arguments, refs = refs[:6], refs[6:]
    out, cross, high_ref, low_ref, *held, block, left_ref, small_sems, panel_sems, out_sems = refs
    groups, day_cols = held[5].shape
    unit_rows = held[0].shape[0]
    small = fetch(arguments[1:], held[1:], small_sems)
    parts = fetch_rows(arguments[0], held[0], panel_sems, chunks)
    panel, cohort, _, post_row, unit_logit, _ = held
    wait_all(small)
    me = lax.axis_index("day")

    @pl.when(me < half)
    def _():
        label = lax.broadcasted_iota(jnp.int32, (groups, unit_rows), 0)
        treated = jnp.where(cohort[...] == label, 1.0, 0.0)
        control = jnp.where(cohort[...] > label, 1.0, 0.0)
        raised = jnp.exp(unit_logit[...]) * control
        left_ref[...] = left_of(raised, treated)
        lane = lax.broadcasted_iota(jnp.int32, (groups, lanes), 1)
        block[:, 2 * day_cols :] = jnp.where(
            lane == 0,
            jnp.sum(raised, axis=1, keepdims=True),
            jnp.where(
                lane == 1, jnp.sum(treated, axis=1, keepdims=True), jnp.sum(control, axis=1, keepdims=True)
            ),
        )
        product = jnp.zeros((4 * groups, day_cols), f32)
        for blocks, copy in parts:
            copy.wait()
            for here in blocks:
                high, low = split_panel(panel[here, :])
                if here.start < high_ref.shape[0]:
                    high_ref[here, :] = high
                    low_ref[here, :] = low
                product += rows_dot(left_ref[:, here], high, low)
        block[:, :day_cols] = add_terms(product, groups)
        block[:, day_cols : 2 * day_cols] = product[3 * groups :]
        repeat_out(block, out, out_sems)

    @pl.when(me >= half)
    def _():
        post_start = column(post_row)
        after = jnp.where(days_of(me, (groups, day_cols)) >= post_start, 1.0, 0.0)
        left = left_of(after / (all_count - post_start).astype(f32))
        for blocks, copy in parts:
            copy.wait()
            for here in blocks:
                cross[:, here] = add_terms(days_dot(left, *split_panel(panel[here, :])), groups)


def second_kernel(chunks, unit_devices, *refs):
    arguments, refs = refs[:6], refs[6:]
    sums, high_ref, low_ref, pack, norms, raised_units, ends, more_high, more_low, *refs = refs
    held, small_sems, panel_sems = refs[:6], refs[6], refs[7]
    groups, unit_rows = raised_units.shape
    resident, day_cols = high_ref.shape
    panel, cohort, pre_row, _, unit_logit, time_logit = held
    small = fetch(arguments[1:], held[1:], small_sems)
    parts = fetch_rows(arguments[0], panel, panel_sems, chunks, resident)
    total = tree_sum(sums[pl.ds(u * groups, groups), :] for u in range(unit_devices))
    unit_norm = total[:, 2 * day_cols : 2 * day_cols + 1]
    treat_count = jnp.maximum(total[:, 2 * day_cols + 1 : 2 * day_cols + 2], 1.0)
    norms[...] = total[:, 2 * day_cols :]
    gap = total[:, :day_cols] / unit_norm - total[:, day_cols : 2 * day_cols] / treat_count
    wait_all(small)
    pre_end = column(pre_row)
    ends[...] = jnp.broadcast_to(pre_end.astype(f32), ends.shape)
    before = days_of(lax.axis_index("day"), (groups, day_cols)) < pre_end
    raised_time = jnp.where(before, jnp.exp(time_logit[...]), 0.0)
    pack[:groups, unit_rows:] = raised_time
    pack[groups:, unit_rows:] = jnp.zeros_like(raised_time)
    left = split_left(jnp.where(before, gap, 0.0)) + split_left(raised_time)
    left = jnp.concatenate(left, axis=0).astype(bf16)
    label = lax.broadcasted_iota(jnp.int32, (groups, unit_rows), 0)
    raised_units[...] = jnp.where(cohort[...] > label, jnp.exp(unit_logit[...]), 0.0)

    def multiply(here, high, low):
        product = days_dot(left, high, low)
        pack[:groups, here] = add_terms(product, groups)
        pack[groups:, here] = add_terms(product[3 * groups :], groups)

    for start in range(0, resident, block_rows):
        here = pl.ds(start, block_rows)
        multiply(here, high_ref[here, :], low_ref[here, :])
    for blocks, copy in parts:
        copy.wait()
        for here in blocks:
            there = pl.ds(here.start - resident, block_rows)
            high, low = split_panel(panel[here, :])
            more_high[there, :] = high
            more_low[there, :] = low
            multiply(here, high, low)


def join_kernel(pack, post, out):
    rows, width = pack.shape
    out[:rows, :] = pack[...]
    out[rows:, : post.shape[1]] = post[...]
    out[rows:, post.shape[1] :] = jnp.zeros((post.shape[0], width - post.shape[1]), f32)


def third_kernel(half, *refs):
    parts, refs = refs[:half], refs[half:]
    high_ref, low_ref, more_high, more_low, norms, raised_units, ends, scaled, lam, out, block, out_sems = refs
    groups, unit_rows = raised_units.shape
    resident, day_cols = high_ref.shape
    unit_norm, ctrl_count = norms[:, 0:1], norms[:, 2:3]
    factor = -step_rate / jnp.sqrt(ends[:, 0:1])
    raised_days = [ref[:groups, unit_rows:] for ref in parts]
    time_norm = tree_sum(jnp.sum(value, axis=1, keepdims=True) for value in raised_days)
    lam[...] = raised_days[0] / time_norm
    time_grad = jnp.zeros((groups, day_cols), f32)
    new_sum = jnp.zeros((groups, 1), f32)
    for start in range(0, unit_rows, 2 * block_rows):
        here = pl.ds(start, 2 * block_rows)
        whole = tree_sum(ref[:, here] for ref in parts)
        raised = raised_units[:, here]
        new = raised / unit_norm * jnp.exp(whole[:groups] * factor)
        new_sum += jnp.sum(new, axis=1, keepdims=True)
        scaled[:, here] = new * ctrl_count
        shortfall = whole[groups : 2 * groups] / time_norm - whole[2 * groups :]
        left = left_of(jnp.where(raised > 0.0, shortfall, 0.0))
        if start < resident:
            high, low = high_ref[here, :], low_ref[here, :]
        else:
            there = pl.ds(start - resident, 2 * block_rows)
            high, low = more_high[there, :], more_low[there, :]
        time_grad += add_terms(rows_dot(left, high, low), groups)
    block[:, :day_cols] = time_grad
    block[:, day_cols:] = jnp.broadcast_to(new_sum, (groups, lanes))
    repeat_out(block, out, out_sems)


def fourth_kernel(unit_devices, grads, lam, norms, moved, moved_sum, totals):
    groups, day_cols = lam.shape
    total = tree_sum(grads[pl.ds(u * groups, groups), :] for u in range(unit_devices))
    root = jnp.sqrt(jnp.maximum(norms[:, 2:3], 1.0))
    new = lam[...] * jnp.exp(total[:, :day_cols] * (-step_rate / root))
    moved[...] = new
    totals[...] = total[:, day_cols:]
    moved_sum[...] = jnp.broadcast_to(jnp.sum(new, axis=1, keepdims=True), moved_sum.shape)


def fifth_kernel(half, *refs):
    moved_sums, refs = refs[:half], refs[half:]
    totals, scaled, moved, ends, unit_weights, time_weights = refs
    first = lax.axis_index("day") < half
    unit_weights[...] = scaled[...] / totals[:, 0:1]
    day_total = tree_sum(ref[:, 0:1] for ref in moved_sums)
    time_weights[...] = jnp.where(first, moved[...] / day_total * ends[:, 0:1], 0.0)


def sixth_kernel(half, sent_totals, sent_scaled, _, unit_weights, block, out_sem):
    @pl.when(lax.axis_index("day") >= half)
    def _():
        block[...] = sent_scaled[...] / sent_totals[:, 0:1]
        wait_all(fetch([block], [unit_weights], out_sem))


def local(outcomes, cohort, pre_end, post_start, unit_logit, time_logit):
    groups = pre_end.shape[0]
    unit_rows, day_cols = outcomes.shape
    day_devices = lax.axis_size("day")
    unit_devices = lax.axis_size("unit")
    half = day_devices // 2
    assert half * 2 == day_devices and half & (half - 1) == 0
    assert unit_devices & (unit_devices - 1) == 0
    chunks = 4
    resident = unit_rows * 5 // 8 // (2 * block_rows) * (2 * block_rows)
    def spread(value, day_xor, up):
        pairs = [
            (u * day_devices + d, u * day_devices + (d ^ day_xor) + up) for u in range(unit_devices) for d in range(half)
        ]
        return lax.ppermute(value, ("unit", "day"), pairs)

    def over_days(value):
        return [value] + [spread(value, k, 0) for k in range(1, half)]

    def over_units(value):
        return lax.all_to_all(value, "unit", split_axis=0, concat_axis=0, tiled=True)

    def call(kernel, shapes, name, args, in_specs=None, out_specs=None, **more):
        return pl.pallas_call(
            kernel,
            in_specs=in_specs or [vmem] * len(args),
            out_specs=out_specs or [vmem] * len(shapes),
            out_shape=[
                shape if isinstance(shape, type(in_hbm)) else jax.ShapeDtypeStruct(*shape) for shape in shapes
            ],
            compiler_params=params,
            name=name,
            **more,
        )(*args)

    arguments = (outcomes, cohort[None, :], pre_end[None, :], post_start[None, :], unit_logit, time_logit)
    fixed = [pltpu.with_memory_space_constraint(argument, pltpu.HBM) for argument in arguments]
    held = [pltpu.VMEM(argument.shape, argument.dtype) for argument in arguments]
    small_sems, panel_sems = pltpu.SemaphoreType.DMA((5,)), pltpu.SemaphoreType.DMA((chunks,))
    panel_terms = [((resident, day_cols), bf16)] * 2
    other_terms = [((unit_rows - resident, day_cols), bf16)] * 2
    out_sems = pltpu.SemaphoreType.DMA((unit_devices,))
    width = 2 * day_cols + lanes
    in_hbm = pltpu.HBM((unit_devices * groups, width), f32)
    sums, cross, high, low = call(
        functools.partial(first_kernel, day_devices * day_cols, half, chunks),
        [in_hbm, ((groups, unit_rows), f32), *panel_terms],
        "first_product",
        fixed,
        in_specs=[hbm] * 6,
        out_specs=[hbm, vmem, vmem, vmem],
        scratch_shapes=held
        + [
            pltpu.VMEM((groups, width), f32),
            pltpu.VMEM((4 * groups, unit_rows), bf16),
            small_sems,
            panel_sems,
            out_sems,
        ],
    )
    downward = [
        (u * day_devices + d + half, u * day_devices + d) for u in range(unit_devices) for d in range(half)
    ]
    post = lax.ppermute(cross, ("unit", "day"), downward)
    pack, norms, raised_units, ends, more_high, more_low = call(
        functools.partial(second_kernel, 3, unit_devices),
        [
            ((2 * groups, unit_rows + day_cols), f32),
            ((groups, lanes), f32),
            ((groups, unit_rows), f32),
            ((groups, lanes), f32),
            *other_terms,
        ],
        "unit_gradient",
        (*fixed, over_units(sums), high, low),
        in_specs=[hbm] * 6 + [vmem] * 3,
        scratch_shapes=held + [small_sems, panel_sems],
    )
    (pack,) = call(
        join_kernel, [((3 * groups, unit_rows + day_cols), f32)], "join_post", (pack, post)
    )
    width = day_cols + lanes
    scaled, lam, grads = call(
        functools.partial(third_kernel, half),
        [
            ((groups, unit_rows), f32),
            ((groups, day_cols), f32),
            pltpu.HBM((unit_devices * groups, width), f32),
        ],
        "time_gradient",
        (*over_days(pack), high, low, more_high, more_low, norms, raised_units, ends),
        out_specs=[vmem, vmem, hbm],
        scratch_shapes=[pltpu.VMEM((groups, width), f32), out_sems],
    )
    sent_scaled = spread(scaled, 0, half)
    moved, moved_sum, totals = call(
        functools.partial(fourth_kernel, unit_devices),
        [((groups, day_cols), f32), ((groups, lanes), f32), ((groups, lanes), f32)],
        "new_time_weights",
        (over_units(grads), lam, norms),
    )
    unit_weights, time_weights = call(
        functools.partial(fifth_kernel, half),
        [((groups, unit_rows), f32), ((groups, day_cols), f32)],
        "scale_weights",
        (*over_days(moved_sum), totals, scaled, moved, ends),
    )
    (unit_weights,) = call(
        functools.partial(sixth_kernel, half),
        [((groups, unit_rows), f32)],
        "other_half",
        (spread(totals, 0, half), sent_scaled, unit_weights),
        in_specs=[vmem, vmem, hbm],
        out_specs=[hbm],
        input_output_aliases={2: 0},
        scratch_shapes=[pltpu.VMEM((groups, unit_rows), f32), pltpu.SemaphoreType.DMA((1,))],
    )
    return unit_weights, time_weights


def solution(mesh):
    return jax.shard_map(
        local,
        mesh=mesh,
        in_specs=(P("unit", "day"), P("unit"), P(), P(), P(None, "unit"), P(None, "day")),
        out_specs=(P(None, "unit"), P(None, "day")),
        check_vma=False,
    )
```

```python
import functools

import jax
import jax.numpy as jnp
from jax import lax
from jax.experimental import pallas as pl
from jax.experimental.pallas import tpu as pltpu
from jax.sharding import PartitionSpec as P

step_rate = 16.0
f32 = jnp.float32
bf16 = jnp.bfloat16
lanes = 128
block_rows = 256
params = pltpu.CompilerParams(vmem_limit_bytes=24 * 1024 * 1024)
vmem = pl.BlockSpec(memory_space=pltpu.VMEM)
hbm = pl.BlockSpec(memory_space=pltpu.HBM)


def split_left(value):
    first = value.astype(bf16).astype(f32)
    rest = value - first
    second = rest.astype(bf16).astype(f32)
    return [first, second, rest - second]


def left_of(value, other=None):
    other = jnp.zeros_like(value) if other is None else other
    return jnp.concatenate(split_left(value) + [other], axis=0).astype(bf16)


def split_panel(value):
    high = value.astype(bf16)
    return high, (value - high.astype(f32)).astype(bf16)


def rows_dot(left, high, low):
    return jnp.dot(left, high, preferred_element_type=f32) + jnp.dot(left, low, preferred_element_type=f32)


def days_dot(left, high, low):
    dims = (((1,), (1,)), ((), ()))
    return lax.dot_general(left, high, dims, preferred_element_type=f32) + lax.dot_general(
        left, low, dims, preferred_element_type=f32
    )


def add_terms(stack, groups):
    return stack[:groups] + stack[groups : 2 * groups] + stack[2 * groups : 3 * groups]


def tree_sum(values):
    values = list(values)
    while len(values) > 1:
        values = [values[i] + values[i + 1] for i in range(0, len(values), 2)]
    return values[0]


def column(row_ref):
    count = row_ref.shape[1]
    wide = jnp.broadcast_to(row_ref[...].astype(f32), (count, count))
    row = lax.broadcasted_iota(jnp.int32, (count, count), 0)
    lane = lax.broadcasted_iota(jnp.int32, (count, count), 1)
    return jnp.sum(jnp.where(row == lane, wide, 0.0), axis=1, keepdims=True).astype(jnp.int32)


def days_of(device, shape):
    return device * shape[1] + lax.broadcasted_iota(jnp.int32, shape, 1)


def fetch(sources, targets, sems):
    copies = [pltpu.make_async_copy(*pair, sems.at[i]) for i, pair in enumerate(zip(sources, targets))]
    for copy in copies:
        copy.start()
    return copies


def fetch_rows(source, target, sems, chunks, first=0):
    rows = (source.shape[0] - first) // chunks
    parts = [pl.ds(first + chunk * rows, rows) for chunk in range(chunks)]
    copies = fetch([source.at[here] for here in parts], [target.at[here] for here in parts], sems)
    blocks = [[pl.ds(part.start + i, block_rows) for i in range(0, rows, block_rows)] for part in parts]
    return list(zip(blocks, copies))


def wait_all(copies):
    for copy in copies:
        copy.wait()


def repeat_out(block, out, sems):
    rows = block.shape[0]
    places = [out.at[pl.ds(i * rows, rows)] for i in range(out.shape[0] // rows)]
    wait_all(fetch([block] * len(places), places, sems))


def first_kernel(all_count, half, chunks, *refs):
    arguments, refs = refs[:6], refs[6:]
    out, cross, raised_units, raised_days, ends, high_ref, low_ref, *held, block, left_ref, small_sems, panel_sems, out_sems = refs
    groups, day_cols = held[5].shape
    unit_rows = held[0].shape[0]
    small = fetch(arguments[1:], held[1:], small_sems)
    parts = fetch_rows(arguments[0], held[0], panel_sems, chunks)
    panel, cohort, pre_row, post_row, unit_logit, time_logit = held
    wait_all(small)
    me = lax.axis_index("day")

    @pl.when(me < half)
    def _():
        label = lax.broadcasted_iota(jnp.int32, (groups, unit_rows), 0)
        treated = jnp.where(cohort[...] == label, 1.0, 0.0)
        control = jnp.where(cohort[...] > label, 1.0, 0.0)
        raised = jnp.exp(unit_logit[...]) * control
        raised_units[...] = raised
        left_ref[...] = left_of(raised, treated)
        pre_end = column(pre_row)
        ends[...] = jnp.broadcast_to(pre_end.astype(f32), ends.shape)
        before = days_of(me, (groups, day_cols)) < pre_end
        raised_days[...] = jnp.where(before, jnp.exp(time_logit[...]), 0.0)
        lane = lax.broadcasted_iota(jnp.int32, (groups, lanes), 1)
        block[:, 2 * day_cols :] = jnp.where(
            lane == 0,
            jnp.sum(raised, axis=1, keepdims=True),
            jnp.where(
                lane == 1, jnp.sum(treated, axis=1, keepdims=True), jnp.sum(control, axis=1, keepdims=True)
            ),
        )
        product = jnp.zeros((4 * groups, day_cols), f32)
        for blocks, copy in parts:
            copy.wait()
            for here in blocks:
                high, low = split_panel(panel[here, :])
                if here.start < high_ref.shape[0]:
                    high_ref[here, :] = high
                    low_ref[here, :] = low
                product += rows_dot(left_ref[:, here], high, low)
        block[:, :day_cols] = add_terms(product, groups)
        block[:, day_cols : 2 * day_cols] = product[3 * groups :]
        repeat_out(block, out, out_sems)

    @pl.when(me >= half)
    def _():
        post_start = column(post_row)
        after = jnp.where(days_of(me, (groups, day_cols)) >= post_start, 1.0, 0.0)
        left = left_of(after / (all_count - post_start).astype(f32))
        for blocks, copy in parts:
            copy.wait()
            for here in blocks:
                cross[:, here] = add_terms(days_dot(left, *split_panel(panel[here, :])), groups)


def second_kernel(chunks, unit_devices, panel, sums, raised_days, ends, high_ref, low_ref, *refs):
    pack, norms, more_high, more_low, held, panel_sems = refs
    groups, day_cols = raised_days.shape
    unit_rows, resident = panel.shape[0], high_ref.shape[0]
    parts = fetch_rows(panel, held, panel_sems, chunks, resident)
    total = tree_sum(sums[pl.ds(u * groups, groups), :] for u in range(unit_devices))
    unit_norm = total[:, 2 * day_cols : 2 * day_cols + 1]
    treat_count = jnp.maximum(total[:, 2 * day_cols + 1 : 2 * day_cols + 2], 1.0)
    norms[...] = total[:, 2 * day_cols :]
    gap = total[:, :day_cols] / unit_norm - total[:, day_cols : 2 * day_cols] / treat_count
    before = days_of(lax.axis_index("day"), (groups, day_cols)).astype(f32) < ends[:, 0:1]
    raised_time = raised_days[...]
    pack[:groups, unit_rows:] = raised_time
    pack[groups:, unit_rows:] = jnp.zeros_like(raised_time)
    left = split_left(jnp.where(before, gap, 0.0)) + split_left(raised_time)
    left = jnp.concatenate(left, axis=0).astype(bf16)

    def multiply(here, high, low):
        product = days_dot(left, high, low)
        pack[:groups, here] = add_terms(product, groups)
        pack[groups:, here] = add_terms(product[3 * groups :], groups)

    for start in range(0, resident, block_rows):
        here = pl.ds(start, block_rows)
        multiply(here, high_ref[here, :], low_ref[here, :])
    for blocks, copy in parts:
        copy.wait()
        for here in blocks:
            there = pl.ds(here.start - resident, block_rows)
            high, low = split_panel(held[here, :])
            more_high[there, :] = high
            more_low[there, :] = low
            multiply(here, high, low)


def join_kernel(pack, post, out):
    rows, width = pack.shape
    out[:rows, :] = pack[...]
    out[rows:, : post.shape[1]] = post[...]
    out[rows:, post.shape[1] :] = jnp.zeros((post.shape[0], width - post.shape[1]), f32)


def third_kernel(half, *refs):
    parts, refs = refs[:half], refs[half:]
    high_ref, low_ref, more_high, more_low, norms, raised_units, ends, scaled, lam, out, block, out_sems = refs
    groups, unit_rows = raised_units.shape
    resident, day_cols = high_ref.shape
    unit_norm, ctrl_count = norms[:, 0:1], norms[:, 2:3]
    factor = -step_rate / jnp.sqrt(ends[:, 0:1])
    raised_days = [ref[:groups, unit_rows:] for ref in parts]
    time_norm = tree_sum(jnp.sum(value, axis=1, keepdims=True) for value in raised_days)
    lam[...] = raised_days[0] / time_norm
    time_grad = jnp.zeros((groups, day_cols), f32)
    new_sum = jnp.zeros((groups, 1), f32)
    for start in range(0, unit_rows, 2 * block_rows):
        here = pl.ds(start, 2 * block_rows)
        whole = tree_sum(ref[:, here] for ref in parts)
        raised = raised_units[:, here]
        new = raised / unit_norm * jnp.exp(whole[:groups] * factor)
        new_sum += jnp.sum(new, axis=1, keepdims=True)
        scaled[:, here] = new * ctrl_count
        shortfall = whole[groups : 2 * groups] / time_norm - whole[2 * groups :]
        left = left_of(jnp.where(raised > 0.0, shortfall, 0.0))
        if start < resident:
            high, low = high_ref[here, :], low_ref[here, :]
        else:
            there = pl.ds(start - resident, 2 * block_rows)
            high, low = more_high[there, :], more_low[there, :]
        time_grad += add_terms(rows_dot(left, high, low), groups)
    block[:, :day_cols] = time_grad
    block[:, day_cols:] = jnp.broadcast_to(new_sum, (groups, lanes))
    repeat_out(block, out, out_sems)


def fourth_kernel(unit_devices, grads, lam, norms, moved, moved_sum, totals):
    groups, day_cols = lam.shape
    total = tree_sum(grads[pl.ds(u * groups, groups), :] for u in range(unit_devices))
    root = jnp.sqrt(jnp.maximum(norms[:, 2:3], 1.0))
    new = lam[...] * jnp.exp(total[:, :day_cols] * (-step_rate / root))
    moved[...] = new
    totals[...] = total[:, day_cols:]
    moved_sum[...] = jnp.broadcast_to(jnp.sum(new, axis=1, keepdims=True), moved_sum.shape)


def fifth_kernel(half, *refs):
    moved_sums, refs = refs[:half], refs[half:]
    totals, scaled, moved, ends, unit_weights, time_weights = refs
    first = lax.axis_index("day") < half
    unit_weights[...] = scaled[...] / totals[:, 0:1]
    day_total = tree_sum(ref[:, 0:1] for ref in moved_sums)
    time_weights[...] = jnp.where(first, moved[...] / day_total * ends[:, 0:1], 0.0)


def sixth_kernel(half, sent_totals, sent_scaled, _, unit_weights, block, out_sem):
    @pl.when(lax.axis_index("day") >= half)
    def _():
        block[...] = sent_scaled[...] / sent_totals[:, 0:1]
        wait_all(fetch([block], [unit_weights], out_sem))


def local(outcomes, cohort, pre_end, post_start, unit_logit, time_logit):
    groups = pre_end.shape[0]
    unit_rows, day_cols = outcomes.shape
    day_devices = lax.axis_size("day")
    unit_devices = lax.axis_size("unit")
    half = day_devices // 2
    assert half * 2 == day_devices and half & (half - 1) == 0
    assert unit_devices & (unit_devices - 1) == 0
    chunks = 4
    resident = unit_rows * 5 // 8 // (2 * block_rows) * (2 * block_rows)
    def spread(value, day_xor, up):
        pairs = [
            (u * day_devices + d, u * day_devices + (d ^ day_xor) + up) for u in range(unit_devices) for d in range(half)
        ]
        return lax.ppermute(value, ("unit", "day"), pairs)

    def over_days(value):
        return [value] + [spread(value, k, 0) for k in range(1, half)]

    def over_units(value):
        members = list(reversed(range(unit_devices)))
        return lax.all_to_all(value, "unit", split_axis=0, concat_axis=0, axis_index_groups=[members], tiled=True)

    def call(kernel, shapes, name, args, in_specs=None, out_specs=None, **more):
        return pl.pallas_call(
            kernel,
            in_specs=in_specs or [vmem] * len(args),
            out_specs=out_specs or [vmem] * len(shapes),
            out_shape=[
                shape if isinstance(shape, type(in_hbm)) else jax.ShapeDtypeStruct(*shape) for shape in shapes
            ],
            compiler_params=params,
            name=name,
            **more,
        )(*args)

    arguments = (outcomes, cohort[None, :], pre_end[None, :], post_start[None, :], unit_logit, time_logit)
    fixed = [pltpu.with_memory_space_constraint(argument, pltpu.HBM) for argument in arguments]
    held = [pltpu.VMEM(argument.shape, argument.dtype) for argument in arguments]
    small_sems, panel_sems = pltpu.SemaphoreType.DMA((5,)), pltpu.SemaphoreType.DMA((chunks,))
    panel_terms = [((resident, day_cols), bf16)] * 2
    other_terms = [((unit_rows - resident, day_cols), bf16)] * 2
    out_sems = pltpu.SemaphoreType.DMA((unit_devices,))
    width = 2 * day_cols + lanes
    in_hbm = pltpu.HBM((unit_devices * groups, width), f32)
    sums, cross, raised_units, raised_days, ends, high, low = call(
        functools.partial(first_kernel, day_devices * day_cols, half, chunks),
        [
            in_hbm,
            ((groups, unit_rows), f32),
            ((groups, unit_rows), f32),
            ((groups, day_cols), f32),
            ((groups, lanes), f32),
            *panel_terms,
        ],
        "first_product",
        fixed,
        in_specs=[hbm] * 6,
        out_specs=[hbm] + [vmem] * 6,
        scratch_shapes=held
        + [
            pltpu.VMEM((groups, width), f32),
            pltpu.VMEM((4 * groups, unit_rows), bf16),
            small_sems,
            panel_sems,
            out_sems,
        ],
    )
    downward = [
        (u * day_devices + d + half, u * day_devices + d) for u in range(unit_devices) for d in range(half)
    ]
    post = lax.ppermute(cross, ("unit", "day"), downward)
    pack, norms, more_high, more_low = call(
        functools.partial(second_kernel, 3, unit_devices),
        [
            ((2 * groups, unit_rows + day_cols), f32),
            ((groups, lanes), f32),
            *other_terms,
        ],
        "unit_gradient",
        (fixed[0], over_units(sums), raised_days, ends, high, low),
        in_specs=[hbm] + [vmem] * 5,
        scratch_shapes=[held[0], panel_sems],
    )
    (pack,) = call(
        join_kernel, [((3 * groups, unit_rows + day_cols), f32)], "join_post", (pack, post)
    )
    width = day_cols + lanes
    scaled, lam, grads = call(
        functools.partial(third_kernel, half),
        [
            ((groups, unit_rows), f32),
            ((groups, day_cols), f32),
            pltpu.HBM((unit_devices * groups, width), f32),
        ],
        "time_gradient",
        (*over_days(pack), high, low, more_high, more_low, norms, raised_units, ends),
        out_specs=[vmem, vmem, hbm],
        scratch_shapes=[pltpu.VMEM((groups, width), f32), out_sems],
    )
    sent_scaled = spread(scaled, 0, half)
    moved, moved_sum, totals = call(
        functools.partial(fourth_kernel, unit_devices),
        [((groups, day_cols), f32), ((groups, lanes), f32), ((groups, lanes), f32)],
        "new_time_weights",
        (over_units(grads), lam, norms),
    )
    unit_weights, time_weights = call(
        functools.partial(fifth_kernel, half),
        [((groups, unit_rows), f32), ((groups, day_cols), f32)],
        "scale_weights",
        (*over_days(moved_sum), totals, scaled, moved, ends),
    )
    (unit_weights,) = call(
        functools.partial(sixth_kernel, half),
        [((groups, unit_rows), f32)],
        "other_half",
        (spread(totals, 0, half), sent_scaled, unit_weights),
        in_specs=[vmem, vmem, hbm],
        out_specs=[hbm],
        input_output_aliases={2: 0},
        scratch_shapes=[pltpu.VMEM((groups, unit_rows), f32), pltpu.SemaphoreType.DMA((1,))],
    )
    return unit_weights, time_weights


def solution(mesh):
    return jax.shard_map(
        local,
        mesh=mesh,
        in_specs=(P("unit", "day"), P("unit"), P(), P(), P(None, "unit"), P(None, "day")),
        out_specs=(P(None, "unit"), P(None, "day")),
        check_vma=False,
    )
```

```python
import functools

import jax
import jax.numpy as jnp
from jax import lax
from jax.experimental import pallas as pl
from jax.experimental.pallas import tpu as pltpu
from jax.sharding import PartitionSpec as P

step_rate = 16.0
f32 = jnp.float32
bf16 = jnp.bfloat16
lanes = 128
block_rows = 256
params = pltpu.CompilerParams(vmem_limit_bytes=24 * 1024 * 1024)
vmem = pl.BlockSpec(memory_space=pltpu.VMEM)
hbm = pl.BlockSpec(memory_space=pltpu.HBM)


def split_left(value):
    first = value.astype(bf16).astype(f32)
    return [first, value - first]


def left_of(*values):
    return jnp.concatenate([term for value in values for term in split_left(value)], axis=0).astype(bf16)


def split_panel(value):
    high = value.astype(bf16)
    return high, (value - high.astype(f32)).astype(bf16)


def rows_dot(left, high, low):
    return jnp.dot(left, high, preferred_element_type=f32) + jnp.dot(left, low, preferred_element_type=f32)


def days_dot(left, high, low):
    dims = (((1,), (1,)), ((), ()))
    return lax.dot_general(left, high, dims, preferred_element_type=f32) + lax.dot_general(
        left, low, dims, preferred_element_type=f32
    )


def add_terms(stack, groups, place=0):
    return stack[2 * place * groups :][:groups] + stack[(2 * place + 1) * groups :][:groups]


def tree_sum(values):
    values = list(values)
    while len(values) > 1:
        values = [values[i] + values[i + 1] for i in range(0, len(values), 2)]
    return values[0]


def column(row_ref):
    count = row_ref.shape[1]
    wide = jnp.broadcast_to(row_ref[...].astype(f32), (count, count))
    row = lax.broadcasted_iota(jnp.int32, (count, count), 0)
    lane = lax.broadcasted_iota(jnp.int32, (count, count), 1)
    return jnp.sum(jnp.where(row == lane, wide, 0.0), axis=1, keepdims=True).astype(jnp.int32)


def days_of(device, shape):
    return device * shape[1] + lax.broadcasted_iota(jnp.int32, shape, 1)


def fetch(sources, targets, sems):
    copies = [pltpu.make_async_copy(*pair, sems.at[i]) for i, pair in enumerate(zip(sources, targets))]
    for copy in copies:
        copy.start()
    return copies


def fetch_rows(source, target, sems, chunks, first=0):
    rows = (source.shape[0] - first) // chunks
    starts = [first + chunk * rows for chunk in range(chunks)]
    parts = [pl.ds(start, rows) for start in starts]
    copies = fetch([source.at[here] for here in parts], [target.at[here] for here in parts], sems)
    return [(start, rows, copy) for start, copy in zip(starts, copies)]


def blocks_of(start, rows):
    return [pl.ds(here, block_rows) for here in range(start, start + rows, block_rows)]


def split_chunk(panel, start, rows, high_ref, low_ref, offset):
    for here in blocks_of(start, rows):
        there = pl.ds(here.start - offset, block_rows)
        high_ref[there, :], low_ref[there, :] = split_panel(panel[here, :])


def wait_all(copies):
    for copy in copies:
        copy.wait()


def repeat_out(block, out, sems):
    rows = block.shape[0]
    places = [out.at[pl.ds(i * rows, rows)] for i in range(out.shape[0] // rows)]
    wait_all(fetch([block] * len(places), places, sems))


def first_kernel(all_count, half, chunks, *refs):
    arguments, refs = refs[:6], refs[6:]
    out, cross, raised_units, raised_days, ends, high_ref, low_ref, *held, block, left_ref, more_high, more_low, small_sems, panel_sems, out_sems = refs
    groups, day_cols = held[5].shape
    unit_rows, resident = held[0].shape[0], high_ref.shape[0]
    small = fetch(arguments[1:], held[1:], small_sems)
    parts = fetch_rows(arguments[0], held[0], panel_sems, chunks)
    panel, cohort, pre_row, post_row, unit_logit, time_logit = held
    wait_all(small)
    me = lax.axis_index("day")

    @pl.when(me < half)
    def _():
        label = lax.broadcasted_iota(jnp.int32, (groups, unit_rows), 0)
        treated = jnp.where(cohort[...] == label, 1.0, 0.0)
        control = jnp.where(cohort[...] > label, 1.0, 0.0)
        raised = jnp.exp(unit_logit[...]) * control
        raised_units[...] = raised
        left_ref[...] = left_of(raised, treated)
        pre_end = column(pre_row)
        ends[...] = jnp.broadcast_to(pre_end.astype(f32), ends.shape)
        before = days_of(me, (groups, day_cols)) < pre_end
        raised_days[...] = jnp.where(before, jnp.exp(time_logit[...]), 0.0)
        lane = lax.broadcasted_iota(jnp.int32, (groups, lanes), 1)
        block[:, 2 * day_cols :] = jnp.where(
            lane == 0,
            jnp.sum(raised, axis=1, keepdims=True),
            jnp.where(
                lane == 1, jnp.sum(treated, axis=1, keepdims=True), jnp.sum(control, axis=1, keepdims=True)
            ),
        )
        product = jnp.zeros((4 * groups, day_cols), f32)

        def terms_of(start):
            if start < resident:
                return high_ref, low_ref, 0
            return more_high, more_low, resident

        def multiply(start, rows):
            high, low, offset = terms_of(start)
            there = pl.ds(start - offset, rows)
            return rows_dot(left_ref[:, start : start + rows], high[there, :], low[there, :])

        before_it = None
        for start, rows, copy in parts:
            copy.wait()
            if before_it:
                product += multiply(*before_it)
            split_chunk(panel, start, rows, *terms_of(start))
            before_it = start, rows
        product += multiply(*before_it)
        block[:, :day_cols] = add_terms(product, groups)
        block[:, day_cols : 2 * day_cols] = product[2 * groups :][:groups]
        repeat_out(block, out, out_sems)

    @pl.when(me >= half)
    def _():
        post_start = column(post_row)
        after = jnp.where(days_of(me, (groups, day_cols)) >= post_start, 1.0, 0.0)
        left = left_of(after / (all_count - post_start).astype(f32))
        for start, rows, copy in parts:
            copy.wait()
            for here in blocks_of(start, rows):
                cross[:, here] = add_terms(days_dot(left, *split_panel(panel[here, :])), groups)


def second_kernel(chunks, unit_devices, panel, sums, raised_days, ends, high_ref, low_ref, *refs):
    pack, norms, more_high, more_low, held, panel_sems = refs
    groups, day_cols = raised_days.shape
    unit_rows, resident = panel.shape[0], high_ref.shape[0]
    parts = fetch_rows(panel, held, panel_sems, chunks, resident)
    total = tree_sum(sums[pl.ds(u * groups, groups), :] for u in range(unit_devices))
    unit_norm = total[:, 2 * day_cols : 2 * day_cols + 1]
    treat_count = jnp.maximum(total[:, 2 * day_cols + 1 : 2 * day_cols + 2], 1.0)
    norms[...] = total[:, 2 * day_cols :]
    gap = total[:, :day_cols] / unit_norm - total[:, day_cols : 2 * day_cols] / treat_count
    before = days_of(lax.axis_index("day"), (groups, day_cols)).astype(f32) < ends[:, 0:1]
    raised_time = raised_days[...]
    pack[:groups, unit_rows:] = raised_time
    pack[groups:, unit_rows:] = jnp.zeros_like(raised_time)
    left = left_of(jnp.where(before, gap, 0.0), raised_time)

    def multiply(start, rows, high, low, offset):
        for here in blocks_of(start, rows):
            there = pl.ds(here.start - offset, block_rows)
            product = days_dot(left, high[there, :], low[there, :])
            pack[:groups, here] = add_terms(product, groups)
            pack[groups:, here] = add_terms(product, groups, 1)

    early = resident // block_rows // 2 * block_rows
    multiply(0, early, high_ref, low_ref, 0)
    before_it = early, resident - early, high_ref, low_ref, 0
    for start, rows, copy in parts:
        copy.wait()
        multiply(*before_it)
        split_chunk(held, start, rows, more_high, more_low, resident)
        before_it = start, rows, more_high, more_low, resident
    multiply(*before_it)


def join_kernel(pack, post, out):
    rows, width = pack.shape
    out[:rows, :] = pack[...]
    out[rows:, : post.shape[1]] = post[...]
    out[rows:, post.shape[1] :] = jnp.zeros((post.shape[0], width - post.shape[1]), f32)


def third_kernel(half, *refs):
    parts, refs = refs[:half], refs[half:]
    high_ref, low_ref, more_high, more_low, norms, raised_units, ends, scaled, lam, out, block, out_sems = refs
    groups, unit_rows = raised_units.shape
    resident, day_cols = high_ref.shape
    unit_norm, ctrl_count = norms[:, 0:1], norms[:, 2:3]
    factor = -step_rate / jnp.sqrt(ends[:, 0:1])
    raised_days = [ref[:groups, unit_rows:] for ref in parts]
    over_time = 1.0 / tree_sum(jnp.sum(value, axis=1, keepdims=True) for value in raised_days)
    over_unit = 1.0 / unit_norm
    lam[...] = raised_days[0] * over_time
    time_grad = jnp.zeros((groups, day_cols), f32)
    new_sum = jnp.zeros((groups, 1), f32)
    for start in range(0, unit_rows, 2 * block_rows):
        here = pl.ds(start, 2 * block_rows)
        whole = tree_sum(ref[:, here] for ref in parts)
        raised = raised_units[:, here]
        new = raised * over_unit * jnp.exp(whole[:groups] * factor)
        new_sum += jnp.sum(new, axis=1, keepdims=True)
        scaled[:, here] = new * ctrl_count
        shortfall = whole[groups : 2 * groups] * over_time - whole[2 * groups :]
        left = left_of(jnp.where(raised > 0.0, shortfall, 0.0))
        if start < resident:
            high, low = high_ref[here, :], low_ref[here, :]
        else:
            there = pl.ds(start - resident, 2 * block_rows)
            high, low = more_high[there, :], more_low[there, :]
        time_grad += add_terms(rows_dot(left, high, low), groups)
    block[:, :day_cols] = time_grad
    block[:, day_cols:] = jnp.broadcast_to(new_sum, (groups, lanes))
    repeat_out(block, out, out_sems)


def fourth_kernel(unit_devices, grads, lam, norms, moved, moved_sum, totals):
    groups, day_cols = lam.shape
    total = tree_sum(grads[pl.ds(u * groups, groups), :] for u in range(unit_devices))
    root = jnp.sqrt(jnp.maximum(norms[:, 2:3], 1.0))
    new = lam[...] * jnp.exp(total[:, :day_cols] * (-step_rate / root))
    moved[...] = new
    totals[...] = total[:, day_cols:]
    moved_sum[...] = jnp.broadcast_to(jnp.sum(new, axis=1, keepdims=True), moved_sum.shape)


def fifth_kernel(half, *refs):
    moved_sums, refs = refs[:half], refs[half:]
    totals, scaled, moved, ends, unit_weights, time_weights = refs
    first = lax.axis_index("day") < half
    unit_weights[...] = scaled[...] / totals[:, 0:1]
    day_total = tree_sum(ref[:, 0:1] for ref in moved_sums)
    time_weights[...] = jnp.where(first, moved[...] / day_total * ends[:, 0:1], 0.0)


def sixth_kernel(half, sent_totals, sent_scaled, _, unit_weights, block, out_sem):
    @pl.when(lax.axis_index("day") >= half)
    def _():
        block[...] = sent_scaled[...] / sent_totals[:, 0:1]
        wait_all(fetch([block], [unit_weights], out_sem))


def local(outcomes, cohort, pre_end, post_start, unit_logit, time_logit):
    groups = pre_end.shape[0]
    unit_rows, day_cols = outcomes.shape
    day_devices = lax.axis_size("day")
    unit_devices = lax.axis_size("unit")
    half = day_devices // 2
    assert half * 2 == day_devices and half & (half - 1) == 0
    assert unit_devices & (unit_devices - 1) == 0
    chunks = 8
    resident = unit_rows * 5 // 8 // (2 * block_rows) * (2 * block_rows)
    def spread(value, day_xor, up):
        pairs = [
            (u * day_devices + d, u * day_devices + (d ^ day_xor) + up) for u in range(unit_devices) for d in range(half)
        ]
        return lax.ppermute(value, ("unit", "day"), pairs)

    def over_days(value):
        return [value] + [spread(value, k, 0) for k in range(1, half)]

    def over_units(value):
        members = list(reversed(range(unit_devices)))
        return lax.all_to_all(value, "unit", split_axis=0, concat_axis=0, axis_index_groups=[members], tiled=True)

    def call(kernel, shapes, name, args, in_specs=None, out_specs=None, **more):
        return pl.pallas_call(
            kernel,
            in_specs=in_specs or [vmem] * len(args),
            out_specs=out_specs or [vmem] * len(shapes),
            out_shape=[
                shape if isinstance(shape, type(in_hbm)) else jax.ShapeDtypeStruct(*shape) for shape in shapes
            ],
            compiler_params=params,
            name=name,
            **more,
        )(*args)

    arguments = (outcomes, cohort[None, :], pre_end[None, :], post_start[None, :], unit_logit, time_logit)
    fixed = [pltpu.with_memory_space_constraint(argument, pltpu.HBM) for argument in arguments]
    held = [pltpu.VMEM(argument.shape, argument.dtype) for argument in arguments]
    small_sems, panel_sems = pltpu.SemaphoreType.DMA((5,)), pltpu.SemaphoreType.DMA((chunks,))
    panel_terms = [((resident, day_cols), bf16)] * 2
    other_terms = [((unit_rows - resident, day_cols), bf16)] * 2
    out_sems = pltpu.SemaphoreType.DMA((unit_devices,))
    width = 2 * day_cols + lanes
    in_hbm = pltpu.HBM((unit_devices * groups, width), f32)
    sums, cross, raised_units, raised_days, ends, high, low = call(
        functools.partial(first_kernel, day_devices * day_cols, half, chunks),
        [
            in_hbm,
            ((groups, unit_rows), f32),
            ((groups, unit_rows), f32),
            ((groups, day_cols), f32),
            ((groups, lanes), f32),
            *panel_terms,
        ],
        "first_product",
        fixed,
        in_specs=[hbm] * 6,
        out_specs=[hbm] + [vmem] * 6,
        scratch_shapes=held
        + [
            pltpu.VMEM((groups, width), f32),
            pltpu.VMEM((4 * groups, unit_rows), bf16),
            *[pltpu.VMEM(*shape) for shape in other_terms],
            small_sems,
            panel_sems,
            out_sems,
        ],
    )
    downward = [
        (u * day_devices + d + half, u * day_devices + d) for u in range(unit_devices) for d in range(half)
    ]
    post = lax.ppermute(cross, ("unit", "day"), downward)
    pack, norms, more_high, more_low = call(
        functools.partial(second_kernel, 3, unit_devices),
        [
            ((2 * groups, unit_rows + day_cols), f32),
            ((groups, lanes), f32),
            *other_terms,
        ],
        "unit_gradient",
        (fixed[0], over_units(sums), raised_days, ends, high, low),
        in_specs=[hbm] + [vmem] * 5,
        scratch_shapes=[held[0], panel_sems],
    )
    (pack,) = call(
        join_kernel, [((3 * groups, unit_rows + day_cols), f32)], "join_post", (pack, post)
    )
    width = day_cols + lanes
    scaled, lam, grads = call(
        functools.partial(third_kernel, half),
        [
            ((groups, unit_rows), f32),
            ((groups, day_cols), f32),
            pltpu.HBM((unit_devices * groups, width), f32),
        ],
        "time_gradient",
        (*over_days(pack), high, low, more_high, more_low, norms, raised_units, ends),
        out_specs=[vmem, vmem, hbm],
        scratch_shapes=[pltpu.VMEM((groups, width), f32), out_sems],
    )
    sent_scaled = spread(scaled, 0, half)
    moved, moved_sum, totals = call(
        functools.partial(fourth_kernel, unit_devices),
        [((groups, day_cols), f32), ((groups, lanes), f32), ((groups, lanes), f32)],
        "new_time_weights",
        (over_units(grads), lam, norms),
    )
    unit_weights, time_weights = call(
        functools.partial(fifth_kernel, half),
        [((groups, unit_rows), f32), ((groups, day_cols), f32)],
        "scale_weights",
        (*over_days(moved_sum), totals, scaled, moved, ends),
    )
    (unit_weights,) = call(
        functools.partial(sixth_kernel, half),
        [((groups, unit_rows), f32)],
        "other_half",
        (spread(totals, 0, half), sent_scaled, unit_weights),
        in_specs=[vmem, vmem, hbm],
        out_specs=[hbm],
        input_output_aliases={2: 0},
        scratch_shapes=[pltpu.VMEM((groups, unit_rows), f32), pltpu.SemaphoreType.DMA((1,))],
    )
    return unit_weights, time_weights


def solution(mesh):
    return jax.shard_map(
        local,
        mesh=mesh,
        in_specs=(P("unit", "day"), P("unit"), P(), P(), P(None, "unit"), P(None, "day")),
        out_specs=(P(None, "unit"), P(None, "day")),
        check_vma=False,
    )
```

```python
import functools

import jax
import jax.numpy as jnp
from jax import lax
from jax.experimental import pallas as pl
from jax.experimental.pallas import tpu as pltpu
from jax.sharding import PartitionSpec as P

step_rate = 16.0
f32 = jnp.float32
bf16 = jnp.bfloat16
lanes = 128
block_rows = 256
params = pltpu.CompilerParams(vmem_limit_bytes=24 * 1024 * 1024)
vmem = pl.BlockSpec(memory_space=pltpu.VMEM)
hbm = pl.BlockSpec(memory_space=pltpu.HBM)


def split_left(value):
    first = value.astype(bf16).astype(f32)
    return [first, value - first]


def left_of(*values):
    return jnp.concatenate([term for value in values for term in split_left(value)], axis=0).astype(bf16)


def split_panel(value):
    high = value.astype(bf16)
    return high, (value - high.astype(f32)).astype(bf16)


def rows_dot(left, high, low):
    return jnp.dot(left, high, preferred_element_type=f32) + jnp.dot(left, low, preferred_element_type=f32)


def days_dot(left, high, low):
    dims = (((1,), (1,)), ((), ()))
    return lax.dot_general(left, high, dims, preferred_element_type=f32) + lax.dot_general(
        left, low, dims, preferred_element_type=f32
    )


def add_terms(stack, groups, place=0):
    return stack[2 * place * groups :][:groups] + stack[(2 * place + 1) * groups :][:groups]


def tree_sum(values):
    values = list(values)
    while len(values) > 1:
        values = [values[i] + values[i + 1] for i in range(0, len(values), 2)]
    return values[0]


def column(row_ref):
    count = row_ref.shape[1]
    wide = jnp.broadcast_to(row_ref[...].astype(f32), (count, count))
    row = lax.broadcasted_iota(jnp.int32, (count, count), 0)
    lane = lax.broadcasted_iota(jnp.int32, (count, count), 1)
    return jnp.sum(jnp.where(row == lane, wide, 0.0), axis=1, keepdims=True).astype(jnp.int32)


def days_of(device, shape):
    return device * shape[1] + lax.broadcasted_iota(jnp.int32, shape, 1)


def fetch(sources, targets, sems):
    copies = [pltpu.make_async_copy(*pair, sems.at[i]) for i, pair in enumerate(zip(sources, targets))]
    for copy in copies:
        copy.start()
    return copies


def fetch_rows(source, target, sems, starts):
    spans = [(start, stop - start) for start, stop in zip(starts, starts[1:])]
    parts = [pl.ds(*span) for span in spans]
    copies = fetch([source.at[here] for here in parts], [target.at[here] for here in parts], sems)
    return [(*span, copy) for span, copy in zip(spans, copies)]


def blocks_of(start, rows):
    return [pl.ds(here, block_rows) for here in range(start, start + rows, block_rows)]


def wait_all(copies):
    for copy in copies:
        copy.wait()


def repeat_out(block, out, sems):
    rows = block.shape[0]
    places = [out.at[pl.ds(i * rows, rows)] for i in range(out.shape[0] // rows)]
    wait_all(fetch([block] * len(places), places, sems))


def first_kernel(all_count, half, starts, *refs):
    arguments, refs = refs[:6], refs[6:]
    out, cross, raised_units, raised_days, ends, high_ref, low_ref, *held, block, left_ref, small_sems, panel_sems, out_sems = refs
    groups, day_cols = held[5].shape
    unit_rows, resident = held[0].shape[0], high_ref.shape[0]
    small = fetch(arguments[1:], held[1:], small_sems)
    parts = fetch_rows(arguments[0], held[0], panel_sems, starts)
    panel, cohort, pre_row, post_row, unit_logit, time_logit = held
    wait_all(small)
    me = lax.axis_index("day")

    @pl.when(me < half)
    def _():
        label = lax.broadcasted_iota(jnp.int32, (groups, unit_rows), 0)
        treated = jnp.where(cohort[...] == label, 1.0, 0.0)
        control = jnp.where(cohort[...] > label, 1.0, 0.0)
        raised = jnp.exp(unit_logit[...]) * control
        raised_units[...] = raised
        left_ref[...] = left_of(raised, treated)
        pre_end = column(pre_row)
        ends[...] = jnp.broadcast_to(pre_end.astype(f32), ends.shape)
        before = days_of(me, (groups, day_cols)) < pre_end
        raised_days[...] = jnp.where(before, jnp.exp(time_logit[...]), 0.0)
        lane = lax.broadcasted_iota(jnp.int32, (groups, lanes), 1)
        block[:, 2 * day_cols :] = jnp.where(
            lane == 0,
            jnp.sum(raised, axis=1, keepdims=True),
            jnp.where(
                lane == 1, jnp.sum(treated, axis=1, keepdims=True), jnp.sum(control, axis=1, keepdims=True)
            ),
        )
        product = jnp.zeros((4 * groups, 2 * day_cols), f32)
        for start, rows, copy in parts:
            copy.wait()
            for here in blocks_of(start, rows):
                high, low = split_panel(panel[here, :])
                if here.start < resident:
                    high_ref[here, :] = high
                    low_ref[here, :] = low
                both = jnp.concatenate([high, low], axis=1)
                product += jnp.dot(left_ref[:, here], both, preferred_element_type=f32)
        product = product[:, :day_cols] + product[:, day_cols:]
        block[:, :day_cols] = add_terms(product, groups)
        block[:, day_cols : 2 * day_cols] = product[2 * groups :][:groups]
        repeat_out(block, out, out_sems)

    @pl.when(me >= half)
    def _():
        post_start = column(post_row)
        after = jnp.where(days_of(me, (groups, day_cols)) >= post_start, 1.0, 0.0)
        left = left_of(after / (all_count - post_start).astype(f32))
        for start, rows, copy in parts:
            copy.wait()
            for here in blocks_of(start, rows):
                cross[:, here] = add_terms(days_dot(left, *split_panel(panel[here, :])), groups)


def second_kernel(unit_devices, panel, sums, raised_days, ends, high_ref, low_ref, *refs):
    pack, norms, more_high, more_low, held, panel_sems = refs
    groups, day_cols = raised_days.shape
    unit_rows, resident = panel.shape[0], high_ref.shape[0]
    rest = pl.ds(resident, unit_rows - resident)
    (copy,) = fetch([panel.at[rest]], [held.at[rest]], panel_sems)
    total = tree_sum(sums[pl.ds(u * groups, groups), :] for u in range(unit_devices))
    unit_norm = total[:, 2 * day_cols : 2 * day_cols + 1]
    treat_count = jnp.maximum(total[:, 2 * day_cols + 1 : 2 * day_cols + 2], 1.0)
    norms[...] = total[:, 2 * day_cols :]
    gap = total[:, :day_cols] / unit_norm - total[:, day_cols : 2 * day_cols] / treat_count
    before = days_of(lax.axis_index("day"), (groups, day_cols)).astype(f32) < ends[:, 0:1]
    raised_time = raised_days[...]
    pack[:groups, unit_rows:] = raised_time
    pack[groups:, unit_rows:] = jnp.zeros_like(raised_time)
    left = left_of(jnp.where(before, gap, 0.0), raised_time)

    def multiply(here, high, low):
        product = days_dot(left, high, low)
        pack[:groups, here] = add_terms(product, groups)
        pack[groups:, here] = add_terms(product, groups, 1)

    for here in blocks_of(0, resident):
        multiply(here, high_ref[here, :], low_ref[here, :])
    copy.wait()
    for here in blocks_of(resident, unit_rows - resident):
        there = pl.ds(here.start - resident, block_rows)
        high, low = split_panel(held[here, :])
        more_high[there, :] = high
        more_low[there, :] = low
        multiply(here, high, low)


def join_kernel(pack, post, out):
    rows, width = pack.shape
    out[:rows, :] = pack[...]
    out[rows:, : post.shape[1]] = post[...]
    out[rows:, post.shape[1] :] = jnp.zeros((post.shape[0], width - post.shape[1]), f32)


def third_kernel(half, *refs):
    parts, refs = refs[:half], refs[half:]
    high_ref, low_ref, more_high, more_low, norms, raised_units, ends, scaled, lam, out, block, out_sems = refs
    groups, unit_rows = raised_units.shape
    resident, day_cols = high_ref.shape
    unit_norm, ctrl_count = norms[:, 0:1], norms[:, 2:3]
    factor = -step_rate / jnp.sqrt(ends[:, 0:1])
    raised_days = [ref[:groups, unit_rows:] for ref in parts]
    over_time = 1.0 / tree_sum(jnp.sum(value, axis=1, keepdims=True) for value in raised_days)
    over_unit = 1.0 / unit_norm
    me = lax.rem(lax.axis_index("day"), half)
    for day in range(half):
        here = raised_days[0]
        for k in range(1, half):
            here = jnp.where(jnp.bitwise_xor(me, k) == day, raised_days[k], here)
        lam[:, day * day_cols : (day + 1) * day_cols] = here * over_time
    time_grad = jnp.zeros((groups, day_cols), f32)
    new_sum = jnp.zeros((groups, 1), f32)
    for start in range(0, unit_rows, 2 * block_rows):
        here = pl.ds(start, 2 * block_rows)
        whole = tree_sum(ref[:, here] for ref in parts)
        raised = raised_units[:, here]
        new = raised * over_unit * jnp.exp(whole[:groups] * factor)
        new_sum += jnp.sum(new, axis=1, keepdims=True)
        scaled[:, here] = new * ctrl_count
        shortfall = whole[groups : 2 * groups] * over_time - whole[2 * groups :]
        left = left_of(jnp.where(raised > 0.0, shortfall, 0.0))
        if start < resident:
            high, low = high_ref[here, :], low_ref[here, :]
        else:
            there = pl.ds(start - resident, 2 * block_rows)
            high, low = more_high[there, :], more_low[there, :]
        time_grad += add_terms(rows_dot(left, high, low), groups)
    lane = lax.broadcasted_iota(jnp.int32, (groups, day_cols), 1)
    spare = (lane == day_cols - 1) & (me == half - 1)
    block[...] = jnp.where(spare, new_sum, time_grad)
    repeat_out(block, out, out_sems)


def fourth_kernel(unit_devices, half, grads, lam, norms, ends, own_days, totals):
    groups, day_cols = own_days.shape
    root = jnp.sqrt(jnp.maximum(norms[:, 2:3], 1.0))
    me = lax.axis_index("day")
    moved_total = jnp.zeros((groups, 1), f32)
    own = jnp.zeros((groups, day_cols), f32)
    for day in range(half):
        places = [(unit * half + half - 1 - day) * groups for unit in range(unit_devices)]
        total = tree_sum(grads[pl.ds(place, groups), :] for place in places)
        moved = lam[:, day * day_cols : (day + 1) * day_cols] * jnp.exp(total * (-step_rate / root))
        moved_total += jnp.sum(moved, axis=1, keepdims=True)
        own = jnp.where(me == day, moved, own)
    totals[...] = jnp.broadcast_to(total[:, day_cols - 1 :], totals.shape)
    own_days[...] = own * (ends[:, 0:1] / moved_total)


def fifth_kernel(half, totals, scaled, own_days, unit_weights, time_weights):
    unit_weights[...] = scaled[...] / totals[:, 0:1]
    time_weights[...] = jnp.where(lax.axis_index("day") < half, own_days[...], 0.0)


def sixth_kernel(half, sent_totals, sent_scaled, _, unit_weights, block, out_sem):
    @pl.when(lax.axis_index("day") >= half)
    def _():
        block[...] = sent_scaled[...] / sent_totals[:, 0:1]
        wait_all(fetch([block], [unit_weights], out_sem))


def local(outcomes, cohort, pre_end, post_start, unit_logit, time_logit):
    groups = pre_end.shape[0]
    unit_rows, day_cols = outcomes.shape
    day_devices = lax.axis_size("day")
    unit_devices = lax.axis_size("unit")
    half = day_devices // 2
    assert half * 2 == day_devices and half & (half - 1) == 0
    assert unit_devices & (unit_devices - 1) == 0
    panel_starts = [0, unit_rows // 4, unit_rows // 8 * 5, unit_rows]
    resident = unit_rows * 5 // 8 // (2 * block_rows) * (2 * block_rows)
    def spread(value, day_xor, up):
        pairs = [
            (u * day_devices + d, u * day_devices + (d ^ day_xor) + up) for u in range(unit_devices) for d in range(half)
        ]
        return lax.ppermute(value, ("unit", "day"), pairs)

    def over_days(value):
        return [value] + [spread(value, k, 0) for k in range(1, half)]

    def over_first_half(value):
        members = [
            [unit * day_devices + day for unit in reversed(range(unit_devices)) for day in reversed(days)]
            for days in (range(half), range(half, day_devices))
        ]
        return lax.all_to_all(
            value, ("unit", "day"), split_axis=0, concat_axis=0, axis_index_groups=members, tiled=True
        )

    def over_units(value):
        members = list(reversed(range(unit_devices)))
        return lax.all_to_all(value, "unit", split_axis=0, concat_axis=0, axis_index_groups=[members], tiled=True)

    def call(kernel, shapes, name, args, in_specs=None, out_specs=None, **more):
        return pl.pallas_call(
            kernel,
            in_specs=in_specs or [vmem] * len(args),
            out_specs=out_specs or [vmem] * len(shapes),
            out_shape=[
                shape if isinstance(shape, type(in_hbm)) else jax.ShapeDtypeStruct(*shape) for shape in shapes
            ],
            compiler_params=params,
            name=name,
            **more,
        )(*args)

    arguments = (outcomes, cohort[None, :], pre_end[None, :], post_start[None, :], unit_logit, time_logit)
    fixed = [pltpu.with_memory_space_constraint(argument, pltpu.HBM) for argument in arguments]
    held = [pltpu.VMEM(argument.shape, argument.dtype) for argument in arguments]
    small_sems, panel_sems = pltpu.SemaphoreType.DMA((5,)), pltpu.SemaphoreType.DMA((3,))
    panel_terms = [((resident, day_cols), bf16)] * 2
    other_terms = [((unit_rows - resident, day_cols), bf16)] * 2
    out_sems = pltpu.SemaphoreType.DMA((unit_devices,))
    width = 2 * day_cols + lanes
    in_hbm = pltpu.HBM((unit_devices * groups, width), f32)
    sums, cross, raised_units, raised_days, ends, high, low = call(
        functools.partial(first_kernel, day_devices * day_cols, half, panel_starts),
        [
            in_hbm,
            ((groups, unit_rows), f32),
            ((groups, unit_rows), f32),
            ((groups, day_cols), f32),
            ((groups, lanes), f32),
            *panel_terms,
        ],
        "first_product",
        fixed,
        in_specs=[hbm] * 6,
        out_specs=[hbm] + [vmem] * 6,
        scratch_shapes=held
        + [
            pltpu.VMEM((groups, width), f32),
            pltpu.VMEM((4 * groups, unit_rows), bf16),
            small_sems,
            panel_sems,
            out_sems,
        ],
    )
    downward = [
        (u * day_devices + d + half, u * day_devices + d) for u in range(unit_devices) for d in range(half)
    ]
    post = lax.ppermute(cross, ("unit", "day"), downward)
    pack, norms, more_high, more_low = call(
        functools.partial(second_kernel, unit_devices),
        [
            ((2 * groups, unit_rows + day_cols), f32),
            ((groups, lanes), f32),
            *other_terms,
        ],
        "unit_gradient",
        (fixed[0], over_units(sums), raised_days, ends, high, low),
        in_specs=[hbm] + [vmem] * 5,
        scratch_shapes=[held[0], panel_sems],
    )
    (pack,) = call(
        join_kernel, [((3 * groups, unit_rows + day_cols), f32)], "join_post", (pack, post)
    )
    members = unit_devices * half
    scaled, lam, grads = call(
        functools.partial(third_kernel, half),
        [
            ((groups, unit_rows), f32),
            ((groups, half * day_cols), f32),
            pltpu.HBM((members * groups, day_cols), f32),
        ],
        "time_gradient",
        (*over_days(pack), high, low, more_high, more_low, norms, raised_units, ends),
        out_specs=[vmem, vmem, hbm],
        scratch_shapes=[pltpu.VMEM((groups, day_cols), f32), pltpu.SemaphoreType.DMA((members,))],
    )
    sent_scaled = spread(scaled, 0, half)
    own_days, totals = call(
        functools.partial(fourth_kernel, unit_devices, half),
        [((groups, day_cols), f32), ((groups, lanes), f32)],
        "new_time_weights",
        (over_first_half(grads), lam, norms, ends),
    )
    unit_weights, time_weights = call(
        functools.partial(fifth_kernel, half),
        [((groups, unit_rows), f32), ((groups, day_cols), f32)],
        "scale_weights",
        (totals, scaled, own_days),
    )
    (unit_weights,) = call(
        functools.partial(sixth_kernel, half),
        [((groups, unit_rows), f32)],
        "other_half",
        (spread(totals, 0, half), sent_scaled, unit_weights),
        in_specs=[vmem, vmem, hbm],
        out_specs=[hbm],
        input_output_aliases={2: 0},
        scratch_shapes=[pltpu.VMEM((groups, unit_rows), f32), pltpu.SemaphoreType.DMA((1,))],
    )
    return unit_weights, time_weights


def solution(mesh):
    return jax.shard_map(
        local,
        mesh=mesh,
        in_specs=(P("unit", "day"), P("unit"), P(), P(), P(None, "unit"), P(None, "day")),
        out_specs=(P(None, "unit"), P(None, "day")),
        check_vma=False,
    )
```

```python
import functools

import jax
import jax.numpy as jnp
from jax import lax
from jax.experimental import pallas as pl
from jax.experimental.pallas import tpu as pltpu
from jax.sharding import PartitionSpec as P

step_rate = 16.0
f32 = jnp.float32
bf16 = jnp.bfloat16
lanes = 128
block_rows = 256
params = pltpu.CompilerParams(vmem_limit_bytes=24 * 1024 * 1024)
vmem = pl.BlockSpec(memory_space=pltpu.VMEM)
hbm = pl.BlockSpec(memory_space=pltpu.HBM)


def split_left(value):
    first = value.astype(bf16).astype(f32)
    return [first, value - first]


def left_of(*values):
    return jnp.concatenate([term for value in values for term in split_left(value)], axis=0).astype(bf16)


def split_panel(value):
    high = value.astype(bf16)
    return high, (value - high.astype(f32)).astype(bf16)


def rows_dot(left, high, low):
    return jnp.dot(left, high, preferred_element_type=f32) + jnp.dot(left, low, preferred_element_type=f32)


def days_dot(left, high, low):
    dims = (((1,), (1,)), ((), ()))
    return lax.dot_general(left, high, dims, preferred_element_type=f32) + lax.dot_general(
        left, low, dims, preferred_element_type=f32
    )


def add_terms(stack, groups, place=0):
    return stack[2 * place * groups :][:groups] + stack[(2 * place + 1) * groups :][:groups]


def tree_sum(values):
    values = list(values)
    while len(values) > 1:
        values = [values[i] + values[i + 1] for i in range(0, len(values), 2)]
    return values[0]


def column(row_ref):
    count = row_ref.shape[1]
    wide = jnp.broadcast_to(row_ref[...].astype(f32), (count, count))
    row = lax.broadcasted_iota(jnp.int32, (count, count), 0)
    lane = lax.broadcasted_iota(jnp.int32, (count, count), 1)
    return jnp.sum(jnp.where(row == lane, wide, 0.0), axis=1, keepdims=True).astype(jnp.int32)


def days_of(device, shape):
    return device * shape[1] + lax.broadcasted_iota(jnp.int32, shape, 1)


def fetch(sources, targets, sems):
    copies = [pltpu.make_async_copy(*pair, sems.at[i]) for i, pair in enumerate(zip(sources, targets))]
    for copy in copies:
        copy.start()
    return copies


def fetch_rows(source, target, sems, starts):
    spans = [(start, stop - start) for start, stop in zip(starts, starts[1:])]
    parts = [pl.ds(*span) for span in spans]
    copies = fetch([source.at[here] for here in parts], [target.at[here] for here in parts], sems)
    return [(*span, copy) for span, copy in zip(spans, copies)]


def blocks_of(start, rows):
    return [pl.ds(here, block_rows) for here in range(start, start + rows, block_rows)]


def wait_all(copies):
    for copy in copies:
        copy.wait()


def repeat_out(block, out, sems):
    rows = block.shape[0]
    places = [out.at[pl.ds(i * rows, rows)] for i in range(out.shape[0] // rows)]
    wait_all(fetch([block] * len(places), places, sems))


def first_kernel(all_count, half, starts, *refs):
    arguments, refs = refs[:6], refs[6:]
    out, cross, raised_days, ends, high_ref, low_ref, *held, block, left_ref, cross_block, small_sems, panel_sems, out_sems = refs
    groups, day_cols = held[5].shape
    unit_rows, resident = held[0].shape[0], high_ref.shape[0]
    small = fetch(arguments[1:], held[1:], small_sems)
    parts = fetch_rows(arguments[0], held[0], panel_sems, starts)
    panel, cohort, pre_row, post_row, unit_logit, time_logit = held
    wait_all(small)
    me = lax.axis_index("day")

    @pl.when(me < half)
    def _():
        label = lax.broadcasted_iota(jnp.int32, (groups, unit_rows), 0)
        treated = jnp.where(cohort[...] == label, 1.0, 0.0)
        control = jnp.where(cohort[...] > label, 1.0, 0.0)
        raised = jnp.exp(unit_logit[...]) * control
        left_ref[...] = left_of(raised, treated)
        pre_end = column(pre_row)
        ends[...] = jnp.broadcast_to(pre_end.astype(f32), ends.shape)
        before = days_of(me, (groups, day_cols)) < pre_end
        raised_days[...] = jnp.where(before, jnp.exp(time_logit[...]), 0.0)
        lane = lax.broadcasted_iota(jnp.int32, (groups, lanes), 1)
        block[:, 2 * day_cols :] = jnp.where(
            lane == 0,
            jnp.sum(raised, axis=1, keepdims=True),
            jnp.where(
                lane == 1, jnp.sum(treated, axis=1, keepdims=True), jnp.sum(control, axis=1, keepdims=True)
            ),
        )
        product = jnp.zeros((4 * groups, 2 * day_cols), f32)
        for start, rows, copy in parts:
            copy.wait()
            for here in blocks_of(start, rows):
                high, low = split_panel(panel[here, :])
                if here.start < resident:
                    high_ref[here, :] = high
                    low_ref[here, :] = low
                both = jnp.concatenate([high, low], axis=1)
                product += jnp.dot(left_ref[:, here], both, preferred_element_type=f32)
        product = product[:, :day_cols] + product[:, day_cols:]
        block[:, :day_cols] = add_terms(product, groups)
        block[:, day_cols : 2 * day_cols] = product[2 * groups :][:groups]
        repeat_out(block, out, out_sems)

    @pl.when(me >= half)
    def _():
        post_start = column(post_row)
        after = jnp.where(days_of(me, (groups, day_cols)) >= post_start, 1.0, 0.0)
        left = left_of(after / (all_count - post_start).astype(f32))
        for start, rows, copy in parts:
            copy.wait()
            for here in blocks_of(start, rows):
                cross_block[:, here] = add_terms(days_dot(left, *split_panel(panel[here, :])), groups)
        wait_all(fetch([cross_block], [cross], out_sems))


def second_kernel(unit_devices, panel, cohort, unit_logit, sums, raised_days, ends, high_ref, low_ref, *refs):
    pack, norms, raised_units, more_high, more_low, held, held_cohort, held_logit, sems = refs
    groups, day_cols = raised_days.shape
    unit_rows, resident = panel.shape[0], high_ref.shape[0]
    rest = pl.ds(resident, unit_rows - resident)
    copies = fetch([panel.at[rest], cohort, unit_logit], [held, held_cohort, held_logit], sems)
    total = tree_sum(sums[pl.ds(u * groups, groups), :] for u in range(unit_devices))
    unit_norm = total[:, 2 * day_cols : 2 * day_cols + 1]
    treat_count = jnp.maximum(total[:, 2 * day_cols + 1 : 2 * day_cols + 2], 1.0)
    norms[...] = total[:, 2 * day_cols :]
    gap = total[:, :day_cols] / unit_norm - total[:, day_cols : 2 * day_cols] / treat_count
    before = days_of(lax.axis_index("day"), (groups, day_cols)).astype(f32) < ends[:, 0:1]
    raised_time = raised_days[...]
    pack[:groups, unit_rows:] = raised_time
    pack[groups:, unit_rows:] = jnp.zeros_like(raised_time)
    left = left_of(jnp.where(before, gap, 0.0), raised_time)

    def multiply(here, high, low):
        product = days_dot(left, high, low)
        pack[:groups, here] = add_terms(product, groups)
        pack[groups:, here] = add_terms(product, groups, 1)

    for here in blocks_of(0, resident):
        multiply(here, high_ref[here, :], low_ref[here, :])
    wait_all(copies)
    label = lax.broadcasted_iota(jnp.int32, raised_units.shape, 0)
    raised_units[...] = jnp.where(held_cohort[...] > label, jnp.exp(held_logit[...]), 0.0)
    for here in blocks_of(resident, unit_rows - resident):
        there = pl.ds(here.start - resident, block_rows)
        high, low = split_panel(held[there, :])
        more_high[there, :] = high
        more_low[there, :] = low
        multiply(here, high, low)


def join_kernel(pack, post, out):
    rows, width = pack.shape
    out[:rows, :] = pack[...]
    out[rows:, : post.shape[1]] = post[...]
    out[rows:, post.shape[1] :] = jnp.zeros((post.shape[0], width - post.shape[1]), f32)


def third_kernel(half, *refs):
    parts, refs = [refs[0].at[day] for day in range(half)], refs[1:]
    high_ref, low_ref, more_high, more_low, norms, raised_units, ends, scaled, lam, out, block, out_sems = refs
    groups, unit_rows = raised_units.shape
    resident, day_cols = high_ref.shape
    unit_norm, ctrl_count = norms[:, 0:1], norms[:, 2:3]
    factor = -step_rate / jnp.sqrt(ends[:, 0:1])
    raised_days = [ref[:groups, unit_rows:] for ref in parts]
    over_time = 1.0 / tree_sum(jnp.sum(value, axis=1, keepdims=True) for value in raised_days)
    over_unit = 1.0 / unit_norm
    me = lax.rem(lax.axis_index("day"), half)
    for day in range(half):
        lam[:, day * day_cols : (day + 1) * day_cols] = raised_days[day] * over_time
    time_grad = jnp.zeros((groups, day_cols), f32)
    new_sum = jnp.zeros((groups, 1), f32)
    for start in range(0, unit_rows, 2 * block_rows):
        here = pl.ds(start, 2 * block_rows)
        whole = tree_sum(ref[:, here] for ref in parts)
        raised = raised_units[:, here]
        new = raised * over_unit * jnp.exp(whole[:groups] * factor)
        new_sum += jnp.sum(new, axis=1, keepdims=True)
        scaled[:, here] = new * ctrl_count
        shortfall = whole[groups : 2 * groups] * over_time - whole[2 * groups :]
        left = left_of(jnp.where(raised > 0.0, shortfall, 0.0))
        if start < resident:
            high, low = high_ref[here, :], low_ref[here, :]
        else:
            there = pl.ds(start - resident, 2 * block_rows)
            high, low = more_high[there, :], more_low[there, :]
        time_grad += add_terms(rows_dot(left, high, low), groups)
    lane = lax.broadcasted_iota(jnp.int32, (groups, day_cols), 1)
    spare = (lane == day_cols - 1) & (me == half - 1)
    block[...] = jnp.where(spare, new_sum, time_grad)
    repeat_out(block, out, out_sems)


def fourth_kernel(unit_devices, half, grads, lam, norms, ends, own_days, totals):
    groups, day_cols = own_days.shape
    root = jnp.sqrt(jnp.maximum(norms[:, 2:3], 1.0))
    me = lax.axis_index("day")
    moved_total = jnp.zeros((groups, 1), f32)
    own = jnp.zeros((groups, day_cols), f32)
    for day in range(half):
        places = [(unit * half + half - 1 - day) * groups for unit in range(unit_devices)]
        total = tree_sum(grads[pl.ds(place, groups), :] for place in places)
        moved = lam[:, day * day_cols : (day + 1) * day_cols] * jnp.exp(total * (-step_rate / root))
        moved_total += jnp.sum(moved, axis=1, keepdims=True)
        own = jnp.where(me == day, moved, own)
    totals[...] = jnp.broadcast_to(total[:, day_cols - 1 :], totals.shape)
    own_days[...] = own * (ends[:, 0:1] / moved_total)


def fifth_kernel(half, totals, scaled, own_days, unit_weights, time_weights):
    unit_weights[...] = scaled[...] / totals[:, 0:1]
    time_weights[...] = jnp.where(lax.axis_index("day") < half, own_days[...], 0.0)


def sixth_kernel(half, sent_totals, sent_scaled, _, unit_weights, block, out_sem):
    @pl.when(lax.axis_index("day") >= half)
    def _():
        block[...] = sent_scaled[...] / sent_totals[:, 0:1]
        wait_all(fetch([block], [unit_weights], out_sem))


def local(outcomes, cohort, pre_end, post_start, unit_logit, time_logit):
    groups = pre_end.shape[0]
    unit_rows, day_cols = outcomes.shape
    day_devices = lax.axis_size("day")
    unit_devices = lax.axis_size("unit")
    half = day_devices // 2
    assert half * 2 == day_devices and half & (half - 1) == 0
    assert unit_devices & (unit_devices - 1) == 0
    panel_starts = [0, unit_rows // 4, unit_rows // 8 * 5, unit_rows]
    resident = unit_rows * 3 // 4 // (2 * block_rows) * (2 * block_rows)
    def to_other_half(value):
        pairs = [(u * day_devices + d, u * day_devices + d + half) for u in range(unit_devices) for d in range(half)]
        return lax.ppermute(value, ("unit", "day"), pairs)

    def over_days(value):
        halves = [list(range(half)), list(range(half, day_devices))]
        return lax.all_gather(value, "day", axis_index_groups=halves)

    def over_first_half(value):
        members = [
            [unit * day_devices + day for unit in reversed(range(unit_devices)) for day in reversed(days)]
            for days in (range(half), range(half, day_devices))
        ]
        return lax.all_to_all(
            value, ("unit", "day"), split_axis=0, concat_axis=0, axis_index_groups=members, tiled=True
        )

    def over_units(value):
        members = list(reversed(range(unit_devices)))
        return lax.all_to_all(value, "unit", split_axis=0, concat_axis=0, axis_index_groups=[members], tiled=True)

    def call(kernel, shapes, name, args, in_specs=None, out_specs=None, **more):
        return pl.pallas_call(
            kernel,
            in_specs=in_specs or [vmem] * len(args),
            out_specs=out_specs or [vmem] * len(shapes),
            out_shape=[
                shape if isinstance(shape, type(in_hbm)) else jax.ShapeDtypeStruct(*shape) for shape in shapes
            ],
            compiler_params=params,
            name=name,
            **more,
        )(*args)

    arguments = (outcomes, cohort[None, :], pre_end[None, :], post_start[None, :], unit_logit, time_logit)
    fixed = [pltpu.with_memory_space_constraint(argument, pltpu.HBM) for argument in arguments]
    held = [pltpu.VMEM(argument.shape, argument.dtype) for argument in arguments]
    small_sems, panel_sems = pltpu.SemaphoreType.DMA((5,)), pltpu.SemaphoreType.DMA((3,))
    panel_terms = [((resident, day_cols), bf16)] * 2
    other_terms = [((unit_rows - resident, day_cols), bf16)] * 2
    out_sems = pltpu.SemaphoreType.DMA((unit_devices,))
    width = 2 * day_cols + lanes
    in_hbm = pltpu.HBM((unit_devices * groups, width), f32)
    sums, cross, raised_days, ends, high, low = call(
        functools.partial(first_kernel, day_devices * day_cols, half, panel_starts),
        [
            in_hbm,
            pltpu.HBM((groups, unit_rows), f32),
            ((groups, day_cols), f32),
            ((groups, lanes), f32),
            *panel_terms,
        ],
        "first_product",
        fixed,
        in_specs=[hbm] * 6,
        out_specs=[hbm, hbm] + [vmem] * 4,
        scratch_shapes=held
        + [
            pltpu.VMEM((groups, width), f32),
            pltpu.VMEM((4 * groups, unit_rows), bf16),
            pltpu.VMEM((groups, unit_rows), f32),
            small_sems,
            panel_sems,
            out_sems,
        ],
    )
    downward = [
        (u * day_devices + d + half, u * day_devices + d) for u in range(unit_devices) for d in range(half)
    ]
    post = lax.ppermute(cross, ("unit", "day"), downward)
    pack, norms, raised_units, more_high, more_low = call(
        functools.partial(second_kernel, unit_devices),
        [
            ((2 * groups, unit_rows + day_cols), f32),
            ((groups, lanes), f32),
            ((groups, unit_rows), f32),
            *other_terms,
        ],
        "unit_gradient",
        (fixed[0], fixed[1], fixed[4], over_units(sums), raised_days, ends, high, low),
        in_specs=[hbm] * 3 + [vmem] * 5,
        scratch_shapes=[pltpu.VMEM((unit_rows - resident, day_cols), f32), held[1], held[4], panel_sems],
    )
    (pack,) = call(
        join_kernel, [((3 * groups, unit_rows + day_cols), f32)], "join_post", (pack, post)
    )
    members = unit_devices * half
    scaled, lam, grads = call(
        functools.partial(third_kernel, half),
        [
            ((groups, unit_rows), f32),
            ((groups, half * day_cols), f32),
            pltpu.HBM((members * groups, day_cols), f32),
        ],
        "time_gradient",
        (over_days(pack), high, low, more_high, more_low, norms, raised_units, ends),
        out_specs=[vmem, vmem, hbm],
        scratch_shapes=[pltpu.VMEM((groups, day_cols), f32), pltpu.SemaphoreType.DMA((members,))],
    )
    sent_scaled = to_other_half(scaled)
    own_days, totals = call(
        functools.partial(fourth_kernel, unit_devices, half),
        [((groups, day_cols), f32), ((groups, lanes), f32)],
        "new_time_weights",
        (over_first_half(grads), lam, norms, ends),
    )
    unit_weights, time_weights = call(
        functools.partial(fifth_kernel, half),
        [((groups, unit_rows), f32), ((groups, day_cols), f32)],
        "scale_weights",
        (totals, scaled, own_days),
    )
    (unit_weights,) = call(
        functools.partial(sixth_kernel, half),
        [((groups, unit_rows), f32)],
        "other_half",
        (to_other_half(totals), sent_scaled, unit_weights),
        in_specs=[vmem, vmem, hbm],
        out_specs=[hbm],
        input_output_aliases={2: 0},
        scratch_shapes=[pltpu.VMEM((groups, unit_rows), f32), pltpu.SemaphoreType.DMA((1,))],
    )
    return unit_weights, time_weights


def solution(mesh):
    return jax.shard_map(
        local,
        mesh=mesh,
        in_specs=(P("unit", "day"), P("unit"), P(), P(), P(None, "unit"), P(None, "day")),
        out_specs=(P(None, "unit"), P(None, "day")),
        check_vma=False,
    )
```

```python
import functools

import jax
import jax.numpy as jnp
from jax import lax
from jax.experimental import pallas as pl
from jax.experimental.pallas import tpu as pltpu
from jax.sharding import PartitionSpec as P

step_rate = 16.0
f32 = jnp.float32
bf16 = jnp.bfloat16
lanes = 128
block_rows = 512
params = pltpu.CompilerParams(vmem_limit_bytes=24 * 1024 * 1024)
vmem = pl.BlockSpec(memory_space=pltpu.VMEM)
hbm = pl.BlockSpec(memory_space=pltpu.HBM)


def split_left(value):
    first = value.astype(bf16).astype(f32)
    return [first, value - first]


def left_of(*values):
    return jnp.concatenate([term for value in values for term in split_left(value)], axis=0).astype(bf16)


def split_panel(value):
    high = value.astype(bf16)
    return high, (value - high.astype(f32)).astype(bf16)


def rows_dot(left, high, low):
    return jnp.dot(left, high, preferred_element_type=f32) + jnp.dot(left, low, preferred_element_type=f32)


def days_dot(left, high, low):
    dims = (((1,), (1,)), ((), ()))
    return lax.dot_general(left, high, dims, preferred_element_type=f32) + lax.dot_general(
        left, low, dims, preferred_element_type=f32
    )


def add_terms(stack, groups, place=0):
    return stack[2 * place * groups :][:groups] + stack[(2 * place + 1) * groups :][:groups]


def tree_sum(values):
    values = list(values)
    while len(values) > 1:
        values = [values[i] + values[i + 1] for i in range(0, len(values), 2)]
    return values[0]


def column(row_ref):
    count = row_ref.shape[1]
    wide = jnp.broadcast_to(row_ref[...].astype(f32), (count, count))
    row = lax.broadcasted_iota(jnp.int32, (count, count), 0)
    lane = lax.broadcasted_iota(jnp.int32, (count, count), 1)
    return jnp.sum(jnp.where(row == lane, wide, 0.0), axis=1, keepdims=True).astype(jnp.int32)


def days_of(device, shape):
    return device * shape[1] + lax.broadcasted_iota(jnp.int32, shape, 1)


def first_half_only(kernel):
    @functools.wraps(kernel)
    def guarded(half, *refs):
        @pl.when(lax.axis_index("day") < half)
        def _():
            kernel(half, *refs)

    return guarded


def fetch(sources, targets, sems):
    copies = [pltpu.make_async_copy(*pair, sems.at[i]) for i, pair in enumerate(zip(sources, targets))]
    for copy in copies:
        copy.start()
    return copies


def fetch_rows(source, target, sems, starts):
    spans = [(start, stop - start) for start, stop in zip(starts, starts[1:])]
    parts = [pl.ds(*span) for span in spans]
    copies = fetch([source.at[here] for here in parts], [target.at[here] for here in parts], sems)
    return [(*span, copy) for span, copy in zip(spans, copies)]


def blocks_of(start, rows):
    return [pl.ds(here, block_rows) for here in range(start, start + rows, block_rows)]


def wait_all(copies):
    for copy in copies:
        copy.wait()


def repeat_out(block, out, sems):
    rows = block.shape[0]
    places = [out.at[pl.ds(i * rows, rows)] for i in range(out.shape[0] // rows)]
    wait_all(fetch([block] * len(places), places, sems))


def first_kernel(all_count, half, starts, *refs):
    arguments, refs = refs[:6], refs[6:]
    out, cross, raised_days, ends, high_ref, low_ref, *held, block, left_ref, cross_block, small_sems, panel_sems, out_sems = refs
    groups, day_cols = held[5].shape
    unit_rows, resident = held[0].shape[0], high_ref.shape[0]
    small = fetch(arguments[1:], held[1:], small_sems)
    parts = fetch_rows(arguments[0], held[0], panel_sems, starts)
    panel, cohort, pre_row, post_row, unit_logit, time_logit = held
    wait_all(small)
    me = lax.axis_index("day")

    @pl.when(me < half)
    def _():
        label = lax.broadcasted_iota(jnp.int32, (groups, unit_rows), 0)
        treated = jnp.where(cohort[...] == label, 1.0, 0.0)
        control = jnp.where(cohort[...] > label, 1.0, 0.0)
        raised = jnp.exp(unit_logit[...]) * control
        left_ref[...] = left_of(raised, treated)
        pre_end = column(pre_row)
        ends[...] = jnp.broadcast_to(pre_end.astype(f32), ends.shape)
        before = days_of(me, (groups, day_cols)) < pre_end
        raised_days[...] = jnp.where(before, jnp.exp(time_logit[...]), 0.0)
        lane = lax.broadcasted_iota(jnp.int32, (groups, lanes), 1)
        block[:, 2 * day_cols :] = jnp.where(
            lane == 0,
            jnp.sum(raised, axis=1, keepdims=True),
            jnp.where(
                lane == 1, jnp.sum(treated, axis=1, keepdims=True), jnp.sum(control, axis=1, keepdims=True)
            ),
        )
        product = jnp.zeros((4 * groups, 2 * day_cols), f32)
        for start, rows, copy in parts:
            copy.wait()
            for here in blocks_of(start, rows):
                high, low = split_panel(panel[here, :])
                if here.start < resident:
                    high_ref[here, :] = high
                    low_ref[here, :] = low
                both = jnp.concatenate([high, low], axis=1)
                product += jnp.dot(left_ref[:, here], both, preferred_element_type=f32)
        product = product[:, :day_cols] + product[:, day_cols:]
        block[:, :day_cols] = add_terms(product, groups)
        block[:, day_cols : 2 * day_cols] = product[2 * groups :][:groups]
        repeat_out(block, out, out_sems)

    @pl.when(me >= half)
    def _():
        post_start = column(post_row)
        after = jnp.where(days_of(me, (groups, day_cols)) >= post_start, 1.0, 0.0)
        left = left_of(after / (all_count - post_start).astype(f32))
        for start, rows, copy in parts:
            copy.wait()
            for here in blocks_of(start, rows):
                cross_block[:, here] = add_terms(days_dot(left, *split_panel(panel[here, :])), groups)
        wait_all(fetch([cross_block], [cross], out_sems))


@first_half_only
def second_kernel(half, unit_devices, panel, cohort, unit_logit, sums, raised_days, ends, high_ref, low_ref, *refs):
    pack, norms, raised_units, more_high, more_low, held, held_cohort, held_logit, sems = refs
    groups, day_cols = raised_days.shape
    unit_rows, resident = panel.shape[0], high_ref.shape[0]
    rest = pl.ds(resident, unit_rows - resident)
    copies = fetch([panel.at[rest], cohort, unit_logit], [held, held_cohort, held_logit], sems)
    total = tree_sum(sums[pl.ds(u * groups, groups), :] for u in range(unit_devices))
    unit_norm = total[:, 2 * day_cols : 2 * day_cols + 1]
    treat_count = jnp.maximum(total[:, 2 * day_cols + 1 : 2 * day_cols + 2], 1.0)
    norms[...] = total[:, 2 * day_cols :]
    gap = total[:, :day_cols] / unit_norm - total[:, day_cols : 2 * day_cols] / treat_count
    before = days_of(lax.axis_index("day"), (groups, day_cols)).astype(f32) < ends[:, 0:1]
    raised_time = raised_days[...]
    pack[:groups, unit_rows:] = raised_time
    pack[groups:, unit_rows:] = jnp.zeros_like(raised_time)
    left = left_of(jnp.where(before, gap, 0.0), raised_time)

    def multiply(here, high, low):
        product = days_dot(left, high, low)
        pack[:groups, here] = add_terms(product, groups)
        pack[groups:, here] = add_terms(product, groups, 1)

    for here in blocks_of(0, resident):
        multiply(here, high_ref[here, :], low_ref[here, :])
    wait_all(copies)
    label = lax.broadcasted_iota(jnp.int32, raised_units.shape, 0)
    raised_units[...] = jnp.where(held_cohort[...] > label, jnp.exp(held_logit[...]), 0.0)
    for here in blocks_of(resident, unit_rows - resident):
        there = pl.ds(here.start - resident, block_rows)
        high, low = split_panel(held[there, :])
        more_high[there, :] = high
        more_low[there, :] = low
        multiply(here, high, low)


@first_half_only
def join_kernel(half, pack, post, out):
    rows, width = pack.shape
    out[:rows, :] = pack[...]
    out[rows:, : post.shape[1]] = post[...]
    out[rows:, post.shape[1] :] = jnp.zeros((post.shape[0], width - post.shape[1]), f32)


@first_half_only
def third_kernel(half, *refs):
    parts, refs = [refs[0].at[day] for day in range(half)], refs[1:]
    high_ref, low_ref, more_high, more_low, norms, raised_units, ends, scaled, lam, out, block, out_sems = refs
    groups, unit_rows = raised_units.shape
    resident, day_cols = high_ref.shape
    unit_norm, ctrl_count = norms[:, 0:1], norms[:, 2:3]
    factor = -step_rate / jnp.sqrt(ends[:, 0:1])
    raised_days = [ref[:groups, unit_rows:] for ref in parts]
    over_time = 1.0 / tree_sum(jnp.sum(value, axis=1, keepdims=True) for value in raised_days)
    over_unit = 1.0 / unit_norm
    me = lax.rem(lax.axis_index("day"), half)
    for day in range(half):
        lam[:, day * day_cols : (day + 1) * day_cols] = raised_days[day] * over_time
    time_grad = jnp.zeros((groups, day_cols), f32)
    new_sum = jnp.zeros((groups, 1), f32)
    for start in range(0, unit_rows, block_rows):
        here = pl.ds(start, block_rows)
        whole = tree_sum(ref[:, here] for ref in parts)
        raised = raised_units[:, here]
        new = raised * over_unit * jnp.exp(whole[:groups] * factor)
        new_sum += jnp.sum(new, axis=1, keepdims=True)
        scaled[:, here] = new * ctrl_count
        shortfall = whole[groups : 2 * groups] * over_time - whole[2 * groups :]
        left = left_of(jnp.where(raised > 0.0, shortfall, 0.0))
        if start < resident:
            high, low = high_ref[here, :], low_ref[here, :]
        else:
            there = pl.ds(start - resident, block_rows)
            high, low = more_high[there, :], more_low[there, :]
        time_grad += add_terms(rows_dot(left, high, low), groups)
    lane = lax.broadcasted_iota(jnp.int32, (groups, day_cols), 1)
    spare = (lane == day_cols - 1) & (me == half - 1)
    block[...] = jnp.where(spare, new_sum, time_grad)
    repeat_out(block, out, out_sems)


@first_half_only
def fourth_kernel(half, unit_devices, grads, lam, norms, ends, own_days, totals):
    groups, day_cols = own_days.shape
    root = jnp.sqrt(jnp.maximum(norms[:, 2:3], 1.0))
    me = lax.axis_index("day")
    moved_total = jnp.zeros((groups, 1), f32)
    own = jnp.zeros((groups, day_cols), f32)
    for day in range(half):
        places = [(unit * half + half - 1 - day) * groups for unit in range(unit_devices)]
        total = tree_sum(grads[pl.ds(place, groups), :] for place in places)
        moved = lam[:, day * day_cols : (day + 1) * day_cols] * jnp.exp(total * (-step_rate / root))
        moved_total += jnp.sum(moved, axis=1, keepdims=True)
        own = jnp.where(me == day, moved, own)
    totals[...] = jnp.broadcast_to(total[:, day_cols - 1 :], totals.shape)
    own_days[...] = own * (ends[:, 0:1] / moved_total)


def fifth_kernel(half, totals, scaled, own_days, unit_weights, time_weights):
    unit_weights[...] = scaled[...] / totals[:, 0:1]
    time_weights[...] = jnp.where(lax.axis_index("day") < half, own_days[...], 0.0)


def sixth_kernel(half, sent_totals, sent_scaled, _, unit_weights, block, out_sem):
    @pl.when(lax.axis_index("day") >= half)
    def _():
        block[...] = sent_scaled[...] / sent_totals[:, 0:1]
        wait_all(fetch([block], [unit_weights], out_sem))


def local(outcomes, cohort, pre_end, post_start, unit_logit, time_logit):
    groups = pre_end.shape[0]
    unit_rows, day_cols = outcomes.shape
    day_devices = lax.axis_size("day")
    unit_devices = lax.axis_size("unit")
    half = day_devices // 2
    assert half * 2 == day_devices and half & (half - 1) == 0
    assert unit_devices & (unit_devices - 1) == 0
    panel_starts = [0, unit_rows // 4, unit_rows // 8 * 5, unit_rows]
    resident = unit_rows * 3 // 4 // block_rows * block_rows
    def to_other_half(value):
        pairs = [(u * day_devices + d, u * day_devices + d + half) for u in range(unit_devices) for d in range(half)]
        return lax.ppermute(value, ("unit", "day"), pairs)

    def over_days(value):
        halves = [list(range(half)), list(range(half, day_devices))]
        return lax.all_gather(value, "day", axis_index_groups=halves)

    def over_first_half(value):
        members = [
            [unit * day_devices + day for unit in reversed(range(unit_devices)) for day in reversed(days)]
            for days in (range(half), range(half, day_devices))
        ]
        return lax.all_to_all(
            value, ("unit", "day"), split_axis=0, concat_axis=0, axis_index_groups=members, tiled=True
        )

    def over_units(value):
        members = list(reversed(range(unit_devices)))
        return lax.all_to_all(value, "unit", split_axis=0, concat_axis=0, axis_index_groups=[members], tiled=True)

    def call(kernel, shapes, name, args, in_specs=None, out_specs=None, **more):
        return pl.pallas_call(
            kernel,
            in_specs=in_specs or [vmem] * len(args),
            out_specs=out_specs or [vmem] * len(shapes),
            out_shape=[
                shape if isinstance(shape, type(in_hbm)) else jax.ShapeDtypeStruct(*shape) for shape in shapes
            ],
            compiler_params=params,
            name=name,
            **more,
        )(*args)

    arguments = (outcomes, cohort[None, :], pre_end[None, :], post_start[None, :], unit_logit, time_logit)
    fixed = [pltpu.with_memory_space_constraint(argument, pltpu.HBM) for argument in arguments]
    held = [pltpu.VMEM(argument.shape, argument.dtype) for argument in arguments]
    small_sems, panel_sems = pltpu.SemaphoreType.DMA((5,)), pltpu.SemaphoreType.DMA((3,))
    panel_terms = [((resident, day_cols), bf16)] * 2
    other_terms = [((unit_rows - resident, day_cols), bf16)] * 2
    out_sems = pltpu.SemaphoreType.DMA((unit_devices,))
    width = 2 * day_cols + lanes
    in_hbm = pltpu.HBM((unit_devices * groups, width), f32)
    sums, cross, raised_days, ends, high, low = call(
        functools.partial(first_kernel, day_devices * day_cols, half, panel_starts),
        [
            in_hbm,
            pltpu.HBM((groups, unit_rows), f32),
            ((groups, day_cols), f32),
            ((groups, lanes), f32),
            *panel_terms,
        ],
        "first_product",
        fixed,
        in_specs=[hbm] * 6,
        out_specs=[hbm, hbm] + [vmem] * 4,
        scratch_shapes=held
        + [
            pltpu.VMEM((groups, width), f32),
            pltpu.VMEM((4 * groups, unit_rows), bf16),
            pltpu.VMEM((groups, unit_rows), f32),
            small_sems,
            panel_sems,
            out_sems,
        ],
    )
    downward = [
        (u * day_devices + d + half, u * day_devices + d) for u in range(unit_devices) for d in range(half)
    ]
    post = lax.ppermute(cross, ("unit", "day"), downward)
    pack, norms, raised_units, more_high, more_low = call(
        functools.partial(second_kernel, half, unit_devices),
        [
            ((2 * groups, unit_rows + day_cols), f32),
            ((groups, lanes), f32),
            ((groups, unit_rows), f32),
            *other_terms,
        ],
        "unit_gradient",
        (fixed[0], fixed[1], fixed[4], over_units(sums), raised_days, ends, high, low),
        in_specs=[hbm] * 3 + [vmem] * 5,
        scratch_shapes=[pltpu.VMEM((unit_rows - resident, day_cols), f32), held[1], held[4], panel_sems],
    )
    (pack,) = call(
        functools.partial(join_kernel, half), [((3 * groups, unit_rows + day_cols), f32)], "join_post", (pack, post)
    )
    members = unit_devices * half
    scaled, lam, grads = call(
        functools.partial(third_kernel, half),
        [
            ((groups, unit_rows), f32),
            ((groups, half * day_cols), f32),
            pltpu.HBM((members * groups, day_cols), f32),
        ],
        "time_gradient",
        (over_days(pack), high, low, more_high, more_low, norms, raised_units, ends),
        out_specs=[vmem, vmem, hbm],
        scratch_shapes=[pltpu.VMEM((groups, day_cols), f32), pltpu.SemaphoreType.DMA((members,))],
    )
    sent_scaled = to_other_half(scaled)
    own_days, totals = call(
        functools.partial(fourth_kernel, half, unit_devices),
        [((groups, day_cols), f32), ((groups, lanes), f32)],
        "new_time_weights",
        (over_first_half(grads), lam, norms, ends),
    )
    unit_weights, time_weights = call(
        functools.partial(fifth_kernel, half),
        [((groups, unit_rows), f32), ((groups, day_cols), f32)],
        "scale_weights",
        (totals, scaled, own_days),
    )
    (unit_weights,) = call(
        functools.partial(sixth_kernel, half),
        [((groups, unit_rows), f32)],
        "other_half",
        (to_other_half(totals), sent_scaled, unit_weights),
        in_specs=[vmem, vmem, hbm],
        out_specs=[hbm],
        input_output_aliases={2: 0},
        scratch_shapes=[pltpu.VMEM((groups, unit_rows), f32), pltpu.SemaphoreType.DMA((1,))],
    )
    return unit_weights, time_weights


def solution(mesh):
    return jax.shard_map(
        local,
        mesh=mesh,
        in_specs=(P("unit", "day"), P("unit"), P(), P(), P(None, "unit"), P(None, "day")),
        out_specs=(P(None, "unit"), P(None, "day")),
        check_vma=False,
    )
```

```python
import functools

import jax
import jax.numpy as jnp
from jax import lax
from jax.experimental import pallas as pl
from jax.experimental.pallas import tpu as pltpu
from jax.sharding import PartitionSpec as P

step_rate = 16.0
f32 = jnp.float32
bf16 = jnp.bfloat16
lanes = 128
block_rows = 512
params = pltpu.CompilerParams(vmem_limit_bytes=24 * 1024 * 1024)
vmem = pl.BlockSpec(memory_space=pltpu.VMEM)
hbm = pl.BlockSpec(memory_space=pltpu.HBM)


def split_left(value):
    first = value.astype(bf16).astype(f32)
    return [first, value - first]


def left_of(*values):
    return jnp.concatenate([term for value in values for term in split_left(value)], axis=0).astype(bf16)


def split_panel(value):
    high = value.astype(bf16)
    return high, (value - high.astype(f32)).astype(bf16)


def rows_dot(left, high, low):
    return jnp.dot(left, high, preferred_element_type=f32) + jnp.dot(left, low, preferred_element_type=f32)


def days_dot(left, high, low):
    dims = (((1,), (1,)), ((), ()))
    return lax.dot_general(left, high, dims, preferred_element_type=f32) + lax.dot_general(
        left, low, dims, preferred_element_type=f32
    )


def add_terms(stack, groups, place=0):
    return stack[2 * place * groups :][:groups] + stack[(2 * place + 1) * groups :][:groups]


def tree_sum(values):
    values = list(values)
    while len(values) > 1:
        values = [values[i] + values[i + 1] for i in range(0, len(values), 2)]
    return values[0]


def column(row_ref):
    count = row_ref.shape[1]
    wide = jnp.broadcast_to(row_ref[...].astype(f32), (count, count))
    row = lax.broadcasted_iota(jnp.int32, (count, count), 0)
    lane = lax.broadcasted_iota(jnp.int32, (count, count), 1)
    return jnp.sum(jnp.where(row == lane, wide, 0.0), axis=1, keepdims=True).astype(jnp.int32)


def days_of(device, shape):
    return device * shape[1] + lax.broadcasted_iota(jnp.int32, shape, 1)


def first_half_only(kernel):
    @functools.wraps(kernel)
    def guarded(half, *refs):
        @pl.when(lax.axis_index("day") < half)
        def _():
            kernel(half, *refs)

    return guarded


def fetch(sources, targets, sems):
    copies = [pltpu.make_async_copy(*pair, sems.at[i]) for i, pair in enumerate(zip(sources, targets))]
    for copy in copies:
        copy.start()
    return copies


def fetch_rows(source, target, sems, starts):
    spans = [(start, stop - start) for start, stop in zip(starts, starts[1:])]
    parts = [pl.ds(*span) for span in spans]
    copies = fetch([source.at[here] for here in parts], [target.at[here] for here in parts], sems)
    return [(*span, copy) for span, copy in zip(spans, copies)]


def blocks_of(start, rows):
    return [pl.ds(here, block_rows) for here in range(start, start + rows, block_rows)]


def wait_all(copies):
    for copy in copies:
        copy.wait()


def repeat_out(block, out, sems):
    rows = block.shape[0]
    places = [out.at[pl.ds(i * rows, rows)] for i in range(out.shape[0] // rows)]
    wait_all(fetch([block] * len(places), places, sems))


def first_kernel(all_count, half, starts, *refs):
    arguments, refs = refs[:6], refs[6:]
    out, cross, raised_days, ends, high_ref, low_ref, *held, block, left_ref, cross_block, small_sems, panel_sems, out_sems = refs
    groups, day_cols = held[5].shape
    unit_rows, resident = held[0].shape[0], high_ref.shape[0]
    small = fetch(arguments[1:], held[1:], small_sems)
    parts = fetch_rows(arguments[0], held[0], panel_sems, starts)
    panel, cohort, pre_row, post_row, unit_logit, time_logit = held
    wait_all(small)
    me = lax.axis_index("day")

    @pl.when(me < half)
    def _():
        label = lax.broadcasted_iota(jnp.int32, (groups, unit_rows), 0)
        treated = jnp.where(cohort[...] == label, 1.0, 0.0)
        control = jnp.where(cohort[...] > label, 1.0, 0.0)
        raised = jnp.exp(unit_logit[...]) * control
        left_ref[...] = left_of(raised, treated)
        pre_end = column(pre_row)
        ends[...] = jnp.broadcast_to(pre_end.astype(f32), ends.shape)
        before = days_of(me, (groups, day_cols)) < pre_end
        raised_days[...] = jnp.where(before, jnp.exp(time_logit[...]), 0.0)
        lane = lax.broadcasted_iota(jnp.int32, (groups, lanes), 1)
        block[:, 2 * day_cols :] = jnp.where(
            lane == 0,
            jnp.sum(raised, axis=1, keepdims=True),
            jnp.where(
                lane == 1, jnp.sum(treated, axis=1, keepdims=True), jnp.sum(control, axis=1, keepdims=True)
            ),
        )
        product = jnp.zeros((4 * groups, 2 * day_cols), f32)
        for start, rows, copy in parts:
            copy.wait()
            for here in blocks_of(start, rows):
                high, low = split_panel(panel[here, :])
                if here.start < resident:
                    high_ref[here, :] = high
                    low_ref[here, :] = low
                both = jnp.concatenate([high, low], axis=1)
                product += jnp.dot(left_ref[:, here], both, preferred_element_type=f32)
        product = product[:, :day_cols] + product[:, day_cols:]
        block[:, :day_cols] = add_terms(product, groups)
        block[:, day_cols : 2 * day_cols] = product[2 * groups :][:groups]
        repeat_out(block, out, out_sems)

    @pl.when(me >= half)
    def _():
        post_start = column(post_row)
        after = jnp.where(days_of(me, (groups, day_cols)) >= post_start, 1.0, 0.0)
        left = left_of(after / (all_count - post_start).astype(f32))
        for start, rows, copy in parts:
            copy.wait()
            for here in blocks_of(start, rows):
                cross_block[:, here] = add_terms(days_dot(left, *split_panel(panel[here, :])), groups)
        wait_all(fetch([cross_block], [cross], out_sems))


@first_half_only
def second_kernel(half, unit_devices, panel, cohort, unit_logit, sums, raised_days, ends, high_ref, low_ref, *refs):
    pack, norms, raised_units, more_high, more_low, held, held_cohort, held_logit, sems = refs
    groups, day_cols = raised_days.shape
    unit_rows, resident = panel.shape[0], high_ref.shape[0]
    rest = pl.ds(resident, unit_rows - resident)
    copies = fetch([panel.at[rest], cohort, unit_logit], [held, held_cohort, held_logit], sems)
    total = tree_sum(sums[pl.ds(u * groups, groups), :] for u in range(unit_devices))
    unit_norm = total[:, 2 * day_cols : 2 * day_cols + 1]
    treat_count = jnp.maximum(total[:, 2 * day_cols + 1 : 2 * day_cols + 2], 1.0)
    norms[...] = total[:, 2 * day_cols :]
    gap = total[:, :day_cols] / unit_norm - total[:, day_cols : 2 * day_cols] / treat_count
    before = days_of(lax.axis_index("day"), (groups, day_cols)).astype(f32) < ends[:, 0:1]
    raised_time = raised_days[...]
    pack[:groups, unit_rows:] = raised_time
    pack[groups:, unit_rows:] = jnp.zeros_like(raised_time)
    left = left_of(jnp.where(before, gap, 0.0), raised_time)

    def multiply(here, high, low):
        product = days_dot(left, high, low)
        pack[:groups, here] = add_terms(product, groups)
        pack[groups:, here] = add_terms(product, groups, 1)

    for here in blocks_of(0, resident):
        multiply(here, high_ref[here, :], low_ref[here, :])
    wait_all(copies)
    label = lax.broadcasted_iota(jnp.int32, raised_units.shape, 0)
    raised_units[...] = jnp.where(held_cohort[...] > label, jnp.exp(held_logit[...]), 0.0)
    for here in blocks_of(resident, unit_rows - resident):
        there = pl.ds(here.start - resident, block_rows)
        high, low = split_panel(held[there, :])
        more_high[there, :] = high
        more_low[there, :] = low
        multiply(here, high, low)


@first_half_only
def join_kernel(half, pack, post, out):
    rows, width = pack.shape
    out[:rows, :] = pack[...]
    out[rows:, : post.shape[1]] = post[...]
    out[rows:, post.shape[1] :] = jnp.zeros((post.shape[0], width - post.shape[1]), f32)


@first_half_only
def third_kernel(half, *refs):
    parts, refs = [refs[0].at[day] for day in range(half)], refs[1:]
    high_ref, low_ref, more_high, more_low, norms, raised_units, ends, scaled, lam, out, block, out_sems = refs
    groups, unit_rows = raised_units.shape
    resident, day_cols = high_ref.shape
    unit_norm, ctrl_count = norms[:, 0:1], norms[:, 2:3]
    factor = -step_rate / jnp.sqrt(ends[:, 0:1])
    raised_days = [ref[:groups, unit_rows:] for ref in parts]
    over_time = 1.0 / tree_sum(jnp.sum(value, axis=1, keepdims=True) for value in raised_days)
    over_unit = 1.0 / unit_norm
    me = lax.rem(lax.axis_index("day"), half)
    for day in range(half):
        lam[:, day * day_cols : (day + 1) * day_cols] = raised_days[day] * over_time
    time_grad = jnp.zeros((groups, day_cols), f32)
    new_sum = jnp.zeros((groups, 1), f32)
    for start in range(0, unit_rows, block_rows):
        here = pl.ds(start, block_rows)
        whole = tree_sum(ref[:, here] for ref in parts)
        raised = raised_units[:, here]
        new = raised * over_unit * jnp.exp(whole[:groups] * factor)
        new_sum += jnp.sum(new, axis=1, keepdims=True)
        scaled[:, here] = new * ctrl_count
        shortfall = whole[groups : 2 * groups] * over_time - whole[2 * groups :]
        left = left_of(jnp.where(raised > 0.0, shortfall, 0.0))
        if start < resident:
            high, low = high_ref[here, :], low_ref[here, :]
        else:
            there = pl.ds(start - resident, block_rows)
            high, low = more_high[there, :], more_low[there, :]
        time_grad += add_terms(rows_dot(left, high, low), groups)
    lane = lax.broadcasted_iota(jnp.int32, (groups, day_cols), 1)
    spare = (lane == day_cols - 1) & (me == half - 1)
    block[...] = jnp.where(spare, new_sum, time_grad)
    repeat_out(block, out, out_sems)


@first_half_only
def fourth_kernel(half, unit_devices, grads, lam, norms, ends, own_days, totals):
    groups, day_cols = own_days.shape
    root = jnp.sqrt(jnp.maximum(norms[:, 2:3], 1.0))
    me = lax.axis_index("day")
    moved_total = jnp.zeros((groups, 1), f32)
    own = jnp.zeros((groups, day_cols), f32)
    for day in range(half):
        places = [(unit * half + half - 1 - day) * groups for unit in range(unit_devices)]
        total = tree_sum(grads[pl.ds(place, groups), :] for place in places)
        moved = lam[:, day * day_cols : (day + 1) * day_cols] * jnp.exp(total * (-step_rate / root))
        moved_total += jnp.sum(moved, axis=1, keepdims=True)
        own = jnp.where(me == day, moved, own)
    totals[...] = jnp.broadcast_to(total[:, day_cols - 1 :], totals.shape)
    own_days[...] = own * (ends[:, 0:1] / moved_total)


def fifth_kernel(half, totals, scaled, own_days, unit_weights, time_weights):
    unit_weights[...] = scaled[...] / totals[:, 0:1]
    time_weights[...] = jnp.where(lax.axis_index("day") < half, own_days[...], 0.0)


def sixth_kernel(half, sent_totals, sent_scaled, _, unit_weights, block, out_sem):
    @pl.when(lax.axis_index("day") >= half)
    def _():
        block[...] = sent_scaled[...] / sent_totals[:, 0:1]
        wait_all(fetch([block], [unit_weights], out_sem))


def local(outcomes, cohort, pre_end, post_start, unit_logit, time_logit):
    groups = pre_end.shape[0]
    unit_rows, day_cols = outcomes.shape
    day_devices = lax.axis_size("day")
    unit_devices = lax.axis_size("unit")
    half = day_devices // 2
    assert half * 2 == day_devices and half & (half - 1) == 0
    assert unit_devices & (unit_devices - 1) == 0
    panel_starts = [0, unit_rows // 4, unit_rows // 8 * 5, unit_rows]
    resident = unit_rows * 3 // 4 // block_rows * block_rows
    middle = unit_devices // 2 - 1
    unit_order = [middle] + [unit for unit in reversed(range(unit_devices)) if unit != middle]

    def to_other_half(value):
        pairs = [(u * day_devices + d, u * day_devices + d + half) for u in range(unit_devices) for d in range(half)]
        return lax.ppermute(value, ("unit", "day"), pairs)

    def over_days(value):
        halves = [list(range(half)), list(range(half, day_devices))]
        return lax.all_gather(value, "day", axis_index_groups=halves)

    def over_first_half(value):
        members = [
            [unit * day_devices + day for unit in unit_order for day in reversed(days)]
            for days in (range(half), range(half, day_devices))
        ]
        return lax.all_to_all(
            value, ("unit", "day"), split_axis=0, concat_axis=0, axis_index_groups=members, tiled=True
        )

    def over_units(value):
        return lax.all_to_all(value, "unit", split_axis=0, concat_axis=0, axis_index_groups=[unit_order], tiled=True)

    def call(kernel, shapes, name, args, in_specs=None, out_specs=None, **more):
        return pl.pallas_call(
            kernel,
            in_specs=in_specs or [vmem] * len(args),
            out_specs=out_specs or [vmem] * len(shapes),
            out_shape=[
                shape if isinstance(shape, type(in_hbm)) else jax.ShapeDtypeStruct(*shape) for shape in shapes
            ],
            compiler_params=params,
            name=name,
            **more,
        )(*args)

    arguments = (outcomes, cohort[None, :], pre_end[None, :], post_start[None, :], unit_logit, time_logit)
    fixed = [pltpu.with_memory_space_constraint(argument, pltpu.HBM) for argument in arguments]
    held = [pltpu.VMEM(argument.shape, argument.dtype) for argument in arguments]
    small_sems, panel_sems = pltpu.SemaphoreType.DMA((5,)), pltpu.SemaphoreType.DMA((3,))
    panel_terms = [((resident, day_cols), bf16)] * 2
    other_terms = [((unit_rows - resident, day_cols), bf16)] * 2
    out_sems = pltpu.SemaphoreType.DMA((unit_devices,))
    width = 2 * day_cols + lanes
    in_hbm = pltpu.HBM((unit_devices * groups, width), f32)
    sums, cross, raised_days, ends, high, low = call(
        functools.partial(first_kernel, day_devices * day_cols, half, panel_starts),
        [
            in_hbm,
            pltpu.HBM((groups, unit_rows), f32),
            ((groups, day_cols), f32),
            ((groups, lanes), f32),
            *panel_terms,
        ],
        "first_product",
        fixed,
        in_specs=[hbm] * 6,
        out_specs=[hbm, hbm] + [vmem] * 4,
        scratch_shapes=held
        + [
            pltpu.VMEM((groups, width), f32),
            pltpu.VMEM((4 * groups, unit_rows), bf16),
            pltpu.VMEM((groups, unit_rows), f32),
            small_sems,
            panel_sems,
            out_sems,
        ],
    )
    downward = [
        (u * day_devices + d + half, u * day_devices + d) for u in range(unit_devices) for d in range(half)
    ]
    post = lax.ppermute(cross, ("unit", "day"), downward)
    pack, norms, raised_units, more_high, more_low = call(
        functools.partial(second_kernel, half, unit_devices),
        [
            ((2 * groups, unit_rows + day_cols), f32),
            ((groups, lanes), f32),
            ((groups, unit_rows), f32),
            *other_terms,
        ],
        "unit_gradient",
        (fixed[0], fixed[1], fixed[4], over_units(sums), raised_days, ends, high, low),
        in_specs=[hbm] * 3 + [vmem] * 5,
        scratch_shapes=[pltpu.VMEM((unit_rows - resident, day_cols), f32), held[1], held[4], panel_sems],
    )
    (pack,) = call(
        functools.partial(join_kernel, half), [((3 * groups, unit_rows + day_cols), f32)], "join_post", (pack, post)
    )
    members = unit_devices * half
    scaled, lam, grads = call(
        functools.partial(third_kernel, half),
        [
            ((groups, unit_rows), f32),
            ((groups, half * day_cols), f32),
            pltpu.HBM((members * groups, day_cols), f32),
        ],
        "time_gradient",
        (over_days(pack), high, low, more_high, more_low, norms, raised_units, ends),
        out_specs=[vmem, vmem, hbm],
        scratch_shapes=[pltpu.VMEM((groups, day_cols), f32), pltpu.SemaphoreType.DMA((members,))],
    )
    sent_scaled = to_other_half(scaled)
    own_days, totals = call(
        functools.partial(fourth_kernel, half, unit_devices),
        [((groups, day_cols), f32), ((groups, lanes), f32)],
        "new_time_weights",
        (over_first_half(grads), lam, norms, ends),
    )
    unit_weights, time_weights = call(
        functools.partial(fifth_kernel, half),
        [((groups, unit_rows), f32), ((groups, day_cols), f32)],
        "scale_weights",
        (totals, scaled, own_days),
    )
    (unit_weights,) = call(
        functools.partial(sixth_kernel, half),
        [((groups, unit_rows), f32)],
        "other_half",
        (to_other_half(totals), sent_scaled, unit_weights),
        in_specs=[vmem, vmem, hbm],
        out_specs=[hbm],
        input_output_aliases={2: 0},
        scratch_shapes=[pltpu.VMEM((groups, unit_rows), f32), pltpu.SemaphoreType.DMA((1,))],
    )
    return unit_weights, time_weights


def solution(mesh):
    return jax.shard_map(
        local,
        mesh=mesh,
        in_specs=(P("unit", "day"), P("unit"), P(), P(), P(None, "unit"), P(None, "day")),
        out_specs=(P(None, "unit"), P(None, "day")),
        check_vma=False,
    )
```

```python
import functools

import jax
import jax.numpy as jnp
from jax import lax
from jax.experimental import pallas as pl
from jax.experimental.pallas import tpu as pltpu
from jax.sharding import PartitionSpec as P

step_rate = 16.0
f32 = jnp.float32
bf16 = jnp.bfloat16
lanes = 128
block_rows = 512
params = pltpu.CompilerParams(vmem_limit_bytes=24 * 1024 * 1024)
vmem = pl.BlockSpec(memory_space=pltpu.VMEM)
hbm = pl.BlockSpec(memory_space=pltpu.HBM)


def split_left(value):
    first = value.astype(bf16).astype(f32)
    return [first, value - first]


def left_of(*values):
    return jnp.concatenate([term for value in values for term in split_left(value)], axis=0).astype(bf16)


def split_panel(value):
    high = value.astype(bf16)
    return high, (value - high.astype(f32)).astype(bf16)


def rows_dot(left, high, low):
    return jnp.dot(left, high, preferred_element_type=f32) + jnp.dot(left, low, preferred_element_type=f32)


def days_dot(left, high, low):
    dims = (((1,), (1,)), ((), ()))
    return lax.dot_general(left, high, dims, preferred_element_type=f32) + lax.dot_general(
        left, low, dims, preferred_element_type=f32
    )


def add_terms(stack, groups, place=0):
    return stack[2 * place * groups :][:groups] + stack[(2 * place + 1) * groups :][:groups]


def tree_sum(values):
    values = list(values)
    while len(values) > 1:
        values = [values[i] + values[i + 1] for i in range(0, len(values), 2)]
    return values[0]


def column(row_ref):
    count = row_ref.shape[1]
    wide = jnp.broadcast_to(row_ref[...].astype(f32), (count, count))
    row = lax.broadcasted_iota(jnp.int32, (count, count), 0)
    lane = lax.broadcasted_iota(jnp.int32, (count, count), 1)
    return jnp.sum(jnp.where(row == lane, wide, 0.0), axis=1, keepdims=True).astype(jnp.int32)


def days_of(device, shape):
    return device * shape[1] + lax.broadcasted_iota(jnp.int32, shape, 1)


def first_half_only(kernel):
    @functools.wraps(kernel)
    def guarded(half, *refs):
        @pl.when(lax.axis_index("day") < half)
        def _():
            kernel(half, *refs)

    return guarded


def fetch(sources, targets, sems):
    copies = [pltpu.make_async_copy(*pair, sems.at[i]) for i, pair in enumerate(zip(sources, targets))]
    for copy in copies:
        copy.start()
    return copies


def fetch_rows(source, target, sems, starts):
    spans = [(start, stop - start) for start, stop in zip(starts, starts[1:])]
    parts = [pl.ds(*span) for span in spans]
    copies = fetch([source.at[here] for here in parts], [target.at[here] for here in parts], sems)
    return [(*span, copy) for span, copy in zip(spans, copies)]


def blocks_of(start, rows):
    return [pl.ds(here, block_rows) for here in range(start, start + rows, block_rows)]


def wait_all(copies):
    for copy in copies:
        copy.wait()


def repeat_start(block, out, sems):
    rows = block.shape[0]
    places = [out.at[pl.ds(i * rows, rows)] for i in range(out.shape[0] // rows)]
    return fetch([block] * len(places), places, sems)


def first_kernel(all_count, half, starts, *refs):
    arguments, refs = refs[:6], refs[6:]
    out, cross, raised_days, ends, high_ref, low_ref, *held, block, left_ref, cross_block, small_sems, panel_sems, out_sems = refs
    groups, day_cols = held[5].shape
    unit_rows, resident = held[0].shape[0], high_ref.shape[0]
    units = (1, 4)
    days = (2, 3, 5)
    unit_copies = fetch([arguments[i] for i in units], [held[i] for i in units], small_sems)
    parts = fetch_rows(arguments[0], held[0], panel_sems, starts)
    day_copies = fetch([arguments[i] for i in days], [held[i] for i in days], small_sems.at[pl.ds(2, 3)])
    panel, cohort, pre_row, post_row, unit_logit, time_logit = held
    wait_all(unit_copies)
    me = lax.axis_index("day")

    @pl.when(me < half)
    def _():
        label = lax.broadcasted_iota(jnp.int32, (groups, unit_rows), 0)
        treated = jnp.where(cohort[...] == label, 1.0, 0.0)
        control = jnp.where(cohort[...] > label, 1.0, 0.0)
        raised = jnp.exp(unit_logit[...]) * control
        left_ref[...] = left_of(raised, treated)
        lane = lax.broadcasted_iota(jnp.int32, (groups, lanes), 1)
        block[:, 2 * day_cols :] = jnp.where(
            lane == 0,
            jnp.sum(raised, axis=1, keepdims=True),
            jnp.where(
                lane == 1, jnp.sum(treated, axis=1, keepdims=True), jnp.sum(control, axis=1, keepdims=True)
            ),
        )
        product = jnp.zeros((4 * groups, 2 * day_cols), f32)
        for start, rows, copy in parts:
            copy.wait()
            for here in blocks_of(start, rows):
                high, low = split_panel(panel[here, :])
                if here.start < resident:
                    high_ref[here, :] = high
                    low_ref[here, :] = low
                both = jnp.concatenate([high, low], axis=1)
                product += jnp.dot(left_ref[:, here], both, preferred_element_type=f32)
        product = product[:, :day_cols] + product[:, day_cols:]
        block[:, :day_cols] = add_terms(product, groups)
        block[:, day_cols : 2 * day_cols] = product[2 * groups :][:groups]
        sends = repeat_start(block, out, out_sems)
        wait_all(day_copies)
        pre_end = column(pre_row)
        ends[...] = jnp.broadcast_to(pre_end.astype(f32), ends.shape)
        before = days_of(me, (groups, day_cols)) < pre_end
        raised_days[...] = jnp.where(before, jnp.exp(time_logit[...]), 0.0)
        wait_all(sends)

    @pl.when(me >= half)
    def _():
        wait_all(day_copies)
        post_start = column(post_row)
        after = jnp.where(days_of(me, (groups, day_cols)) >= post_start, 1.0, 0.0)
        left = left_of(after / (all_count - post_start).astype(f32))
        for start, rows, copy in parts:
            copy.wait()
            for here in blocks_of(start, rows):
                cross_block[:, here] = add_terms(days_dot(left, *split_panel(panel[here, :])), groups)
        wait_all(fetch([cross_block], [cross], out_sems))


@first_half_only
def second_kernel(half, unit_devices, panel, cohort, unit_logit, sums, raised_days, ends, high_ref, low_ref, *refs):
    pack, norms, raised_units, more_high, more_low, held, held_cohort, held_logit, sems = refs
    groups, day_cols = raised_days.shape
    unit_rows, resident = panel.shape[0], high_ref.shape[0]
    rest = pl.ds(resident, unit_rows - resident)
    copies = fetch([panel.at[rest], cohort, unit_logit], [held, held_cohort, held_logit], sems)
    total = tree_sum(sums[pl.ds(u * groups, groups), :] for u in range(unit_devices))
    unit_norm = total[:, 2 * day_cols : 2 * day_cols + 1]
    treat_count = jnp.maximum(total[:, 2 * day_cols + 1 : 2 * day_cols + 2], 1.0)
    norms[...] = total[:, 2 * day_cols :]
    gap = total[:, :day_cols] / unit_norm - total[:, day_cols : 2 * day_cols] / treat_count
    before = days_of(lax.axis_index("day"), (groups, day_cols)).astype(f32) < ends[:, 0:1]
    raised_time = raised_days[...]
    pack[:groups, unit_rows:] = raised_time
    pack[groups:, unit_rows:] = jnp.zeros_like(raised_time)
    left = left_of(jnp.where(before, gap, 0.0), raised_time)

    def multiply(here, high, low):
        product = days_dot(left, high, low)
        pack[:groups, here] = add_terms(product, groups)
        pack[groups:, here] = add_terms(product, groups, 1)

    for here in blocks_of(0, resident):
        multiply(here, high_ref[here, :], low_ref[here, :])
    wait_all(copies)
    label = lax.broadcasted_iota(jnp.int32, raised_units.shape, 0)
    raised_units[...] = jnp.where(held_cohort[...] > label, jnp.exp(held_logit[...]), 0.0)
    for here in blocks_of(resident, unit_rows - resident):
        there = pl.ds(here.start - resident, block_rows)
        high, low = split_panel(held[there, :])
        more_high[there, :] = high
        more_low[there, :] = low
        multiply(here, high, low)


@first_half_only
def join_kernel(half, pack, post, out):
    rows, width = pack.shape
    out[:rows, :] = pack[...]
    out[rows:, : post.shape[1]] = post[...]
    out[rows:, post.shape[1] :] = jnp.zeros((post.shape[0], width - post.shape[1]), f32)


@first_half_only
def third_kernel(half, *refs):
    parts, refs = [refs[0].at[day] for day in range(half)], refs[1:]
    high_ref, low_ref, more_high, more_low, norms, raised_units, ends, scaled, lam, out, block, out_sems = refs
    groups, unit_rows = raised_units.shape
    resident, day_cols = high_ref.shape
    unit_norm, ctrl_count = norms[:, 0:1], norms[:, 2:3]
    factor = -step_rate / jnp.sqrt(ends[:, 0:1])
    raised_days = [ref[:groups, unit_rows:] for ref in parts]
    over_time = 1.0 / tree_sum(jnp.sum(value, axis=1, keepdims=True) for value in raised_days)
    over_unit = 1.0 / unit_norm
    me = lax.rem(lax.axis_index("day"), half)
    for day in range(half):
        lam[:, day * day_cols : (day + 1) * day_cols] = raised_days[day] * over_time
    time_grad = jnp.zeros((groups, day_cols), f32)
    new_sum = jnp.zeros((groups, 1), f32)
    for start in range(0, unit_rows, block_rows):
        here = pl.ds(start, block_rows)
        whole = tree_sum(ref[:, here] for ref in parts)
        raised = raised_units[:, here]
        new = raised * over_unit * jnp.exp(whole[:groups] * factor)
        new_sum += jnp.sum(new, axis=1, keepdims=True)
        scaled[:, here] = new * ctrl_count
        shortfall = whole[groups : 2 * groups] * over_time - whole[2 * groups :]
        left = left_of(jnp.where(raised > 0.0, shortfall, 0.0))
        if start < resident:
            high, low = high_ref[here, :], low_ref[here, :]
        else:
            there = pl.ds(start - resident, block_rows)
            high, low = more_high[there, :], more_low[there, :]
        time_grad += add_terms(rows_dot(left, high, low), groups)
    lane = lax.broadcasted_iota(jnp.int32, (groups, day_cols), 1)
    spare = (lane == day_cols - 1) & (me == half - 1)
    block[...] = jnp.where(spare, new_sum, time_grad)
    wait_all(repeat_start(block, out, out_sems))


def time_grad_of(grads, unit_devices, half, day, groups):
    places = [(unit * half + half - 1 - day) * groups for unit in range(unit_devices)]
    return tree_sum(grads[pl.ds(place, groups), :] for place in places)


@first_half_only
def fourth_kernel(half, unit_devices, grads, totals):
    groups, day_cols = totals.shape[0], grads.shape[1]
    last = time_grad_of(grads, unit_devices, half, half - 1, groups)
    totals[...] = jnp.broadcast_to(last[:, day_cols - 1 :], totals.shape)


def fifth_kernel(half, unit_devices, totals, scaled, grads, lam, norms, ends, unit_weights, time_weights):
    groups, day_cols = time_weights.shape
    me = lax.axis_index("day")

    @pl.when(me < half)
    def _():
        unit_weights[...] = scaled[...] * (1.0 / totals[:, 0:1])
        root = jnp.sqrt(jnp.maximum(norms[:, 2:3], 1.0))
        moved_total = jnp.zeros((groups, 1), f32)
        own = jnp.zeros((groups, day_cols), f32)
        for day in range(half):
            total = time_grad_of(grads, unit_devices, half, day, groups)
            moved = lam[:, day * day_cols : (day + 1) * day_cols] * jnp.exp(total * (-step_rate / root))
            moved_total += jnp.sum(moved, axis=1, keepdims=True)
            own = jnp.where(me == day, moved, own)
        time_weights[...] = own * (ends[:, 0:1] / moved_total)

    @pl.when(me >= half)
    def _():
        time_weights[...] = jnp.zeros_like(time_weights)


def sixth_kernel(half, sent_totals, sent_scaled, _, unit_weights, block, out_sem):
    @pl.when(lax.axis_index("day") >= half)
    def _():
        block[...] = sent_scaled[...] * (1.0 / sent_totals[:, 0:1])
        wait_all(fetch([block], [unit_weights], out_sem))


def local(outcomes, cohort, pre_end, post_start, unit_logit, time_logit):
    groups = pre_end.shape[0]
    unit_rows, day_cols = outcomes.shape
    day_devices = lax.axis_size("day")
    unit_devices = lax.axis_size("unit")
    half = day_devices // 2
    assert half * 2 == day_devices and half & (half - 1) == 0
    assert unit_devices & (unit_devices - 1) == 0
    panel_starts = [0, unit_rows // 2, unit_rows]
    resident = unit_rows * 3 // 4 // block_rows * block_rows
    middle = unit_devices // 2 - 1
    unit_order = [middle] + [unit for unit in reversed(range(unit_devices)) if unit != middle]

    def to_other_half(value):
        pairs = [(u * day_devices + d, u * day_devices + d + half) for u in range(unit_devices) for d in range(half)]
        return lax.ppermute(value, ("unit", "day"), pairs)

    def over_days(value):
        halves = [list(range(half)), list(range(half, day_devices))]
        return lax.all_gather(value, "day", axis_index_groups=halves)

    def over_first_half(value):
        members = [
            [unit * day_devices + day for unit in unit_order for day in reversed(days)]
            for days in (range(half), range(half, day_devices))
        ]
        return lax.all_to_all(
            value, ("unit", "day"), split_axis=0, concat_axis=0, axis_index_groups=members, tiled=True
        )

    def over_units(value):
        return lax.all_to_all(value, "unit", split_axis=0, concat_axis=0, axis_index_groups=[unit_order], tiled=True)

    def call(kernel, shapes, name, args, in_specs=None, out_specs=None, **more):
        return pl.pallas_call(
            kernel,
            in_specs=in_specs or [vmem] * len(args),
            out_specs=out_specs or [vmem] * len(shapes),
            out_shape=[
                shape if isinstance(shape, type(in_hbm)) else jax.ShapeDtypeStruct(*shape) for shape in shapes
            ],
            compiler_params=params,
            name=name,
            **more,
        )(*args)

    arguments = (outcomes, cohort[None, :], pre_end[None, :], post_start[None, :], unit_logit, time_logit)
    fixed = [pltpu.with_memory_space_constraint(argument, pltpu.HBM) for argument in arguments]
    held = [pltpu.VMEM(argument.shape, argument.dtype) for argument in arguments]
    small_sems, panel_sems = pltpu.SemaphoreType.DMA((5,)), pltpu.SemaphoreType.DMA((3,))
    panel_terms = [((resident, day_cols), bf16)] * 2
    other_terms = [((unit_rows - resident, day_cols), bf16)] * 2
    out_sems = pltpu.SemaphoreType.DMA((unit_devices,))
    width = 2 * day_cols + lanes
    in_hbm = pltpu.HBM((unit_devices * groups, width), f32)
    sums, cross, raised_days, ends, high, low = call(
        functools.partial(first_kernel, day_devices * day_cols, half, panel_starts),
        [
            in_hbm,
            pltpu.HBM((groups, unit_rows), f32),
            ((groups, day_cols), f32),
            ((groups, lanes), f32),
            *panel_terms,
        ],
        "first_product",
        fixed,
        in_specs=[hbm] * 6,
        out_specs=[hbm, hbm] + [vmem] * 4,
        scratch_shapes=held
        + [
            pltpu.VMEM((groups, width), f32),
            pltpu.VMEM((4 * groups, unit_rows), bf16),
            pltpu.VMEM((groups, unit_rows), f32),
            small_sems,
            panel_sems,
            out_sems,
        ],
    )
    downward = [
        (u * day_devices + d + half, u * day_devices + d) for u in range(unit_devices) for d in range(half)
    ]
    post = lax.ppermute(cross, ("unit", "day"), downward)
    pack, norms, raised_units, more_high, more_low = call(
        functools.partial(second_kernel, half, unit_devices),
        [
            ((2 * groups, unit_rows + day_cols), f32),
            ((groups, lanes), f32),
            ((groups, unit_rows), f32),
            *other_terms,
        ],
        "unit_gradient",
        (fixed[0], fixed[1], fixed[4], over_units(sums), raised_days, ends, high, low),
        in_specs=[hbm] * 3 + [vmem] * 5,
        scratch_shapes=[pltpu.VMEM((unit_rows - resident, day_cols), f32), held[1], held[4], panel_sems],
    )
    (pack,) = call(
        functools.partial(join_kernel, half), [((3 * groups, unit_rows + day_cols), f32)], "join_post", (pack, post)
    )
    members = unit_devices * half
    scaled, lam, grads = call(
        functools.partial(third_kernel, half),
        [
            ((groups, unit_rows), f32),
            ((groups, half * day_cols), f32),
            pltpu.HBM((members * groups, day_cols), f32),
        ],
        "time_gradient",
        (over_days(pack), high, low, more_high, more_low, norms, raised_units, ends),
        out_specs=[vmem, vmem, hbm],
        scratch_shapes=[pltpu.VMEM((groups, day_cols), f32), pltpu.SemaphoreType.DMA((members,))],
    )
    sent_scaled = to_other_half(scaled)
    all_grads = over_first_half(grads)
    (totals,) = call(
        functools.partial(fourth_kernel, half, unit_devices), [((groups, lanes), f32)], "unit_totals", (all_grads,)
    )
    unit_weights, time_weights = call(
        functools.partial(fifth_kernel, half, unit_devices),
        [((groups, unit_rows), f32), ((groups, day_cols), f32)],
        "scale_weights",
        (totals, scaled, all_grads, lam, norms, ends),
    )
    (unit_weights,) = call(
        functools.partial(sixth_kernel, half),
        [((groups, unit_rows), f32)],
        "other_half",
        (to_other_half(totals), sent_scaled, unit_weights),
        in_specs=[vmem, vmem, hbm],
        out_specs=[hbm],
        input_output_aliases={2: 0},
        scratch_shapes=[pltpu.VMEM((groups, unit_rows), f32), pltpu.SemaphoreType.DMA((1,))],
    )
    return unit_weights, time_weights


def solution(mesh):
    return jax.shard_map(
        local,
        mesh=mesh,
        in_specs=(P("unit", "day"), P("unit"), P(), P(), P(None, "unit"), P(None, "day")),
        out_specs=(P(None, "unit"), P(None, "day")),
        check_vma=False,
    )
```

```python
import functools

import jax
import jax.numpy as jnp
from jax import lax
from jax.experimental import pallas as pl
from jax.experimental.pallas import tpu as pltpu
from jax.sharding import PartitionSpec as P

step_rate = 16.0
f32 = jnp.float32
bf16 = jnp.bfloat16
lanes = 128
block_rows = 512
params = pltpu.CompilerParams(vmem_limit_bytes=24 * 1024 * 1024)
vmem = pl.BlockSpec(memory_space=pltpu.VMEM)
hbm = pl.BlockSpec(memory_space=pltpu.HBM)


def split_left(value):
    first = value.astype(bf16).astype(f32)
    return [first, value - first]


def left_of(*values):
    return jnp.concatenate([term for value in values for term in split_left(value)], axis=0).astype(bf16)


def split_panel(value):
    high = value.astype(bf16)
    return high, (value - high.astype(f32)).astype(bf16)


def rows_dot(left, high, low):
    return jnp.dot(left, high, preferred_element_type=f32) + jnp.dot(left, low, preferred_element_type=f32)


def days_dot(left, high, low):
    dims = (((1,), (1,)), ((), ()))
    return lax.dot_general(left, high, dims, preferred_element_type=f32) + lax.dot_general(
        left, low, dims, preferred_element_type=f32
    )


def add_terms(stack, groups, place=0):
    return stack[2 * place * groups :][:groups] + stack[(2 * place + 1) * groups :][:groups]


def tree_sum(values):
    values = list(values)
    while len(values) > 1:
        values = [values[i] + values[i + 1] for i in range(0, len(values), 2)]
    return values[0]


def column(row_ref):
    count = row_ref.shape[1]
    wide = jnp.broadcast_to(row_ref[...].astype(f32), (count, count))
    row = lax.broadcasted_iota(jnp.int32, (count, count), 0)
    lane = lax.broadcasted_iota(jnp.int32, (count, count), 1)
    return jnp.sum(jnp.where(row == lane, wide, 0.0), axis=1, keepdims=True).astype(jnp.int32)


def days_of(device, shape):
    return device * shape[1] + lax.broadcasted_iota(jnp.int32, shape, 1)


def first_half_only(kernel):
    @functools.wraps(kernel)
    def guarded(half, *refs):
        @pl.when(lax.axis_index("day") < half)
        def _():
            kernel(half, *refs)

    return guarded


def fetch(sources, targets, sems):
    copies = [pltpu.make_async_copy(*pair, sems.at[i]) for i, pair in enumerate(zip(sources, targets))]
    for copy in copies:
        copy.start()
    return copies


def fetch_rows(source, target, sems, starts):
    spans = [(start, stop - start) for start, stop in zip(starts, starts[1:])]
    parts = [pl.ds(*span) for span in spans]
    copies = fetch([source.at[here] for here in parts], [target.at[here] for here in parts], sems)
    return [(*span, copy) for span, copy in zip(spans, copies)]


def blocks_of(start, rows):
    return [pl.ds(here, block_rows) for here in range(start, start + rows, block_rows)]


def wait_all(copies):
    for copy in copies:
        copy.wait()


def repeat_start(block, out, sems):
    places = [out.at[i] for i in range(out.shape[0])]
    return fetch([block] * len(places), places, sems)


def first_kernel(all_count, half, starts, *refs):
    arguments, refs = refs[:6], refs[6:]
    out, cross, raised_days, ends, high_ref, low_ref, *held, block, left_ref, cross_block, small_sems, panel_sems, out_sems = refs
    groups, day_cols = held[5].shape
    unit_rows, resident = held[0].shape[0], high_ref.shape[0]
    units = (1, 4)
    days = (2, 3, 5)
    unit_copies = fetch([arguments[i] for i in units], [held[i] for i in units], small_sems)
    parts = fetch_rows(arguments[0], held[0], panel_sems, starts)
    day_copies = fetch([arguments[i] for i in days], [held[i] for i in days], small_sems.at[pl.ds(2, 3)])
    panel, cohort, pre_row, post_row, unit_logit, time_logit = held
    wait_all(unit_copies)
    me = lax.axis_index("day")

    @pl.when(me < half)
    def _():
        label = lax.broadcasted_iota(jnp.int32, (groups, unit_rows), 0)
        treated = jnp.where(cohort[...] == label, 1.0, 0.0)
        control = jnp.where(cohort[...] > label, 1.0, 0.0)
        raised = jnp.exp(unit_logit[...]) * control
        left_ref[...] = left_of(raised, treated)
        lane = lax.broadcasted_iota(jnp.int32, (groups, lanes), 1)
        counts = [jnp.sum(value, axis=1, keepdims=True) for value in (raised, treated, control)]
        slot = lax.broadcasted_iota(jnp.int32, (groups, lanes), 0)
        norms = jnp.zeros((groups, lanes), f32)
        for i, count in enumerate(counts):
            norms += jnp.where(lane == i * groups + slot, count, 0.0)
        block[:, 2 * groups * day_cols :] = jnp.sum(norms, axis=0, keepdims=True)
        product = jnp.zeros((4 * groups, 2 * day_cols), f32)
        for start, rows, copy in parts:
            copy.wait()
            for here in blocks_of(start, rows):
                high, low = split_panel(panel[here, :])
                if here.start < resident:
                    high_ref[here, :] = high
                    low_ref[here, :] = low
                both = jnp.concatenate([high, low], axis=1)
                product += jnp.dot(left_ref[:, here], both, preferred_element_type=f32)
        product = product[:, :day_cols] + product[:, day_cols:]
        both_sums = jnp.concatenate([add_terms(product, groups), product[2 * groups :][:groups]], axis=0)
        for row in range(2 * groups):
            block[:, row * day_cols : (row + 1) * day_cols] = both_sums[row : row + 1, :]
        sends = repeat_start(block, out, out_sems)
        wait_all(day_copies)
        pre_end = column(pre_row)
        ends[...] = jnp.broadcast_to(pre_end.astype(f32), ends.shape)
        before = days_of(me, (groups, day_cols)) < pre_end
        raised_days[...] = jnp.where(before, jnp.exp(time_logit[...]), 0.0)
        wait_all(sends)

    @pl.when(me >= half)
    def _():
        wait_all(day_copies)
        post_start = column(post_row)
        after = jnp.where(days_of(me, (groups, day_cols)) >= post_start, 1.0, 0.0)
        left = left_of(after / (all_count - post_start).astype(f32))
        for start, rows, copy in parts:
            copy.wait()
            for here in blocks_of(start, rows):
                cross_block[:, here] = add_terms(days_dot(left, *split_panel(panel[here, :])), groups)
        wait_all(fetch([cross_block], [cross], out_sems))


@first_half_only
def second_kernel(half, unit_devices, panel, cohort, unit_logit, sums, raised_days, ends, high_ref, low_ref, *refs):
    pack, norms, raised_units, more_high, more_low, held, held_cohort, held_logit, sems = refs
    groups, day_cols = raised_days.shape
    unit_rows, resident = panel.shape[0], high_ref.shape[0]
    rest = pl.ds(resident, unit_rows - resident)
    rows = (unit_rows - resident) // 4
    quarters = [pl.ds(i * rows, rows) for i in range(4)]
    copies = fetch([panel.at[rest].at[here] for here in quarters], [held.at[here] for here in quarters], sems)
    copies += fetch([cohort, unit_logit], [held_cohort, held_logit], sems.at[pl.ds(4, 2)])
    total = tree_sum(sums[u] for u in range(unit_devices))

    def group_rows(first):
        starts = [(first + row) * day_cols for row in range(groups)]
        return jnp.concatenate([total[:, start : start + day_cols] for start in starts], axis=0)

    counts = jnp.broadcast_to(total[:, 2 * groups * day_cols :], (groups, lanes))
    slot = lax.broadcasted_iota(jnp.int32, (groups, lanes), 0)
    lane = lax.broadcasted_iota(jnp.int32, (groups, lanes), 1)
    unit_norm, treat_count, ctrl_count = [
        jnp.sum(jnp.where(lane == i * groups + slot, counts, 0.0), axis=1, keepdims=True) for i in range(3)
    ]
    norms[...] = jnp.where(lane == 0, unit_norm, ctrl_count)
    gap = group_rows(0) / unit_norm - group_rows(groups) / jnp.maximum(treat_count, 1.0)
    before = days_of(lax.axis_index("day"), (groups, day_cols)).astype(f32) < ends[:, 0:1]
    raised_time = raised_days[...]
    pack[:groups, unit_rows:] = raised_time
    pack[groups:, unit_rows:] = jnp.zeros_like(raised_time)
    left = left_of(jnp.where(before, gap, 0.0), raised_time)

    def multiply(here, high, low):
        product = days_dot(left, high, low)
        pack[:groups, here] = add_terms(product, groups)
        pack[groups:, here] = add_terms(product, groups, 1)

    for here in blocks_of(0, resident):
        multiply(here, high_ref[here, :], low_ref[here, :])
    wait_all(copies)
    label = lax.broadcasted_iota(jnp.int32, raised_units.shape, 0)
    raised_units[...] = jnp.where(held_cohort[...] > label, jnp.exp(held_logit[...]), 0.0)
    for here in blocks_of(resident, unit_rows - resident):
        there = pl.ds(here.start - resident, block_rows)
        high, low = split_panel(held[there, :])
        more_high[there, :] = high
        more_low[there, :] = low
        multiply(here, high, low)


@first_half_only
def join_kernel(half, pack, post, out):
    rows, width = pack.shape
    out[:rows, :] = pack[...]
    out[rows:, : post.shape[1]] = post[...]
    out[rows:, post.shape[1] :] = jnp.zeros((post.shape[0], width - post.shape[1]), f32)


@first_half_only
def third_kernel(half, *refs):
    parts, refs = [refs[0].at[day] for day in range(half)], refs[1:]
    high_ref, low_ref, more_high, more_low, norms, raised_units, ends, scaled, lam, out, block, out_sems = refs
    groups, unit_rows = raised_units.shape
    resident, day_cols = high_ref.shape
    unit_norm, ctrl_count = norms[:, 0:1], norms[:, 1:2]
    factor = -step_rate / jnp.sqrt(ends[:, 0:1])
    raised_days = [ref[:groups, unit_rows:] for ref in parts]
    over_time = 1.0 / tree_sum(jnp.sum(value, axis=1, keepdims=True) for value in raised_days)
    over_unit = 1.0 / unit_norm
    me = lax.rem(lax.axis_index("day"), half)
    for day in range(half):
        lam[:, day * day_cols : (day + 1) * day_cols] = raised_days[day] * over_time
    time_grad = jnp.zeros((groups, day_cols), f32)
    new_sum = jnp.zeros((groups, 1), f32)
    for start in range(0, unit_rows, block_rows):
        here = pl.ds(start, block_rows)
        whole = tree_sum(ref[:, here] for ref in parts)
        raised = raised_units[:, here]
        new = raised * over_unit * jnp.exp(whole[:groups] * factor)
        new_sum += jnp.sum(new, axis=1, keepdims=True)
        scaled[:, here] = new * ctrl_count
        shortfall = whole[groups : 2 * groups] * over_time - whole[2 * groups :]
        left = left_of(jnp.where(raised > 0.0, shortfall, 0.0))
        if start < resident:
            high, low = high_ref[here, :], low_ref[here, :]
        else:
            there = pl.ds(start - resident, block_rows)
            high, low = more_high[there, :], more_low[there, :]
        time_grad += add_terms(rows_dot(left, high, low), groups)
    lane = lax.broadcasted_iota(jnp.int32, (groups, day_cols), 1)
    spare = (lane == day_cols - 1) & (me == half - 1)
    block[...] = jnp.where(spare, new_sum, time_grad)
    wait_all(repeat_start(block, out, out_sems))


def time_grad_of(grads, unit_devices, half, day):
    return tree_sum(grads[unit * half + half - 1 - day] for unit in range(unit_devices))


@first_half_only
def fourth_kernel(half, unit_devices, grads, totals):
    day_cols = grads.shape[2]
    last = time_grad_of(grads, unit_devices, half, half - 1)
    totals[...] = jnp.broadcast_to(last[:, day_cols - 1 :], totals.shape)


def fifth_kernel(half, unit_devices, totals, scaled, grads, lam, norms, ends, unit_weights, time_weights):
    groups, day_cols = time_weights.shape
    me = lax.axis_index("day")

    @pl.when(me < half)
    def _():
        unit_weights[...] = scaled[...] * (1.0 / totals[:, 0:1])
        root = jnp.sqrt(jnp.maximum(norms[:, 1:2], 1.0))
        moved_total = jnp.zeros((groups, 1), f32)
        own = jnp.zeros((groups, day_cols), f32)
        for day in range(half):
            total = time_grad_of(grads, unit_devices, half, day)
            moved = lam[:, day * day_cols : (day + 1) * day_cols] * jnp.exp(total * (-step_rate / root))
            moved_total += jnp.sum(moved, axis=1, keepdims=True)
            own = jnp.where(me == day, moved, own)
        time_weights[...] = own * (ends[:, 0:1] / moved_total)

    @pl.when(me >= half)
    def _():
        time_weights[...] = jnp.zeros_like(time_weights)


def sixth_kernel(half, sent_totals, sent_scaled, _, unit_weights, block, out_sem):
    @pl.when(lax.axis_index("day") >= half)
    def _():
        block[...] = sent_scaled[...] * (1.0 / sent_totals[:, 0:1])
        wait_all(fetch([block], [unit_weights], out_sem))


def local(outcomes, cohort, pre_end, post_start, unit_logit, time_logit):
    groups = pre_end.shape[0]
    unit_rows, day_cols = outcomes.shape
    day_devices = lax.axis_size("day")
    unit_devices = lax.axis_size("unit")
    half = day_devices // 2
    assert half * 2 == day_devices and half & (half - 1) == 0
    assert unit_devices & (unit_devices - 1) == 0
    panel_starts = [0, unit_rows // 4, unit_rows // 8 * 5, unit_rows]
    resident = unit_rows * 3 // 4 // block_rows * block_rows
    middle = unit_devices // 2 - 1
    unit_order = [middle] + [unit for unit in reversed(range(unit_devices)) if unit != middle]

    def to_other_half(value):
        pairs = [(u * day_devices + d, u * day_devices + d + half) for u in range(unit_devices) for d in range(half)]
        return lax.ppermute(value, ("unit", "day"), pairs)

    def over_days(value):
        halves = [list(range(half)), list(range(half, day_devices))]
        return lax.all_gather(value, "day", axis_index_groups=halves)

    def over_first_half(value):
        members = [
            [unit * day_devices + day for unit in unit_order for day in reversed(days)]
            for days in (range(half), range(half, day_devices))
        ]
        return lax.all_to_all(
            value, ("unit", "day"), split_axis=0, concat_axis=0, axis_index_groups=members, tiled=True
        )

    def over_units(value):
        return lax.all_to_all(value, "unit", split_axis=0, concat_axis=0, axis_index_groups=[unit_order], tiled=True)

    def call(kernel, shapes, name, args, in_specs=None, out_specs=None, **more):
        return pl.pallas_call(
            kernel,
            in_specs=in_specs or [vmem] * len(args),
            out_specs=out_specs or [vmem] * len(shapes),
            out_shape=[
                shape if isinstance(shape, type(in_hbm)) else jax.ShapeDtypeStruct(*shape) for shape in shapes
            ],
            compiler_params=params,
            name=name,
            **more,
        )(*args)

    arguments = (outcomes, cohort[None, :], pre_end[None, :], post_start[None, :], unit_logit, time_logit)
    fixed = [pltpu.with_memory_space_constraint(argument, pltpu.HBM) for argument in arguments]
    held = [pltpu.VMEM(argument.shape, argument.dtype) for argument in arguments]
    small_sems, panel_sems = pltpu.SemaphoreType.DMA((5,)), pltpu.SemaphoreType.DMA((3,))
    panel_terms = [((resident, day_cols), bf16)] * 2
    other_terms = [((unit_rows - resident, day_cols), bf16)] * 2
    out_sems = pltpu.SemaphoreType.DMA((unit_devices,))
    width = 2 * groups * day_cols + lanes
    in_hbm = pltpu.HBM((unit_devices, 1, width), f32)
    sums, cross, raised_days, ends, high, low = call(
        functools.partial(first_kernel, day_devices * day_cols, half, panel_starts),
        [
            in_hbm,
            pltpu.HBM((groups, unit_rows), f32),
            ((groups, day_cols), f32),
            ((groups, lanes), f32),
            *panel_terms,
        ],
        "first_product",
        fixed,
        in_specs=[hbm] * 6,
        out_specs=[hbm, hbm] + [vmem] * 4,
        scratch_shapes=held
        + [
            pltpu.VMEM((1, width), f32),
            pltpu.VMEM((4 * groups, unit_rows), bf16),
            pltpu.VMEM((groups, unit_rows), f32),
            small_sems,
            panel_sems,
            out_sems,
        ],
    )
    downward = [
        (u * day_devices + d + half, u * day_devices + d) for u in range(unit_devices) for d in range(half)
    ]
    post = lax.ppermute(cross, ("unit", "day"), downward)
    pack, norms, raised_units, more_high, more_low = call(
        functools.partial(second_kernel, half, unit_devices),
        [
            ((2 * groups, unit_rows + day_cols), f32),
            ((groups, lanes), f32),
            ((groups, unit_rows), f32),
            *other_terms,
        ],
        "unit_gradient",
        (fixed[0], fixed[1], fixed[4], over_units(sums), raised_days, ends, high, low),
        in_specs=[hbm] * 3 + [vmem] * 5,
        scratch_shapes=[
            pltpu.VMEM((unit_rows - resident, day_cols), f32),
            held[1],
            held[4],
            pltpu.SemaphoreType.DMA((6,)),
        ],
    )
    (pack,) = call(
        functools.partial(join_kernel, half), [((3 * groups, unit_rows + day_cols), f32)], "join_post", (pack, post)
    )
    members = unit_devices * half
    scaled, lam, grads = call(
        functools.partial(third_kernel, half),
        [
            ((groups, unit_rows), f32),
            ((groups, half * day_cols), f32),
            pltpu.HBM((members, groups, day_cols), f32),
        ],
        "time_gradient",
        (over_days(pack), high, low, more_high, more_low, norms, raised_units, ends),
        out_specs=[vmem, vmem, hbm],
        scratch_shapes=[pltpu.VMEM((groups, day_cols), f32), pltpu.SemaphoreType.DMA((members,))],
    )
    sent_scaled = to_other_half(scaled)
    all_grads = over_first_half(grads)
    (totals,) = call(
        functools.partial(fourth_kernel, half, unit_devices), [((groups, lanes), f32)], "unit_totals", (all_grads,)
    )
    unit_weights, time_weights = call(
        functools.partial(fifth_kernel, half, unit_devices),
        [((groups, unit_rows), f32), ((groups, day_cols), f32)],
        "scale_weights",
        (totals, scaled, all_grads, lam, norms, ends),
    )
    (unit_weights,) = call(
        functools.partial(sixth_kernel, half),
        [((groups, unit_rows), f32)],
        "other_half",
        (to_other_half(totals), sent_scaled, unit_weights),
        in_specs=[vmem, vmem, hbm],
        out_specs=[hbm],
        input_output_aliases={2: 0},
        scratch_shapes=[pltpu.VMEM((groups, unit_rows), f32), pltpu.SemaphoreType.DMA((1,))],
    )
    return unit_weights, time_weights


def solution(mesh):
    return jax.shard_map(
        local,
        mesh=mesh,
        in_specs=(P("unit", "day"), P("unit"), P(), P(), P(None, "unit"), P(None, "day")),
        out_specs=(P(None, "unit"), P(None, "day")),
        check_vma=False,
    )
```

```python
import functools

import jax
import jax.numpy as jnp
from jax import lax
from jax.experimental import pallas as pl
from jax.experimental.pallas import tpu as pltpu
from jax.sharding import PartitionSpec as P

step_rate = 16.0
f32 = jnp.float32
bf16 = jnp.bfloat16
lanes = 128
block_rows = 512
params = pltpu.CompilerParams(vmem_limit_bytes=24 * 1024 * 1024)
vmem = pl.BlockSpec(memory_space=pltpu.VMEM)
hbm = pl.BlockSpec(memory_space=pltpu.HBM)


def split_left(value):
    first = value.astype(bf16).astype(f32)
    return [first, value - first]


def left_of(*values):
    return jnp.concatenate([term for value in values for term in split_left(value)], axis=0).astype(bf16)


def split_panel(value):
    high = value.astype(bf16)
    return high, (value - high.astype(f32)).astype(bf16)


def rows_dot(left, high, low):
    return jnp.dot(left, high, preferred_element_type=f32) + jnp.dot(left, low, preferred_element_type=f32)


def days_dot(left, high, low):
    dims = (((1,), (1,)), ((), ()))
    return lax.dot_general(left, high, dims, preferred_element_type=f32) + lax.dot_general(
        left, low, dims, preferred_element_type=f32
    )


def add_terms(stack, groups, place=0):
    return stack[2 * place * groups :][:groups] + stack[(2 * place + 1) * groups :][:groups]


def tree_sum(values):
    values = list(values)
    while len(values) > 1:
        values = [values[i] + values[i + 1] for i in range(0, len(values), 2)]
    return values[0]


def column(row_ref):
    count = row_ref.shape[1]
    wide = jnp.broadcast_to(row_ref[...].astype(f32), (count, count))
    row = lax.broadcasted_iota(jnp.int32, (count, count), 0)
    lane = lax.broadcasted_iota(jnp.int32, (count, count), 1)
    return jnp.sum(jnp.where(row == lane, wide, 0.0), axis=1, keepdims=True).astype(jnp.int32)


def days_of(device, shape):
    return device * shape[1] + lax.broadcasted_iota(jnp.int32, shape, 1)


def first_half_only(kernel):
    @functools.wraps(kernel)
    def guarded(half, *refs):
        @pl.when(lax.axis_index("day") < half)
        def _():
            kernel(half, *refs)

    return guarded


def fetch(sources, targets, sems):
    copies = [pltpu.make_async_copy(*pair, sems.at[i]) for i, pair in enumerate(zip(sources, targets))]
    for copy in copies:
        copy.start()
    return copies


def fetch_rows(source, target, sems, starts):
    spans = [(start, stop - start) for start, stop in zip(starts, starts[1:])]
    parts = [pl.ds(*span) for span in spans]
    copies = fetch([source.at[here] for here in parts], [target.at[here] for here in parts], sems)
    return [(*span, copy) for span, copy in zip(spans, copies)]


def blocks_of(start, rows):
    return [pl.ds(here, block_rows) for here in range(start, start + rows, block_rows)]


def wait_all(copies):
    for copy in copies:
        copy.wait()


def repeat_start(block, out, sems):
    places = [out.at[i] for i in range(out.shape[0])]
    return fetch([block] * len(places), places, sems)


def first_kernel(all_count, half, starts, *refs):
    arguments, refs = refs[:6], refs[6:]
    out, cross, raised_units, raised_days, time_norm, ends, high_ref, low_ref, *held, block, left_ref, cross_block, small_sems, panel_sems, out_sems = refs
    groups, day_cols = held[5].shape
    unit_rows, resident = held[0].shape[0], high_ref.shape[0]
    (post_copy,) = fetch(arguments[3:4], held[3:4], small_sems)
    unit_copies = fetch(arguments[1:5:3], held[1:5:3], small_sems.at[pl.ds(1, 2)])
    parts = fetch_rows(arguments[0], held[0], panel_sems, starts)
    day_copies = fetch(arguments[2:6:3], held[2:6:3], small_sems.at[pl.ds(3, 2)])
    panel, cohort, pre_row, post_row, unit_logit, time_logit = held
    post_copy.wait()
    wait_all(unit_copies)
    me = lax.axis_index("day")

    @pl.when(me < half)
    def _():
        label = lax.broadcasted_iota(jnp.int32, (groups, unit_rows), 0)
        treated = jnp.where(cohort[...] == label, 1.0, 0.0)
        control = jnp.where(cohort[...] > label, 1.0, 0.0)
        raised = jnp.exp(unit_logit[...]) * control
        raised_units[...] = raised
        left_ref[...] = left_of(raised, treated)
        lane = lax.broadcasted_iota(jnp.int32, (groups, lanes), 1)
        counts = [jnp.sum(value, axis=1, keepdims=True) for value in (raised, treated, control)]
        slot = lax.broadcasted_iota(jnp.int32, (groups, lanes), 0)
        norms = jnp.zeros((groups, lanes), f32)
        for i, count in enumerate(counts):
            norms += jnp.where(lane == i * groups + slot, count, 0.0)
        block[:, 2 * groups * day_cols :] = jnp.sum(norms, axis=0, keepdims=True)
        product = jnp.zeros((4 * groups, 2 * day_cols), f32)
        for start, rows, copy in parts:
            copy.wait()
            for here in blocks_of(start, rows):
                high, low = split_panel(panel[here, :])
                if here.start < resident:
                    high_ref[here, :] = high
                    low_ref[here, :] = low
                both = jnp.concatenate([high, low], axis=1)
                product += jnp.dot(left_ref[:, here], both, preferred_element_type=f32)
        product = product[:, :day_cols] + product[:, day_cols:]
        both_sums = jnp.concatenate([add_terms(product, groups), product[2 * groups :][:groups]], axis=0)
        for row in range(2 * groups):
            block[:, row * day_cols : (row + 1) * day_cols] = both_sums[row : row + 1, :]
        sends = repeat_start(block, out, out_sems)
        wait_all(day_copies)
        pre_end = column(pre_row)
        ends[...] = jnp.broadcast_to(pre_end.astype(f32), ends.shape)
        before = days_of(me, (groups, day_cols)) < pre_end
        raised_time = jnp.where(before, jnp.exp(time_logit[...]), 0.0)
        raised_days[...] = raised_time
        time_norm[...] = jnp.broadcast_to(jnp.sum(raised_time, axis=1, keepdims=True), time_norm.shape)
        wait_all(sends)

    @pl.when(me >= half)
    def _():
        post_start = column(post_row)
        after = jnp.where(days_of(me, (groups, day_cols)) >= post_start, 1.0, 0.0)
        left = left_of(after / (all_count - post_start).astype(f32))
        for start, rows, copy in parts:
            copy.wait()
            for here in blocks_of(start, rows):
                cross_block[:, here] = add_terms(days_dot(left, *split_panel(panel[here, :])), groups)
        sends = fetch([cross_block], [cross], out_sems)
        wait_all(day_copies)
        wait_all(sends)


@first_half_only
def second_kernel(half, unit_devices, panel, sums, raised_days, ends, high_ref, low_ref, *refs):
    pack, norms, more_high, more_low, held, sems = refs
    groups, day_cols = raised_days.shape
    unit_rows, resident = panel.shape[0], high_ref.shape[0]
    rest = pl.ds(resident, unit_rows - resident)
    (copy,) = fetch([panel.at[rest]], [held], sems)
    total = tree_sum(sums[u] for u in range(unit_devices))

    def group_rows(first):
        starts = [(first + row) * day_cols for row in range(groups)]
        return jnp.concatenate([total[:, start : start + day_cols] for start in starts], axis=0)

    counts = jnp.broadcast_to(total[:, 2 * groups * day_cols :], (groups, lanes))
    slot = lax.broadcasted_iota(jnp.int32, (groups, lanes), 0)
    lane = lax.broadcasted_iota(jnp.int32, (groups, lanes), 1)
    unit_norm, treat_count, ctrl_count = [
        jnp.sum(jnp.where(lane == i * groups + slot, counts, 0.0), axis=1, keepdims=True) for i in range(3)
    ]
    norms[...] = jnp.where(lane == 0, unit_norm, ctrl_count)
    gap = group_rows(0) / unit_norm - group_rows(groups) / jnp.maximum(treat_count, 1.0)
    before = days_of(lax.axis_index("day"), (groups, day_cols)).astype(f32) < ends[:, 0:1]
    raised_time = raised_days[...]
    pack[:groups, unit_rows:] = raised_time
    pack[groups:, unit_rows:] = jnp.zeros_like(raised_time)
    left = left_of(jnp.where(before, gap, 0.0), raised_time)

    def multiply(here, high, low):
        product = days_dot(left, high, low)
        pack[:groups, here] = add_terms(product, groups)
        pack[groups:, here] = add_terms(product, groups, 1)

    for here in blocks_of(0, resident):
        multiply(here, high_ref[here, :], low_ref[here, :])
    copy.wait()
    for here in blocks_of(resident, unit_rows - resident):
        there = pl.ds(here.start - resident, block_rows)
        high, low = split_panel(held[there, :])
        more_high[there, :] = high
        more_low[there, :] = low
        multiply(here, high, low)


@first_half_only
def join_kernel(half, pack, post, *refs):
    norms, out = refs[:half], refs[half]
    groups, unit_rows = post.shape
    over_time = 1.0 / tree_sum(ref[:, 0:1] for ref in norms)
    out[:groups, :unit_rows] = pack[:groups, :unit_rows]
    out[:groups, unit_rows:] = pack[:groups, unit_rows:] * over_time
    out[groups:, :unit_rows] = pack[groups:, :unit_rows] * over_time - post[...]
    out[groups:, unit_rows:] = pack[groups:, unit_rows:]


@first_half_only
def third_kernel(half, *refs):
    parts, refs = [refs[0].at[day] for day in range(half)], refs[1:]
    high_ref, low_ref, more_high, more_low, norms, raised_units, ends, scaled, lam, out, block, out_sems = refs
    groups, unit_rows = raised_units.shape
    resident, day_cols = high_ref.shape
    unit_norm, ctrl_count = norms[:, 0:1], norms[:, 1:2]
    factor = -step_rate / jnp.sqrt(ends[:, 0:1])
    over_unit = 1.0 / unit_norm
    me = lax.rem(lax.axis_index("day"), half)
    for day in range(half):
        lam[:, day * day_cols : (day + 1) * day_cols] = parts[day][:groups, unit_rows:]
    time_grad = jnp.zeros((groups, day_cols), f32)
    new_sum = jnp.zeros((groups, 1), f32)
    for start in range(0, unit_rows, block_rows):
        here = pl.ds(start, block_rows)
        whole = tree_sum(ref[:, here] for ref in parts)
        raised = raised_units[:, here]
        new = raised * over_unit * jnp.exp(whole[:groups] * factor)
        new_sum += jnp.sum(new, axis=1, keepdims=True)
        scaled[:, here] = new * ctrl_count
        left = left_of(jnp.where(raised > 0.0, whole[groups:], 0.0))
        if start < resident:
            high, low = high_ref[here, :], low_ref[here, :]
        else:
            there = pl.ds(start - resident, block_rows)
            high, low = more_high[there, :], more_low[there, :]
        time_grad += add_terms(rows_dot(left, high, low), groups)
    lane = lax.broadcasted_iota(jnp.int32, (groups, day_cols), 1)
    spare = (lane == day_cols - 1) & (me == half - 1)
    block[...] = jnp.where(spare, new_sum, time_grad)
    wait_all(repeat_start(block, out, out_sems))


def time_grad_of(grads, unit_devices, half, day):
    return tree_sum(grads[unit * half + half - 1 - day] for unit in range(unit_devices))


@first_half_only
def fourth_kernel(half, unit_devices, grads, totals):
    day_cols = grads.shape[2]
    last = time_grad_of(grads, unit_devices, half, half - 1)
    totals[...] = jnp.broadcast_to(last[:, day_cols - 1 :], totals.shape)


def fifth_kernel(half, unit_devices, totals, scaled, grads, lam, norms, ends, unit_weights, time_weights):
    groups, day_cols = time_weights.shape
    me = lax.axis_index("day")

    @pl.when(me < half)
    def _():
        unit_weights[...] = scaled[...] * (1.0 / totals[:, 0:1])
        root = jnp.sqrt(jnp.maximum(norms[:, 1:2], 1.0))
        moved_total = jnp.zeros((groups, 1), f32)
        own = jnp.zeros((groups, day_cols), f32)
        for day in range(half):
            total = time_grad_of(grads, unit_devices, half, day)
            moved = lam[:, day * day_cols : (day + 1) * day_cols] * jnp.exp(total * (-step_rate / root))
            moved_total += jnp.sum(moved, axis=1, keepdims=True)
            own = jnp.where(me == day, moved, own)
        time_weights[...] = own * (ends[:, 0:1] / moved_total)

    @pl.when(me >= half)
    def _():
        time_weights[...] = jnp.zeros_like(time_weights)


def sixth_kernel(half, sent_totals, sent_scaled, _, unit_weights, block, out_sem):
    @pl.when(lax.axis_index("day") >= half)
    def _():
        block[...] = sent_scaled[...] * (1.0 / sent_totals[:, 0:1])
        wait_all(fetch([block], [unit_weights], out_sem))


def local(outcomes, cohort, pre_end, post_start, unit_logit, time_logit):
    groups = pre_end.shape[0]
    unit_rows, day_cols = outcomes.shape
    day_devices = lax.axis_size("day")
    unit_devices = lax.axis_size("unit")
    half = day_devices // 2
    assert half * 2 == day_devices and half & (half - 1) == 0
    assert unit_devices & (unit_devices - 1) == 0
    panel_starts = [0, unit_rows // 4, unit_rows // 8 * 5, unit_rows]
    resident = unit_rows * 3 // 4 // block_rows * block_rows
    middle = unit_devices // 2 - 1
    unit_order = [middle] + [unit for unit in reversed(range(unit_devices)) if unit != middle]

    def to_other_half(value):
        pairs = [(u * day_devices + d, u * day_devices + d + half) for u in range(unit_devices) for d in range(half)]
        return lax.ppermute(value, ("unit", "day"), pairs)

    def over_days(value):
        halves = [list(range(half)), list(range(half, day_devices))]
        return lax.all_gather(value, "day", axis_index_groups=halves)

    def over_first_half(value):
        members = [
            [unit * day_devices + day for unit in unit_order for day in reversed(days)]
            for days in (range(half), range(half, day_devices))
        ]
        return lax.all_to_all(
            value, ("unit", "day"), split_axis=0, concat_axis=0, axis_index_groups=members, tiled=True
        )

    def over_units(value):
        return lax.all_to_all(value, "unit", split_axis=0, concat_axis=0, axis_index_groups=[unit_order], tiled=True)

    def call(kernel, shapes, name, args, in_specs=None, out_specs=None, **more):
        return pl.pallas_call(
            kernel,
            in_specs=in_specs or [vmem] * len(args),
            out_specs=out_specs or [vmem] * len(shapes),
            out_shape=[
                shape if isinstance(shape, type(in_hbm)) else jax.ShapeDtypeStruct(*shape) for shape in shapes
            ],
            compiler_params=params,
            name=name,
            **more,
        )(*args)

    arguments = (outcomes, cohort[None, :], pre_end[None, :], post_start[None, :], unit_logit, time_logit)
    fixed = [pltpu.with_memory_space_constraint(argument, pltpu.HBM) for argument in arguments]
    held = [pltpu.VMEM(argument.shape, argument.dtype) for argument in arguments]
    small_sems, panel_sems = pltpu.SemaphoreType.DMA((5,)), pltpu.SemaphoreType.DMA((3,))
    panel_terms = [((resident, day_cols), bf16)] * 2
    other_terms = [((unit_rows - resident, day_cols), bf16)] * 2
    out_sems = pltpu.SemaphoreType.DMA((unit_devices,))
    width = 2 * groups * day_cols + lanes
    in_hbm = pltpu.HBM((unit_devices, 1, width), f32)
    sums, cross, raised_units, raised_days, time_norm, ends, high, low = call(
        functools.partial(first_kernel, day_devices * day_cols, half, panel_starts),
        [
            in_hbm,
            pltpu.HBM((groups, unit_rows), f32),
            ((groups, unit_rows), f32),
            ((groups, day_cols), f32),
            ((groups, lanes), f32),
            ((groups, lanes), f32),
            *panel_terms,
        ],
        "first_product",
        fixed,
        in_specs=[hbm] * 6,
        out_specs=[hbm, hbm] + [vmem] * 6,
        scratch_shapes=held
        + [
            pltpu.VMEM((1, width), f32),
            pltpu.VMEM((4 * groups, unit_rows), bf16),
            pltpu.VMEM((groups, unit_rows), f32),
            small_sems,
            panel_sems,
            out_sems,
        ],
    )
    downward = [
        (u * day_devices + d + half, u * day_devices + d) for u in range(unit_devices) for d in range(half)
    ]
    post = lax.ppermute(cross, ("unit", "day"), downward)
    pack, norms, more_high, more_low = call(
        functools.partial(second_kernel, half, unit_devices),
        [
            ((2 * groups, unit_rows + day_cols), f32),
            ((groups, lanes), f32),
            *other_terms,
        ],
        "unit_gradient",
        (fixed[0], over_units(sums), raised_days, ends, high, low),
        in_specs=[hbm] + [vmem] * 5,
        scratch_shapes=[
            pltpu.VMEM((unit_rows - resident, day_cols), f32),
            pltpu.SemaphoreType.DMA((1,)),
        ],
    )
    time_norms = [time_norm]
    for k in range(1, half):
        pairs = [(u * day_devices + d, u * day_devices + (d ^ k)) for u in range(unit_devices) for d in range(half)]
        time_norms.append(lax.ppermute(time_norm, ("unit", "day"), pairs))
    (pack,) = call(
        functools.partial(join_kernel, half),
        [((2 * groups, unit_rows + day_cols), f32)],
        "join_post",
        (pack, post, *time_norms),
    )
    members = unit_devices * half
    scaled, lam, grads = call(
        functools.partial(third_kernel, half),
        [
            ((groups, unit_rows), f32),
            ((groups, half * day_cols), f32),
            pltpu.HBM((members, groups, day_cols), f32),
        ],
        "time_gradient",
        (over_days(pack), high, low, more_high, more_low, norms, raised_units, ends),
        out_specs=[vmem, vmem, hbm],
        scratch_shapes=[pltpu.VMEM((groups, day_cols), f32), pltpu.SemaphoreType.DMA((members,))],
    )
    sent_scaled = to_other_half(scaled)
    all_grads = over_first_half(grads)
    (totals,) = call(
        functools.partial(fourth_kernel, half, unit_devices), [((groups, lanes), f32)], "unit_totals", (all_grads,)
    )
    unit_weights, time_weights = call(
        functools.partial(fifth_kernel, half, unit_devices),
        [((groups, unit_rows), f32), ((groups, day_cols), f32)],
        "scale_weights",
        (totals, scaled, all_grads, lam, norms, ends),
    )
    (unit_weights,) = call(
        functools.partial(sixth_kernel, half),
        [((groups, unit_rows), f32)],
        "other_half",
        (to_other_half(totals), sent_scaled, unit_weights),
        in_specs=[vmem, vmem, hbm],
        out_specs=[hbm],
        input_output_aliases={2: 0},
        scratch_shapes=[pltpu.VMEM((groups, unit_rows), f32), pltpu.SemaphoreType.DMA((1,))],
    )
    return unit_weights, time_weights


def solution(mesh):
    return jax.shard_map(
        local,
        mesh=mesh,
        in_specs=(P("unit", "day"), P("unit"), P(), P(), P(None, "unit"), P(None, "day")),
        out_specs=(P(None, "unit"), P(None, "day")),
        check_vma=False,
    )
```

```python
import functools

import jax
import jax.numpy as jnp
from jax import lax
from jax.experimental import pallas as pl
from jax.experimental.pallas import tpu as pltpu
from jax.sharding import PartitionSpec as P

step_rate = 16.0
f32 = jnp.float32
bf16 = jnp.bfloat16
lanes = 128
block_rows = 512
params = pltpu.CompilerParams(vmem_limit_bytes=24 * 1024 * 1024)
vmem = pl.BlockSpec(memory_space=pltpu.VMEM)
hbm = pl.BlockSpec(memory_space=pltpu.HBM)


def split_left(value):
    first = value.astype(bf16).astype(f32)
    return [first, value - first]


def left_of(*values):
    return jnp.concatenate([term for value in values for term in split_left(value)], axis=0).astype(bf16)


def split_panel(value):
    high = value.astype(bf16)
    return high, (value - high.astype(f32)).astype(bf16)


def rows_dot(left, high, low):
    return jnp.dot(left, high, preferred_element_type=f32) + jnp.dot(left, low, preferred_element_type=f32)


def days_dot(left, high, low):
    dims = (((1,), (1,)), ((), ()))
    return lax.dot_general(left, high, dims, preferred_element_type=f32) + lax.dot_general(
        left, low, dims, preferred_element_type=f32
    )


def add_terms(stack, groups, place=0):
    return stack[2 * place * groups :][:groups] + stack[(2 * place + 1) * groups :][:groups]


def tree_sum(values):
    values = list(values)
    while len(values) > 1:
        values = [values[i] + values[i + 1] for i in range(0, len(values), 2)]
    return values[0]


def column(row_ref):
    count = row_ref.shape[1]
    wide = jnp.broadcast_to(row_ref[...].astype(f32), (count, count))
    row = lax.broadcasted_iota(jnp.int32, (count, count), 0)
    lane = lax.broadcasted_iota(jnp.int32, (count, count), 1)
    return jnp.sum(jnp.where(row == lane, wide, 0.0), axis=1, keepdims=True).astype(jnp.int32)


def days_of(device, shape):
    return device * shape[1] + lax.broadcasted_iota(jnp.int32, shape, 1)


def first_half_only(kernel):
    @functools.wraps(kernel)
    def guarded(half, *refs):
        @pl.when(lax.axis_index("day") < half)
        def _():
            kernel(half, *refs)

    return guarded


def fetch(sources, targets, sems):
    copies = [pltpu.make_async_copy(*pair, sems.at[i]) for i, pair in enumerate(zip(sources, targets))]
    for copy in copies:
        copy.start()
    return copies


def fetch_rows(source, target, sems, starts):
    spans = [(start, stop - start) for start, stop in zip(starts, starts[1:])]
    parts = [pl.ds(*span) for span in spans]
    copies = fetch([source.at[here] for here in parts], [target.at[here] for here in parts], sems)
    return [(*span, copy) for span, copy in zip(spans, copies)]


def blocks_of(start, rows):
    return [pl.ds(here, block_rows) for here in range(start, start + rows, block_rows)]


def wait_all(copies):
    for copy in copies:
        copy.wait()


def repeat_start(block, out, sems):
    places = [out.at[i] for i in range(out.shape[0])]
    return fetch([block] * len(places), places, sems)


def first_kernel(all_count, half, starts, *refs):
    arguments, refs = refs[:6], refs[6:]
    out, cross, raised_days, time_norm, ends, high_ref, low_ref, *held, block, left_ref, cross_block, small_sems, panel_sems, out_sems = refs
    groups, day_cols = held[5].shape
    unit_rows, resident = held[0].shape[0], high_ref.shape[0]
    (post_copy,) = fetch(arguments[3:4], held[3:4], small_sems)
    unit_copies = fetch(arguments[1:5:3], held[1:5:3], small_sems.at[pl.ds(1, 2)])
    parts = fetch_rows(arguments[0], held[0], panel_sems, starts)
    day_copies = fetch(arguments[2:6:3], held[2:6:3], small_sems.at[pl.ds(3, 2)])
    panel, cohort, pre_row, post_row, unit_logit, time_logit = held
    post_copy.wait()
    wait_all(unit_copies)
    me = lax.axis_index("day")

    @pl.when(me < half)
    def _():
        label = lax.broadcasted_iota(jnp.int32, (groups, unit_rows), 0)
        treated = jnp.where(cohort[...] == label, 1.0, 0.0)
        control = jnp.where(cohort[...] > label, 1.0, 0.0)
        raised = jnp.exp(unit_logit[...]) * control
        left_ref[...] = left_of(raised, treated)
        lane = lax.broadcasted_iota(jnp.int32, (groups, lanes), 1)
        counts = [jnp.sum(value, axis=1, keepdims=True) for value in (raised, treated, control)]
        slot = lax.broadcasted_iota(jnp.int32, (groups, lanes), 0)
        norms = jnp.zeros((groups, lanes), f32)
        for i, count in enumerate(counts):
            norms += jnp.where(lane == i * groups + slot, count, 0.0)
        block[:, 2 * groups * day_cols :] = jnp.sum(norms, axis=0, keepdims=True)
        product = jnp.zeros((4 * groups, 2 * day_cols), f32)
        for start, rows, copy in parts:
            copy.wait()
            for here in blocks_of(start, rows):
                high, low = split_panel(panel[here, :])
                if here.start < resident:
                    high_ref[here, :] = high
                    low_ref[here, :] = low
                both = jnp.concatenate([high, low], axis=1)
                product += jnp.dot(left_ref[:, here], both, preferred_element_type=f32)
        product = product[:, :day_cols] + product[:, day_cols:]
        both_sums = jnp.concatenate([add_terms(product, groups), product[2 * groups :][:groups]], axis=0)
        for row in range(2 * groups):
            block[:, row * day_cols : (row + 1) * day_cols] = both_sums[row : row + 1, :]
        sends = repeat_start(block, out, out_sems)
        wait_all(day_copies)
        pre_end = column(pre_row)
        ends[...] = jnp.broadcast_to(pre_end.astype(f32), ends.shape)
        before = days_of(me, (groups, day_cols)) < pre_end
        raised_time = jnp.where(before, jnp.exp(time_logit[...]), 0.0)
        raised_days[...] = raised_time
        time_norm[...] = jnp.broadcast_to(jnp.sum(raised_time, axis=1, keepdims=True), time_norm.shape)
        wait_all(sends)

    @pl.when(me >= half)
    def _():
        post_start = column(post_row)
        after = jnp.where(days_of(me, (groups, day_cols)) >= post_start, 1.0, 0.0)
        left = left_of(after / (all_count - post_start).astype(f32))
        for start, rows, copy in parts:
            copy.wait()
            for here in blocks_of(start, rows):
                cross_block[:, here] = add_terms(days_dot(left, *split_panel(panel[here, :])), groups)
        sends = fetch([cross_block], [cross], out_sems)
        wait_all(day_copies)
        wait_all(sends)


@first_half_only
def second_kernel(half, unit_order, panel, cohort, unit_logit, sums, raised_days, ends, high_ref, low_ref, *refs):
    pack, norms, raised_units, more_high, more_low, held, held_cohort, held_logit, sems = refs
    groups, day_cols = raised_days.shape
    unit_rows, resident = panel.shape[0], high_ref.shape[0]
    rest = pl.ds(resident, unit_rows - resident)
    copies = fetch([panel.at[rest], cohort, unit_logit], [held, held_cohort, held_logit], sems)
    odd = lax.rem(lax.axis_index("day"), 2) == 1
    total = tree_sum(sums[jnp.where(odd, unit, unit_order.index(unit))] for unit in range(len(unit_order)))

    def group_rows(first):
        starts = [(first + row) * day_cols for row in range(groups)]
        return jnp.concatenate([total[:, start : start + day_cols] for start in starts], axis=0)

    counts = jnp.broadcast_to(total[:, 2 * groups * day_cols :], (groups, lanes))
    slot = lax.broadcasted_iota(jnp.int32, (groups, lanes), 0)
    lane = lax.broadcasted_iota(jnp.int32, (groups, lanes), 1)
    unit_norm, treat_count, ctrl_count = [
        jnp.sum(jnp.where(lane == i * groups + slot, counts, 0.0), axis=1, keepdims=True) for i in range(3)
    ]
    norms[...] = jnp.where(lane == 0, unit_norm, ctrl_count)
    gap = group_rows(0) / unit_norm - group_rows(groups) / jnp.maximum(treat_count, 1.0)
    before = days_of(lax.axis_index("day"), (groups, day_cols)).astype(f32) < ends[:, 0:1]
    raised_time = raised_days[...]
    pack[:groups, unit_rows:] = raised_time
    pack[groups:, unit_rows:] = jnp.zeros_like(raised_time)
    left = left_of(jnp.where(before, gap, 0.0), raised_time)

    def multiply(here, high, low):
        product = days_dot(left, high, low)
        pack[:groups, here] = add_terms(product, groups)
        pack[groups:, here] = add_terms(product, groups, 1)

    for here in blocks_of(0, resident):
        multiply(here, high_ref[here, :], low_ref[here, :])
    wait_all(copies)
    label = lax.broadcasted_iota(jnp.int32, raised_units.shape, 0)
    raised_units[...] = jnp.where(held_cohort[...] > label, jnp.exp(held_logit[...]), 0.0)
    for here in blocks_of(resident, unit_rows - resident):
        there = pl.ds(here.start - resident, block_rows)
        high, low = split_panel(held[there, :])
        more_high[there, :] = high
        more_low[there, :] = low
        multiply(here, high, low)


@first_half_only
def join_kernel(half, pack, post, *refs):
    norms, out = refs[:half], refs[half]
    groups, unit_rows = post.shape
    over_time = 1.0 / tree_sum(ref[:, 0:1] for ref in norms)
    out[:groups, :unit_rows] = pack[:groups, :unit_rows]
    out[:groups, unit_rows:] = pack[:groups, unit_rows:] * over_time
    out[groups:, :unit_rows] = pack[groups:, :unit_rows] * over_time - post[...]
    out[groups:, unit_rows:] = pack[groups:, unit_rows:]


@first_half_only
def third_kernel(half, *refs):
    parts, refs = [refs[0].at[day] for day in range(half)], refs[1:]
    high_ref, low_ref, more_high, more_low, norms, raised_units, ends, scaled, lam, out, block, out_sems = refs
    groups, unit_rows = raised_units.shape
    resident, day_cols = high_ref.shape
    unit_norm, ctrl_count = norms[:, 0:1], norms[:, 1:2]
    factor = -step_rate / jnp.sqrt(ends[:, 0:1])
    over_unit = 1.0 / unit_norm
    me = lax.rem(lax.axis_index("day"), half)
    for day in range(half):
        lam[:, day * day_cols : (day + 1) * day_cols] = parts[day][:groups, unit_rows:]
    time_grad = jnp.zeros((groups, day_cols), f32)
    new_sum = jnp.zeros((groups, 1), f32)
    for start in range(0, unit_rows, block_rows):
        here = pl.ds(start, block_rows)
        whole = tree_sum(ref[:, here] for ref in parts)
        raised = raised_units[:, here]
        new = raised * over_unit * jnp.exp(whole[:groups] * factor)
        new_sum += jnp.sum(new, axis=1, keepdims=True)
        scaled[:, here] = new * ctrl_count
        left = left_of(jnp.where(raised > 0.0, whole[groups:], 0.0))
        if start < resident:
            high, low = high_ref[here, :], low_ref[here, :]
        else:
            there = pl.ds(start - resident, block_rows)
            high, low = more_high[there, :], more_low[there, :]
        time_grad += add_terms(rows_dot(left, high, low), groups)
    lane = lax.broadcasted_iota(jnp.int32, (groups, day_cols), 1)
    spare = (lane == day_cols - 1) & (me == half - 1)
    block[...] = jnp.where(spare, new_sum, time_grad)
    wait_all(repeat_start(block, out, out_sems))


def time_grad_of(grads, unit_devices, half, day):
    return tree_sum(grads[unit * half + half - 1 - day] for unit in range(unit_devices))


@first_half_only
def fourth_kernel(half, unit_devices, grads, totals):
    day_cols = grads.shape[2]
    last = time_grad_of(grads, unit_devices, half, half - 1)
    totals[...] = jnp.broadcast_to(last[:, day_cols - 1 :], totals.shape)


def fifth_kernel(half, unit_devices, totals, scaled, grads, lam, norms, ends, unit_weights, time_weights):
    groups, day_cols = time_weights.shape
    me = lax.axis_index("day")

    @pl.when(me < half)
    def _():
        unit_weights[...] = scaled[...] * (1.0 / totals[:, 0:1])
        root = jnp.sqrt(jnp.maximum(norms[:, 1:2], 1.0))
        moved_total = jnp.zeros((groups, 1), f32)
        own = jnp.zeros((groups, day_cols), f32)
        for day in range(half):
            total = time_grad_of(grads, unit_devices, half, day)
            moved = lam[:, day * day_cols : (day + 1) * day_cols] * jnp.exp(total * (-step_rate / root))
            moved_total += jnp.sum(moved, axis=1, keepdims=True)
            own = jnp.where(me == day, moved, own)
        time_weights[...] = own * (ends[:, 0:1] / moved_total)

    @pl.when(me >= half)
    def _():
        time_weights[...] = jnp.zeros_like(time_weights)


def sixth_kernel(half, sent_totals, sent_scaled, _, unit_weights, block, out_sem):
    @pl.when(lax.axis_index("day") >= half)
    def _():
        block[...] = sent_scaled[...] * (1.0 / sent_totals[:, 0:1])
        wait_all(fetch([block], [unit_weights], out_sem))


def local(outcomes, cohort, pre_end, post_start, unit_logit, time_logit):
    groups = pre_end.shape[0]
    unit_rows, day_cols = outcomes.shape
    day_devices = lax.axis_size("day")
    unit_devices = lax.axis_size("unit")
    half = day_devices // 2
    assert half * 2 == day_devices and half & (half - 1) == 0
    assert unit_devices & (unit_devices - 1) == 0
    panel_starts = [0, unit_rows // 4, unit_rows // 8 * 5, unit_rows]
    resident = unit_rows * 3 // 4 // block_rows * block_rows
    middle = unit_devices // 2 - 1
    unit_order = [middle] + [unit for unit in reversed(range(unit_devices)) if unit != middle]

    def to_other_half(value):
        pairs = [(u * day_devices + d, u * day_devices + d + half) for u in range(unit_devices) for d in range(half)]
        return lax.ppermute(value, ("unit", "day"), pairs)

    def over_days(value):
        halves = [list(range(half)), list(range(half, day_devices))]
        return lax.all_gather(value, "day", axis_index_groups=halves)

    def over_first_half(value):
        members = [
            [unit * day_devices + day for unit in unit_order for day in reversed(days)]
            for days in (range(half), range(half, day_devices))
        ]
        return lax.all_to_all(
            value, ("unit", "day"), split_axis=0, concat_axis=0, axis_index_groups=members, tiled=True
        )

    def over_units(value):
        members = [
            [unit * day_devices + day for unit in (range(unit_devices) if day % 2 else unit_order)]
            for day in range(day_devices)
        ]
        return lax.all_to_all(
            value, ("unit", "day"), split_axis=0, concat_axis=0, axis_index_groups=members, tiled=True
        )

    def call(kernel, shapes, name, args, in_specs=None, out_specs=None, **more):
        return pl.pallas_call(
            kernel,
            in_specs=in_specs or [vmem] * len(args),
            out_specs=out_specs or [vmem] * len(shapes),
            out_shape=[
                shape if isinstance(shape, type(in_hbm)) else jax.ShapeDtypeStruct(*shape) for shape in shapes
            ],
            compiler_params=params,
            name=name,
            **more,
        )(*args)

    arguments = (outcomes, cohort[None, :], pre_end[None, :], post_start[None, :], unit_logit, time_logit)
    fixed = [pltpu.with_memory_space_constraint(argument, pltpu.HBM) for argument in arguments]
    held = [pltpu.VMEM(argument.shape, argument.dtype) for argument in arguments]
    small_sems, panel_sems = pltpu.SemaphoreType.DMA((5,)), pltpu.SemaphoreType.DMA((3,))
    panel_terms = [((resident, day_cols), bf16)] * 2
    other_terms = [((unit_rows - resident, day_cols), bf16)] * 2
    out_sems = pltpu.SemaphoreType.DMA((unit_devices,))
    width = 2 * groups * day_cols + lanes
    in_hbm = pltpu.HBM((unit_devices, 1, width), f32)
    sums, cross, raised_days, time_norm, ends, high, low = call(
        functools.partial(first_kernel, day_devices * day_cols, half, panel_starts),
        [
            in_hbm,
            pltpu.HBM((groups, unit_rows), f32),
            ((groups, day_cols), f32),
            ((groups, lanes), f32),
            ((groups, lanes), f32),
            *panel_terms,
        ],
        "first_product",
        fixed,
        in_specs=[hbm] * 6,
        out_specs=[hbm, hbm] + [vmem] * 5,
        scratch_shapes=held
        + [
            pltpu.VMEM((1, width), f32),
            pltpu.VMEM((4 * groups, unit_rows), bf16),
            pltpu.VMEM((groups, unit_rows), f32),
            small_sems,
            panel_sems,
            out_sems,
        ],
    )
    downward = [
        (u * day_devices + d + half, u * day_devices + d) for u in range(unit_devices) for d in range(half)
    ]
    post = lax.ppermute(cross, ("unit", "day"), downward)
    pack, norms, raised_units, more_high, more_low = call(
        functools.partial(second_kernel, half, unit_order),
        [
            ((2 * groups, unit_rows + day_cols), f32),
            ((groups, lanes), f32),
            ((groups, unit_rows), f32),
            *other_terms,
        ],
        "unit_gradient",
        (fixed[0], fixed[1], fixed[4], over_units(sums), raised_days, ends, high, low),
        in_specs=[hbm] * 3 + [vmem] * 5,
        scratch_shapes=[
            pltpu.VMEM((unit_rows - resident, day_cols), f32),
            held[1],
            held[4],
            pltpu.SemaphoreType.DMA((3,)),
        ],
    )
    time_norms = [time_norm]
    for k in range(1, half):
        pairs = [(u * day_devices + d, u * day_devices + (d ^ k)) for u in range(unit_devices) for d in range(half)]
        time_norms.append(lax.ppermute(time_norm, ("unit", "day"), pairs))
    (pack,) = call(
        functools.partial(join_kernel, half),
        [((2 * groups, unit_rows + day_cols), f32)],
        "join_post",
        (pack, post, *time_norms),
    )
    members = unit_devices * half
    scaled, lam, grads = call(
        functools.partial(third_kernel, half),
        [
            ((groups, unit_rows), f32),
            ((groups, half * day_cols), f32),
            pltpu.HBM((members, groups, day_cols), f32),
        ],
        "time_gradient",
        (over_days(pack), high, low, more_high, more_low, norms, raised_units, ends),
        out_specs=[vmem, vmem, hbm],
        scratch_shapes=[pltpu.VMEM((groups, day_cols), f32), pltpu.SemaphoreType.DMA((members,))],
    )
    sent_scaled = to_other_half(scaled)
    all_grads = over_first_half(grads)
    (totals,) = call(
        functools.partial(fourth_kernel, half, unit_devices), [((groups, lanes), f32)], "unit_totals", (all_grads,)
    )
    unit_weights, time_weights = call(
        functools.partial(fifth_kernel, half, unit_devices),
        [((groups, unit_rows), f32), ((groups, day_cols), f32)],
        "scale_weights",
        (totals, scaled, all_grads, lam, norms, ends),
    )
    (unit_weights,) = call(
        functools.partial(sixth_kernel, half),
        [((groups, unit_rows), f32)],
        "other_half",
        (to_other_half(totals), sent_scaled, unit_weights),
        in_specs=[vmem, vmem, hbm],
        out_specs=[hbm],
        input_output_aliases={2: 0},
        scratch_shapes=[pltpu.VMEM((groups, unit_rows), f32), pltpu.SemaphoreType.DMA((1,))],
    )
    return unit_weights, time_weights


def solution(mesh):
    return jax.shard_map(
        local,
        mesh=mesh,
        in_specs=(P("unit", "day"), P("unit"), P(), P(), P(None, "unit"), P(None, "day")),
        out_specs=(P(None, "unit"), P(None, "day")),
        check_vma=False,
    )
```

```python
import functools

import jax
import jax.numpy as jnp
from jax import lax
from jax.experimental import pallas as pl
from jax.experimental.pallas import tpu as pltpu
from jax.sharding import PartitionSpec as P

step_rate = 16.0
f32 = jnp.float32
bf16 = jnp.bfloat16
lanes = 128
block_rows = 512
params = pltpu.CompilerParams(vmem_limit_bytes=24 * 1024 * 1024)
vmem = pl.BlockSpec(memory_space=pltpu.VMEM)
hbm = pl.BlockSpec(memory_space=pltpu.HBM)


def split_left(value):
    first = value.astype(bf16).astype(f32)
    return [first, value - first]


def left_of(*values):
    return jnp.concatenate([term for value in values for term in split_left(value)], axis=0).astype(bf16)


def split_panel(value):
    high = value.astype(bf16)
    return high, (value - high.astype(f32)).astype(bf16)


def rows_dot(left, high, low):
    return jnp.dot(left, high, preferred_element_type=f32) + jnp.dot(left, low, preferred_element_type=f32)


def days_dot(left, high, low):
    dims = (((1,), (1,)), ((), ()))
    return lax.dot_general(left, high, dims, preferred_element_type=f32) + lax.dot_general(
        left, low, dims, preferred_element_type=f32
    )


def add_terms(stack, groups, place=0):
    return stack[2 * place * groups :][:groups] + stack[(2 * place + 1) * groups :][:groups]


def tree_sum(values):
    values = list(values)
    while len(values) > 1:
        values = [values[i] + values[i + 1] for i in range(0, len(values), 2)]
    return values[0]


def column(row_ref):
    count = row_ref.shape[1]
    wide = jnp.broadcast_to(row_ref[...].astype(f32), (count, count))
    row = lax.broadcasted_iota(jnp.int32, (count, count), 0)
    lane = lax.broadcasted_iota(jnp.int32, (count, count), 1)
    return jnp.sum(jnp.where(row == lane, wide, 0.0), axis=1, keepdims=True).astype(jnp.int32)


def days_of(device, shape):
    return device * shape[1] + lax.broadcasted_iota(jnp.int32, shape, 1)


def first_half_only(kernel):
    @functools.wraps(kernel)
    def guarded(half, *refs):
        @pl.when(lax.axis_index("day") < half)
        def _():
            kernel(half, *refs)

    return guarded


def fetch(sources, targets, sems):
    copies = [pltpu.make_async_copy(*pair, sems.at[i]) for i, pair in enumerate(zip(sources, targets))]
    for copy in copies:
        copy.start()
    return copies


def fetch_rows(source, target, sems, starts):
    spans = [(start, stop - start) for start, stop in zip(starts, starts[1:])]
    parts = [pl.ds(*span) for span in spans]
    copies = fetch([source.at[here] for here in parts], [target.at[here] for here in parts], sems)
    return [(*span, copy) for span, copy in zip(spans, copies)]


def blocks_of(start, rows):
    return [pl.ds(here, block_rows) for here in range(start, start + rows, block_rows)]


def wait_all(copies):
    for copy in copies:
        copy.wait()


def repeat_start(block, out, sems):
    places = [out.at[i] for i in range(out.shape[0])]
    return fetch([block] * len(places), places, sems)


def first_kernel(all_count, half, starts, *refs):
    arguments, refs = refs[:6], refs[6:]
    out, cross, raised_days, time_norm, ends, high_ref, low_ref, *held, block, left_ref, cross_block, small_sems, panel_sems, out_sems = refs
    groups, day_cols = held[5].shape
    unit_rows, resident = held[0].shape[0], high_ref.shape[0]
    (post_copy,) = fetch(arguments[3:4], held[3:4], small_sems)
    unit_copies = fetch(arguments[1:5:3], held[1:5:3], small_sems.at[pl.ds(1, 2)])
    parts = fetch_rows(arguments[0], held[0], panel_sems, starts)
    day_copies = fetch(arguments[2:6:3], held[2:6:3], small_sems.at[pl.ds(3, 2)])
    panel, cohort, pre_row, post_row, unit_logit, time_logit = held
    post_copy.wait()
    wait_all(unit_copies)
    me = lax.axis_index("day")

    @pl.when(me < half)
    def _():
        label = lax.broadcasted_iota(jnp.int32, (groups, unit_rows), 0)
        treated = jnp.where(cohort[...] == label, 1.0, 0.0)
        control = jnp.where(cohort[...] > label, 1.0, 0.0)
        raised = jnp.exp(unit_logit[...]) * control
        left_ref[...] = left_of(raised, treated)
        lane = lax.broadcasted_iota(jnp.int32, (groups, lanes), 1)
        counts = [jnp.sum(value, axis=1, keepdims=True) for value in (raised, treated, control)]
        slot = lax.broadcasted_iota(jnp.int32, (groups, lanes), 0)
        norms = jnp.zeros((groups, lanes), f32)
        for i, count in enumerate(counts):
            norms += jnp.where(lane == i * groups + slot, count, 0.0)
        block[:, 2 * groups * day_cols :] = jnp.sum(norms, axis=0, keepdims=True)
        product = jnp.zeros((4 * groups, 2 * day_cols), f32)
        for start, rows, copy in parts:
            copy.wait()
            for here in blocks_of(start, rows):
                high, low = split_panel(panel[here, :])
                if here.start < resident:
                    high_ref[here, :] = high
                    low_ref[here, :] = low
                both = jnp.concatenate([high, low], axis=1)
                product += jnp.dot(left_ref[:, here], both, preferred_element_type=f32)
        product = product[:, :day_cols] + product[:, day_cols:]
        both_sums = jnp.concatenate([add_terms(product, groups), product[2 * groups :][:groups]], axis=0)
        for row in range(2 * groups):
            block[:, row * day_cols : (row + 1) * day_cols] = both_sums[row : row + 1, :]
        sends = repeat_start(block, out, out_sems)
        wait_all(day_copies)
        pre_end = column(pre_row)
        ends[...] = jnp.broadcast_to(pre_end.astype(f32), ends.shape)
        before = days_of(me, (groups, day_cols)) < pre_end
        raised_time = jnp.where(before, jnp.exp(time_logit[...]), 0.0)
        raised_days[...] = raised_time
        time_norm[...] = jnp.broadcast_to(jnp.sum(raised_time, axis=1, keepdims=True), time_norm.shape)
        wait_all(sends)

    @pl.when(me >= half)
    def _():
        post_start = column(post_row)
        after = jnp.where(days_of(me, (groups, day_cols)) >= post_start, 1.0, 0.0)
        left = left_of(after / (all_count - post_start).astype(f32))
        for start, rows, copy in parts:
            copy.wait()

            @pl.loop(start // block_rows, (start + rows) // block_rows)
            def _(block):
                here = pl.ds(pl.multiple_of(block * block_rows, block_rows), block_rows)
                cross_block[:, here] = add_terms(days_dot(left, *split_panel(panel[here, :])), groups)

        sends = fetch([cross_block], [cross], out_sems)
        wait_all(day_copies)
        wait_all(sends)


@first_half_only
def second_kernel(half, unit_devices, panel, cohort, unit_logit, sums, raised_days, ends, high_ref, low_ref, *refs):
    pack, norms, raised_units, more_high, more_low, held, held_cohort, held_logit, sems = refs
    groups, day_cols = raised_days.shape
    unit_rows, resident = panel.shape[0], high_ref.shape[0]
    rest = pl.ds(resident, unit_rows - resident)
    copies = fetch([panel.at[rest], cohort, unit_logit], [held, held_cohort, held_logit], sems)
    total = tree_sum(sums[u] for u in range(unit_devices))

    def group_rows(first):
        starts = [(first + row) * day_cols for row in range(groups)]
        return jnp.concatenate([total[:, start : start + day_cols] for start in starts], axis=0)

    counts = jnp.broadcast_to(total[:, 2 * groups * day_cols :], (groups, lanes))
    slot = lax.broadcasted_iota(jnp.int32, (groups, lanes), 0)
    lane = lax.broadcasted_iota(jnp.int32, (groups, lanes), 1)
    unit_norm, treat_count, ctrl_count = [
        jnp.sum(jnp.where(lane == i * groups + slot, counts, 0.0), axis=1, keepdims=True) for i in range(3)
    ]
    norms[...] = jnp.where(lane == 0, unit_norm, ctrl_count)
    gap = group_rows(0) / unit_norm - group_rows(groups) / jnp.maximum(treat_count, 1.0)
    before = days_of(lax.axis_index("day"), (groups, day_cols)).astype(f32) < ends[:, 0:1]
    raised_time = raised_days[...]
    pack[:groups, unit_rows:] = raised_time
    pack[groups:, unit_rows:] = jnp.zeros_like(raised_time)
    left = left_of(jnp.where(before, gap, 0.0), raised_time)

    def multiply(here, high, low):
        product = days_dot(left, high, low)
        pack[:groups, here] = add_terms(product, groups)
        pack[groups:, here] = add_terms(product, groups, 1)

    @pl.loop(0, resident // block_rows)
    def _(block):
        here = pl.ds(pl.multiple_of(block * block_rows, block_rows), block_rows)
        multiply(here, high_ref[here, :], low_ref[here, :])

    wait_all(copies)
    label = lax.broadcasted_iota(jnp.int32, raised_units.shape, 0)
    raised_units[...] = jnp.where(held_cohort[...] > label, jnp.exp(held_logit[...]), 0.0)
    for here in blocks_of(resident, unit_rows - resident):
        there = pl.ds(here.start - resident, block_rows)
        high, low = split_panel(held[there, :])
        more_high[there, :] = high
        more_low[there, :] = low
        multiply(here, high, low)


@first_half_only
def join_kernel(half, pack, post, *refs):
    norms, out = refs[:half], refs[half]
    groups, unit_rows = post.shape
    over_time = 1.0 / tree_sum(ref[:, 0:1] for ref in norms)
    out[:groups, :unit_rows] = pack[:groups, :unit_rows]
    out[:groups, unit_rows:] = pack[:groups, unit_rows:] * over_time
    out[groups:, :unit_rows] = pack[groups:, :unit_rows] * over_time - post[...]
    out[groups:, unit_rows:] = pack[groups:, unit_rows:]


@first_half_only
def third_kernel(half, *refs):
    parts, refs = [refs[0].at[day] for day in range(half)], refs[1:]
    high_ref, low_ref, more_high, more_low, norms, raised_units, ends, scaled, lam, out, block, out_sems = refs
    groups, unit_rows = raised_units.shape
    resident, day_cols = high_ref.shape
    unit_norm, ctrl_count = norms[:, 0:1], norms[:, 1:2]
    factor = -step_rate / jnp.sqrt(ends[:, 0:1])
    over_unit = 1.0 / unit_norm
    me = lax.rem(lax.axis_index("day"), half)
    for day in range(half):
        lam[:, day * day_cols : (day + 1) * day_cols] = parts[day][:groups, unit_rows:]
    time_grad = jnp.zeros((groups, day_cols), f32)
    new_sum = jnp.zeros((groups, 1), f32)
    for start in range(0, unit_rows, block_rows):
        here = pl.ds(start, block_rows)
        whole = tree_sum(ref[:, here] for ref in parts)
        raised = raised_units[:, here]
        new = raised * over_unit * jnp.exp(whole[:groups] * factor)
        new_sum += jnp.sum(new, axis=1, keepdims=True)
        scaled[:, here] = new * ctrl_count
        left = left_of(jnp.where(raised > 0.0, whole[groups:], 0.0))
        if start < resident:
            high, low = high_ref[here, :], low_ref[here, :]
        else:
            there = pl.ds(start - resident, block_rows)
            high, low = more_high[there, :], more_low[there, :]
        time_grad += add_terms(rows_dot(left, high, low), groups)
    lane = lax.broadcasted_iota(jnp.int32, (groups, day_cols), 1)
    spare = (lane == day_cols - 1) & (me == half - 1)
    block[...] = jnp.where(spare, new_sum, time_grad)
    wait_all(repeat_start(block, out, out_sems))


def time_grad_of(grads, unit_devices, half, day):
    return tree_sum(grads[unit * half + half - 1 - day] for unit in range(unit_devices))


@first_half_only
def fourth_kernel(half, unit_devices, grads, totals):
    day_cols = grads.shape[2]
    last = time_grad_of(grads, unit_devices, half, half - 1)
    totals[...] = jnp.broadcast_to(last[:, day_cols - 1 :], totals.shape)


def fifth_kernel(half, unit_devices, totals, scaled, grads, lam, norms, ends, unit_weights, time_weights):
    groups, day_cols = time_weights.shape
    me = lax.axis_index("day")

    @pl.when(me < half)
    def _():
        unit_weights[...] = scaled[...] * (1.0 / totals[:, 0:1])
        root = jnp.sqrt(jnp.maximum(norms[:, 1:2], 1.0))
        moved_total = jnp.zeros((groups, 1), f32)
        own = jnp.zeros((groups, day_cols), f32)
        for day in range(half):
            total = time_grad_of(grads, unit_devices, half, day)
            moved = lam[:, day * day_cols : (day + 1) * day_cols] * jnp.exp(total * (-step_rate / root))
            moved_total += jnp.sum(moved, axis=1, keepdims=True)
            own = jnp.where(me == day, moved, own)
        time_weights[...] = own * (ends[:, 0:1] / moved_total)

    @pl.when(me >= half)
    def _():
        time_weights[...] = jnp.zeros_like(time_weights)


def sixth_kernel(half, sent_totals, sent_scaled, _, unit_weights, block, out_sem):
    @pl.when(lax.axis_index("day") >= half)
    def _():
        block[...] = sent_scaled[...] * (1.0 / sent_totals[:, 0:1])
        wait_all(fetch([block], [unit_weights], out_sem))


def local(outcomes, cohort, pre_end, post_start, unit_logit, time_logit):
    groups = pre_end.shape[0]
    unit_rows, day_cols = outcomes.shape
    day_devices = lax.axis_size("day")
    unit_devices = lax.axis_size("unit")
    half = day_devices // 2
    assert half * 2 == day_devices and half & (half - 1) == 0
    assert unit_devices & (unit_devices - 1) == 0
    panel_starts = [0, unit_rows // 4, unit_rows // 8 * 5, unit_rows]
    resident = unit_rows * 3 // 4 // block_rows * block_rows
    middle = unit_devices // 2 - 1
    unit_order = [middle] + [unit for unit in reversed(range(unit_devices)) if unit != middle]

    def to_other_half(value):
        pairs = [(u * day_devices + d, u * day_devices + d + half) for u in range(unit_devices) for d in range(half)]
        return lax.ppermute(value, ("unit", "day"), pairs)

    def over_days(value):
        halves = [list(range(half)), list(range(half, day_devices))]
        return lax.all_gather(value, "day", axis_index_groups=halves)

    def over_first_half(value):
        members = [
            [unit * day_devices + day for unit in unit_order for day in reversed(days)]
            for days in (range(half), range(half, day_devices))
        ]
        return lax.all_to_all(
            value, ("unit", "day"), split_axis=0, concat_axis=0, axis_index_groups=members, tiled=True
        )

    def over_units(value):
        return lax.all_to_all(value, "unit", split_axis=0, concat_axis=0, axis_index_groups=[unit_order], tiled=True)

    def call(kernel, shapes, name, args, in_specs=None, out_specs=None, **more):
        return pl.pallas_call(
            kernel,
            in_specs=in_specs or [vmem] * len(args),
            out_specs=out_specs or [vmem] * len(shapes),
            out_shape=[
                shape if isinstance(shape, type(in_hbm)) else jax.ShapeDtypeStruct(*shape) for shape in shapes
            ],
            compiler_params=params,
            name=name,
            **more,
        )(*args)

    arguments = (outcomes, cohort[None, :], pre_end[None, :], post_start[None, :], unit_logit, time_logit)
    fixed = [pltpu.with_memory_space_constraint(argument, pltpu.HBM) for argument in arguments]
    held = [pltpu.VMEM(argument.shape, argument.dtype) for argument in arguments]
    small_sems, panel_sems = pltpu.SemaphoreType.DMA((5,)), pltpu.SemaphoreType.DMA((3,))
    panel_terms = [((resident, day_cols), bf16)] * 2
    other_terms = [((unit_rows - resident, day_cols), bf16)] * 2
    out_sems = pltpu.SemaphoreType.DMA((unit_devices,))
    width = 2 * groups * day_cols + lanes
    in_hbm = pltpu.HBM((unit_devices, 1, width), f32)
    sums, cross, raised_days, time_norm, ends, high, low = call(
        functools.partial(first_kernel, day_devices * day_cols, half, panel_starts),
        [
            in_hbm,
            pltpu.HBM((groups, unit_rows), f32),
            ((groups, day_cols), f32),
            ((groups, lanes), f32),
            ((groups, lanes), f32),
            *panel_terms,
        ],
        "first_product",
        fixed,
        in_specs=[hbm] * 6,
        out_specs=[hbm, hbm] + [vmem] * 5,
        scratch_shapes=held
        + [
            pltpu.VMEM((1, width), f32),
            pltpu.VMEM((4 * groups, unit_rows), bf16),
            pltpu.VMEM((groups, unit_rows), f32),
            small_sems,
            panel_sems,
            out_sems,
        ],
    )
    downward = [
        (u * day_devices + d + half, u * day_devices + d) for u in range(unit_devices) for d in range(half)
    ]
    post = lax.ppermute(cross, ("unit", "day"), downward)
    pack, norms, raised_units, more_high, more_low = call(
        functools.partial(second_kernel, half, unit_devices),
        [
            ((2 * groups, unit_rows + day_cols), f32),
            ((groups, lanes), f32),
            ((groups, unit_rows), f32),
            *other_terms,
        ],
        "unit_gradient",
        (fixed[0], fixed[1], fixed[4], over_units(sums), raised_days, ends, high, low),
        in_specs=[hbm] * 3 + [vmem] * 5,
        scratch_shapes=[
            pltpu.VMEM((unit_rows - resident, day_cols), f32),
            held[1],
            held[4],
            pltpu.SemaphoreType.DMA((3,)),
        ],
    )
    time_norms = [time_norm]
    for k in range(1, half):
        pairs = [(u * day_devices + d, u * day_devices + (d ^ k)) for u in range(unit_devices) for d in range(half)]
        time_norms.append(lax.ppermute(time_norm, ("unit", "day"), pairs))
    (pack,) = call(
        functools.partial(join_kernel, half),
        [((2 * groups, unit_rows + day_cols), f32)],
        "join_post",
        (pack, post, *time_norms),
    )
    members = unit_devices * half
    scaled, lam, grads = call(
        functools.partial(third_kernel, half),
        [
            ((groups, unit_rows), f32),
            ((groups, half * day_cols), f32),
            pltpu.HBM((members, groups, day_cols), f32),
        ],
        "time_gradient",
        (over_days(pack), high, low, more_high, more_low, norms, raised_units, ends),
        out_specs=[vmem, vmem, hbm],
        scratch_shapes=[pltpu.VMEM((groups, day_cols), f32), pltpu.SemaphoreType.DMA((members,))],
    )
    sent_scaled = to_other_half(scaled)
    all_grads = over_first_half(grads)
    (totals,) = call(
        functools.partial(fourth_kernel, half, unit_devices), [((groups, lanes), f32)], "unit_totals", (all_grads,)
    )
    unit_weights, time_weights = call(
        functools.partial(fifth_kernel, half, unit_devices),
        [((groups, unit_rows), f32), ((groups, day_cols), f32)],
        "scale_weights",
        (totals, scaled, all_grads, lam, norms, ends),
    )
    (unit_weights,) = call(
        functools.partial(sixth_kernel, half),
        [((groups, unit_rows), f32)],
        "other_half",
        (to_other_half(totals), sent_scaled, unit_weights),
        in_specs=[vmem, vmem, hbm],
        out_specs=[hbm],
        input_output_aliases={2: 0},
        scratch_shapes=[pltpu.VMEM((groups, unit_rows), f32), pltpu.SemaphoreType.DMA((1,))],
    )
    return unit_weights, time_weights


def solution(mesh):
    return jax.shard_map(
        local,
        mesh=mesh,
        in_specs=(P("unit", "day"), P("unit"), P(), P(), P(None, "unit"), P(None, "day")),
        out_specs=(P(None, "unit"), P(None, "day")),
        check_vma=False,
    )
```

```python
import functools

import jax
import jax.numpy as jnp
from jax import lax
from jax.experimental import pallas as pl
from jax.experimental.pallas import tpu as pltpu
from jax.sharding import PartitionSpec as P

step_rate = 16.0
f32 = jnp.float32
bf16 = jnp.bfloat16
lanes = 128
block_rows = 512
params = pltpu.CompilerParams(vmem_limit_bytes=24 * 1024 * 1024)
vmem = pl.BlockSpec(memory_space=pltpu.VMEM)
hbm = pl.BlockSpec(memory_space=pltpu.HBM)


def split_left(value):
    first = value.astype(bf16).astype(f32)
    return [first, value - first]


def left_of(*values):
    return jnp.concatenate([term for value in values for term in split_left(value)], axis=0).astype(bf16)


def split_panel(value):
    high = value.astype(bf16)
    return high, (value - high.astype(f32)).astype(bf16)


def rows_dot(left, high, low):
    return jnp.dot(left, high, preferred_element_type=f32) + jnp.dot(left, low, preferred_element_type=f32)


def days_dot(left, high, low):
    dims = (((1,), (1,)), ((), ()))
    return lax.dot_general(left, high, dims, preferred_element_type=f32) + lax.dot_general(
        left, low, dims, preferred_element_type=f32
    )


def add_terms(stack, groups, place=0):
    return stack[2 * place * groups :][:groups] + stack[(2 * place + 1) * groups :][:groups]


def tree_sum(values):
    values = list(values)
    while len(values) > 1:
        values = [values[i] + values[i + 1] for i in range(0, len(values), 2)]
    return values[0]


def column(row_ref):
    count = row_ref.shape[1]
    wide = jnp.broadcast_to(row_ref[...].astype(f32), (count, count))
    row = lax.broadcasted_iota(jnp.int32, (count, count), 0)
    lane = lax.broadcasted_iota(jnp.int32, (count, count), 1)
    return jnp.sum(jnp.where(row == lane, wide, 0.0), axis=1, keepdims=True).astype(jnp.int32)


def days_of(device, shape):
    return device * shape[1] + lax.broadcasted_iota(jnp.int32, shape, 1)


def first_half_only(kernel):
    @functools.wraps(kernel)
    def guarded(half, *refs):
        @pl.when(lax.axis_index("day") < half)
        def _():
            kernel(half, *refs)

    return guarded


def fetch(sources, targets, sems):
    copies = [pltpu.make_async_copy(*pair, sems.at[i]) for i, pair in enumerate(zip(sources, targets))]
    for copy in copies:
        copy.start()
    return copies


def fetch_rows(source, target, sems, starts):
    spans = [(start, stop - start) for start, stop in zip(starts, starts[1:])]
    parts = [pl.ds(*span) for span in spans]
    copies = fetch([source.at[here] for here in parts], [target.at[here] for here in parts], sems)
    return [(*span, copy) for span, copy in zip(spans, copies)]


def block_at(index):
    return pl.ds(pl.multiple_of(index * block_rows, block_rows), block_rows)


def blocks_of(start, rows):
    return [pl.ds(here, block_rows) for here in range(start, start + rows, block_rows)]


def wait_all(copies):
    for copy in copies:
        copy.wait()


def repeat_start(block, out, sems):
    places = [out.at[i] for i in range(out.shape[0])]
    return fetch([block] * len(places), places, sems)


def first_kernel(all_count, half, starts, *refs):
    arguments, refs = refs[:6], refs[6:]
    out, cross, raised_days, time_norm, ends, high_ref, low_ref, *held, block, left_ref, cross_block, small_sems, panel_sems, out_sems = refs
    groups, day_cols = held[5].shape
    unit_rows, resident = held[0].shape[0], high_ref.shape[0]
    (post_copy,) = fetch(arguments[3:4], held[3:4], small_sems)
    unit_copies = fetch(arguments[1:5:3], held[1:5:3], small_sems.at[pl.ds(1, 2)])
    parts = fetch_rows(arguments[0], held[0], panel_sems, starts)
    day_copies = fetch(arguments[2:6:3], held[2:6:3], small_sems.at[pl.ds(3, 2)])
    panel, cohort, pre_row, post_row, unit_logit, time_logit = held
    post_copy.wait()
    wait_all(unit_copies)
    me = lax.axis_index("day")

    @pl.when(me < half)
    def _():
        label = lax.broadcasted_iota(jnp.int32, (groups, unit_rows), 0)
        treated = jnp.where(cohort[...] == label, 1.0, 0.0)
        control = jnp.where(cohort[...] > label, 1.0, 0.0)
        raised = jnp.exp(unit_logit[...]) * control
        left_ref[...] = left_of(raised, treated)
        lane = lax.broadcasted_iota(jnp.int32, (groups, lanes), 1)
        counts = [jnp.sum(value, axis=1, keepdims=True) for value in (raised, treated, control)]
        slot = lax.broadcasted_iota(jnp.int32, (groups, lanes), 0)
        norms = jnp.zeros((groups, lanes), f32)
        for i, count in enumerate(counts):
            norms += jnp.where(lane == i * groups + slot, count, 0.0)
        block[:, 2 * groups * day_cols :] = jnp.sum(norms, axis=0, keepdims=True)
        product = jnp.zeros((4 * groups, 2 * day_cols), f32)
        for start, rows, copy in parts:
            copy.wait()
            for here in blocks_of(start, rows):
                high, low = split_panel(panel[here, :])
                if here.start < resident:
                    high_ref[here, :] = high
                    low_ref[here, :] = low
                both = jnp.concatenate([high, low], axis=1)
                product += jnp.dot(left_ref[:, here], both, preferred_element_type=f32)
        product = product[:, :day_cols] + product[:, day_cols:]
        both_sums = jnp.concatenate([add_terms(product, groups), product[2 * groups :][:groups]], axis=0)
        for row in range(2 * groups):
            block[:, row * day_cols : (row + 1) * day_cols] = both_sums[row : row + 1, :]
        sends = repeat_start(block, out, out_sems)
        wait_all(day_copies)
        pre_end = column(pre_row)
        ends[...] = jnp.broadcast_to(pre_end.astype(f32), ends.shape)
        before = days_of(me, (groups, day_cols)) < pre_end
        raised_time = jnp.where(before, jnp.exp(time_logit[...]), 0.0)
        raised_days[...] = raised_time
        time_norm[...] = jnp.broadcast_to(jnp.sum(raised_time, axis=1, keepdims=True), time_norm.shape)
        wait_all(sends)

    @pl.when(me >= half)
    def _():
        post_start = column(post_row)
        after = jnp.where(days_of(me, (groups, day_cols)) >= post_start, 1.0, 0.0)
        left = left_of(after / (all_count - post_start).astype(f32))
        for start, rows, copy in parts:
            copy.wait()
            for here in blocks_of(start, rows):
                cross_block[:, here] = add_terms(days_dot(left, *split_panel(panel[here, :])), groups)
        sends = fetch([cross_block], [cross], out_sems)
        wait_all(day_copies)
        wait_all(sends)


@first_half_only
def second_kernel(half, unit_devices, panel, cohort, unit_logit, sums, raised_days, ends, high_ref, low_ref, *refs):
    pack, norms, raised_units, more_high, more_low, held, held_cohort, held_logit, sems = refs
    groups, day_cols = raised_days.shape
    unit_rows, resident = panel.shape[0], high_ref.shape[0]
    rest = pl.ds(resident, unit_rows - resident)
    copies = fetch([panel.at[rest], cohort, unit_logit], [held, held_cohort, held_logit], sems)
    total = tree_sum(sums[u] for u in range(unit_devices))

    def group_rows(first):
        starts = [(first + row) * day_cols for row in range(groups)]
        return jnp.concatenate([total[:, start : start + day_cols] for start in starts], axis=0)

    counts = jnp.broadcast_to(total[:, 2 * groups * day_cols :], (groups, lanes))
    slot = lax.broadcasted_iota(jnp.int32, (groups, lanes), 0)
    lane = lax.broadcasted_iota(jnp.int32, (groups, lanes), 1)
    unit_norm, treat_count, ctrl_count = [
        jnp.sum(jnp.where(lane == i * groups + slot, counts, 0.0), axis=1, keepdims=True) for i in range(3)
    ]
    norms[...] = jnp.where(lane == 0, unit_norm, ctrl_count)
    gap = group_rows(0) / unit_norm - group_rows(groups) / jnp.maximum(treat_count, 1.0)
    before = days_of(lax.axis_index("day"), (groups, day_cols)).astype(f32) < ends[:, 0:1]
    raised_time = raised_days[...]
    pack[:groups, unit_rows:] = raised_time
    pack[groups:, unit_rows:] = jnp.zeros_like(raised_time)
    left = left_of(jnp.where(before, gap, 0.0), raised_time)

    def multiply(here, high, low):
        product = days_dot(left, high, low)
        pack[:groups, here] = add_terms(product, groups)
        pack[groups:, here] = add_terms(product, groups, 1)

    @pl.loop(0, resident // block_rows)
    def _(block):
        here = block_at(block)
        multiply(here, high_ref[here, :], low_ref[here, :])

    wait_all(copies)
    label = lax.broadcasted_iota(jnp.int32, raised_units.shape, 0)
    raised_units[...] = jnp.where(held_cohort[...] > label, jnp.exp(held_logit[...]), 0.0)

    @pl.loop(0, (unit_rows - resident) // block_rows)
    def _(block):
        there = block_at(block)
        high, low = split_panel(held[there, :])
        more_high[there, :] = high
        more_low[there, :] = low
        multiply(block_at(block + resident // block_rows), high, low)


@first_half_only
def join_kernel(half, pack, post, *refs):
    norms, out = refs[:half], refs[half]
    groups, unit_rows = post.shape
    over_time = 1.0 / tree_sum(ref[:, 0:1] for ref in norms)
    out[:groups, :unit_rows] = pack[:groups, :unit_rows]
    out[:groups, unit_rows:] = pack[:groups, unit_rows:] * over_time
    out[groups:, :unit_rows] = pack[groups:, :unit_rows] * over_time - post[...]
    out[groups:, unit_rows:] = pack[groups:, unit_rows:]


@first_half_only
def third_kernel(half, *refs):
    parts, refs = [refs[0].at[day] for day in range(half)], refs[1:]
    high_ref, low_ref, more_high, more_low, norms, raised_units, ends, scaled, lam, out, block, out_sems = refs
    groups, unit_rows = raised_units.shape
    resident, day_cols = high_ref.shape
    unit_norm, ctrl_count = norms[:, 0:1], norms[:, 1:2]
    factor = -step_rate / jnp.sqrt(ends[:, 0:1])
    over_unit = 1.0 / unit_norm
    me = lax.rem(lax.axis_index("day"), half)
    for day in range(half):
        lam[:, day * day_cols : (day + 1) * day_cols] = parts[day][:groups, unit_rows:]

    def add_block(here, high, low, sums):
        time_grad, new_sum = sums
        whole = tree_sum(ref[:, here] for ref in parts)
        raised = raised_units[:, here]
        new = raised * over_unit * jnp.exp(whole[:groups] * factor)
        scaled[:, here] = new * ctrl_count
        left = left_of(jnp.where(raised > 0.0, whole[groups:], 0.0))
        return time_grad + add_terms(rows_dot(left, high, low), groups), new_sum + new

    def add_resident(block, sums):
        here = block_at(block)
        return add_block(here, high_ref[here, :], low_ref[here, :], sums)

    def add_other(block, sums):
        there = block_at(block)
        return add_block(block_at(block + resident // block_rows), more_high[there, :], more_low[there, :], sums)

    sums = jnp.zeros((groups, day_cols), f32), jnp.zeros((groups, block_rows), f32)
    sums = lax.fori_loop(0, resident // block_rows, add_resident, sums)
    time_grad, new_sum = lax.fori_loop(0, (unit_rows - resident) // block_rows, add_other, sums)
    new_sum = jnp.sum(new_sum, axis=1, keepdims=True)
    lane = lax.broadcasted_iota(jnp.int32, (groups, day_cols), 1)
    spare = (lane == day_cols - 1) & (me == half - 1)
    block[...] = jnp.where(spare, new_sum, time_grad)
    wait_all(repeat_start(block, out, out_sems))


def time_grad_of(grads, unit_devices, half, day):
    return tree_sum(grads[unit * half + half - 1 - day] for unit in range(unit_devices))


@first_half_only
def fourth_kernel(half, unit_devices, grads, totals):
    day_cols = grads.shape[2]
    last = time_grad_of(grads, unit_devices, half, half - 1)
    totals[...] = jnp.broadcast_to(last[:, day_cols - 1 :], totals.shape)


def fifth_kernel(half, unit_devices, totals, scaled, grads, lam, norms, ends, unit_weights, time_weights):
    groups, day_cols = time_weights.shape
    me = lax.axis_index("day")

    @pl.when(me < half)
    def _():
        unit_weights[...] = scaled[...] * (1.0 / totals[:, 0:1])
        root = jnp.sqrt(jnp.maximum(norms[:, 1:2], 1.0))
        moved_total = jnp.zeros((groups, 1), f32)
        own = jnp.zeros((groups, day_cols), f32)
        for day in range(half):
            total = time_grad_of(grads, unit_devices, half, day)
            moved = lam[:, day * day_cols : (day + 1) * day_cols] * jnp.exp(total * (-step_rate / root))
            moved_total += jnp.sum(moved, axis=1, keepdims=True)
            own = jnp.where(me == day, moved, own)
        time_weights[...] = own * (ends[:, 0:1] / moved_total)

    @pl.when(me >= half)
    def _():
        time_weights[...] = jnp.zeros_like(time_weights)


def sixth_kernel(half, sent_totals, sent_scaled, _, unit_weights, block, out_sem):
    @pl.when(lax.axis_index("day") >= half)
    def _():
        block[...] = sent_scaled[...] * (1.0 / sent_totals[:, 0:1])
        wait_all(fetch([block], [unit_weights], out_sem))


def local(outcomes, cohort, pre_end, post_start, unit_logit, time_logit):
    groups = pre_end.shape[0]
    unit_rows, day_cols = outcomes.shape
    day_devices = lax.axis_size("day")
    unit_devices = lax.axis_size("unit")
    half = day_devices // 2
    assert half * 2 == day_devices and half & (half - 1) == 0
    assert unit_devices & (unit_devices - 1) == 0
    panel_starts = [0, unit_rows // 4, unit_rows // 8 * 5, unit_rows]
    resident = unit_rows * 3 // 4 // block_rows * block_rows
    middle = unit_devices // 2 - 1
    unit_order = [middle] + [unit for unit in reversed(range(unit_devices)) if unit != middle]

    def to_other_half(value):
        pairs = [(u * day_devices + d, u * day_devices + d + half) for u in range(unit_devices) for d in range(half)]
        return lax.ppermute(value, ("unit", "day"), pairs)

    def over_days(value):
        halves = [list(range(half)), list(range(half, day_devices))]
        return lax.all_gather(value, "day", axis_index_groups=halves)

    def over_first_half(value):
        members = [
            [unit * day_devices + day for unit in unit_order for day in reversed(days)]
            for days in (range(half), range(half, day_devices))
        ]
        return lax.all_to_all(
            value, ("unit", "day"), split_axis=0, concat_axis=0, axis_index_groups=members, tiled=True
        )

    def over_units(value):
        return lax.all_to_all(value, "unit", split_axis=0, concat_axis=0, axis_index_groups=[unit_order], tiled=True)

    def call(kernel, shapes, name, args, in_specs=None, out_specs=None, **more):
        return pl.pallas_call(
            kernel,
            in_specs=in_specs or [vmem] * len(args),
            out_specs=out_specs or [vmem] * len(shapes),
            out_shape=[
                shape if isinstance(shape, type(in_hbm)) else jax.ShapeDtypeStruct(*shape) for shape in shapes
            ],
            compiler_params=params,
            name=name,
            **more,
        )(*args)

    arguments = (outcomes, cohort[None, :], pre_end[None, :], post_start[None, :], unit_logit, time_logit)
    fixed = [pltpu.with_memory_space_constraint(argument, pltpu.HBM) for argument in arguments]
    held = [pltpu.VMEM(argument.shape, argument.dtype) for argument in arguments]
    small_sems, panel_sems = pltpu.SemaphoreType.DMA((5,)), pltpu.SemaphoreType.DMA((3,))
    panel_terms = [((resident, day_cols), bf16)] * 2
    other_terms = [((unit_rows - resident, day_cols), bf16)] * 2
    out_sems = pltpu.SemaphoreType.DMA((unit_devices,))
    width = 2 * groups * day_cols + lanes
    in_hbm = pltpu.HBM((unit_devices, 1, width), f32)
    sums, cross, raised_days, time_norm, ends, high, low = call(
        functools.partial(first_kernel, day_devices * day_cols, half, panel_starts),
        [
            in_hbm,
            pltpu.HBM((groups, unit_rows), f32),
            ((groups, day_cols), f32),
            ((groups, lanes), f32),
            ((groups, lanes), f32),
            *panel_terms,
        ],
        "first_product",
        fixed,
        in_specs=[hbm] * 6,
        out_specs=[hbm, hbm] + [vmem] * 5,
        scratch_shapes=held
        + [
            pltpu.VMEM((1, width), f32),
            pltpu.VMEM((4 * groups, unit_rows), bf16),
            pltpu.VMEM((groups, unit_rows), f32),
            small_sems,
            panel_sems,
            out_sems,
        ],
    )
    downward = [
        (u * day_devices + d + half, u * day_devices + d) for u in range(unit_devices) for d in range(half)
    ]
    post = lax.ppermute(cross, ("unit", "day"), downward)
    pack, norms, raised_units, more_high, more_low = call(
        functools.partial(second_kernel, half, unit_devices),
        [
            ((2 * groups, unit_rows + day_cols), f32),
            ((groups, lanes), f32),
            ((groups, unit_rows), f32),
            *other_terms,
        ],
        "unit_gradient",
        (fixed[0], fixed[1], fixed[4], over_units(sums), raised_days, ends, high, low),
        in_specs=[hbm] * 3 + [vmem] * 5,
        scratch_shapes=[
            pltpu.VMEM((unit_rows - resident, day_cols), f32),
            held[1],
            held[4],
            pltpu.SemaphoreType.DMA((3,)),
        ],
    )
    time_norms = [time_norm]
    for k in range(1, half):
        pairs = [(u * day_devices + d, u * day_devices + (d ^ k)) for u in range(unit_devices) for d in range(half)]
        time_norms.append(lax.ppermute(time_norm, ("unit", "day"), pairs))
    (pack,) = call(
        functools.partial(join_kernel, half),
        [((2 * groups, unit_rows + day_cols), f32)],
        "join_post",
        (pack, post, *time_norms),
    )
    members = unit_devices * half
    scaled, lam, grads = call(
        functools.partial(third_kernel, half),
        [
            ((groups, unit_rows), f32),
            ((groups, half * day_cols), f32),
            pltpu.HBM((members, groups, day_cols), f32),
        ],
        "time_gradient",
        (over_days(pack), high, low, more_high, more_low, norms, raised_units, ends),
        out_specs=[vmem, vmem, hbm],
        scratch_shapes=[pltpu.VMEM((groups, day_cols), f32), pltpu.SemaphoreType.DMA((members,))],
    )
    sent_scaled = to_other_half(scaled)
    all_grads = over_first_half(grads)
    (totals,) = call(
        functools.partial(fourth_kernel, half, unit_devices), [((groups, lanes), f32)], "unit_totals", (all_grads,)
    )
    unit_weights, time_weights = call(
        functools.partial(fifth_kernel, half, unit_devices),
        [((groups, unit_rows), f32), ((groups, day_cols), f32)],
        "scale_weights",
        (totals, scaled, all_grads, lam, norms, ends),
    )
    (unit_weights,) = call(
        functools.partial(sixth_kernel, half),
        [((groups, unit_rows), f32)],
        "other_half",
        (to_other_half(totals), sent_scaled, unit_weights),
        in_specs=[vmem, vmem, hbm],
        out_specs=[hbm],
        input_output_aliases={2: 0},
        scratch_shapes=[pltpu.VMEM((groups, unit_rows), f32), pltpu.SemaphoreType.DMA((1,))],
    )
    return unit_weights, time_weights


def solution(mesh):
    return jax.shard_map(
        local,
        mesh=mesh,
        in_specs=(P("unit", "day"), P("unit"), P(), P(), P(None, "unit"), P(None, "day")),
        out_specs=(P(None, "unit"), P(None, "day")),
        check_vma=False,
    )
```

```python
import functools

import jax
import jax.numpy as jnp
from jax import lax
from jax.experimental import pallas as pl
from jax.experimental.pallas import tpu as pltpu
from jax.sharding import PartitionSpec as P

step_rate = 16.0
f32 = jnp.float32
bf16 = jnp.bfloat16
lanes = 128
block_rows = 512
params = pltpu.CompilerParams(vmem_limit_bytes=24 * 1024 * 1024)
vmem = pl.BlockSpec(memory_space=pltpu.VMEM)
hbm = pl.BlockSpec(memory_space=pltpu.HBM)


def split_left(value):
    first = value.astype(bf16).astype(f32)
    return [first, value - first]


def left_of(*values):
    return jnp.concatenate([term for value in values for term in split_left(value)], axis=0).astype(bf16)


def split_panel(value):
    high = value.astype(bf16)
    return high, (value - high.astype(f32)).astype(bf16)


def rows_dot(left, high, low):
    return jnp.dot(left, high, preferred_element_type=f32) + jnp.dot(left, low, preferred_element_type=f32)


def days_dot(left, high, low):
    dims = (((1,), (1,)), ((), ()))
    return lax.dot_general(left, high, dims, preferred_element_type=f32) + lax.dot_general(
        left, low, dims, preferred_element_type=f32
    )


def add_terms(stack, groups, place=0):
    return stack[2 * place * groups :][:groups] + stack[(2 * place + 1) * groups :][:groups]


def tree_sum(values):
    values = list(values)
    while len(values) > 1:
        values = [values[i] + values[i + 1] for i in range(0, len(values), 2)]
    return values[0]


def column(row_ref):
    count = row_ref.shape[1]
    wide = jnp.broadcast_to(row_ref[...].astype(f32), (count, count))
    row = lax.broadcasted_iota(jnp.int32, (count, count), 0)
    lane = lax.broadcasted_iota(jnp.int32, (count, count), 1)
    return jnp.sum(jnp.where(row == lane, wide, 0.0), axis=1, keepdims=True).astype(jnp.int32)


def days_of(device, shape):
    return device * shape[1] + lax.broadcasted_iota(jnp.int32, shape, 1)


def first_half_only(kernel):
    @functools.wraps(kernel)
    def guarded(half, *refs):
        @pl.when(lax.axis_index("day") < half)
        def _():
            kernel(half, *refs)

    return guarded


def fetch(sources, targets, sems):
    copies = [pltpu.make_async_copy(*pair, sems.at[i]) for i, pair in enumerate(zip(sources, targets))]
    for copy in copies:
        copy.start()
    return copies


def fetch_rows(source, target, sems, starts):
    spans = [(start, stop - start) for start, stop in zip(starts, starts[1:])]
    parts = [pl.ds(*span) for span in spans]
    copies = fetch([source.at[here] for here in parts], [target.at[here] for here in parts], sems)
    return [(*span, copy) for span, copy in zip(spans, copies)]


def blocks_of(start, rows):
    return [pl.ds(here, block_rows) for here in range(start, start + rows, block_rows)]


def wait_all(copies):
    for copy in copies:
        copy.wait()


def repeat_start(block, out, sems):
    places = [out.at[i] for i in range(out.shape[0])]
    return fetch([block] * len(places), places, sems)


def first_kernel(all_count, half, starts, *refs):
    arguments, refs = refs[:6], refs[6:]
    out, cross, raised_days, time_norm, ends, high_ref, low_ref, *held, block, left_ref, cross_block, small_sems, panel_sems, out_sems = refs
    groups, day_cols = held[5].shape
    unit_rows, resident = held[0].shape[0], high_ref.shape[0]
    (post_copy,) = fetch(arguments[3:4], held[3:4], small_sems)
    unit_copies = fetch(arguments[1:5:3], held[1:5:3], small_sems.at[pl.ds(1, 2)])
    parts = fetch_rows(arguments[0], held[0], panel_sems, starts)
    day_copies = fetch(arguments[2:6:3], held[2:6:3], small_sems.at[pl.ds(3, 2)])
    panel, cohort, pre_row, post_row, unit_logit, time_logit = held
    post_copy.wait()
    wait_all(unit_copies)
    me = lax.axis_index("day")

    @pl.when(me < half)
    def _():
        label = lax.broadcasted_iota(jnp.int32, (groups, unit_rows), 0)
        treated = jnp.where(cohort[...] == label, 1.0, 0.0)
        control = jnp.where(cohort[...] > label, 1.0, 0.0)
        raised = jnp.exp(unit_logit[...]) * control
        left_ref[...] = left_of(raised, treated)
        lane = lax.broadcasted_iota(jnp.int32, (groups, lanes), 1)
        counts = [jnp.sum(value, axis=1, keepdims=True) for value in (raised, treated, control)]
        slot = lax.broadcasted_iota(jnp.int32, (groups, lanes), 0)
        norms = jnp.zeros((groups, lanes), f32)
        for i, count in enumerate(counts):
            norms += jnp.where(lane == i * groups + slot, count, 0.0)
        block[:, 2 * groups * day_cols :] = jnp.sum(norms, axis=0, keepdims=True)
        product = jnp.zeros((4 * groups, 2 * day_cols), f32)
        for start, rows, copy in parts:
            copy.wait()
            for here in blocks_of(start, rows):
                high, low = split_panel(panel[here, :])
                if here.start < resident:
                    high_ref[here, :] = high
                    low_ref[here, :] = low
                both = jnp.concatenate([high, low], axis=1)
                product += jnp.dot(left_ref[:, here], both, preferred_element_type=f32)
        product = product[:, :day_cols] + product[:, day_cols:]
        both_sums = jnp.concatenate([add_terms(product, groups), product[2 * groups :][:groups]], axis=0)
        for row in range(2 * groups):
            block[:, row * day_cols : (row + 1) * day_cols] = both_sums[row : row + 1, :]
        sends = repeat_start(block, out, out_sems)
        wait_all(day_copies)
        pre_end = column(pre_row)
        ends[...] = jnp.broadcast_to(pre_end.astype(f32), ends.shape)
        before = days_of(me, (groups, day_cols)) < pre_end
        raised_time = jnp.where(before, jnp.exp(time_logit[...]), 0.0)
        raised_days[...] = raised_time
        time_norm[...] = jnp.broadcast_to(jnp.sum(raised_time, axis=1, keepdims=True), time_norm.shape)
        wait_all(sends)

    @pl.when(me >= half)
    def _():
        post_start = column(post_row)
        after = jnp.where(days_of(me, (groups, day_cols)) >= post_start, 1.0, 0.0)
        left = left_of(after / (all_count - post_start).astype(f32))
        for start, rows, copy in parts:
            copy.wait()
            for here in blocks_of(start, rows):
                cross_block[:, here] = add_terms(days_dot(left, *split_panel(panel[here, :])), groups)
        sends = fetch([cross_block], [cross], out_sems)
        wait_all(day_copies)
        wait_all(sends)


@first_half_only
def second_kernel(half, unit_devices, panel, cohort, unit_logit, sums, raised_days, ends, high_ref, low_ref, *refs):
    pack, norms, raised_units, more_high, more_low, held, held_cohort, held_logit, sems = refs
    groups, day_cols = raised_days.shape
    unit_rows, resident = panel.shape[0], high_ref.shape[0]
    rest = pl.ds(resident, unit_rows - resident)
    copies = fetch([panel.at[rest], cohort, unit_logit], [held, held_cohort, held_logit], sems)

    @pl.when(lax.axis_index("day") < half)
    def _():
        total = tree_sum(sums[u] for u in range(unit_devices))

        def group_rows(first):
            starts = [(first + row) * day_cols for row in range(groups)]
            return jnp.concatenate([total[:, start : start + day_cols] for start in starts], axis=0)

        counts = jnp.broadcast_to(total[:, 2 * groups * day_cols :], (groups, lanes))
        slot = lax.broadcasted_iota(jnp.int32, (groups, lanes), 0)
        lane = lax.broadcasted_iota(jnp.int32, (groups, lanes), 1)
        unit_norm, treat_count, ctrl_count = [
            jnp.sum(jnp.where(lane == i * groups + slot, counts, 0.0), axis=1, keepdims=True) for i in range(3)
        ]
        norms[...] = jnp.where(lane == 0, unit_norm, ctrl_count)
        gap = group_rows(0) / unit_norm - group_rows(groups) / jnp.maximum(treat_count, 1.0)
        before = days_of(lax.axis_index("day"), (groups, day_cols)).astype(f32) < ends[:, 0:1]
        raised_time = raised_days[...]
        pack[:groups, unit_rows:] = raised_time
        pack[groups:, unit_rows:] = jnp.zeros_like(raised_time)
        left = left_of(jnp.where(before, gap, 0.0), raised_time)

        def multiply(here, high, low):
            product = days_dot(left, high, low)
            pack[:groups, here] = add_terms(product, groups)
            pack[groups:, here] = add_terms(product, groups, 1)

        for here in blocks_of(0, resident):
            multiply(here, high_ref[here, :], low_ref[here, :])
        wait_all(copies)
        label = lax.broadcasted_iota(jnp.int32, raised_units.shape, 0)
        raised_units[...] = jnp.where(held_cohort[...] > label, jnp.exp(held_logit[...]), 0.0)
        for here in blocks_of(resident, unit_rows - resident):
            there = pl.ds(here.start - resident, block_rows)
            high, low = split_panel(held[there, :])
            more_high[there, :] = high
            more_low[there, :] = low
            multiply(here, high, low)


@first_half_only
def join_kernel(half, pack, post, *refs):
    norms, out = refs[:half], refs[half]
    groups, unit_rows = post.shape
    over_time = 1.0 / tree_sum(ref[:, 0:1] for ref in norms)
    out[:groups, :unit_rows] = pack[:groups, :unit_rows]
    out[:groups, unit_rows:] = pack[:groups, unit_rows:] * over_time
    out[groups:, :unit_rows] = pack[groups:, :unit_rows] * over_time - post[...]
    out[groups:, unit_rows:] = pack[groups:, unit_rows:]


@first_half_only
def third_kernel(half, *refs):
    parts, refs = [refs[0].at[day] for day in range(half)], refs[1:]
    high_ref, low_ref, more_high, more_low, norms, raised_units, ends, scaled, lam, out, block, out_sems = refs
    groups, unit_rows = raised_units.shape
    resident, day_cols = high_ref.shape
    unit_norm, ctrl_count = norms[:, 0:1], norms[:, 1:2]
    factor = -step_rate / jnp.sqrt(ends[:, 0:1])
    over_unit = 1.0 / unit_norm
    me = lax.rem(lax.axis_index("day"), half)
    for day in range(half):
        lam[:, day * day_cols : (day + 1) * day_cols] = parts[day][:groups, unit_rows:]
    time_grad = jnp.zeros((groups, day_cols), f32)
    new_sum = jnp.zeros((groups, 1), f32)
    for start in range(0, unit_rows, block_rows):
        here = pl.ds(start, block_rows)
        whole = tree_sum(ref[:, here] for ref in parts)
        raised = raised_units[:, here]
        new = raised * over_unit * jnp.exp(whole[:groups] * factor)
        new_sum += jnp.sum(new, axis=1, keepdims=True)
        scaled[:, here] = new * ctrl_count
        left = left_of(jnp.where(raised > 0.0, whole[groups:], 0.0))
        if start < resident:
            high, low = high_ref[here, :], low_ref[here, :]
        else:
            there = pl.ds(start - resident, block_rows)
            high, low = more_high[there, :], more_low[there, :]
        time_grad += add_terms(rows_dot(left, high, low), groups)
    lane = lax.broadcasted_iota(jnp.int32, (groups, day_cols), 1)
    spare = (lane == day_cols - 1) & (me == half - 1)
    block[...] = jnp.where(spare, new_sum, time_grad)
    wait_all(repeat_start(block, out, out_sems))


def time_grad_of(grads, unit_devices, half, day):
    return tree_sum(grads[unit * half + half - 1 - day] for unit in range(unit_devices))


@first_half_only
def fourth_kernel(half, unit_devices, grads, totals):
    day_cols = grads.shape[2]
    last = time_grad_of(grads, unit_devices, half, half - 1)
    totals[...] = jnp.broadcast_to(last[:, day_cols - 1 :], totals.shape)


def fifth_kernel(half, unit_devices, totals, scaled, grads, lam, norms, ends, unit_weights, time_weights):
    groups, day_cols = time_weights.shape
    me = lax.axis_index("day")

    @pl.when(me < half)
    def _():
        unit_weights[...] = scaled[...] * (1.0 / totals[:, 0:1])
        root = jnp.sqrt(jnp.maximum(norms[:, 1:2], 1.0))
        moved_total = jnp.zeros((groups, 1), f32)
        own = jnp.zeros((groups, day_cols), f32)
        for day in range(half):
            total = time_grad_of(grads, unit_devices, half, day)
            moved = lam[:, day * day_cols : (day + 1) * day_cols] * jnp.exp(total * (-step_rate / root))
            moved_total += jnp.sum(moved, axis=1, keepdims=True)
            own = jnp.where(me == day, moved, own)
        time_weights[...] = own * (ends[:, 0:1] / moved_total)

    @pl.when(me >= half)
    def _():
        time_weights[...] = jnp.zeros_like(time_weights)


def sixth_kernel(half, sent_totals, sent_scaled, _, unit_weights, block, out_sem):
    @pl.when(lax.axis_index("day") >= half)
    def _():
        block[...] = sent_scaled[...] * (1.0 / sent_totals[:, 0:1])
        wait_all(fetch([block], [unit_weights], out_sem))


def local(outcomes, cohort, pre_end, post_start, unit_logit, time_logit):
    groups = pre_end.shape[0]
    unit_rows, day_cols = outcomes.shape
    day_devices = lax.axis_size("day")
    unit_devices = lax.axis_size("unit")
    half = day_devices // 2
    assert half * 2 == day_devices and half & (half - 1) == 0
    assert unit_devices & (unit_devices - 1) == 0
    panel_starts = [0, unit_rows // 4, unit_rows // 8 * 5, unit_rows]
    resident = unit_rows * 3 // 4 // block_rows * block_rows
    middle = unit_devices // 2 - 1
    unit_order = [middle] + [unit for unit in reversed(range(unit_devices)) if unit != middle]

    def to_other_half(value):
        pairs = [(u * day_devices + d, u * day_devices + d + half) for u in range(unit_devices) for d in range(half)]
        return lax.ppermute(value, ("unit", "day"), pairs)

    def over_days(value):
        halves = [list(range(half)), list(range(half, day_devices))]
        return lax.all_gather(value, "day", axis_index_groups=halves)

    def over_first_half(value):
        members = [
            [unit * day_devices + day for unit in unit_order for day in reversed(days)]
            for days in (range(half), range(half, day_devices))
        ]
        return lax.all_to_all(
            value, ("unit", "day"), split_axis=0, concat_axis=0, axis_index_groups=members, tiled=True
        )

    def over_units(value):
        return lax.all_to_all(value, "unit", split_axis=0, concat_axis=0, axis_index_groups=[unit_order], tiled=True)

    def call(kernel, shapes, name, args, in_specs=None, out_specs=None, **more):
        return pl.pallas_call(
            kernel,
            in_specs=in_specs or [vmem] * len(args),
            out_specs=out_specs or [vmem] * len(shapes),
            out_shape=[
                shape if isinstance(shape, type(in_hbm)) else jax.ShapeDtypeStruct(*shape) for shape in shapes
            ],
            compiler_params=params,
            name=name,
            **more,
        )(*args)

    arguments = (outcomes, cohort[None, :], pre_end[None, :], post_start[None, :], unit_logit, time_logit)
    fixed = [pltpu.with_memory_space_constraint(argument, pltpu.HBM) for argument in arguments]
    held = [pltpu.VMEM(argument.shape, argument.dtype) for argument in arguments]
    small_sems, panel_sems = pltpu.SemaphoreType.DMA((5,)), pltpu.SemaphoreType.DMA((3,))
    panel_terms = [((resident, day_cols), bf16)] * 2
    other_terms = [((unit_rows - resident, day_cols), bf16)] * 2
    out_sems = pltpu.SemaphoreType.DMA((unit_devices,))
    width = 2 * groups * day_cols + lanes
    in_hbm = pltpu.HBM((unit_devices, 1, width), f32)
    sums, cross, raised_days, time_norm, ends, high, low = call(
        functools.partial(first_kernel, day_devices * day_cols, half, panel_starts),
        [
            in_hbm,
            pltpu.HBM((groups, unit_rows), f32),
            ((groups, day_cols), f32),
            ((groups, lanes), f32),
            ((groups, lanes), f32),
            *panel_terms,
        ],
        "first_product",
        fixed,
        in_specs=[hbm] * 6,
        out_specs=[hbm, hbm] + [vmem] * 5,
        scratch_shapes=held
        + [
            pltpu.VMEM((1, width), f32),
            pltpu.VMEM((4 * groups, unit_rows), bf16),
            pltpu.VMEM((groups, unit_rows), f32),
            small_sems,
            panel_sems,
            out_sems,
        ],
    )
    downward = [
        (u * day_devices + d + half, u * day_devices + d) for u in range(unit_devices) for d in range(half)
    ]
    post = lax.ppermute(cross, ("unit", "day"), downward)
    pack, norms, raised_units, more_high, more_low = call(
        functools.partial(second_kernel, half, unit_devices),
        [
            ((2 * groups, unit_rows + day_cols), f32),
            ((groups, lanes), f32),
            ((groups, unit_rows), f32),
            *other_terms,
        ],
        "unit_gradient",
        (fixed[0], fixed[1], fixed[4], over_units(sums), raised_days, ends, high, low),
        in_specs=[hbm] * 3 + [vmem] * 5,
        scratch_shapes=[
            pltpu.VMEM((unit_rows - resident, day_cols), f32),
            held[1],
            held[4],
            pltpu.SemaphoreType.DMA((3,)),
        ],
    )
    time_norms = [time_norm]
    for k in range(1, half):
        pairs = [(u * day_devices + d, u * day_devices + (d ^ k)) for u in range(unit_devices) for d in range(half)]
        time_norms.append(lax.ppermute(time_norm, ("unit", "day"), pairs))
    (pack,) = call(
        functools.partial(join_kernel, half),
        [((2 * groups, unit_rows + day_cols), f32)],
        "join_post",
        (pack, post, *time_norms),
    )
    members = unit_devices * half
    scaled, lam, grads = call(
        functools.partial(third_kernel, half),
        [
            ((groups, unit_rows), f32),
            ((groups, half * day_cols), f32),
            pltpu.HBM((members, groups, day_cols), f32),
        ],
        "time_gradient",
        (over_days(pack), high, low, more_high, more_low, norms, raised_units, ends),
        out_specs=[vmem, vmem, hbm],
        scratch_shapes=[pltpu.VMEM((groups, day_cols), f32), pltpu.SemaphoreType.DMA((members,))],
    )
    sent_scaled = to_other_half(scaled)
    all_grads = over_first_half(grads)
    (totals,) = call(
        functools.partial(fourth_kernel, half, unit_devices), [((groups, lanes), f32)], "unit_totals", (all_grads,)
    )
    unit_weights, time_weights = call(
        functools.partial(fifth_kernel, half, unit_devices),
        [((groups, unit_rows), f32), ((groups, day_cols), f32)],
        "scale_weights",
        (totals, scaled, all_grads, lam, norms, ends),
    )
    (unit_weights,) = call(
        functools.partial(sixth_kernel, half),
        [((groups, unit_rows), f32)],
        "other_half",
        (to_other_half(totals), sent_scaled, unit_weights),
        in_specs=[vmem, vmem, hbm],
        out_specs=[hbm],
        input_output_aliases={2: 0},
        scratch_shapes=[pltpu.VMEM((groups, unit_rows), f32), pltpu.SemaphoreType.DMA((1,))],
    )
    return unit_weights, time_weights


def solution(mesh):
    return jax.shard_map(
        local,
        mesh=mesh,
        in_specs=(P("unit", "day"), P("unit"), P(), P(), P(None, "unit"), P(None, "day")),
        out_specs=(P(None, "unit"), P(None, "day")),
        check_vma=False,
    )
```

```python
import functools

import jax
import jax.numpy as jnp
from jax import lax
from jax.experimental import pallas as pl
from jax.experimental.pallas import tpu as pltpu
from jax.sharding import PartitionSpec as P

step_rate = 16.0
f32 = jnp.float32
bf16 = jnp.bfloat16
lanes = 128
block_rows = 512
params = pltpu.CompilerParams(vmem_limit_bytes=24 * 1024 * 1024)
vmem = pl.BlockSpec(memory_space=pltpu.VMEM)
hbm = pl.BlockSpec(memory_space=pltpu.HBM)


def split_left(value):
    first = value.astype(bf16).astype(f32)
    return [first, value - first]


def left_of(*values):
    return jnp.concatenate([term for value in values for term in split_left(value)], axis=0).astype(bf16)


def split_panel(value):
    high = value.astype(bf16)
    return high, (value - high.astype(f32)).astype(bf16)


def rows_dot(left, high, low):
    return jnp.dot(left, high, preferred_element_type=f32) + jnp.dot(left, low, preferred_element_type=f32)


def days_dot(left, high, low):
    dims = (((1,), (1,)), ((), ()))
    return lax.dot_general(left, high, dims, preferred_element_type=f32) + lax.dot_general(
        left, low, dims, preferred_element_type=f32
    )


def add_terms(stack, groups, place=0):
    return stack[2 * place * groups :][:groups] + stack[(2 * place + 1) * groups :][:groups]


def tree_sum(values):
    values = list(values)
    while len(values) > 1:
        values = [values[i] + values[i + 1] for i in range(0, len(values), 2)]
    return values[0]


def column(row_ref):
    count = row_ref.shape[1]
    wide = jnp.broadcast_to(row_ref[...].astype(f32), (count, count))
    row = lax.broadcasted_iota(jnp.int32, (count, count), 0)
    lane = lax.broadcasted_iota(jnp.int32, (count, count), 1)
    return jnp.sum(jnp.where(row == lane, wide, 0.0), axis=1, keepdims=True).astype(jnp.int32)


def days_of(device, shape):
    return device * shape[1] + lax.broadcasted_iota(jnp.int32, shape, 1)


def first_half_only(kernel):
    @functools.wraps(kernel)
    def guarded(half, *refs):
        @pl.when(lax.axis_index("day") < half)
        def _():
            kernel(half, *refs)

    return guarded


def fetch(sources, targets, sems):
    copies = [pltpu.make_async_copy(*pair, sems.at[i]) for i, pair in enumerate(zip(sources, targets))]
    for copy in copies:
        copy.start()
    return copies


def fetch_rows(source, target, sems, starts):
    spans = [(start, stop - start) for start, stop in zip(starts, starts[1:])]
    parts = [pl.ds(*span) for span in spans]
    copies = fetch([source.at[here] for here in parts], [target.at[here] for here in parts], sems)
    return [(*span, copy) for span, copy in zip(spans, copies)]


def blocks_of(start, rows):
    return [pl.ds(here, block_rows) for here in range(start, start + rows, block_rows)]


def wait_all(copies):
    for copy in copies:
        copy.wait()


def repeat_start(block, out, sems):
    places = [out.at[i] for i in range(out.shape[0])]
    return fetch([block] * len(places), places, sems)


def first_kernel(all_count, half, starts, *refs):
    arguments, refs = refs[:6], refs[6:]
    out, cross, raised_days, time_norm, ends, high_ref, low_ref, *held, block, left_ref, cross_block, small_sems, panel_sems, out_sems = refs
    groups, day_cols = held[5].shape
    unit_rows, resident = held[0].shape[0], high_ref.shape[0]
    (post_copy,) = fetch(arguments[3:4], held[3:4], small_sems)
    unit_copies = fetch(arguments[1:5:3], held[1:5:3], small_sems.at[pl.ds(1, 2)])
    parts = fetch_rows(arguments[0], held[0], panel_sems, starts)
    day_copies = fetch(arguments[2:6:3], held[2:6:3], small_sems.at[pl.ds(3, 2)])
    panel, cohort, pre_row, post_row, unit_logit, time_logit = held
    post_copy.wait()
    wait_all(unit_copies)
    me = lax.axis_index("day")

    @pl.when(me < half)
    def _():
        label = lax.broadcasted_iota(jnp.int32, (groups, unit_rows), 0)
        treated = jnp.where(cohort[...] == label, 1.0, 0.0)
        control = jnp.where(cohort[...] > label, 1.0, 0.0)
        raised = jnp.exp(unit_logit[...]) * control
        left_ref[...] = left_of(raised, treated)
        lane = lax.broadcasted_iota(jnp.int32, (groups, lanes), 1)
        counts = [jnp.sum(value, axis=1, keepdims=True) for value in (raised, treated, control)]
        slot = lax.broadcasted_iota(jnp.int32, (groups, lanes), 0)
        norms = jnp.zeros((groups, lanes), f32)
        for i, count in enumerate(counts):
            norms += jnp.where(lane == i * groups + slot, count, 0.0)
        block[:, 2 * groups * day_cols :] = jnp.sum(norms, axis=0, keepdims=True)
        product = jnp.zeros((4 * groups, 2 * day_cols), f32)
        for start, rows, copy in parts:
            copy.wait()
            for here in blocks_of(start, rows):
                high, low = split_panel(panel[here, :])
                if here.start < resident:
                    high_ref[here, :] = high
                    low_ref[here, :] = low
                both = jnp.concatenate([high, low], axis=1)
                product += jnp.dot(left_ref[:, here], both, preferred_element_type=f32)
        product = product[:, :day_cols] + product[:, day_cols:]
        both_sums = jnp.concatenate([add_terms(product, groups), product[2 * groups :][:groups]], axis=0)
        for row in range(2 * groups):
            block[:, row * day_cols : (row + 1) * day_cols] = both_sums[row : row + 1, :]
        sends = repeat_start(block, out, out_sems)
        wait_all(day_copies)
        pre_end = column(pre_row)
        ends[...] = jnp.broadcast_to(pre_end.astype(f32), ends.shape)
        before = days_of(me, (groups, day_cols)) < pre_end
        raised_time = jnp.where(before, jnp.exp(time_logit[...]), 0.0)
        raised_days[...] = raised_time
        time_norm[...] = jnp.broadcast_to(jnp.sum(raised_time, axis=1, keepdims=True), time_norm.shape)
        wait_all(sends)

    @pl.when(me >= half)
    def _():
        post_start = column(post_row)
        after = jnp.where(days_of(me, (groups, day_cols)) >= post_start, 1.0, 0.0)
        left = left_of(after / (all_count - post_start).astype(f32))
        for start, rows, copy in parts:
            copy.wait()
            for here in blocks_of(start, rows):
                cross_block[:, here] = add_terms(days_dot(left, *split_panel(panel[here, :])), groups)
        sends = fetch([cross_block], [cross], out_sems)
        wait_all(day_copies)
        wait_all(sends)


@first_half_only
def second_kernel(half, unit_devices, panel, cohort, unit_logit, sums, raised_days, ends, high_ref, low_ref, *refs):
    pack, norms, raised_units, more_high, more_low, held, held_cohort, held_logit, sems = refs
    groups, day_cols = raised_days.shape
    unit_rows, resident = panel.shape[0], high_ref.shape[0]
    rest = pl.ds(resident, unit_rows - resident)
    copies = fetch([panel.at[rest], cohort, unit_logit], [held, held_cohort, held_logit], sems)

    @pl.when(lax.axis_index("day") < half)
    def _():
        total = tree_sum(sums[u] for u in range(unit_devices))

        def group_rows(first):
            starts = [(first + row) * day_cols for row in range(groups)]
            return jnp.concatenate([total[:, start : start + day_cols] for start in starts], axis=0)

        counts = jnp.broadcast_to(total[:, 2 * groups * day_cols :], (groups, lanes))
        slot = lax.broadcasted_iota(jnp.int32, (groups, lanes), 0)
        lane = lax.broadcasted_iota(jnp.int32, (groups, lanes), 1)
        unit_norm, treat_count, ctrl_count = [
            jnp.sum(jnp.where(lane == i * groups + slot, counts, 0.0), axis=1, keepdims=True) for i in range(3)
        ]
        norms[...] = jnp.where(lane == 0, unit_norm, ctrl_count)
        gap = group_rows(0) / unit_norm - group_rows(groups) / jnp.maximum(treat_count, 1.0)
        before = days_of(lax.axis_index("day"), (groups, day_cols)).astype(f32) < ends[:, 0:1]
        raised_time = raised_days[...]
        pack[:groups, unit_rows:] = raised_time
        pack[groups:, unit_rows:] = jnp.zeros_like(raised_time)
        left = left_of(jnp.where(before, gap, 0.0), raised_time)

        def multiply(here, high, low):
            product = days_dot(left, high, low)
            pack[:groups, here] = add_terms(product, groups)
            pack[groups:, here] = add_terms(product, groups, 1)

        late = resident - 2 * block_rows

        @pl.loop(0, late // block_rows)
        def _(block):
            here = pl.ds(pl.multiple_of(block * block_rows, block_rows), block_rows)
            multiply(here, high_ref[here, :], low_ref[here, :])

        wait_all(copies)
        label = lax.broadcasted_iota(jnp.int32, raised_units.shape, 0)
        raised_units[...] = jnp.where(held_cohort[...] > label, jnp.exp(held_logit[...]), 0.0)
        for there in blocks_of(0, unit_rows - resident):
            more_high[there, :], more_low[there, :] = split_panel(held[there, :])
        for here in blocks_of(late, resident - late):
            multiply(here, high_ref[here, :], low_ref[here, :])
        for there in blocks_of(0, unit_rows - resident):
            multiply(pl.ds(resident + there.start, block_rows), more_high[there, :], more_low[there, :])


@first_half_only
def join_kernel(half, pack, post, *refs):
    norms, out = refs[:half], refs[half]
    groups, unit_rows = post.shape
    over_time = 1.0 / tree_sum(ref[:, 0:1] for ref in norms)
    out[:groups, :unit_rows] = pack[:groups, :unit_rows]
    out[:groups, unit_rows:] = pack[:groups, unit_rows:] * over_time
    out[groups:, :unit_rows] = pack[groups:, :unit_rows] * over_time - post[...]
    out[groups:, unit_rows:] = pack[groups:, unit_rows:]


@first_half_only
def third_kernel(half, *refs):
    parts, refs = [refs[0].at[day] for day in range(half)], refs[1:]
    high_ref, low_ref, more_high, more_low, norms, raised_units, ends, scaled, lam, out, block, out_sems = refs
    groups, unit_rows = raised_units.shape
    resident, day_cols = high_ref.shape
    unit_norm, ctrl_count = norms[:, 0:1], norms[:, 1:2]
    factor = -step_rate / jnp.sqrt(ends[:, 0:1])
    over_unit = 1.0 / unit_norm
    me = lax.rem(lax.axis_index("day"), half)
    for day in range(half):
        lam[:, day * day_cols : (day + 1) * day_cols] = parts[day][:groups, unit_rows:]
    time_grad = jnp.zeros((groups, day_cols), f32)
    new_sum = jnp.zeros((groups, 1), f32)
    for start in range(0, unit_rows, block_rows):
        here = pl.ds(start, block_rows)
        whole = tree_sum(ref[:, here] for ref in parts)
        raised = raised_units[:, here]
        new = raised * over_unit * jnp.exp(whole[:groups] * factor)
        new_sum += jnp.sum(new, axis=1, keepdims=True)
        scaled[:, here] = new * ctrl_count
        left = left_of(jnp.where(raised > 0.0, whole[groups:], 0.0))
        if start < resident:
            high, low = high_ref[here, :], low_ref[here, :]
        else:
            there = pl.ds(start - resident, block_rows)
            high, low = more_high[there, :], more_low[there, :]
        time_grad += add_terms(rows_dot(left, high, low), groups)
    lane = lax.broadcasted_iota(jnp.int32, (groups, day_cols), 1)
    spare = (lane == day_cols - 1) & (me == half - 1)
    block[...] = jnp.where(spare, new_sum, time_grad)
    wait_all(repeat_start(block, out, out_sems))


def time_grad_of(grads, unit_devices, half, day):
    return tree_sum(grads[unit * half + half - 1 - day] for unit in range(unit_devices))


@first_half_only
def fourth_kernel(half, unit_devices, grads, totals):
    day_cols = grads.shape[2]
    last = time_grad_of(grads, unit_devices, half, half - 1)
    totals[...] = jnp.broadcast_to(last[:, day_cols - 1 :], totals.shape)


def fifth_kernel(half, unit_devices, totals, scaled, grads, lam, norms, ends, unit_weights, time_weights):
    groups, day_cols = time_weights.shape
    me = lax.axis_index("day")

    @pl.when(me < half)
    def _():
        unit_weights[...] = scaled[...] * (1.0 / totals[:, 0:1])
        root = jnp.sqrt(jnp.maximum(norms[:, 1:2], 1.0))
        moved_total = jnp.zeros((groups, 1), f32)
        own = jnp.zeros((groups, day_cols), f32)
        for day in range(half):
            total = time_grad_of(grads, unit_devices, half, day)
            moved = lam[:, day * day_cols : (day + 1) * day_cols] * jnp.exp(total * (-step_rate / root))
            moved_total += jnp.sum(moved, axis=1, keepdims=True)
            own = jnp.where(me == day, moved, own)
        time_weights[...] = own * (ends[:, 0:1] / moved_total)

    @pl.when(me >= half)
    def _():
        time_weights[...] = jnp.zeros_like(time_weights)


def sixth_kernel(half, sent_totals, sent_scaled, _, unit_weights, block, out_sem):
    @pl.when(lax.axis_index("day") >= half)
    def _():
        block[...] = sent_scaled[...] * (1.0 / sent_totals[:, 0:1])
        wait_all(fetch([block], [unit_weights], out_sem))


def local(outcomes, cohort, pre_end, post_start, unit_logit, time_logit):
    groups = pre_end.shape[0]
    unit_rows, day_cols = outcomes.shape
    day_devices = lax.axis_size("day")
    unit_devices = lax.axis_size("unit")
    half = day_devices // 2
    assert half * 2 == day_devices and half & (half - 1) == 0
    assert unit_devices & (unit_devices - 1) == 0
    panel_starts = [0, unit_rows // 4, unit_rows // 8 * 5, unit_rows]
    resident = unit_rows * 3 // 4 // block_rows * block_rows
    middle = unit_devices // 2 - 1
    unit_order = [middle] + [unit for unit in reversed(range(unit_devices)) if unit != middle]

    def to_other_half(value):
        pairs = [(u * day_devices + d, u * day_devices + d + half) for u in range(unit_devices) for d in range(half)]
        return lax.ppermute(value, ("unit", "day"), pairs)

    def over_days(value):
        halves = [list(range(half)), list(range(half, day_devices))]
        return lax.all_gather(value, "day", axis_index_groups=halves)

    def over_first_half(value):
        members = [
            [unit * day_devices + day for unit in unit_order for day in reversed(days)]
            for days in (range(half), range(half, day_devices))
        ]
        return lax.all_to_all(
            value, ("unit", "day"), split_axis=0, concat_axis=0, axis_index_groups=members, tiled=True
        )

    def over_units(value):
        return lax.all_to_all(value, "unit", split_axis=0, concat_axis=0, axis_index_groups=[unit_order], tiled=True)

    def call(kernel, shapes, name, args, in_specs=None, out_specs=None, **more):
        return pl.pallas_call(
            kernel,
            in_specs=in_specs or [vmem] * len(args),
            out_specs=out_specs or [vmem] * len(shapes),
            out_shape=[
                shape if isinstance(shape, type(in_hbm)) else jax.ShapeDtypeStruct(*shape) for shape in shapes
            ],
            compiler_params=params,
            name=name,
            **more,
        )(*args)

    arguments = (outcomes, cohort[None, :], pre_end[None, :], post_start[None, :], unit_logit, time_logit)
    fixed = [pltpu.with_memory_space_constraint(argument, pltpu.HBM) for argument in arguments]
    held = [pltpu.VMEM(argument.shape, argument.dtype) for argument in arguments]
    small_sems, panel_sems = pltpu.SemaphoreType.DMA((5,)), pltpu.SemaphoreType.DMA((3,))
    panel_terms = [((resident, day_cols), bf16)] * 2
    other_terms = [((unit_rows - resident, day_cols), bf16)] * 2
    out_sems = pltpu.SemaphoreType.DMA((unit_devices,))
    width = 2 * groups * day_cols + lanes
    in_hbm = pltpu.HBM((unit_devices, 1, width), f32)
    sums, cross, raised_days, time_norm, ends, high, low = call(
        functools.partial(first_kernel, day_devices * day_cols, half, panel_starts),
        [
            in_hbm,
            pltpu.HBM((groups, unit_rows), f32),
            ((groups, day_cols), f32),
            ((groups, lanes), f32),
            ((groups, lanes), f32),
            *panel_terms,
        ],
        "first_product",
        fixed,
        in_specs=[hbm] * 6,
        out_specs=[hbm, hbm] + [vmem] * 5,
        scratch_shapes=held
        + [
            pltpu.VMEM((1, width), f32),
            pltpu.VMEM((4 * groups, unit_rows), bf16),
            pltpu.VMEM((groups, unit_rows), f32),
            small_sems,
            panel_sems,
            out_sems,
        ],
    )
    downward = [
        (u * day_devices + d + half, u * day_devices + d) for u in range(unit_devices) for d in range(half)
    ]
    post = lax.ppermute(cross, ("unit", "day"), downward)
    pack, norms, raised_units, more_high, more_low = call(
        functools.partial(second_kernel, half, unit_devices),
        [
            ((2 * groups, unit_rows + day_cols), f32),
            ((groups, lanes), f32),
            ((groups, unit_rows), f32),
            *other_terms,
        ],
        "unit_gradient",
        (fixed[0], fixed[1], fixed[4], over_units(sums), raised_days, ends, high, low),
        in_specs=[hbm] * 3 + [vmem] * 5,
        scratch_shapes=[
            pltpu.VMEM((unit_rows - resident, day_cols), f32),
            held[1],
            held[4],
            pltpu.SemaphoreType.DMA((3,)),
        ],
    )
    time_norms = [time_norm]
    for k in range(1, half):
        pairs = [(u * day_devices + d, u * day_devices + (d ^ k)) for u in range(unit_devices) for d in range(half)]
        time_norms.append(lax.ppermute(time_norm, ("unit", "day"), pairs))
    (pack,) = call(
        functools.partial(join_kernel, half),
        [((2 * groups, unit_rows + day_cols), f32)],
        "join_post",
        (pack, post, *time_norms),
    )
    members = unit_devices * half
    scaled, lam, grads = call(
        functools.partial(third_kernel, half),
        [
            ((groups, unit_rows), f32),
            ((groups, half * day_cols), f32),
            pltpu.HBM((members, groups, day_cols), f32),
        ],
        "time_gradient",
        (over_days(pack), high, low, more_high, more_low, norms, raised_units, ends),
        out_specs=[vmem, vmem, hbm],
        scratch_shapes=[pltpu.VMEM((groups, day_cols), f32), pltpu.SemaphoreType.DMA((members,))],
    )
    sent_scaled = to_other_half(scaled)
    all_grads = over_first_half(grads)
    (totals,) = call(
        functools.partial(fourth_kernel, half, unit_devices), [((groups, lanes), f32)], "unit_totals", (all_grads,)
    )
    unit_weights, time_weights = call(
        functools.partial(fifth_kernel, half, unit_devices),
        [((groups, unit_rows), f32), ((groups, day_cols), f32)],
        "scale_weights",
        (totals, scaled, all_grads, lam, norms, ends),
    )
    (unit_weights,) = call(
        functools.partial(sixth_kernel, half),
        [((groups, unit_rows), f32)],
        "other_half",
        (to_other_half(totals), sent_scaled, unit_weights),
        in_specs=[vmem, vmem, hbm],
        out_specs=[hbm],
        input_output_aliases={2: 0},
        scratch_shapes=[pltpu.VMEM((groups, unit_rows), f32), pltpu.SemaphoreType.DMA((1,))],
    )
    return unit_weights, time_weights


def solution(mesh):
    return jax.shard_map(
        local,
        mesh=mesh,
        in_specs=(P("unit", "day"), P("unit"), P(), P(), P(None, "unit"), P(None, "day")),
        out_specs=(P(None, "unit"), P(None, "day")),
        check_vma=False,
    )
```

```python
import functools

import jax
import jax.numpy as jnp
from jax import lax
from jax.experimental import pallas as pl
from jax.experimental.pallas import tpu as pltpu
from jax.sharding import PartitionSpec as P

step_rate = 16.0
f32 = jnp.float32
bf16 = jnp.bfloat16
lanes = 128
block_rows = 512
params = pltpu.CompilerParams(vmem_limit_bytes=24 * 1024 * 1024)
vmem = pl.BlockSpec(memory_space=pltpu.VMEM)
hbm = pl.BlockSpec(memory_space=pltpu.HBM)


def split_left(value):
    first = value.astype(bf16).astype(f32)
    return [first, value - first]


def left_of(*values):
    return jnp.concatenate([term for value in values for term in split_left(value)], axis=0).astype(bf16)


def split_panel(value):
    high = value.astype(bf16)
    return high, (value - high.astype(f32)).astype(bf16)


def rows_dot(left, high, low):
    return jnp.dot(left, high, preferred_element_type=f32) + jnp.dot(left, low, preferred_element_type=f32)


def days_dot(left, high, low):
    dims = (((1,), (1,)), ((), ()))
    return lax.dot_general(left, high, dims, preferred_element_type=f32) + lax.dot_general(
        left, low, dims, preferred_element_type=f32
    )


def add_terms(stack, groups, place=0):
    return stack[2 * place * groups :][:groups] + stack[(2 * place + 1) * groups :][:groups]


def tree_sum(values):
    values = list(values)
    while len(values) > 1:
        values = [values[i] + values[i + 1] for i in range(0, len(values), 2)]
    return values[0]


def column(row_ref):
    count = row_ref.shape[1]
    wide = jnp.broadcast_to(row_ref[...].astype(f32), (count, count))
    row = lax.broadcasted_iota(jnp.int32, (count, count), 0)
    lane = lax.broadcasted_iota(jnp.int32, (count, count), 1)
    return jnp.sum(jnp.where(row == lane, wide, 0.0), axis=1, keepdims=True).astype(jnp.int32)


def days_of(device, shape):
    return device * shape[1] + lax.broadcasted_iota(jnp.int32, shape, 1)


def first_half_only(kernel):
    @functools.wraps(kernel)
    def guarded(half, *refs):
        @pl.when(lax.axis_index("day") < half)
        def _():
            kernel(half, *refs)

    return guarded


def fetch(sources, targets, sems):
    copies = [pltpu.make_async_copy(*pair, sems.at[i]) for i, pair in enumerate(zip(sources, targets))]
    for copy in copies:
        copy.start()
    return copies


def fetch_rows(source, target, sems, starts):
    spans = [(start, stop - start) for start, stop in zip(starts, starts[1:])]
    parts = [pl.ds(*span) for span in spans]
    copies = fetch([source.at[here] for here in parts], [target.at[here] for here in parts], sems)
    return [(*span, copy) for span, copy in zip(spans, copies)]


def blocks_of(start, rows):
    return [pl.ds(here, block_rows) for here in range(start, start + rows, block_rows)]


def wait_all(copies):
    for copy in copies:
        copy.wait()


def repeat_start(block, out, sems):
    places = [out.at[i] for i in range(out.shape[0])]
    return fetch([block] * len(places), places, sems)


def first_kernel(all_count, half, starts, *refs):
    arguments, refs = refs[:6], refs[6:]
    out, cross, raised_days, time_norm, ends, high_ref, low_ref, *held, block, left_ref, cross_block, small_sems, panel_sems, out_sems = refs
    groups, day_cols = held[5].shape
    unit_rows, resident = held[0].shape[0], high_ref.shape[0]
    (post_copy,) = fetch(arguments[3:4], held[3:4], small_sems)
    unit_copies = fetch(arguments[1:5:3], held[1:5:3], small_sems.at[pl.ds(1, 2)])
    parts = fetch_rows(arguments[0], held[0], panel_sems, starts)
    day_copies = fetch(arguments[2:6:3], held[2:6:3], small_sems.at[pl.ds(3, 2)])
    panel, cohort, pre_row, post_row, unit_logit, time_logit = held
    post_copy.wait()
    wait_all(unit_copies)
    me = lax.axis_index("day")

    @pl.when(me < half)
    def _():
        label = lax.broadcasted_iota(jnp.int32, (groups, unit_rows), 0)
        treated = jnp.where(cohort[...] == label, 1.0, 0.0)
        control = jnp.where(cohort[...] > label, 1.0, 0.0)
        raised = jnp.exp(unit_logit[...]) * control
        left_ref[...] = left_of(raised, treated)
        lane = lax.broadcasted_iota(jnp.int32, (groups, lanes), 1)
        counts = [jnp.sum(value, axis=1, keepdims=True) for value in (raised, treated, control)]
        slot = lax.broadcasted_iota(jnp.int32, (groups, lanes), 0)
        norms = jnp.zeros((groups, lanes), f32)
        for i, count in enumerate(counts):
            norms += jnp.where(lane == i * groups + slot, count, 0.0)
        block[:, 2 * groups * day_cols :] = jnp.sum(norms, axis=0, keepdims=True)
        product = jnp.zeros((4 * groups, 2 * day_cols), f32)
        for start, rows, copy in parts:
            copy.wait()
            for here in blocks_of(start, rows):
                high, low = split_panel(panel[here, :])
                if here.start < resident:
                    high_ref[here, :] = high
                    low_ref[here, :] = low
                both = jnp.concatenate([high, low], axis=1)
                product += jnp.dot(left_ref[:, here], both, preferred_element_type=f32)
        product = product[:, :day_cols] + product[:, day_cols:]
        both_sums = jnp.concatenate([add_terms(product, groups), product[2 * groups :][:groups]], axis=0)
        for row in range(2 * groups):
            block[:, row * day_cols : (row + 1) * day_cols] = both_sums[row : row + 1, :]
        sends = repeat_start(block, out, out_sems)
        wait_all(day_copies)
        pre_end = column(pre_row)
        ends[...] = jnp.broadcast_to(pre_end.astype(f32), ends.shape)
        before = days_of(me, (groups, day_cols)) < pre_end
        raised_time = jnp.where(before, jnp.exp(time_logit[...]), 0.0)
        raised_days[...] = raised_time
        time_norm[...] = jnp.broadcast_to(jnp.sum(raised_time, axis=1, keepdims=True), time_norm.shape)
        wait_all(sends)

    @pl.when(me >= half)
    def _():
        post_start = column(post_row)
        after = jnp.where(days_of(me, (groups, day_cols)) >= post_start, 1.0, 0.0)
        left = left_of(after / (all_count - post_start).astype(f32))
        for start, rows, copy in parts:
            copy.wait()
            for here in blocks_of(start, rows):
                cross_block[:, here] = add_terms(days_dot(left, *split_panel(panel[here, :])), groups)
        sends = fetch([cross_block], [cross], out_sems)
        wait_all(day_copies)
        wait_all(sends)


@first_half_only
def second_kernel(half, unit_devices, panel, cohort, unit_logit, sums, raised_days, ends, high_ref, low_ref, *refs):
    pack, norms, raised_units, more_high, more_low, held, held_cohort, held_logit, sems = refs
    groups, day_cols = raised_days.shape
    unit_rows, resident = panel.shape[0], high_ref.shape[0]
    rest = pl.ds(resident, unit_rows - resident)
    copies = fetch([panel.at[rest], cohort, unit_logit], [held, held_cohort, held_logit], sems)

    @pl.when(lax.axis_index("day") < half)
    def _():
        total = tree_sum(sums[u] for u in range(unit_devices))

        def group_rows(first):
            starts = [(first + row) * day_cols for row in range(groups)]
            return jnp.concatenate([total[:, start : start + day_cols] for start in starts], axis=0)

        counts = jnp.broadcast_to(total[:, 2 * groups * day_cols :], (groups, lanes))
        slot = lax.broadcasted_iota(jnp.int32, (groups, lanes), 0)
        lane = lax.broadcasted_iota(jnp.int32, (groups, lanes), 1)
        unit_norm, treat_count, ctrl_count = [
            jnp.sum(jnp.where(lane == i * groups + slot, counts, 0.0), axis=1, keepdims=True) for i in range(3)
        ]
        norms[...] = jnp.where(lane == 0, unit_norm, ctrl_count)
        gap = group_rows(0) / unit_norm - group_rows(groups) / jnp.maximum(treat_count, 1.0)
        before = days_of(lax.axis_index("day"), (groups, day_cols)).astype(f32) < ends[:, 0:1]
        raised_time = raised_days[...]
        pack[:groups, unit_rows:] = raised_time
        pack[groups:, unit_rows:] = jnp.zeros_like(raised_time)
        left = left_of(jnp.where(before, gap, 0.0), raised_time)

        def multiply(here, high, low):
            product = days_dot(left, high, low)
            pack[:groups, here] = add_terms(product, groups)
            pack[groups:, here] = add_terms(product, groups, 1)

        late = resident - 2 * block_rows

        @pl.loop(0, late // block_rows)
        def _(block):
            here = pl.ds(pl.multiple_of(block * block_rows, block_rows), block_rows)
            multiply(here, high_ref[here, :], low_ref[here, :])

        wait_all(copies)
        label = lax.broadcasted_iota(jnp.int32, raised_units.shape, 0)
        raised_units[...] = jnp.where(held_cohort[...] > label, jnp.exp(held_logit[...]), 0.0)
        for there in blocks_of(0, unit_rows - resident):
            more_high[there, :], more_low[there, :] = split_panel(held[there, :])
        for here in blocks_of(late, resident - late):
            multiply(here, high_ref[here, :], low_ref[here, :])
        for there in blocks_of(0, unit_rows - resident):
            multiply(pl.ds(resident + there.start, block_rows), more_high[there, :], more_low[there, :])


@first_half_only
def join_kernel(half, pack, post, *refs):
    norms, out = refs[:half], refs[half]
    groups, unit_rows = post.shape
    over_time = 1.0 / tree_sum(ref[:, 0:1] for ref in norms)
    out[:groups, :unit_rows] = pack[:groups, :unit_rows]
    out[:groups, unit_rows:] = pack[:groups, unit_rows:] * over_time
    out[groups:, :unit_rows] = pack[groups:, :unit_rows] * over_time - post[...]
    out[groups:, unit_rows:] = pack[groups:, unit_rows:]


@first_half_only
def third_kernel(half, *refs):
    parts, refs = [refs[0].at[day] for day in range(half)], refs[1:]
    high_ref, low_ref, more_high, more_low, norms, raised_units, ends, scaled, lam, out, block, out_sems = refs
    groups, unit_rows = raised_units.shape
    resident, day_cols = high_ref.shape
    unit_norm, ctrl_count = norms[:, 0:1], norms[:, 1:2]
    factor = -step_rate / jnp.sqrt(ends[:, 0:1])
    over_unit = 1.0 / unit_norm
    me = lax.rem(lax.axis_index("day"), half)
    for day in range(half):
        lam[:, day * day_cols : (day + 1) * day_cols] = parts[day][:groups, unit_rows:]
    time_grad = jnp.zeros((groups, day_cols), f32)
    new_sum = jnp.zeros((groups, 1), f32)
    for start in range(0, unit_rows, block_rows):
        here = pl.ds(start, block_rows)
        whole = tree_sum(ref[:, here] for ref in parts)
        raised = raised_units[:, here]
        new = raised * over_unit * jnp.exp(whole[:groups] * factor)
        new_sum += jnp.sum(new, axis=1, keepdims=True)
        scaled[:, here] = new * ctrl_count
        left = left_of(jnp.where(raised > 0.0, whole[groups:], 0.0))
        if start < resident:
            high, low = high_ref[here, :], low_ref[here, :]
        else:
            there = pl.ds(start - resident, block_rows)
            high, low = more_high[there, :], more_low[there, :]
        time_grad += add_terms(rows_dot(left, high, low), groups)
    lane = lax.broadcasted_iota(jnp.int32, (groups, day_cols), 1)
    spare = (lane == day_cols - 1) & (me == half - 1)
    block[...] = jnp.where(spare, new_sum, time_grad)
    wait_all(repeat_start(block, out, out_sems))


def time_grad_of(grads, unit_devices, half, day):
    return tree_sum(grads[unit * half + half - 1 - day] for unit in range(unit_devices))


@first_half_only
def fourth_kernel(half, unit_devices, grads, totals):
    day_cols = grads.shape[2]
    last = time_grad_of(grads, unit_devices, half, half - 1)
    totals[...] = jnp.broadcast_to(last[:, day_cols - 1 :], totals.shape)


def fifth_kernel(half, unit_devices, totals, scaled, grads, lam, norms, ends, unit_weights, time_weights):
    groups, day_cols = time_weights.shape
    me = lax.axis_index("day")

    @pl.when(me < half)
    def _():
        unit_weights[...] = scaled[...] * (1.0 / totals[:, 0:1])
        root = jnp.sqrt(jnp.maximum(norms[:, 1:2], 1.0))
        moved_total = jnp.zeros((groups, 1), f32)
        own = jnp.zeros((groups, day_cols), f32)
        for day in range(half):
            total = time_grad_of(grads, unit_devices, half, day)
            moved = lam[:, day * day_cols : (day + 1) * day_cols] * jnp.exp(total * (-step_rate / root))
            moved_total += jnp.sum(moved, axis=1, keepdims=True)
            own = jnp.where(me == day, moved, own)
        time_weights[...] = own * (ends[:, 0:1] / moved_total)

    @pl.when(me >= half)
    def _():
        time_weights[...] = jnp.zeros_like(time_weights)


def sixth_kernel(half, sent_totals, sent_scaled, _, unit_weights, block, out_sem):
    @pl.when(lax.axis_index("day") >= half)
    def _():
        block[...] = sent_scaled[...] * (1.0 / sent_totals[:, 0:1])
        wait_all(fetch([block], [unit_weights], out_sem))


def local(outcomes, cohort, pre_end, post_start, unit_logit, time_logit):
    groups = pre_end.shape[0]
    unit_rows, day_cols = outcomes.shape
    day_devices = lax.axis_size("day")
    unit_devices = lax.axis_size("unit")
    half = day_devices // 2
    assert half * 2 == day_devices and half & (half - 1) == 0
    assert unit_devices & (unit_devices - 1) == 0
    panel_starts = [0, unit_rows // 4, unit_rows // 8 * 5, unit_rows]
    resident = unit_rows * 3 // 4 // block_rows * block_rows
    def meeting_at(first):
        return [first] + [unit for unit in reversed(range(unit_devices)) if unit != first]

    middle = unit_devices // 2

    def to_other_half(value):
        pairs = [(u * day_devices + d, u * day_devices + d + half) for u in range(unit_devices) for d in range(half)]
        return lax.ppermute(value, ("unit", "day"), pairs)

    def over_days(value):
        halves = [list(range(half)), list(range(half, day_devices))]
        return lax.all_gather(value, "day", axis_index_groups=halves)

    def over_first_half(value):
        members = [
            [unit * day_devices + day for unit in meeting_at(middle + 1) for day in reversed(days)]
            for days in (range(half), range(half, day_devices))
        ]
        return lax.all_to_all(
            value, ("unit", "day"), split_axis=0, concat_axis=0, axis_index_groups=members, tiled=True
        )

    def over_units(value):
        members = [
            [unit * day_devices + day for unit in meeting_at(middle - 1 if day < half else middle)]
            for day in range(day_devices)
        ]
        return lax.all_to_all(
            value, ("unit", "day"), split_axis=0, concat_axis=0, axis_index_groups=members, tiled=True
        )

    def call(kernel, shapes, name, args, in_specs=None, out_specs=None, **more):
        return pl.pallas_call(
            kernel,
            in_specs=in_specs or [vmem] * len(args),
            out_specs=out_specs or [vmem] * len(shapes),
            out_shape=[
                shape if isinstance(shape, type(in_hbm)) else jax.ShapeDtypeStruct(*shape) for shape in shapes
            ],
            compiler_params=params,
            name=name,
            **more,
        )(*args)

    arguments = (outcomes, cohort[None, :], pre_end[None, :], post_start[None, :], unit_logit, time_logit)
    fixed = [pltpu.with_memory_space_constraint(argument, pltpu.HBM) for argument in arguments]
    held = [pltpu.VMEM(argument.shape, argument.dtype) for argument in arguments]
    small_sems, panel_sems = pltpu.SemaphoreType.DMA((5,)), pltpu.SemaphoreType.DMA((3,))
    panel_terms = [((resident, day_cols), bf16)] * 2
    other_terms = [((unit_rows - resident, day_cols), bf16)] * 2
    out_sems = pltpu.SemaphoreType.DMA((unit_devices,))
    width = 2 * groups * day_cols + lanes
    in_hbm = pltpu.HBM((unit_devices, 1, width), f32)
    sums, cross, raised_days, time_norm, ends, high, low = call(
        functools.partial(first_kernel, day_devices * day_cols, half, panel_starts),
        [
            in_hbm,
            pltpu.HBM((groups, unit_rows), f32),
            ((groups, day_cols), f32),
            ((groups, lanes), f32),
            ((groups, lanes), f32),
            *panel_terms,
        ],
        "first_product",
        fixed,
        in_specs=[hbm] * 6,
        out_specs=[hbm, hbm] + [vmem] * 5,
        scratch_shapes=held
        + [
            pltpu.VMEM((1, width), f32),
            pltpu.VMEM((4 * groups, unit_rows), bf16),
            pltpu.VMEM((groups, unit_rows), f32),
            small_sems,
            panel_sems,
            out_sems,
        ],
    )
    downward = [
        (u * day_devices + d + half, u * day_devices + d) for u in range(unit_devices) for d in range(half)
    ]
    post = lax.ppermute(cross, ("unit", "day"), downward)
    pack, norms, raised_units, more_high, more_low = call(
        functools.partial(second_kernel, half, unit_devices),
        [
            ((2 * groups, unit_rows + day_cols), f32),
            ((groups, lanes), f32),
            ((groups, unit_rows), f32),
            *other_terms,
        ],
        "unit_gradient",
        (fixed[0], fixed[1], fixed[4], over_units(sums), raised_days, ends, high, low),
        in_specs=[hbm] * 3 + [vmem] * 5,
        scratch_shapes=[
            pltpu.VMEM((unit_rows - resident, day_cols), f32),
            held[1],
            held[4],
            pltpu.SemaphoreType.DMA((3,)),
        ],
    )
    time_norms = [time_norm]
    for k in range(1, half):
        pairs = [(u * day_devices + d, u * day_devices + (d ^ k)) for u in range(unit_devices) for d in range(half)]
        time_norms.append(lax.ppermute(time_norm, ("unit", "day"), pairs))
    (pack,) = call(
        functools.partial(join_kernel, half),
        [((2 * groups, unit_rows + day_cols), f32)],
        "join_post",
        (pack, post, *time_norms),
    )
    members = unit_devices * half
    scaled, lam, grads = call(
        functools.partial(third_kernel, half),
        [
            ((groups, unit_rows), f32),
            ((groups, half * day_cols), f32),
            pltpu.HBM((members, groups, day_cols), f32),
        ],
        "time_gradient",
        (over_days(pack), high, low, more_high, more_low, norms, raised_units, ends),
        out_specs=[vmem, vmem, hbm],
        scratch_shapes=[pltpu.VMEM((groups, day_cols), f32), pltpu.SemaphoreType.DMA((members,))],
    )
    sent_scaled = to_other_half(scaled)
    all_grads = over_first_half(grads)
    (totals,) = call(
        functools.partial(fourth_kernel, half, unit_devices), [((groups, lanes), f32)], "unit_totals", (all_grads,)
    )
    unit_weights, time_weights = call(
        functools.partial(fifth_kernel, half, unit_devices),
        [((groups, unit_rows), f32), ((groups, day_cols), f32)],
        "scale_weights",
        (totals, scaled, all_grads, lam, norms, ends),
    )
    (unit_weights,) = call(
        functools.partial(sixth_kernel, half),
        [((groups, unit_rows), f32)],
        "other_half",
        (to_other_half(totals), sent_scaled, unit_weights),
        in_specs=[vmem, vmem, hbm],
        out_specs=[hbm],
        input_output_aliases={2: 0},
        scratch_shapes=[pltpu.VMEM((groups, unit_rows), f32), pltpu.SemaphoreType.DMA((1,))],
    )
    return unit_weights, time_weights


def solution(mesh):
    return jax.shard_map(
        local,
        mesh=mesh,
        in_specs=(P("unit", "day"), P("unit"), P(), P(), P(None, "unit"), P(None, "day")),
        out_specs=(P(None, "unit"), P(None, "day")),
        check_vma=False,
    )
```

```python
import functools

import jax
import jax.numpy as jnp
from jax import lax
from jax.experimental import pallas as pl
from jax.experimental.pallas import tpu as pltpu
from jax.sharding import PartitionSpec as P

step_rate = 16.0
f32 = jnp.float32
bf16 = jnp.bfloat16
lanes = 128
block_rows = 512
params = pltpu.CompilerParams(vmem_limit_bytes=24 * 1024 * 1024)
vmem = pl.BlockSpec(memory_space=pltpu.VMEM)
hbm = pl.BlockSpec(memory_space=pltpu.HBM)


def split_left(value):
    first = value.astype(bf16).astype(f32)
    return [first, value - first]


def left_of(*values):
    return jnp.concatenate([term for value in values for term in split_left(value)], axis=0).astype(bf16)


def split_panel(value):
    high = value.astype(bf16)
    return high, (value - high.astype(f32)).astype(bf16)


def rows_dot(left, high, low):
    return jnp.dot(left, high, preferred_element_type=f32) + jnp.dot(left, low, preferred_element_type=f32)


def days_dot(left, high, low):
    dims = (((1,), (1,)), ((), ()))
    return lax.dot_general(left, high, dims, preferred_element_type=f32) + lax.dot_general(
        left, low, dims, preferred_element_type=f32
    )


def add_terms(stack, groups, place=0):
    return stack[2 * place * groups :][:groups] + stack[(2 * place + 1) * groups :][:groups]


def tree_sum(values):
    values = list(values)
    while len(values) > 1:
        values = [values[i] + values[i + 1] for i in range(0, len(values), 2)]
    return values[0]


def column(row_ref):
    count = row_ref.shape[1]
    wide = jnp.broadcast_to(row_ref[...].astype(f32), (count, count))
    row = lax.broadcasted_iota(jnp.int32, (count, count), 0)
    lane = lax.broadcasted_iota(jnp.int32, (count, count), 1)
    return jnp.sum(jnp.where(row == lane, wide, 0.0), axis=1, keepdims=True).astype(jnp.int32)


def days_of(device, shape):
    return device * shape[1] + lax.broadcasted_iota(jnp.int32, shape, 1)


def first_half_only(kernel):
    @functools.wraps(kernel)
    def guarded(half, *refs):
        @pl.when(lax.axis_index("day") < half)
        def _():
            kernel(half, *refs)

    return guarded


def fetch(sources, targets, sems):
    copies = [pltpu.make_async_copy(*pair, sems.at[i]) for i, pair in enumerate(zip(sources, targets))]
    for copy in copies:
        copy.start()
    return copies


def fetch_rows(source, target, sems, starts):
    spans = [(start, stop - start) for start, stop in zip(starts, starts[1:])]
    parts = [pl.ds(*span) for span in spans]
    copies = fetch([source.at[here] for here in parts], [target.at[here] for here in parts], sems)
    return [(*span, copy) for span, copy in zip(spans, copies)]


def blocks_of(start, rows):
    return [pl.ds(here, block_rows) for here in range(start, start + rows, block_rows)]


def wait_all(copies):
    for copy in copies:
        copy.wait()


def repeat_start(block, out, sems):
    places = [out.at[i] for i in range(out.shape[0])]
    return fetch([block] * len(places), places, sems)


def first_kernel(all_count, half, starts, *refs):
    arguments, refs = refs[:6], refs[6:]
    out, cross, raised_days, time_norm, ends, high_ref, low_ref, *held, block, left_ref, cross_block, small_sems, panel_sems, out_sems = refs
    groups, day_cols = held[5].shape
    unit_rows, resident = held[0].shape[0], high_ref.shape[0]
    (post_copy,) = fetch(arguments[3:4], held[3:4], small_sems)
    unit_copies = fetch(arguments[1:5:3], held[1:5:3], small_sems.at[pl.ds(1, 2)])
    parts = fetch_rows(arguments[0], held[0], panel_sems, starts)
    day_copies = fetch(arguments[2:6:3], held[2:6:3], small_sems.at[pl.ds(3, 2)])
    panel, cohort, pre_row, post_row, unit_logit, time_logit = held
    post_copy.wait()
    wait_all(unit_copies)
    me = lax.axis_index("day")

    @pl.when(me < half)
    def _():
        label = lax.broadcasted_iota(jnp.int32, (groups, unit_rows), 0)
        treated = jnp.where(cohort[...] == label, 1.0, 0.0)
        control = jnp.where(cohort[...] > label, 1.0, 0.0)
        raised = jnp.exp(unit_logit[...]) * control
        left_ref[...] = left_of(raised, treated)
        lane = lax.broadcasted_iota(jnp.int32, (groups, lanes), 1)
        counts = [jnp.sum(value, axis=1, keepdims=True) for value in (raised, treated, control)]
        slot = lax.broadcasted_iota(jnp.int32, (groups, lanes), 0)
        norms = jnp.zeros((groups, lanes), f32)
        for i, count in enumerate(counts):
            norms += jnp.where(lane == i * groups + slot, count, 0.0)
        block[:, 2 * groups * day_cols :] = jnp.sum(norms, axis=0, keepdims=True)
        product = jnp.zeros((4 * groups, 2 * day_cols), f32)
        for start, rows, copy in parts:
            copy.wait()
            for here in blocks_of(start, rows):
                high, low = split_panel(panel[here, :])
                if here.start < resident:
                    high_ref[here, :] = high
                    low_ref[here, :] = low
                both = jnp.concatenate([high, low], axis=1)
                product += jnp.dot(left_ref[:, here], both, preferred_element_type=f32)
        product = product[:, :day_cols] + product[:, day_cols:]
        both_sums = jnp.concatenate([add_terms(product, groups), product[2 * groups :][:groups]], axis=0)
        for row in range(2 * groups):
            block[:, row * day_cols : (row + 1) * day_cols] = both_sums[row : row + 1, :]
        sends = repeat_start(block, out, out_sems)
        wait_all(day_copies)
        pre_end = column(pre_row)
        ends[...] = jnp.broadcast_to(pre_end.astype(f32), ends.shape)
        before = days_of(me, (groups, day_cols)) < pre_end
        raised_time = jnp.where(before, jnp.exp(time_logit[...]), 0.0)
        raised_days[...] = raised_time
        time_norm[...] = jnp.broadcast_to(jnp.sum(raised_time, axis=1, keepdims=True), time_norm.shape)
        wait_all(sends)

    @pl.when(me >= half)
    def _():
        post_start = column(post_row)
        after = jnp.where(days_of(me, (groups, day_cols)) >= post_start, 1.0, 0.0)
        left = left_of(after / (all_count - post_start).astype(f32))
        for start, rows, copy in parts:
            copy.wait()
            for here in blocks_of(start, rows):
                cross_block[:, here] = add_terms(days_dot(left, *split_panel(panel[here, :])), groups)
        sends = fetch([cross_block], [cross], out_sems)
        wait_all(day_copies)
        wait_all(sends)


@first_half_only
def second_kernel(half, unit_devices, panel, cohort, unit_logit, sums, raised_days, ends, high_ref, low_ref, *refs):
    pack, norms, raised_units, more_high, more_low, held, held_cohort, held_logit, sems = refs
    groups, day_cols = raised_days.shape
    unit_rows, resident = panel.shape[0], high_ref.shape[0]
    rest = pl.ds(resident, unit_rows - resident)
    copies = fetch([panel.at[rest], cohort, unit_logit], [held, held_cohort, held_logit], sems)

    @pl.when(lax.axis_index("day") < half)
    def _():
        total = tree_sum(sums[u] for u in range(unit_devices))

        def group_rows(first):
            starts = [(first + row) * day_cols for row in range(groups)]
            return jnp.concatenate([total[:, start : start + day_cols] for start in starts], axis=0)

        counts = jnp.broadcast_to(total[:, 2 * groups * day_cols :], (groups, lanes))
        slot = lax.broadcasted_iota(jnp.int32, (groups, lanes), 0)
        lane = lax.broadcasted_iota(jnp.int32, (groups, lanes), 1)
        unit_norm, treat_count, ctrl_count = [
            jnp.sum(jnp.where(lane == i * groups + slot, counts, 0.0), axis=1, keepdims=True) for i in range(3)
        ]
        norms[...] = jnp.where(lane == 0, unit_norm, ctrl_count)
        gap = group_rows(0) / unit_norm - group_rows(groups) / jnp.maximum(treat_count, 1.0)
        before = days_of(lax.axis_index("day"), (groups, day_cols)).astype(f32) < ends[:, 0:1]
        raised_time = raised_days[...]
        pack[:groups, unit_rows:] = raised_time
        pack[groups:, unit_rows:] = jnp.zeros_like(raised_time)
        left = left_of(jnp.where(before, gap, 0.0), raised_time)

        def multiply(here, high, low):
            product = days_dot(left, high, low)
            pack[:groups, here] = add_terms(product, groups)
            pack[groups:, here] = add_terms(product, groups, 1)

        late = resident - 2 * block_rows

        @pl.loop(0, late // block_rows)
        def _(block):
            here = pl.ds(pl.multiple_of(block * block_rows, block_rows), block_rows)
            multiply(here, high_ref[here, :], low_ref[here, :])

        wait_all(copies)
        label = lax.broadcasted_iota(jnp.int32, raised_units.shape, 0)
        raised_units[...] = jnp.where(held_cohort[...] > label, jnp.exp(held_logit[...]), 0.0)
        for there in blocks_of(0, unit_rows - resident):
            more_high[there, :], more_low[there, :] = split_panel(held[there, :])
        for here in blocks_of(late, resident - late):
            multiply(here, high_ref[here, :], low_ref[here, :])
        for there in blocks_of(0, unit_rows - resident):
            multiply(pl.ds(resident + there.start, block_rows), more_high[there, :], more_low[there, :])


@first_half_only
def join_kernel(half, pack, post, *refs):
    norms, out = refs[:half], refs[half]
    groups, unit_rows = post.shape
    over_time = 1.0 / tree_sum(ref[:, 0:1] for ref in norms)
    out[:groups, :unit_rows] = pack[:groups, :unit_rows]
    out[:groups, unit_rows:] = pack[:groups, unit_rows:] * over_time
    out[groups:, :unit_rows] = pack[groups:, :unit_rows] * over_time - post[...]
    out[groups:, unit_rows:] = pack[groups:, unit_rows:]


@first_half_only
def third_kernel(half, *refs):
    parts, refs = [refs[0].at[day] for day in range(half)], refs[1:]
    high_ref, low_ref, more_high, more_low, norms, raised_units, ends, scaled, lam, out, block, out_sems = refs
    groups, unit_rows = raised_units.shape
    resident, day_cols = high_ref.shape
    unit_norm, ctrl_count = norms[:, 0:1], norms[:, 1:2]
    factor = -step_rate / jnp.sqrt(ends[:, 0:1])
    over_unit = 1.0 / unit_norm
    me = lax.rem(lax.axis_index("day"), half)
    for day in range(half):
        lam[:, day * day_cols : (day + 1) * day_cols] = parts[day][:groups, unit_rows:]
    time_grad = jnp.zeros((2 * groups, 2 * day_cols), f32)
    new_sum = jnp.zeros((groups, 1), f32)
    for start in range(0, unit_rows, block_rows):
        here = pl.ds(start, block_rows)
        whole = tree_sum(ref[:, here] for ref in parts)
        raised = raised_units[:, here]
        new = raised * over_unit * jnp.exp(whole[:groups] * factor)
        new_sum += jnp.sum(new, axis=1, keepdims=True)
        scaled[:, here] = new * ctrl_count
        left = left_of(jnp.where(raised > 0.0, whole[groups:], 0.0))
        if start < resident:
            high, low = high_ref[here, :], low_ref[here, :]
        else:
            there = pl.ds(start - resident, block_rows)
            high, low = more_high[there, :], more_low[there, :]
        time_grad += jnp.dot(left, jnp.concatenate([high, low], axis=1), preferred_element_type=f32)
    time_grad = add_terms(time_grad[:, :day_cols] + time_grad[:, day_cols:], groups)
    lane = lax.broadcasted_iota(jnp.int32, (groups, day_cols), 1)
    spare = (lane == day_cols - 1) & (me == half - 1)
    block[...] = jnp.where(spare, new_sum, time_grad)
    wait_all(repeat_start(block, out, out_sems))


def time_grad_of(grads, unit_devices, half, day):
    return tree_sum(grads[unit * half + half - 1 - day] for unit in range(unit_devices))


@first_half_only
def fourth_kernel(half, unit_devices, grads, totals):
    day_cols = grads.shape[2]
    last = time_grad_of(grads, unit_devices, half, half - 1)
    totals[...] = jnp.broadcast_to(last[:, day_cols - 1 :], totals.shape)


def fifth_kernel(half, unit_devices, totals, scaled, grads, lam, norms, ends, unit_weights, time_weights):
    groups, day_cols = time_weights.shape
    me = lax.axis_index("day")

    @pl.when(me < half)
    def _():
        unit_weights[...] = scaled[...] * (1.0 / totals[:, 0:1])
        root = jnp.sqrt(jnp.maximum(norms[:, 1:2], 1.0))
        moved_total = jnp.zeros((groups, 1), f32)
        own = jnp.zeros((groups, day_cols), f32)
        for day in range(half):
            total = time_grad_of(grads, unit_devices, half, day)
            moved = lam[:, day * day_cols : (day + 1) * day_cols] * jnp.exp(total * (-step_rate / root))
            moved_total += jnp.sum(moved, axis=1, keepdims=True)
            own = jnp.where(me == day, moved, own)
        time_weights[...] = own * (ends[:, 0:1] / moved_total)

    @pl.when(me >= half)
    def _():
        time_weights[...] = jnp.zeros_like(time_weights)


def sixth_kernel(half, sent_totals, sent_scaled, _, unit_weights, block, out_sem):
    @pl.when(lax.axis_index("day") >= half)
    def _():
        block[...] = sent_scaled[...] * (1.0 / sent_totals[:, 0:1])
        wait_all(fetch([block], [unit_weights], out_sem))


def local(outcomes, cohort, pre_end, post_start, unit_logit, time_logit):
    groups = pre_end.shape[0]
    unit_rows, day_cols = outcomes.shape
    day_devices = lax.axis_size("day")
    unit_devices = lax.axis_size("unit")
    half = day_devices // 2
    assert half * 2 == day_devices and half & (half - 1) == 0
    assert unit_devices & (unit_devices - 1) == 0
    panel_starts = [0, unit_rows // 4, unit_rows // 8 * 5, unit_rows]
    resident = unit_rows * 3 // 4 // block_rows * block_rows
    def meeting_at(first):
        return [first] + [unit for unit in reversed(range(unit_devices)) if unit != first]

    middle = unit_devices // 2

    def to_other_half(value, day_xor=0):
        pairs = [
            (u * day_devices + d, u * day_devices + half + (d ^ day_xor)) for u in range(unit_devices) for d in range(half)
        ]
        return lax.ppermute(value, ("unit", "day"), pairs)

    def over_days(value):
        halves = [list(range(half)), list(range(half, day_devices))]
        return lax.all_gather(value, "day", axis_index_groups=halves)

    def over_first_half(value):
        members = [
            [unit * day_devices + day for unit in meeting_at(middle + 1) for day in reversed(days)]
            for days in (range(half), range(half, day_devices))
        ]
        return lax.all_to_all(
            value, ("unit", "day"), split_axis=0, concat_axis=0, axis_index_groups=members, tiled=True
        )

    def over_units(value):
        members = [
            [unit * day_devices + day for unit in meeting_at(middle - 1 if day < half else middle)]
            for day in range(day_devices)
        ]
        return lax.all_to_all(
            value, ("unit", "day"), split_axis=0, concat_axis=0, axis_index_groups=members, tiled=True
        )

    def call(kernel, shapes, name, args, in_specs=None, out_specs=None, **more):
        return pl.pallas_call(
            kernel,
            in_specs=in_specs or [vmem] * len(args),
            out_specs=out_specs or [vmem] * len(shapes),
            out_shape=[
                shape if isinstance(shape, type(in_hbm)) else jax.ShapeDtypeStruct(*shape) for shape in shapes
            ],
            compiler_params=params,
            name=name,
            **more,
        )(*args)

    arguments = (outcomes, cohort[None, :], pre_end[None, :], post_start[None, :], unit_logit, time_logit)
    fixed = [pltpu.with_memory_space_constraint(argument, pltpu.HBM) for argument in arguments]
    held = [pltpu.VMEM(argument.shape, argument.dtype) for argument in arguments]
    small_sems, panel_sems = pltpu.SemaphoreType.DMA((5,)), pltpu.SemaphoreType.DMA((3,))
    panel_terms = [((resident, day_cols), bf16)] * 2
    other_terms = [((unit_rows - resident, day_cols), bf16)] * 2
    out_sems = pltpu.SemaphoreType.DMA((unit_devices,))
    width = 2 * groups * day_cols + lanes
    in_hbm = pltpu.HBM((unit_devices, 1, width), f32)
    sums, cross, raised_days, time_norm, ends, high, low = call(
        functools.partial(first_kernel, day_devices * day_cols, half, panel_starts),
        [
            in_hbm,
            pltpu.HBM((groups, unit_rows), f32),
            ((groups, day_cols), f32),
            ((groups, lanes), f32),
            ((groups, lanes), f32),
            *panel_terms,
        ],
        "first_product",
        fixed,
        in_specs=[hbm] * 6,
        out_specs=[hbm, hbm] + [vmem] * 5,
        scratch_shapes=held
        + [
            pltpu.VMEM((1, width), f32),
            pltpu.VMEM((4 * groups, unit_rows), bf16),
            pltpu.VMEM((groups, unit_rows), f32),
            small_sems,
            panel_sems,
            out_sems,
        ],
    )
    downward = [
        (u * day_devices + d + half, u * day_devices + d) for u in range(unit_devices) for d in range(half)
    ]
    post = lax.ppermute(cross, ("unit", "day"), downward)
    pack, norms, raised_units, more_high, more_low = call(
        functools.partial(second_kernel, half, unit_devices),
        [
            ((2 * groups, unit_rows + day_cols), f32),
            ((groups, lanes), f32),
            ((groups, unit_rows), f32),
            *other_terms,
        ],
        "unit_gradient",
        (fixed[0], fixed[1], fixed[4], over_units(sums), raised_days, ends, high, low),
        in_specs=[hbm] * 3 + [vmem] * 5,
        scratch_shapes=[
            pltpu.VMEM((unit_rows - resident, day_cols), f32),
            held[1],
            held[4],
            pltpu.SemaphoreType.DMA((3,)),
        ],
    )
    time_norms = [time_norm]
    for k in range(1, half):
        pairs = [(u * day_devices + d, u * day_devices + (d ^ k)) for u in range(unit_devices) for d in range(half)]
        time_norms.append(lax.ppermute(time_norm, ("unit", "day"), pairs))
    (pack,) = call(
        functools.partial(join_kernel, half),
        [((2 * groups, unit_rows + day_cols), f32)],
        "join_post",
        (pack, post, *time_norms),
    )
    members = unit_devices * half
    scaled, lam, grads = call(
        functools.partial(third_kernel, half),
        [
            ((groups, unit_rows), f32),
            ((groups, half * day_cols), f32),
            pltpu.HBM((members, groups, day_cols), f32),
        ],
        "time_gradient",
        (over_days(pack), high, low, more_high, more_low, norms, raised_units, ends),
        out_specs=[vmem, vmem, hbm],
        scratch_shapes=[pltpu.VMEM((groups, day_cols), f32), pltpu.SemaphoreType.DMA((members,))],
    )
    sent_scaled = to_other_half(scaled)
    all_grads = over_first_half(grads)
    (totals,) = call(
        functools.partial(fourth_kernel, half, unit_devices), [((groups, lanes), f32)], "unit_totals", (all_grads,)
    )
    unit_weights, time_weights = call(
        functools.partial(fifth_kernel, half, unit_devices),
        [((groups, unit_rows), f32), ((groups, day_cols), f32)],
        "scale_weights",
        (totals, scaled, all_grads, lam, norms, ends),
    )
    (unit_weights,) = call(
        functools.partial(sixth_kernel, half),
        [((groups, unit_rows), f32)],
        "other_half",
        (to_other_half(totals, half > 1), sent_scaled, unit_weights),
        in_specs=[vmem, vmem, hbm],
        out_specs=[hbm],
        input_output_aliases={2: 0},
        scratch_shapes=[pltpu.VMEM((groups, unit_rows), f32), pltpu.SemaphoreType.DMA((1,))],
    )
    return unit_weights, time_weights


def solution(mesh):
    return jax.shard_map(
        local,
        mesh=mesh,
        in_specs=(P("unit", "day"), P("unit"), P(), P(), P(None, "unit"), P(None, "day")),
        out_specs=(P(None, "unit"), P(None, "day")),
        check_vma=False,
    )
```

```python
import functools

import jax
import jax.numpy as jnp
from jax import lax
from jax.experimental import pallas as pl
from jax.experimental.pallas import tpu as pltpu
from jax.sharding import PartitionSpec as P

step_rate = 16.0
f32 = jnp.float32
bf16 = jnp.bfloat16
lanes = 128
block_rows = 512
params = pltpu.CompilerParams(vmem_limit_bytes=24 * 1024 * 1024)
vmem = pl.BlockSpec(memory_space=pltpu.VMEM)
hbm = pl.BlockSpec(memory_space=pltpu.HBM)


def split_left(value):
    first = value.astype(bf16).astype(f32)
    return [first, value - first]


def left_of(*values):
    return jnp.concatenate([term for value in values for term in split_left(value)], axis=0).astype(bf16)


def split_panel(value):
    high = value.astype(bf16)
    return high, (value - high.astype(f32)).astype(bf16)


def rows_dot(left, high, low):
    return jnp.dot(left, high, preferred_element_type=f32) + jnp.dot(left, low, preferred_element_type=f32)


def days_dot(left, high, low):
    dims = (((1,), (1,)), ((), ()))
    return lax.dot_general(left, high, dims, preferred_element_type=f32) + lax.dot_general(
        left, low, dims, preferred_element_type=f32
    )


def add_terms(stack, groups, place=0):
    return stack[2 * place * groups :][:groups] + stack[(2 * place + 1) * groups :][:groups]


def tree_sum(values):
    values = list(values)
    while len(values) > 1:
        values = [values[i] + values[i + 1] for i in range(0, len(values), 2)]
    return values[0]


def column(row_ref):
    count = row_ref.shape[1]
    wide = jnp.broadcast_to(row_ref[...].astype(f32), (count, count))
    row = lax.broadcasted_iota(jnp.int32, (count, count), 0)
    lane = lax.broadcasted_iota(jnp.int32, (count, count), 1)
    return jnp.sum(jnp.where(row == lane, wide, 0.0), axis=1, keepdims=True).astype(jnp.int32)


def days_of(device, shape):
    return device * shape[1] + lax.broadcasted_iota(jnp.int32, shape, 1)


def first_half_only(kernel):
    @functools.wraps(kernel)
    def guarded(half, *refs):
        @pl.when(lax.axis_index("day") < half)
        def _():
            kernel(half, *refs)

    return guarded


def fetch(sources, targets, sems):
    copies = [pltpu.make_async_copy(*pair, sems.at[i]) for i, pair in enumerate(zip(sources, targets))]
    for copy in copies:
        copy.start()
    return copies


def fetch_rows(source, target, sems, starts):
    spans = [(start, stop - start) for start, stop in zip(starts, starts[1:])]
    parts = [pl.ds(*span) for span in spans]
    copies = fetch([source.at[here] for here in parts], [target.at[here] for here in parts], sems)
    return [(*span, copy) for span, copy in zip(spans, copies)]


def blocks_of(start, rows):
    return [pl.ds(here, block_rows) for here in range(start, start + rows, block_rows)]


def wait_all(copies):
    for copy in copies:
        copy.wait()


def first_kernel(all_count, half, starts, *refs):
    arguments, refs = refs[:6], refs[6:]
    out, cross, raised_days, time_norm, ends, high_ref, low_ref, *held, left_ref, cross_block, small_sems, panel_sems, out_sem = refs
    groups, day_cols = held[5].shape
    unit_rows, resident = held[0].shape[0], high_ref.shape[0]
    (post_copy,) = fetch(arguments[3:4], held[3:4], small_sems)
    unit_copies = fetch(arguments[1:5:3], held[1:5:3], small_sems.at[pl.ds(1, 2)])
    parts = fetch_rows(arguments[0], held[0], panel_sems, starts)
    day_copies = fetch(arguments[2:6:3], held[2:6:3], small_sems.at[pl.ds(3, 2)])
    panel, cohort, pre_row, post_row, unit_logit, time_logit = held
    post_copy.wait()
    wait_all(unit_copies)
    me = lax.axis_index("day")

    @pl.when(me < half)
    def _():
        label = lax.broadcasted_iota(jnp.int32, (groups, unit_rows), 0)
        treated = jnp.where(cohort[...] == label, 1.0, 0.0)
        control = jnp.where(cohort[...] > label, 1.0, 0.0)
        raised = jnp.exp(unit_logit[...]) * control
        left_ref[...] = left_of(raised, treated)
        lane = lax.broadcasted_iota(jnp.int32, (groups, lanes), 1)
        counts = [jnp.sum(value, axis=1, keepdims=True) for value in (raised, treated, control)]
        slot = lax.broadcasted_iota(jnp.int32, (groups, lanes), 0)
        norms = jnp.zeros((groups, lanes), f32)
        for i, count in enumerate(counts):
            norms += jnp.where(lane == i * groups + slot, count, 0.0)
        norms = jnp.sum(norms, axis=0, keepdims=True)
        product = jnp.zeros((4 * groups, 2 * day_cols), f32)
        for start, rows, copy in parts:
            copy.wait()
            for here in blocks_of(start, rows):
                high, low = split_panel(panel[here, :])
                if here.start < resident:
                    high_ref[here, :] = high
                    low_ref[here, :] = low
                both = jnp.concatenate([high, low], axis=1)
                product += jnp.dot(left_ref[:, here], both, preferred_element_type=f32)
        product = product[:, :day_cols] + product[:, day_cols:]
        both_sums = jnp.concatenate([add_terms(product, groups), product[2 * groups :][:groups]], axis=0)
        for member in range(out.shape[0]):
            for row in range(2 * groups):
                out[member, :, row * day_cols : (row + 1) * day_cols] = both_sums[row : row + 1, :]
            out[member, :, 2 * groups * day_cols :] = norms
        wait_all(day_copies)
        pre_end = column(pre_row)
        ends[...] = jnp.broadcast_to(pre_end.astype(f32), ends.shape)
        before = days_of(me, (groups, day_cols)) < pre_end
        raised_time = jnp.where(before, jnp.exp(time_logit[...]), 0.0)
        raised_days[...] = raised_time
        time_norm[...] = jnp.broadcast_to(jnp.sum(raised_time, axis=1, keepdims=True), time_norm.shape)

    @pl.when(me >= half)
    def _():
        post_start = column(post_row)
        after = jnp.where(days_of(me, (groups, day_cols)) >= post_start, 1.0, 0.0)
        left = left_of(after / (all_count - post_start).astype(f32))
        for start, rows, copy in parts:
            copy.wait()
            for here in blocks_of(start, rows):
                cross_block[:, here] = add_terms(days_dot(left, *split_panel(panel[here, :])), groups)
        sends = fetch([cross_block], [cross], out_sem)
        wait_all(day_copies)
        wait_all(sends)


@first_half_only
def second_kernel(half, unit_devices, panel, cohort, unit_logit, sums, raised_days, ends, high_ref, low_ref, *refs):
    pack, norms, raised_units, more_high, more_low, held, held_cohort, held_logit, sems = refs
    groups, day_cols = raised_days.shape
    unit_rows, resident = panel.shape[0], high_ref.shape[0]
    rest = pl.ds(resident, unit_rows - resident)
    copies = fetch([panel.at[rest], cohort, unit_logit], [held, held_cohort, held_logit], sems)

    @pl.when(lax.axis_index("day") < half)
    def _():
        total = tree_sum(sums[u] for u in range(unit_devices))

        def group_rows(first):
            starts = [(first + row) * day_cols for row in range(groups)]
            return jnp.concatenate([total[:, start : start + day_cols] for start in starts], axis=0)

        counts = jnp.broadcast_to(total[:, 2 * groups * day_cols :], (groups, lanes))
        slot = lax.broadcasted_iota(jnp.int32, (groups, lanes), 0)
        lane = lax.broadcasted_iota(jnp.int32, (groups, lanes), 1)
        unit_norm, treat_count, ctrl_count = [
            jnp.sum(jnp.where(lane == i * groups + slot, counts, 0.0), axis=1, keepdims=True) for i in range(3)
        ]
        norms[...] = jnp.where(lane == 0, unit_norm, ctrl_count)
        gap = group_rows(0) / unit_norm - group_rows(groups) / jnp.maximum(treat_count, 1.0)
        before = days_of(lax.axis_index("day"), (groups, day_cols)).astype(f32) < ends[:, 0:1]
        raised_time = raised_days[...]
        pack[:groups, unit_rows:] = raised_time
        pack[groups:, unit_rows:] = jnp.zeros_like(raised_time)
        left = left_of(jnp.where(before, gap, 0.0), raised_time)

        def multiply(here, high, low):
            product = days_dot(left, high, low)
            pack[:groups, here] = add_terms(product, groups)
            pack[groups:, here] = add_terms(product, groups, 1)

        late = resident - 2 * block_rows

        @pl.loop(0, late // block_rows)
        def _(block):
            here = pl.ds(pl.multiple_of(block * block_rows, block_rows), block_rows)
            multiply(here, high_ref[here, :], low_ref[here, :])

        wait_all(copies)
        label = lax.broadcasted_iota(jnp.int32, raised_units.shape, 0)
        raised_units[...] = jnp.where(held_cohort[...] > label, jnp.exp(held_logit[...]), 0.0)
        for there in blocks_of(0, unit_rows - resident):
            more_high[there, :], more_low[there, :] = split_panel(held[there, :])
        for here in blocks_of(late, resident - late):
            multiply(here, high_ref[here, :], low_ref[here, :])
        for there in blocks_of(0, unit_rows - resident):
            multiply(pl.ds(resident + there.start, block_rows), more_high[there, :], more_low[there, :])


@first_half_only
def join_kernel(half, pack, post, *refs):
    norms, out = refs[:half], refs[half]
    groups, unit_rows = post.shape
    over_time = 1.0 / tree_sum(ref[:, 0:1] for ref in norms)
    out[:groups, :unit_rows] = pack[:groups, :unit_rows]
    out[:groups, unit_rows:] = pack[:groups, unit_rows:] * over_time
    out[groups:, :unit_rows] = pack[groups:, :unit_rows] * over_time - post[...]
    out[groups:, unit_rows:] = pack[groups:, unit_rows:]


@first_half_only
def third_kernel(half, *refs):
    parts, refs = [refs[0].at[day] for day in range(half)], refs[1:]
    high_ref, low_ref, more_high, more_low, norms, raised_units, ends, scaled, lam, out = refs
    groups, unit_rows = raised_units.shape
    resident, day_cols = high_ref.shape
    unit_norm, ctrl_count = norms[:, 0:1], norms[:, 1:2]
    factor = -step_rate / jnp.sqrt(ends[:, 0:1])
    over_unit = 1.0 / unit_norm
    me = lax.rem(lax.axis_index("day"), half)
    for day in range(half):
        lam[:, day * day_cols : (day + 1) * day_cols] = parts[day][:groups, unit_rows:]
    time_grad = jnp.zeros((2 * groups, 2 * day_cols), f32)
    new_sum = jnp.zeros((groups, 1), f32)
    for start in range(0, unit_rows, block_rows):
        here = pl.ds(start, block_rows)
        whole = tree_sum(ref[:, here] for ref in parts)
        raised = raised_units[:, here]
        new = raised * over_unit * jnp.exp(whole[:groups] * factor)
        new_sum += jnp.sum(new, axis=1, keepdims=True)
        scaled[:, here] = new * ctrl_count
        left = left_of(jnp.where(raised > 0.0, whole[groups:], 0.0))
        if start < resident:
            high, low = high_ref[here, :], low_ref[here, :]
        else:
            there = pl.ds(start - resident, block_rows)
            high, low = more_high[there, :], more_low[there, :]
        time_grad += jnp.dot(left, jnp.concatenate([high, low], axis=1), preferred_element_type=f32)
    time_grad = add_terms(time_grad[:, :day_cols] + time_grad[:, day_cols:], groups)
    lane = lax.broadcasted_iota(jnp.int32, (groups, day_cols), 1)
    spare = (lane == day_cols - 1) & (me == half - 1)
    block = jnp.where(spare, new_sum, time_grad)
    for member in range(out.shape[0]):
        out[member] = block


def time_grad_of(grads, unit_devices, half, day):
    return tree_sum(grads[unit * half + half - 1 - day] for unit in range(unit_devices))


@first_half_only
def fourth_kernel(half, unit_devices, grads, totals):
    day_cols = grads.shape[2]
    last = time_grad_of(grads, unit_devices, half, half - 1)
    totals[...] = jnp.broadcast_to(last[:, day_cols - 1 :], totals.shape)


def fifth_kernel(half, unit_devices, totals, scaled, grads, lam, norms, ends, unit_weights, time_weights):
    groups, day_cols = time_weights.shape
    me = lax.axis_index("day")

    @pl.when(me < half)
    def _():
        unit_weights[...] = scaled[...] * (1.0 / totals[:, 0:1])
        root = jnp.sqrt(jnp.maximum(norms[:, 1:2], 1.0))
        moved_total = jnp.zeros((groups, 1), f32)
        own = jnp.zeros((groups, day_cols), f32)
        for day in range(half):
            total = time_grad_of(grads, unit_devices, half, day)
            moved = lam[:, day * day_cols : (day + 1) * day_cols] * jnp.exp(total * (-step_rate / root))
            moved_total += jnp.sum(moved, axis=1, keepdims=True)
            own = jnp.where(me == day, moved, own)
        time_weights[...] = own * (ends[:, 0:1] / moved_total)

    @pl.when(me >= half)
    def _():
        time_weights[...] = jnp.zeros_like(time_weights)


def sixth_kernel(half, sent_totals, sent_scaled, _, unit_weights, block, out_sem):
    @pl.when(lax.axis_index("day") >= half)
    def _():
        block[...] = sent_scaled[...] * (1.0 / sent_totals[:, 0:1])
        wait_all(fetch([block], [unit_weights], out_sem))


def local(outcomes, cohort, pre_end, post_start, unit_logit, time_logit):
    groups = pre_end.shape[0]
    unit_rows, day_cols = outcomes.shape
    day_devices = lax.axis_size("day")
    unit_devices = lax.axis_size("unit")
    half = day_devices // 2
    assert half * 2 == day_devices and half & (half - 1) == 0
    assert unit_devices & (unit_devices - 1) == 0
    panel_starts = [0, unit_rows // 4, unit_rows // 8 * 5, unit_rows]
    resident = unit_rows * 3 // 4 // block_rows * block_rows
    def meeting_at(first):
        return [first] + [unit for unit in reversed(range(unit_devices)) if unit != first]

    middle = unit_devices // 2

    def to_other_half(value, day_xor=0):
        pairs = [
            (u * day_devices + d, u * day_devices + half + (d ^ day_xor)) for u in range(unit_devices) for d in range(half)
        ]
        return lax.ppermute(value, ("unit", "day"), pairs)

    def over_days(value):
        halves = [list(range(half)), list(range(half, day_devices))]
        return lax.all_gather(value, "day", axis_index_groups=halves)

    def over_first_half(value):
        members = [
            [unit * day_devices + day for unit in meeting_at(middle + 1) for day in reversed(days)]
            for days in (range(half), range(half, day_devices))
        ]
        return lax.all_to_all(
            value, ("unit", "day"), split_axis=0, concat_axis=0, axis_index_groups=members, tiled=True
        )

    def over_units(value):
        members = [
            [unit * day_devices + day for unit in meeting_at(middle - 1 if day < half else middle)]
            for day in range(day_devices)
        ]
        return lax.all_to_all(
            value, ("unit", "day"), split_axis=0, concat_axis=0, axis_index_groups=members, tiled=True
        )

    def call(kernel, shapes, name, args, in_specs=None, out_specs=None, **more):
        return pl.pallas_call(
            kernel,
            in_specs=in_specs or [vmem] * len(args),
            out_specs=out_specs or [vmem] * len(shapes),
            out_shape=[
                shape if isinstance(shape, type(in_vmem)) else jax.ShapeDtypeStruct(*shape) for shape in shapes
            ],
            compiler_params=params,
            name=name,
            **more,
        )(*args)

    arguments = (outcomes, cohort[None, :], pre_end[None, :], post_start[None, :], unit_logit, time_logit)
    fixed = [pltpu.with_memory_space_constraint(argument, pltpu.HBM) for argument in arguments]
    held = [pltpu.VMEM(argument.shape, argument.dtype) for argument in arguments]
    small_sems, panel_sems = pltpu.SemaphoreType.DMA((5,)), pltpu.SemaphoreType.DMA((3,))
    panel_terms = [((resident, day_cols), bf16)] * 2
    other_terms = [((unit_rows - resident, day_cols), bf16)] * 2
    width = 2 * groups * day_cols + lanes
    in_vmem = pltpu.VMEM((unit_devices, 1, width), f32)
    sums, cross, raised_days, time_norm, ends, high, low = call(
        functools.partial(first_kernel, day_devices * day_cols, half, panel_starts),
        [
            in_vmem,
            pltpu.HBM((groups, unit_rows), f32),
            ((groups, day_cols), f32),
            ((groups, lanes), f32),
            ((groups, lanes), f32),
            *panel_terms,
        ],
        "first_product",
        fixed,
        in_specs=[hbm] * 6,
        out_specs=[vmem, hbm] + [vmem] * 5,
        scratch_shapes=held
        + [
            pltpu.VMEM((4 * groups, unit_rows), bf16),
            pltpu.VMEM((groups, unit_rows), f32),
            small_sems,
            panel_sems,
            pltpu.SemaphoreType.DMA((1,)),
        ],
    )
    downward = [
        (u * day_devices + d + half, u * day_devices + d) for u in range(unit_devices) for d in range(half)
    ]
    post = lax.ppermute(cross, ("unit", "day"), downward)
    pack, norms, raised_units, more_high, more_low = call(
        functools.partial(second_kernel, half, unit_devices),
        [
            ((2 * groups, unit_rows + day_cols), f32),
            ((groups, lanes), f32),
            ((groups, unit_rows), f32),
            *other_terms,
        ],
        "unit_gradient",
        (fixed[0], fixed[1], fixed[4], over_units(sums), raised_days, ends, high, low),
        in_specs=[hbm] * 3 + [vmem] * 5,
        scratch_shapes=[
            pltpu.VMEM((unit_rows - resident, day_cols), f32),
            held[1],
            held[4],
            pltpu.SemaphoreType.DMA((3,)),
        ],
    )
    time_norms = [time_norm]
    for k in range(1, half):
        pairs = [(u * day_devices + d, u * day_devices + (d ^ k)) for u in range(unit_devices) for d in range(half)]
        time_norms.append(lax.ppermute(time_norm, ("unit", "day"), pairs))
    (pack,) = call(
        functools.partial(join_kernel, half),
        [((2 * groups, unit_rows + day_cols), f32)],
        "join_post",
        (pack, post, *time_norms),
    )
    members = unit_devices * half
    scaled, lam, grads = call(
        functools.partial(third_kernel, half),
        [
            ((groups, unit_rows), f32),
            ((groups, half * day_cols), f32),
            pltpu.VMEM((members, groups, day_cols), f32),
        ],
        "time_gradient",
        (over_days(pack), high, low, more_high, more_low, norms, raised_units, ends),
    )
    sent_scaled = to_other_half(scaled)
    all_grads = over_first_half(grads)
    (totals,) = call(
        functools.partial(fourth_kernel, half, unit_devices), [((groups, lanes), f32)], "unit_totals", (all_grads,)
    )
    unit_weights, time_weights = call(
        functools.partial(fifth_kernel, half, unit_devices),
        [((groups, unit_rows), f32), ((groups, day_cols), f32)],
        "scale_weights",
        (totals, scaled, all_grads, lam, norms, ends),
    )
    (unit_weights,) = call(
        functools.partial(sixth_kernel, half),
        [((groups, unit_rows), f32)],
        "other_half",
        (to_other_half(totals, half > 1), sent_scaled, unit_weights),
        in_specs=[vmem, vmem, hbm],
        out_specs=[hbm],
        input_output_aliases={2: 0},
        scratch_shapes=[pltpu.VMEM((groups, unit_rows), f32), pltpu.SemaphoreType.DMA((1,))],
    )
    return unit_weights, time_weights


def solution(mesh):
    return jax.shard_map(
        local,
        mesh=mesh,
        in_specs=(P("unit", "day"), P("unit"), P(), P(), P(None, "unit"), P(None, "day")),
        out_specs=(P(None, "unit"), P(None, "day")),
        check_vma=False,
    )
```

```python
import functools

import jax
import jax.numpy as jnp
from jax import lax
from jax.experimental import pallas as pl
from jax.experimental.pallas import tpu as pltpu
from jax.sharding import PartitionSpec as P

step_rate = 16.0
f32 = jnp.float32
bf16 = jnp.bfloat16
lanes = 128
block_rows = 512
params = pltpu.CompilerParams(vmem_limit_bytes=24 * 1024 * 1024)
vmem = pl.BlockSpec(memory_space=pltpu.VMEM)
hbm = pl.BlockSpec(memory_space=pltpu.HBM)


def split_left(value):
    first = value.astype(bf16).astype(f32)
    return [first, value - first]


def left_of(*values):
    return jnp.concatenate([term for value in values for term in split_left(value)], axis=0).astype(bf16)


def split_panel(value):
    high = value.astype(bf16)
    return high, (value - high.astype(f32)).astype(bf16)


def rows_dot(left, high, low):
    return jnp.dot(left, high, preferred_element_type=f32) + jnp.dot(left, low, preferred_element_type=f32)


def days_dot(left, high, low):
    dims = (((1,), (1,)), ((), ()))
    return lax.dot_general(left, high, dims, preferred_element_type=f32) + lax.dot_general(
        left, low, dims, preferred_element_type=f32
    )


def add_terms(stack, groups, place=0):
    return stack[2 * place * groups :][:groups] + stack[(2 * place + 1) * groups :][:groups]


def tree_sum(values):
    values = list(values)
    while len(values) > 1:
        values = [values[i] + values[i + 1] for i in range(0, len(values), 2)]
    return values[0]


def column(row_ref):
    count = row_ref.shape[1]
    wide = jnp.broadcast_to(row_ref[...].astype(f32), (count, count))
    row = lax.broadcasted_iota(jnp.int32, (count, count), 0)
    lane = lax.broadcasted_iota(jnp.int32, (count, count), 1)
    return jnp.sum(jnp.where(row == lane, wide, 0.0), axis=1, keepdims=True).astype(jnp.int32)


def days_of(device, shape):
    return device * shape[1] + lax.broadcasted_iota(jnp.int32, shape, 1)


def first_half_only(kernel):
    @functools.wraps(kernel)
    def guarded(half, *refs):
        @pl.when(lax.axis_index("day") < half)
        def _():
            kernel(half, *refs)

    return guarded


def fetch(sources, targets, sems):
    copies = [pltpu.make_async_copy(*pair, sems.at[i]) for i, pair in enumerate(zip(sources, targets))]
    for copy in copies:
        copy.start()
    return copies


def fetch_rows(source, target, sems, starts):
    spans = [(start, stop - start) for start, stop in zip(starts, starts[1:])]
    parts = [pl.ds(*span) for span in spans]
    copies = fetch([source.at[here] for here in parts], [target.at[here] for here in parts], sems)
    return [(*span, copy) for span, copy in zip(spans, copies)]


def blocks_of(start, rows):
    return [pl.ds(here, block_rows) for here in range(start, start + rows, block_rows)]


def wait_all(copies):
    for copy in copies:
        copy.wait()


def repeat_start(block, out, sems):
    places = [out.at[i] for i in range(out.shape[0])]
    return fetch([block] * len(places), places, sems)


def first_kernel(all_count, half, starts, *refs):
    arguments, refs = refs[:6], refs[6:]
    out, cross, raised_days, time_norm, ends, high_ref, low_ref, *held, block, left_ref, cross_block, small_sems, panel_sems, out_sems = refs
    groups, day_cols = held[5].shape
    unit_rows, resident = held[0].shape[0], high_ref.shape[0]
    (post_copy,) = fetch(arguments[3:4], held[3:4], small_sems)
    unit_copies = fetch(arguments[1:5:3], held[1:5:3], small_sems.at[pl.ds(1, 2)])
    parts = fetch_rows(arguments[0], held[0], panel_sems, starts)
    day_copies = fetch(arguments[2:6:3], held[2:6:3], small_sems.at[pl.ds(3, 2)])
    panel, cohort, pre_row, post_row, unit_logit, time_logit = held
    post_copy.wait()
    wait_all(unit_copies)
    me = lax.axis_index("day")

    @pl.when(me < half)
    def _():
        label = lax.broadcasted_iota(jnp.int32, (groups, unit_rows), 0)
        treated = jnp.where(cohort[...] == label, 1.0, 0.0)
        control = jnp.where(cohort[...] > label, 1.0, 0.0)
        raised = jnp.exp(unit_logit[...]) * control
        left_ref[...] = left_of(raised, treated)
        lane = lax.broadcasted_iota(jnp.int32, (groups, lanes), 1)
        counts = [jnp.sum(value, axis=1, keepdims=True) for value in (raised, treated, control)]
        slot = lax.broadcasted_iota(jnp.int32, (groups, lanes), 0)
        norms = jnp.zeros((groups, lanes), f32)
        for i, count in enumerate(counts):
            norms += jnp.where(lane == i * groups + slot, count, 0.0)
        block[:, 2 * groups * day_cols :] = jnp.sum(norms, axis=0, keepdims=True)
        product = jnp.zeros((4 * groups, day_cols), f32)
        for start, rows, copy in parts:
            copy.wait()
            for here in blocks_of(start, rows):
                high, low = split_panel(panel[here, :])
                if here.start < resident:
                    high_ref[here, :] = high
                    low_ref[here, :] = low
                product += rows_dot(left_ref[:, here], high, low)
        both_sums = jnp.concatenate([add_terms(product, groups), product[2 * groups :][:groups]], axis=0)
        for row in range(2 * groups):
            block[:, row * day_cols : (row + 1) * day_cols] = both_sums[row : row + 1, :]
        sends = repeat_start(block, out, out_sems)
        wait_all(day_copies)
        pre_end = column(pre_row)
        ends[...] = jnp.broadcast_to(pre_end.astype(f32), ends.shape)
        before = days_of(me, (groups, day_cols)) < pre_end
        raised_time = jnp.where(before, jnp.exp(time_logit[...]), 0.0)
        raised_days[...] = raised_time
        time_norm[...] = jnp.broadcast_to(jnp.sum(raised_time, axis=1, keepdims=True), time_norm.shape)
        wait_all(sends)

    @pl.when(me >= half)
    def _():
        post_start = column(post_row)
        after = jnp.where(days_of(me, (groups, day_cols)) >= post_start, 1.0, 0.0)
        left = left_of(after / (all_count - post_start).astype(f32))
        for start, rows, copy in parts:
            copy.wait()
            for here in blocks_of(start, rows):
                cross_block[:, here] = add_terms(days_dot(left, *split_panel(panel[here, :])), groups)
        sends = fetch([cross_block], [cross], out_sems)
        wait_all(day_copies)
        wait_all(sends)


@first_half_only
def second_kernel(half, unit_devices, panel, cohort, unit_logit, sums, raised_days, ends, high_ref, low_ref, *refs):
    pack, norms, raised_units, more_high, more_low, held, held_cohort, held_logit, sems = refs
    groups, day_cols = raised_days.shape
    unit_rows, resident = panel.shape[0], high_ref.shape[0]
    rest = pl.ds(resident, unit_rows - resident)
    copies = fetch([panel.at[rest], cohort, unit_logit], [held, held_cohort, held_logit], sems)

    @pl.when(lax.axis_index("day") < half)
    def _():
        total = tree_sum(sums[u] for u in range(unit_devices))

        def group_rows(first):
            starts = [(first + row) * day_cols for row in range(groups)]
            return jnp.concatenate([total[:, start : start + day_cols] for start in starts], axis=0)

        counts = jnp.broadcast_to(total[:, 2 * groups * day_cols :], (groups, lanes))
        slot = lax.broadcasted_iota(jnp.int32, (groups, lanes), 0)
        lane = lax.broadcasted_iota(jnp.int32, (groups, lanes), 1)
        unit_norm, treat_count, ctrl_count = [
            jnp.sum(jnp.where(lane == i * groups + slot, counts, 0.0), axis=1, keepdims=True) for i in range(3)
        ]
        norms[...] = jnp.where(lane == 0, unit_norm, ctrl_count)
        gap = group_rows(0) / unit_norm - group_rows(groups) / jnp.maximum(treat_count, 1.0)
        before = days_of(lax.axis_index("day"), (groups, day_cols)).astype(f32) < ends[:, 0:1]
        raised_time = raised_days[...]
        pack[:groups, unit_rows:] = raised_time
        pack[groups:, unit_rows:] = jnp.zeros_like(raised_time)
        left = left_of(jnp.where(before, gap, 0.0), raised_time)

        def multiply(here, high, low):
            product = days_dot(left, high, low)
            pack[:groups, here] = add_terms(product, groups)
            pack[groups:, here] = add_terms(product, groups, 1)

        late = resident - 2 * block_rows

        @pl.loop(0, late // block_rows)
        def _(block):
            here = pl.ds(pl.multiple_of(block * block_rows, block_rows), block_rows)
            multiply(here, high_ref[here, :], low_ref[here, :])

        wait_all(copies)
        label = lax.broadcasted_iota(jnp.int32, raised_units.shape, 0)
        raised_units[...] = jnp.where(held_cohort[...] > label, jnp.exp(held_logit[...]), 0.0)
        for there in blocks_of(0, unit_rows - resident):
            more_high[there, :], more_low[there, :] = split_panel(held[there, :])
        for here in blocks_of(late, resident - late):
            multiply(here, high_ref[here, :], low_ref[here, :])
        for there in blocks_of(0, unit_rows - resident):
            multiply(pl.ds(resident + there.start, block_rows), more_high[there, :], more_low[there, :])


@first_half_only
def join_kernel(half, pack, post, *refs):
    norms, out = refs[:half], refs[half]
    groups, unit_rows = post.shape
    over_time = 1.0 / tree_sum(ref[:, 0:1] for ref in norms)
    out[:groups, :unit_rows] = pack[:groups, :unit_rows]
    out[:groups, unit_rows:] = pack[:groups, unit_rows:] * over_time
    out[groups:, :unit_rows] = pack[groups:, :unit_rows] * over_time - post[...]
    out[groups:, unit_rows:] = pack[groups:, unit_rows:]


@first_half_only
def third_kernel(half, *refs):
    parts, refs = [refs[0].at[day] for day in range(half)], refs[1:]
    high_ref, low_ref, more_high, more_low, norms, raised_units, ends, scaled, lam, out = refs
    groups, unit_rows = raised_units.shape
    resident, day_cols = high_ref.shape
    unit_norm, ctrl_count = norms[:, 0:1], norms[:, 1:2]
    factor = -step_rate / jnp.sqrt(ends[:, 0:1])
    over_unit = 1.0 / unit_norm
    me = lax.rem(lax.axis_index("day"), half)
    for day in range(half):
        lam[:, day * day_cols : (day + 1) * day_cols] = parts[day][:groups, unit_rows:]
    time_grad = jnp.zeros((groups, day_cols), f32)
    new_sum = jnp.zeros((groups, 1), f32)
    for start in range(0, unit_rows, block_rows):
        here = pl.ds(start, block_rows)
        whole = tree_sum(ref[:, here] for ref in parts)
        raised = raised_units[:, here]
        new = raised * over_unit * jnp.exp(whole[:groups] * factor)
        new_sum += jnp.sum(new, axis=1, keepdims=True)
        scaled[:, here] = new * ctrl_count
        left = left_of(jnp.where(raised > 0.0, whole[groups:], 0.0))
        if start < resident:
            high, low = high_ref[here, :], low_ref[here, :]
        else:
            there = pl.ds(start - resident, block_rows)
            high, low = more_high[there, :], more_low[there, :]
        time_grad += add_terms(rows_dot(left, high, low), groups)
    lane = lax.broadcasted_iota(jnp.int32, (groups, day_cols), 1)
    spare = (lane == day_cols - 1) & (me == half - 1)
    block = jnp.where(spare, new_sum, time_grad)
    for member in range(out.shape[0]):
        out[member] = block


def time_grad_of(grads, unit_devices, half, day):
    return tree_sum(grads[unit * half + half - 1 - day] for unit in range(unit_devices))


@first_half_only
def fourth_kernel(half, unit_devices, grads, totals):
    day_cols = grads.shape[2]
    last = time_grad_of(grads, unit_devices, half, half - 1)
    totals[...] = jnp.broadcast_to(last[:, day_cols - 1 :], totals.shape)


def fifth_kernel(half, unit_devices, totals, scaled, grads, lam, norms, ends, unit_weights, time_weights):
    groups, day_cols = time_weights.shape
    me = lax.axis_index("day")

    @pl.when(me < half)
    def _():
        unit_weights[...] = scaled[...] * (1.0 / totals[:, 0:1])
        root = jnp.sqrt(jnp.maximum(norms[:, 1:2], 1.0))
        moved_total = jnp.zeros((groups, 1), f32)
        own = jnp.zeros((groups, day_cols), f32)
        for day in range(half):
            total = time_grad_of(grads, unit_devices, half, day)
            moved = lam[:, day * day_cols : (day + 1) * day_cols] * jnp.exp(total * (-step_rate / root))
            moved_total += jnp.sum(moved, axis=1, keepdims=True)
            own = jnp.where(me == day, moved, own)
        time_weights[...] = own * (ends[:, 0:1] / moved_total)

    @pl.when(me >= half)
    def _():
        time_weights[...] = jnp.zeros_like(time_weights)


def sixth_kernel(half, sent_totals, sent_scaled, _, unit_weights, block, out_sem):
    @pl.when(lax.axis_index("day") >= half)
    def _():
        block[...] = sent_scaled[...] * (1.0 / sent_totals[:, 0:1])
        wait_all(fetch([block], [unit_weights], out_sem))


def local(outcomes, cohort, pre_end, post_start, unit_logit, time_logit):
    groups = pre_end.shape[0]
    unit_rows, day_cols = outcomes.shape
    day_devices = lax.axis_size("day")
    unit_devices = lax.axis_size("unit")
    half = day_devices // 2
    assert half * 2 == day_devices and half & (half - 1) == 0
    assert unit_devices & (unit_devices - 1) == 0
    panel_starts = [0, unit_rows // 8 * 3, unit_rows // 4 * 3, unit_rows]
    resident = unit_rows * 3 // 4 // block_rows * block_rows
    def meeting_at(first):
        return [first] + [unit for unit in reversed(range(unit_devices)) if unit != first]

    middle = unit_devices // 2

    def to_other_half(value, day_xor=0):
        pairs = [
            (u * day_devices + d, u * day_devices + half + (d ^ day_xor)) for u in range(unit_devices) for d in range(half)
        ]
        return lax.ppermute(value, ("unit", "day"), pairs)

    def over_days(value):
        halves = [list(range(half)), list(range(half, day_devices))]
        return lax.all_gather(value, "day", axis_index_groups=halves)

    def over_first_half(value):
        members = [
            [unit * day_devices + day for unit in meeting_at(middle + 1) for day in reversed(days)]
            for days in (range(half), range(half, day_devices))
        ]
        return lax.all_to_all(
            value, ("unit", "day"), split_axis=0, concat_axis=0, axis_index_groups=members, tiled=True
        )

    def over_units(value):
        members = [
            [unit * day_devices + day for unit in meeting_at(middle - 1 if day < half else middle)]
            for day in range(day_devices)
        ]
        return lax.all_to_all(
            value, ("unit", "day"), split_axis=0, concat_axis=0, axis_index_groups=members, tiled=True
        )

    def call(kernel, shapes, name, args, in_specs=None, out_specs=None, **more):
        return pl.pallas_call(
            kernel,
            in_specs=in_specs or [vmem] * len(args),
            out_specs=out_specs or [vmem] * len(shapes),
            out_shape=[
                shape if isinstance(shape, type(in_hbm)) else jax.ShapeDtypeStruct(*shape) for shape in shapes
            ],
            compiler_params=params,
            name=name,
            **more,
        )(*args)

    arguments = (outcomes, cohort[None, :], pre_end[None, :], post_start[None, :], unit_logit, time_logit)
    fixed = [pltpu.with_memory_space_constraint(argument, pltpu.HBM) for argument in arguments]
    held = [pltpu.VMEM(argument.shape, argument.dtype) for argument in arguments]
    small_sems, panel_sems = pltpu.SemaphoreType.DMA((5,)), pltpu.SemaphoreType.DMA((3,))
    panel_terms = [((resident, day_cols), bf16)] * 2
    other_terms = [((unit_rows - resident, day_cols), bf16)] * 2
    out_sems = pltpu.SemaphoreType.DMA((unit_devices,))
    width = 2 * groups * day_cols + lanes
    in_hbm = pltpu.HBM((unit_devices, 1, width), f32)
    sums, cross, raised_days, time_norm, ends, high, low = call(
        functools.partial(first_kernel, day_devices * day_cols, half, panel_starts),
        [
            in_hbm,
            pltpu.HBM((groups, unit_rows), f32),
            ((groups, day_cols), f32),
            ((groups, lanes), f32),
            ((groups, lanes), f32),
            *panel_terms,
        ],
        "first_product",
        fixed,
        in_specs=[hbm] * 6,
        out_specs=[hbm, hbm] + [vmem] * 5,
        scratch_shapes=held
        + [
            pltpu.VMEM((1, width), f32),
            pltpu.VMEM((4 * groups, unit_rows), bf16),
            pltpu.VMEM((groups, unit_rows), f32),
            small_sems,
            panel_sems,
            out_sems,
        ],
    )
    downward = [
        (u * day_devices + d + half, u * day_devices + d) for u in range(unit_devices) for d in range(half)
    ]
    post = lax.ppermute(cross, ("unit", "day"), downward)
    pack, norms, raised_units, more_high, more_low = call(
        functools.partial(second_kernel, half, unit_devices),
        [
            ((2 * groups, unit_rows + day_cols), f32),
            ((groups, lanes), f32),
            ((groups, unit_rows), f32),
            *other_terms,
        ],
        "unit_gradient",
        (fixed[0], fixed[1], fixed[4], over_units(sums), raised_days, ends, high, low),
        in_specs=[hbm] * 3 + [vmem] * 5,
        scratch_shapes=[
            pltpu.VMEM((unit_rows - resident, day_cols), f32),
            held[1],
            held[4],
            pltpu.SemaphoreType.DMA((3,)),
        ],
    )
    time_norms = [time_norm]
    for k in range(1, half):
        pairs = [(u * day_devices + d, u * day_devices + (d ^ k)) for u in range(unit_devices) for d in range(half)]
        time_norms.append(lax.ppermute(time_norm, ("unit", "day"), pairs))
    (pack,) = call(
        functools.partial(join_kernel, half),
        [((2 * groups, unit_rows + day_cols), f32)],
        "join_post",
        (pack, post, *time_norms),
    )
    members = unit_devices * half
    scaled, lam, grads = call(
        functools.partial(third_kernel, half),
        [
            ((groups, unit_rows), f32),
            ((groups, half * day_cols), f32),
            ((members, groups, day_cols), f32),
        ],
        "time_gradient",
        (over_days(pack), high, low, more_high, more_low, norms, raised_units, ends),
    )
    sent_scaled = to_other_half(scaled)
    all_grads = over_first_half(grads)
    (totals,) = call(
        functools.partial(fourth_kernel, half, unit_devices), [((groups, lanes), f32)], "unit_totals", (all_grads,)
    )
    unit_weights, time_weights = call(
        functools.partial(fifth_kernel, half, unit_devices),
        [((groups, unit_rows), f32), ((groups, day_cols), f32)],
        "scale_weights",
        (totals, scaled, all_grads, lam, norms, ends),
    )
    (unit_weights,) = call(
        functools.partial(sixth_kernel, half),
        [((groups, unit_rows), f32)],
        "other_half",
        (to_other_half(totals, half > 1), sent_scaled, unit_weights),
        in_specs=[vmem, vmem, hbm],
        out_specs=[hbm],
        input_output_aliases={2: 0},
        scratch_shapes=[pltpu.VMEM((groups, unit_rows), f32), pltpu.SemaphoreType.DMA((1,))],
    )
    return unit_weights, time_weights


def solution(mesh):
    return jax.shard_map(
        local,
        mesh=mesh,
        in_specs=(P("unit", "day"), P("unit"), P(), P(), P(None, "unit"), P(None, "day")),
        out_specs=(P(None, "unit"), P(None, "day")),
        check_vma=False,
    )
```

```python
import functools

import jax
import jax.numpy as jnp
from jax import lax
from jax.experimental import pallas as pl
from jax.experimental.pallas import tpu as pltpu
from jax.sharding import PartitionSpec as P

step_rate = 16.0
f32 = jnp.float32
bf16 = jnp.bfloat16
lanes = 128
block_rows = 512
params = pltpu.CompilerParams(vmem_limit_bytes=24 * 1024 * 1024)
vmem = pl.BlockSpec(memory_space=pltpu.VMEM)
hbm = pl.BlockSpec(memory_space=pltpu.HBM)


def split_left(value):
    first = value.astype(bf16).astype(f32)
    return [first, value - first]


def left_of(*values):
    return jnp.concatenate([term for value in values for term in split_left(value)], axis=0).astype(bf16)


def split_panel(value):
    high = value.astype(bf16)
    return high, (value - high.astype(f32)).astype(bf16)


def rows_dot(left, high, low):
    return jnp.dot(left, high, preferred_element_type=f32) + jnp.dot(left, low, preferred_element_type=f32)


def days_dot(left, high, low):
    dims = (((1,), (1,)), ((), ()))
    return lax.dot_general(left, high, dims, preferred_element_type=f32) + lax.dot_general(
        left, low, dims, preferred_element_type=f32
    )


def add_terms(stack, groups, place=0):
    return stack[2 * place * groups :][:groups] + stack[(2 * place + 1) * groups :][:groups]


def tree_sum(values):
    values = list(values)
    while len(values) > 1:
        values = [values[i] + values[i + 1] for i in range(0, len(values), 2)]
    return values[0]


def column(row_ref):
    count = row_ref.shape[1]
    wide = jnp.broadcast_to(row_ref[...].astype(f32), (count, count))
    row = lax.broadcasted_iota(jnp.int32, (count, count), 0)
    lane = lax.broadcasted_iota(jnp.int32, (count, count), 1)
    return jnp.sum(jnp.where(row == lane, wide, 0.0), axis=1, keepdims=True).astype(jnp.int32)


def days_of(device, shape):
    return device * shape[1] + lax.broadcasted_iota(jnp.int32, shape, 1)


def first_half_only(kernel):
    @functools.wraps(kernel)
    def guarded(half, *refs):
        @pl.when(lax.axis_index("day") < half)
        def _():
            kernel(half, *refs)

    return guarded


def fetch(sources, targets, sems):
    copies = [pltpu.make_async_copy(*pair, sems.at[i]) for i, pair in enumerate(zip(sources, targets))]
    for copy in copies:
        copy.start()
    return copies


def fetch_rows(source, target, sems, starts):
    spans = [(start, stop - start) for start, stop in zip(starts, starts[1:])]
    parts = [pl.ds(*span) for span in spans]
    copies = fetch([source.at[here] for here in parts], [target.at[here] for here in parts], sems)
    return [(*span, copy) for span, copy in zip(spans, copies)]


def blocks_of(start, rows):
    return [pl.ds(here, block_rows) for here in range(start, start + rows, block_rows)]


def wait_all(copies):
    for copy in copies:
        copy.wait()


def repeat_start(block, out, sems):
    places = [out.at[i] for i in range(out.shape[0])]
    return fetch([block] * len(places), places, sems)


def first_kernel(all_count, half, starts, *refs):
    arguments, refs = refs[:6], refs[6:]
    out, cross, raised_days, time_norm, ends, high_ref, low_ref, *held, block, left_ref, cross_block, small_sems, panel_sems, out_sems = refs
    groups, day_cols = held[5].shape
    unit_rows, resident = held[0].shape[0], high_ref.shape[0]
    (post_copy,) = fetch(arguments[3:4], held[3:4], small_sems)
    unit_copies = fetch(arguments[1:5:3], held[1:5:3], small_sems.at[pl.ds(1, 2)])
    parts = fetch_rows(arguments[0], held[0], panel_sems, starts)
    day_copies = fetch(arguments[2:6:3], held[2:6:3], small_sems.at[pl.ds(3, 2)])
    panel, cohort, pre_row, post_row, unit_logit, time_logit = held
    post_copy.wait()
    wait_all(unit_copies)
    me = lax.axis_index("day")

    @pl.when(me < half)
    def _():
        label = lax.broadcasted_iota(jnp.int32, (groups, unit_rows), 0)
        treated = jnp.where(cohort[...] == label, 1.0, 0.0)
        control = jnp.where(cohort[...] > label, 1.0, 0.0)
        raised = jnp.exp(unit_logit[...]) * control
        left_ref[...] = left_of(raised, treated)
        lane = lax.broadcasted_iota(jnp.int32, (groups, lanes), 1)
        counts = [jnp.sum(value, axis=1, keepdims=True) for value in (raised, treated, control)]
        slot = lax.broadcasted_iota(jnp.int32, (groups, lanes), 0)
        norms = jnp.zeros((groups, lanes), f32)
        for i, count in enumerate(counts):
            norms += jnp.where(lane == i * groups + slot, count, 0.0)
        block[:, 2 * groups * day_cols :] = jnp.sum(norms, axis=0, keepdims=True)
        product = jnp.zeros((4 * groups, day_cols), f32)
        for start, rows, copy in parts:
            copy.wait()
            for here in blocks_of(start, rows):
                high, low = split_panel(panel[here, :])
                if here.start < resident:
                    high_ref[here, :] = high
                    low_ref[here, :] = low
                product += rows_dot(left_ref[:, here], high, low)
        both_sums = jnp.concatenate([add_terms(product, groups), product[2 * groups :][:groups]], axis=0)
        for row in range(2 * groups):
            block[:, row * day_cols : (row + 1) * day_cols] = both_sums[row : row + 1, :]
        sends = repeat_start(block, out, out_sems)
        wait_all(day_copies)
        pre_end = column(pre_row)
        ends[...] = jnp.broadcast_to(pre_end.astype(f32), ends.shape)
        before = days_of(me, (groups, day_cols)) < pre_end
        raised_time = jnp.where(before, jnp.exp(time_logit[...]), 0.0)
        raised_days[...] = raised_time
        time_norm[...] = jnp.broadcast_to(jnp.sum(raised_time, axis=1, keepdims=True), time_norm.shape)
        wait_all(sends)

    @pl.when(me >= half)
    def _():
        post_start = column(post_row)
        after = jnp.where(days_of(me, (groups, day_cols)) >= post_start, 1.0, 0.0)
        left = left_of(after / (all_count - post_start).astype(f32))
        for start, rows, copy in parts:
            copy.wait()
            for here in blocks_of(start, rows):
                cross_block[:, here] = add_terms(days_dot(left, *split_panel(panel[here, :])), groups)
        sends = fetch([cross_block], [cross], out_sems)
        wait_all(day_copies)
        wait_all(sends)


@first_half_only
def second_kernel(half, unit_devices, panel, cohort, unit_logit, sums, raised_days, ends, high_ref, low_ref, *refs):
    pack, norms, raised_units, more_high, more_low, held, held_cohort, held_logit, sems = refs
    groups, day_cols = raised_days.shape
    unit_rows, resident = panel.shape[0], high_ref.shape[0]
    rest = pl.ds(resident, unit_rows - resident)
    copies = fetch([panel.at[rest], cohort, unit_logit], [held, held_cohort, held_logit], sems)

    @pl.when(lax.axis_index("day") < half)
    def _():
        total = tree_sum(sums[u] for u in range(unit_devices))

        def group_rows(first):
            starts = [(first + row) * day_cols for row in range(groups)]
            return jnp.concatenate([total[:, start : start + day_cols] for start in starts], axis=0)

        counts = jnp.broadcast_to(total[:, 2 * groups * day_cols :], (groups, lanes))
        slot = lax.broadcasted_iota(jnp.int32, (groups, lanes), 0)
        lane = lax.broadcasted_iota(jnp.int32, (groups, lanes), 1)
        unit_norm, treat_count, ctrl_count = [
            jnp.sum(jnp.where(lane == i * groups + slot, counts, 0.0), axis=1, keepdims=True) for i in range(3)
        ]
        norms[...] = jnp.where(lane == 0, unit_norm, ctrl_count)
        gap = group_rows(0) / unit_norm - group_rows(groups) / jnp.maximum(treat_count, 1.0)
        before = days_of(lax.axis_index("day"), (groups, day_cols)).astype(f32) < ends[:, 0:1]
        raised_time = raised_days[...]
        pack[:groups, unit_rows:] = raised_time
        pack[groups:, unit_rows:] = jnp.zeros_like(raised_time)
        left = left_of(jnp.where(before, gap, 0.0), raised_time)

        def multiply(here, high, low):
            product = days_dot(left, high, low)
            pack[:groups, here] = add_terms(product, groups)
            pack[groups:, here] = add_terms(product, groups, 1)

        late = resident - 2 * block_rows

        @pl.loop(0, late // (2 * block_rows))
        def _(block):
            here = pl.ds(pl.multiple_of(block * 2 * block_rows, 2 * block_rows), 2 * block_rows)
            multiply(here, high_ref[here, :], low_ref[here, :])

        wait_all(copies)
        label = lax.broadcasted_iota(jnp.int32, raised_units.shape, 0)
        raised_units[...] = jnp.where(held_cohort[...] > label, jnp.exp(held_logit[...]), 0.0)
        for there in blocks_of(0, unit_rows - resident):
            more_high[there, :], more_low[there, :] = split_panel(held[there, :])
        for here in blocks_of(late, resident - late):
            multiply(here, high_ref[here, :], low_ref[here, :])
        for there in blocks_of(0, unit_rows - resident):
            multiply(pl.ds(resident + there.start, block_rows), more_high[there, :], more_low[there, :])


@first_half_only
def join_kernel(half, pack, post, *refs):
    norms, out = refs[:half], refs[half]
    groups, unit_rows = post.shape
    over_time = 1.0 / tree_sum(ref[:, 0:1] for ref in norms)
    out[:groups, :unit_rows] = pack[:groups, :unit_rows]
    out[:groups, unit_rows:] = pack[:groups, unit_rows:] * over_time
    out[groups:, :unit_rows] = pack[groups:, :unit_rows] * over_time - post[...]
    out[groups:, unit_rows:] = pack[groups:, unit_rows:]


@first_half_only
def third_kernel(half, *refs):
    parts, refs = [refs[0].at[day] for day in range(half)], refs[1:]
    high_ref, low_ref, more_high, more_low, norms, raised_units, ends, scaled, lam, out = refs
    groups, unit_rows = raised_units.shape
    resident, day_cols = high_ref.shape
    unit_norm, ctrl_count = norms[:, 0:1], norms[:, 1:2]
    factor = -step_rate / jnp.sqrt(ends[:, 0:1])
    over_unit = 1.0 / unit_norm
    me = lax.rem(lax.axis_index("day"), half)
    for day in range(half):
        lam[:, day * day_cols : (day + 1) * day_cols] = parts[day][:groups, unit_rows:]
    time_grad = jnp.zeros((groups, day_cols), f32)
    new_sum = jnp.zeros((groups, 1), f32)
    for start in range(0, unit_rows, block_rows):
        here = pl.ds(start, block_rows)
        whole = tree_sum(ref[:, here] for ref in parts)
        raised = raised_units[:, here]
        new = raised * over_unit * jnp.exp(whole[:groups] * factor)
        new_sum += jnp.sum(new, axis=1, keepdims=True)
        scaled[:, here] = new * ctrl_count
        left = left_of(jnp.where(raised > 0.0, whole[groups:], 0.0))
        if start < resident:
            high, low = high_ref[here, :], low_ref[here, :]
        else:
            there = pl.ds(start - resident, block_rows)
            high, low = more_high[there, :], more_low[there, :]
        time_grad += add_terms(rows_dot(left, high, low), groups)
    lane = lax.broadcasted_iota(jnp.int32, (groups, day_cols), 1)
    spare = (lane == day_cols - 1) & (me == half - 1)
    block = jnp.where(spare, new_sum, time_grad)
    for member in range(out.shape[0]):
        out[member] = block


def time_grad_of(grads, unit_devices, half, day):
    return tree_sum(grads[unit * half + half - 1 - day] for unit in range(unit_devices))


@first_half_only
def fourth_kernel(half, unit_devices, grads, totals):
    day_cols = grads.shape[2]
    last = time_grad_of(grads, unit_devices, half, half - 1)
    totals[...] = jnp.broadcast_to(last[:, day_cols - 1 :], totals.shape)


def fifth_kernel(half, unit_devices, totals, scaled, grads, lam, norms, ends, unit_weights, time_weights):
    groups, day_cols = time_weights.shape
    me = lax.axis_index("day")

    @pl.when(me < half)
    def _():
        unit_weights[...] = scaled[...] * (1.0 / totals[:, 0:1])
        root = jnp.sqrt(jnp.maximum(norms[:, 1:2], 1.0))
        moved_total = jnp.zeros((groups, 1), f32)
        own = jnp.zeros((groups, day_cols), f32)
        for day in range(half):
            total = time_grad_of(grads, unit_devices, half, day)
            moved = lam[:, day * day_cols : (day + 1) * day_cols] * jnp.exp(total * (-step_rate / root))
            moved_total += jnp.sum(moved, axis=1, keepdims=True)
            own = jnp.where(me == day, moved, own)
        time_weights[...] = own * (ends[:, 0:1] / moved_total)

    @pl.when(me >= half)
    def _():
        time_weights[...] = jnp.zeros_like(time_weights)


def sixth_kernel(half, sent_totals, sent_scaled, _, unit_weights, block, out_sem):
    @pl.when(lax.axis_index("day") >= half)
    def _():
        block[...] = sent_scaled[...] * (1.0 / sent_totals[:, 0:1])
        wait_all(fetch([block], [unit_weights], out_sem))


def local(outcomes, cohort, pre_end, post_start, unit_logit, time_logit):
    groups = pre_end.shape[0]
    unit_rows, day_cols = outcomes.shape
    day_devices = lax.axis_size("day")
    unit_devices = lax.axis_size("unit")
    half = day_devices // 2
    assert half * 2 == day_devices and half & (half - 1) == 0
    assert unit_devices & (unit_devices - 1) == 0
    panel_starts = [0, unit_rows // 8 * 3, unit_rows // 4 * 3, unit_rows]
    resident = unit_rows * 3 // 4 // (2 * block_rows) * (2 * block_rows)
    def meeting_at(first):
        return [first] + [unit for unit in reversed(range(unit_devices)) if unit != first]

    middle = unit_devices // 2

    def to_other_half(value, day_xor=0):
        pairs = [
            (u * day_devices + d, u * day_devices + half + (d ^ day_xor)) for u in range(unit_devices) for d in range(half)
        ]
        return lax.ppermute(value, ("unit", "day"), pairs)

    def over_days(value):
        halves = [list(range(half)), list(range(half, day_devices))]
        return lax.all_gather(value, "day", axis_index_groups=halves)

    def over_first_half(value):
        members = [
            [unit * day_devices + day for unit in meeting_at(middle + 1) for day in reversed(days)]
            for days in (range(half), range(half, day_devices))
        ]
        return lax.all_to_all(
            value, ("unit", "day"), split_axis=0, concat_axis=0, axis_index_groups=members, tiled=True
        )

    def over_units(value):
        members = [
            [unit * day_devices + day for unit in meeting_at(middle - 1 if day < half else middle)]
            for day in range(day_devices)
        ]
        return lax.all_to_all(
            value, ("unit", "day"), split_axis=0, concat_axis=0, axis_index_groups=members, tiled=True
        )

    def call(kernel, shapes, name, args, in_specs=None, out_specs=None, **more):
        return pl.pallas_call(
            kernel,
            in_specs=in_specs or [vmem] * len(args),
            out_specs=out_specs or [vmem] * len(shapes),
            out_shape=[
                shape if isinstance(shape, type(in_hbm)) else jax.ShapeDtypeStruct(*shape) for shape in shapes
            ],
            compiler_params=params,
            name=name,
            **more,
        )(*args)

    arguments = (outcomes, cohort[None, :], pre_end[None, :], post_start[None, :], unit_logit, time_logit)
    fixed = [pltpu.with_memory_space_constraint(argument, pltpu.HBM) for argument in arguments]
    held = [pltpu.VMEM(argument.shape, argument.dtype) for argument in arguments]
    small_sems, panel_sems = pltpu.SemaphoreType.DMA((5,)), pltpu.SemaphoreType.DMA((3,))
    panel_terms = [((resident, day_cols), bf16)] * 2
    other_terms = [((unit_rows - resident, day_cols), bf16)] * 2
    out_sems = pltpu.SemaphoreType.DMA((unit_devices,))
    width = 2 * groups * day_cols + lanes
    in_hbm = pltpu.HBM((unit_devices, 1, width), f32)
    sums, cross, raised_days, time_norm, ends, high, low = call(
        functools.partial(first_kernel, day_devices * day_cols, half, panel_starts),
        [
            in_hbm,
            pltpu.HBM((groups, unit_rows), f32),
            ((groups, day_cols), f32),
            ((groups, lanes), f32),
            ((groups, lanes), f32),
            *panel_terms,
        ],
        "first_product",
        fixed,
        in_specs=[hbm] * 6,
        out_specs=[hbm, hbm] + [vmem] * 5,
        scratch_shapes=held
        + [
            pltpu.VMEM((1, width), f32),
            pltpu.VMEM((4 * groups, unit_rows), bf16),
            pltpu.VMEM((groups, unit_rows), f32),
            small_sems,
            panel_sems,
            out_sems,
        ],
    )
    downward = [
        (u * day_devices + d + half, u * day_devices + d) for u in range(unit_devices) for d in range(half)
    ]
    post = lax.ppermute(cross, ("unit", "day"), downward)
    pack, norms, raised_units, more_high, more_low = call(
        functools.partial(second_kernel, half, unit_devices),
        [
            ((2 * groups, unit_rows + day_cols), f32),
            ((groups, lanes), f32),
            ((groups, unit_rows), f32),
            *other_terms,
        ],
        "unit_gradient",
        (fixed[0], fixed[1], fixed[4], over_units(sums), raised_days, ends, high, low),
        in_specs=[hbm] * 3 + [vmem] * 5,
        scratch_shapes=[
            pltpu.VMEM((unit_rows - resident, day_cols), f32),
            held[1],
            held[4],
            pltpu.SemaphoreType.DMA((3,)),
        ],
    )
    time_norms = [time_norm]
    for k in range(1, half):
        pairs = [(u * day_devices + d, u * day_devices + (d ^ k)) for u in range(unit_devices) for d in range(half)]
        time_norms.append(lax.ppermute(time_norm, ("unit", "day"), pairs))
    (pack,) = call(
        functools.partial(join_kernel, half),
        [((2 * groups, unit_rows + day_cols), f32)],
        "join_post",
        (pack, post, *time_norms),
    )
    members = unit_devices * half
    scaled, lam, grads = call(
        functools.partial(third_kernel, half),
        [
            ((groups, unit_rows), f32),
            ((groups, half * day_cols), f32),
            ((members, groups, day_cols), f32),
        ],
        "time_gradient",
        (over_days(pack), high, low, more_high, more_low, norms, raised_units, ends),
    )
    sent_scaled = to_other_half(scaled)
    all_grads = over_first_half(grads)
    (totals,) = call(
        functools.partial(fourth_kernel, half, unit_devices), [((groups, lanes), f32)], "unit_totals", (all_grads,)
    )
    unit_weights, time_weights = call(
        functools.partial(fifth_kernel, half, unit_devices),
        [((groups, unit_rows), f32), ((groups, day_cols), f32)],
        "scale_weights",
        (totals, scaled, all_grads, lam, norms, ends),
    )
    (unit_weights,) = call(
        functools.partial(sixth_kernel, half),
        [((groups, unit_rows), f32)],
        "other_half",
        (to_other_half(totals, half > 1), sent_scaled, unit_weights),
        in_specs=[vmem, vmem, hbm],
        out_specs=[hbm],
        input_output_aliases={2: 0},
        scratch_shapes=[pltpu.VMEM((groups, unit_rows), f32), pltpu.SemaphoreType.DMA((1,))],
    )
    return unit_weights, time_weights


def solution(mesh):
    return jax.shard_map(
        local,
        mesh=mesh,
        in_specs=(P("unit", "day"), P("unit"), P(), P(), P(None, "unit"), P(None, "day")),
        out_specs=(P(None, "unit"), P(None, "day")),
        check_vma=False,
    )
```

```python
import functools

import jax
import jax.numpy as jnp
from jax import lax
from jax.experimental import pallas as pl
from jax.experimental.pallas import tpu as pltpu
from jax.sharding import PartitionSpec as P

step_rate = 16.0
f32 = jnp.float32
bf16 = jnp.bfloat16
lanes = 128
block_rows = 512
params = pltpu.CompilerParams(vmem_limit_bytes=24 * 1024 * 1024)
vmem = pl.BlockSpec(memory_space=pltpu.VMEM)
hbm = pl.BlockSpec(memory_space=pltpu.HBM)


def split_left(value):
    first = value.astype(bf16).astype(f32)
    return [first, value - first]


def left_of(*values):
    return jnp.concatenate([term for value in values for term in split_left(value)], axis=0).astype(bf16)


def split_panel(value):
    high = value.astype(bf16)
    return high, (value - high.astype(f32)).astype(bf16)


def rows_dot(left, high, low):
    return jnp.dot(left, high, preferred_element_type=f32) + jnp.dot(left, low, preferred_element_type=f32)


def days_dot(left, high, low):
    dims = (((1,), (1,)), ((), ()))
    return lax.dot_general(left, high, dims, preferred_element_type=f32) + lax.dot_general(
        left, low, dims, preferred_element_type=f32
    )


def add_terms(stack, groups, place=0):
    return stack[2 * place * groups :][:groups] + stack[(2 * place + 1) * groups :][:groups]


def tree_sum(values):
    values = list(values)
    while len(values) > 1:
        values = [values[i] + values[i + 1] for i in range(0, len(values), 2)]
    return values[0]


def column(row_ref):
    count = row_ref.shape[1]
    wide = jnp.broadcast_to(row_ref[...].astype(f32), (count, count))
    row = lax.broadcasted_iota(jnp.int32, (count, count), 0)
    lane = lax.broadcasted_iota(jnp.int32, (count, count), 1)
    return jnp.sum(jnp.where(row == lane, wide, 0.0), axis=1, keepdims=True).astype(jnp.int32)


def days_of(device, shape):
    return device * shape[1] + lax.broadcasted_iota(jnp.int32, shape, 1)


def first_half_only(kernel):
    @functools.wraps(kernel)
    def guarded(half, *refs):
        @pl.when(lax.axis_index("day") < half)
        def _():
            kernel(half, *refs)

    return guarded


def fetch(sources, targets, sems):
    copies = [pltpu.make_async_copy(*pair, sems.at[i]) for i, pair in enumerate(zip(sources, targets))]
    for copy in copies:
        copy.start()
    return copies


def fetch_rows(source, target, sems, starts):
    spans = [(start, stop - start) for start, stop in zip(starts, starts[1:])]
    parts = [pl.ds(*span) for span in spans]
    copies = fetch([source.at[here] for here in parts], [target.at[here] for here in parts], sems)
    return [(*span, copy) for span, copy in zip(spans, copies)]


def blocks_of(start, rows):
    return [pl.ds(here, block_rows) for here in range(start, start + rows, block_rows)]


def wait_all(copies):
    for copy in copies:
        copy.wait()


def repeat_start(block, out, sems):
    places = [out.at[i] for i in range(out.shape[0])]
    return fetch([block] * len(places), places, sems)


def first_kernel(all_count, half, starts, *refs):
    arguments, refs = refs[:6], refs[6:]
    out, cross, raised_days, time_norm, ends, high_ref, low_ref, *held, block, left_ref, cross_block, small_sems, panel_sems, out_sems = refs
    groups, day_cols = held[5].shape
    unit_rows, resident = held[0].shape[0], high_ref.shape[0]
    (post_copy,) = fetch(arguments[3:4], held[3:4], small_sems)
    unit_copies = fetch(arguments[1:5:3], held[1:5:3], small_sems.at[pl.ds(1, 2)])
    parts = fetch_rows(arguments[0], held[0], panel_sems, starts)
    day_copies = fetch(arguments[2:6:3], held[2:6:3], small_sems.at[pl.ds(3, 2)])
    panel, cohort, pre_row, post_row, unit_logit, time_logit = held
    post_copy.wait()
    wait_all(unit_copies)
    me = lax.axis_index("day")

    @pl.when(me < half)
    def _():
        counts = []

        def prepare(start, rows):
            here = pl.ds(start, rows)
            label = lax.broadcasted_iota(jnp.int32, (groups, rows), 0)
            treated = jnp.where(cohort[:, here] == label, 1.0, 0.0)
            control = jnp.where(cohort[:, here] > label, 1.0, 0.0)
            raised = jnp.exp(unit_logit[:, here]) * control
            left_ref[:, here] = left_of(raised, treated)
            counts.append([jnp.sum(value, axis=1, keepdims=True) for value in (raised, treated, control)])

        product = jnp.zeros((4 * groups, day_cols), f32)
        prepare(*parts[0][:2])
        for part, (start, rows, copy) in enumerate(parts):
            copy.wait()
            for here in blocks_of(start, rows):
                high, low = split_panel(panel[here, :])
                if here.start < resident:
                    high_ref[here, :] = high
                    low_ref[here, :] = low
                product += rows_dot(left_ref[:, here], high, low)
            if part + 1 < len(parts):
                prepare(*parts[part + 1][:2])
        lane = lax.broadcasted_iota(jnp.int32, (groups, lanes), 1)
        slot = lax.broadcasted_iota(jnp.int32, (groups, lanes), 0)
        norms = jnp.zeros((groups, lanes), f32)
        for i, count in enumerate(zip(*counts)):
            norms += jnp.where(lane == i * groups + slot, sum(count), 0.0)
        block[:, 2 * groups * day_cols :] = jnp.sum(norms, axis=0, keepdims=True)
        both_sums = jnp.concatenate([add_terms(product, groups), product[2 * groups :][:groups]], axis=0)
        for row in range(2 * groups):
            block[:, row * day_cols : (row + 1) * day_cols] = both_sums[row : row + 1, :]
        sends = repeat_start(block, out, out_sems)
        wait_all(day_copies)
        pre_end = column(pre_row)
        ends[...] = jnp.broadcast_to(pre_end.astype(f32), ends.shape)
        before = days_of(me, (groups, day_cols)) < pre_end
        raised_time = jnp.where(before, jnp.exp(time_logit[...]), 0.0)
        raised_days[...] = raised_time
        time_norm[...] = jnp.broadcast_to(jnp.sum(raised_time, axis=1, keepdims=True), time_norm.shape)
        wait_all(sends)

    @pl.when(me >= half)
    def _():
        post_start = column(post_row)
        after = jnp.where(days_of(me, (groups, day_cols)) >= post_start, 1.0, 0.0)
        left = left_of(after / (all_count - post_start).astype(f32))
        for start, rows, copy in parts:
            copy.wait()
            for here in blocks_of(start, rows):
                cross_block[:, here] = add_terms(days_dot(left, *split_panel(panel[here, :])), groups)
        sends = fetch([cross_block], [cross], out_sems)
        wait_all(day_copies)
        wait_all(sends)


@first_half_only
def second_kernel(half, unit_devices, panel, cohort, unit_logit, sums, raised_days, ends, high_ref, low_ref, *refs):
    pack, norms, raised_units, more_high, more_low, held, held_cohort, held_logit, sems = refs
    groups, day_cols = raised_days.shape
    unit_rows, resident = panel.shape[0], high_ref.shape[0]
    rest = pl.ds(resident, unit_rows - resident)
    copies = fetch([panel.at[rest], cohort, unit_logit], [held, held_cohort, held_logit], sems)

    @pl.when(lax.axis_index("day") < half)
    def _():
        total = tree_sum(sums[u] for u in range(unit_devices))

        def group_rows(first):
            starts = [(first + row) * day_cols for row in range(groups)]
            return jnp.concatenate([total[:, start : start + day_cols] for start in starts], axis=0)

        counts = jnp.broadcast_to(total[:, 2 * groups * day_cols :], (groups, lanes))
        slot = lax.broadcasted_iota(jnp.int32, (groups, lanes), 0)
        lane = lax.broadcasted_iota(jnp.int32, (groups, lanes), 1)
        unit_norm, treat_count, ctrl_count = [
            jnp.sum(jnp.where(lane == i * groups + slot, counts, 0.0), axis=1, keepdims=True) for i in range(3)
        ]
        norms[...] = jnp.where(lane == 0, unit_norm, ctrl_count)
        gap = group_rows(0) / unit_norm - group_rows(groups) / jnp.maximum(treat_count, 1.0)
        before = days_of(lax.axis_index("day"), (groups, day_cols)).astype(f32) < ends[:, 0:1]
        raised_time = raised_days[...]
        pack[:groups, unit_rows:] = raised_time
        pack[groups:, unit_rows:] = jnp.zeros_like(raised_time)
        left = left_of(jnp.where(before, gap, 0.0), raised_time)

        def multiply(here, high, low):
            product = days_dot(left, high, low)
            pack[:groups, here] = add_terms(product, groups)
            pack[groups:, here] = add_terms(product, groups, 1)

        late = resident - 2 * block_rows

        @pl.loop(0, late // (2 * block_rows))
        def _(block):
            here = pl.ds(pl.multiple_of(block * 2 * block_rows, 2 * block_rows), 2 * block_rows)
            multiply(here, high_ref[here, :], low_ref[here, :])

        wait_all(copies)
        label = lax.broadcasted_iota(jnp.int32, raised_units.shape, 0)
        raised_units[...] = jnp.where(held_cohort[...] > label, jnp.exp(held_logit[...]), 0.0)
        for there in blocks_of(0, unit_rows - resident):
            more_high[there, :], more_low[there, :] = split_panel(held[there, :])
        for here in blocks_of(late, resident - late):
            multiply(here, high_ref[here, :], low_ref[here, :])
        for there in blocks_of(0, unit_rows - resident):
            multiply(pl.ds(resident + there.start, block_rows), more_high[there, :], more_low[there, :])


@first_half_only
def join_kernel(half, pack, post, *refs):
    norms, out = refs[:half], refs[half]
    groups, unit_rows = post.shape
    over_time = 1.0 / tree_sum(ref[:, 0:1] for ref in norms)
    out[:groups, :unit_rows] = pack[:groups, :unit_rows]
    out[:groups, unit_rows:] = pack[:groups, unit_rows:] * over_time
    out[groups:, :unit_rows] = pack[groups:, :unit_rows] * over_time - post[...]
    out[groups:, unit_rows:] = pack[groups:, unit_rows:]


@first_half_only
def third_kernel(half, *refs):
    parts, refs = [refs[0].at[day] for day in range(half)], refs[1:]
    high_ref, low_ref, more_high, more_low, norms, raised_units, ends, scaled, lam, out = refs
    groups, unit_rows = raised_units.shape
    resident, day_cols = high_ref.shape
    unit_norm, ctrl_count = norms[:, 0:1], norms[:, 1:2]
    factor = -step_rate / jnp.sqrt(ends[:, 0:1])
    over_unit = 1.0 / unit_norm
    me = lax.rem(lax.axis_index("day"), half)
    for day in range(half):
        lam[:, day * day_cols : (day + 1) * day_cols] = parts[day][:groups, unit_rows:]
    time_grad = jnp.zeros((groups, day_cols), f32)
    new_sum = jnp.zeros((groups, 1), f32)
    for start in range(0, unit_rows, block_rows):
        here = pl.ds(start, block_rows)
        whole = tree_sum(ref[:, here] for ref in parts)
        raised = raised_units[:, here]
        new = raised * over_unit * jnp.exp(whole[:groups] * factor)
        new_sum += jnp.sum(new, axis=1, keepdims=True)
        scaled[:, here] = new * ctrl_count
        left = left_of(jnp.where(raised > 0.0, whole[groups:], 0.0))
        if start < resident:
            high, low = high_ref[here, :], low_ref[here, :]
        else:
            there = pl.ds(start - resident, block_rows)
            high, low = more_high[there, :], more_low[there, :]
        time_grad += add_terms(rows_dot(left, high, low), groups)
    lane = lax.broadcasted_iota(jnp.int32, (groups, day_cols), 1)
    spare = (lane == day_cols - 1) & (me == half - 1)
    block = jnp.where(spare, new_sum, time_grad)
    for member in range(out.shape[0]):
        out[member] = block


def time_grad_of(grads, unit_devices, half, day):
    return tree_sum(grads[unit * half + half - 1 - day] for unit in range(unit_devices))


@first_half_only
def fourth_kernel(half, unit_devices, grads, totals):
    day_cols = grads.shape[2]
    last = time_grad_of(grads, unit_devices, half, half - 1)
    totals[...] = jnp.broadcast_to(last[:, day_cols - 1 :], totals.shape)


def fifth_kernel(half, unit_devices, totals, scaled, grads, lam, norms, ends, unit_weights, time_weights):
    groups, day_cols = time_weights.shape
    me = lax.axis_index("day")

    @pl.when(me < half)
    def _():
        unit_weights[...] = scaled[...] * (1.0 / totals[:, 0:1])
        root = jnp.sqrt(jnp.maximum(norms[:, 1:2], 1.0))
        moved_total = jnp.zeros((groups, 1), f32)
        own = jnp.zeros((groups, day_cols), f32)
        for day in range(half):
            total = time_grad_of(grads, unit_devices, half, day)
            moved = lam[:, day * day_cols : (day + 1) * day_cols] * jnp.exp(total * (-step_rate / root))
            moved_total += jnp.sum(moved, axis=1, keepdims=True)
            own = jnp.where(me == day, moved, own)
        time_weights[...] = own * (ends[:, 0:1] / moved_total)

    @pl.when(me >= half)
    def _():
        time_weights[...] = jnp.zeros_like(time_weights)


def sixth_kernel(half, sent_totals, sent_scaled, _, unit_weights, block, out_sem):
    @pl.when(lax.axis_index("day") >= half)
    def _():
        block[...] = sent_scaled[...] * (1.0 / sent_totals[:, 0:1])
        wait_all(fetch([block], [unit_weights], out_sem))


def local(outcomes, cohort, pre_end, post_start, unit_logit, time_logit):
    groups = pre_end.shape[0]
    unit_rows, day_cols = outcomes.shape
    day_devices = lax.axis_size("day")
    unit_devices = lax.axis_size("unit")
    half = day_devices // 2
    assert half * 2 == day_devices and half & (half - 1) == 0
    assert unit_devices & (unit_devices - 1) == 0
    panel_starts = [0, unit_rows // 8 * 3, unit_rows // 4 * 3, unit_rows]
    resident = unit_rows * 3 // 4 // (2 * block_rows) * (2 * block_rows)
    def meeting_at(first):
        return [first] + [unit for unit in reversed(range(unit_devices)) if unit != first]

    middle = unit_devices // 2

    def to_other_half(value, day_xor=0):
        pairs = [
            (u * day_devices + d, u * day_devices + half + (d ^ day_xor)) for u in range(unit_devices) for d in range(half)
        ]
        return lax.ppermute(value, ("unit", "day"), pairs)

    def over_days(value):
        halves = [list(range(half)), list(range(half, day_devices))]
        return lax.all_gather(value, "day", axis_index_groups=halves)

    def over_first_half(value):
        members = [
            [unit * day_devices + day for unit in meeting_at(middle + 1) for day in reversed(days)]
            for days in (range(half), range(half, day_devices))
        ]
        return lax.all_to_all(
            value, ("unit", "day"), split_axis=0, concat_axis=0, axis_index_groups=members, tiled=True
        )

    def over_units(value):
        members = [
            [unit * day_devices + day for unit in meeting_at(middle - 1 if day < half else middle)]
            for day in range(day_devices)
        ]
        return lax.all_to_all(
            value, ("unit", "day"), split_axis=0, concat_axis=0, axis_index_groups=members, tiled=True
        )

    def call(kernel, shapes, name, args, in_specs=None, out_specs=None, **more):
        return pl.pallas_call(
            kernel,
            in_specs=in_specs or [vmem] * len(args),
            out_specs=out_specs or [vmem] * len(shapes),
            out_shape=[
                shape if isinstance(shape, type(in_hbm)) else jax.ShapeDtypeStruct(*shape) for shape in shapes
            ],
            compiler_params=params,
            name=name,
            **more,
        )(*args)

    arguments = (outcomes, cohort[None, :], pre_end[None, :], post_start[None, :], unit_logit, time_logit)
    fixed = [pltpu.with_memory_space_constraint(argument, pltpu.HBM) for argument in arguments]
    held = [pltpu.VMEM(argument.shape, argument.dtype) for argument in arguments]
    small_sems, panel_sems = pltpu.SemaphoreType.DMA((5,)), pltpu.SemaphoreType.DMA((3,))
    panel_terms = [((resident, day_cols), bf16)] * 2
    other_terms = [((unit_rows - resident, day_cols), bf16)] * 2
    out_sems = pltpu.SemaphoreType.DMA((unit_devices,))
    width = 2 * groups * day_cols + lanes
    in_hbm = pltpu.HBM((unit_devices, 1, width), f32)
    sums, cross, raised_days, time_norm, ends, high, low = call(
        functools.partial(first_kernel, day_devices * day_cols, half, panel_starts),
        [
            in_hbm,
            pltpu.HBM((groups, unit_rows), f32),
            ((groups, day_cols), f32),
            ((groups, lanes), f32),
            ((groups, lanes), f32),
            *panel_terms,
        ],
        "first_product",
        fixed,
        in_specs=[hbm] * 6,
        out_specs=[hbm, hbm] + [vmem] * 5,
        scratch_shapes=held
        + [
            pltpu.VMEM((1, width), f32),
            pltpu.VMEM((4 * groups, unit_rows), bf16),
            pltpu.VMEM((groups, unit_rows), f32),
            small_sems,
            panel_sems,
            out_sems,
        ],
    )
    downward = [
        (u * day_devices + d + half, u * day_devices + d) for u in range(unit_devices) for d in range(half)
    ]
    post = lax.ppermute(cross, ("unit", "day"), downward)
    pack, norms, raised_units, more_high, more_low = call(
        functools.partial(second_kernel, half, unit_devices),
        [
            ((2 * groups, unit_rows + day_cols), f32),
            ((groups, lanes), f32),
            ((groups, unit_rows), f32),
            *other_terms,
        ],
        "unit_gradient",
        (fixed[0], fixed[1], fixed[4], over_units(sums), raised_days, ends, high, low),
        in_specs=[hbm] * 3 + [vmem] * 5,
        scratch_shapes=[
            pltpu.VMEM((unit_rows - resident, day_cols), f32),
            held[1],
            held[4],
            pltpu.SemaphoreType.DMA((3,)),
        ],
    )
    time_norms = [time_norm]
    for k in range(1, half):
        pairs = [(u * day_devices + d, u * day_devices + (d ^ k)) for u in range(unit_devices) for d in range(half)]
        time_norms.append(lax.ppermute(time_norm, ("unit", "day"), pairs))
    (pack,) = call(
        functools.partial(join_kernel, half),
        [((2 * groups, unit_rows + day_cols), f32)],
        "join_post",
        (pack, post, *time_norms),
    )
    members = unit_devices * half
    scaled, lam, grads = call(
        functools.partial(third_kernel, half),
        [
            ((groups, unit_rows), f32),
            ((groups, half * day_cols), f32),
            ((members, groups, day_cols), f32),
        ],
        "time_gradient",
        (over_days(pack), high, low, more_high, more_low, norms, raised_units, ends),
    )
    sent_scaled = to_other_half(scaled)
    all_grads = over_first_half(grads)
    (totals,) = call(
        functools.partial(fourth_kernel, half, unit_devices), [((groups, lanes), f32)], "unit_totals", (all_grads,)
    )
    unit_weights, time_weights = call(
        functools.partial(fifth_kernel, half, unit_devices),
        [((groups, unit_rows), f32), ((groups, day_cols), f32)],
        "scale_weights",
        (totals, scaled, all_grads, lam, norms, ends),
    )
    (unit_weights,) = call(
        functools.partial(sixth_kernel, half),
        [((groups, unit_rows), f32)],
        "other_half",
        (to_other_half(totals, half > 1), sent_scaled, unit_weights),
        in_specs=[vmem, vmem, hbm],
        out_specs=[hbm],
        input_output_aliases={2: 0},
        scratch_shapes=[pltpu.VMEM((groups, unit_rows), f32), pltpu.SemaphoreType.DMA((1,))],
    )
    return unit_weights, time_weights


def solution(mesh):
    return jax.shard_map(
        local,
        mesh=mesh,
        in_specs=(P("unit", "day"), P("unit"), P(), P(), P(None, "unit"), P(None, "day")),
        out_specs=(P(None, "unit"), P(None, "day")),
        check_vma=False,
    )
```

```python
import functools

import jax
import jax.numpy as jnp
from jax import lax
from jax.experimental import pallas as pl
from jax.experimental.pallas import tpu as pltpu
from jax.sharding import PartitionSpec as P

step_rate = 16.0
f32 = jnp.float32
bf16 = jnp.bfloat16
lanes = 128
block_rows = 512
params = pltpu.CompilerParams(vmem_limit_bytes=24 * 1024 * 1024)
vmem = pl.BlockSpec(memory_space=pltpu.VMEM)
hbm = pl.BlockSpec(memory_space=pltpu.HBM)


def split_left(value):
    first = value.astype(bf16).astype(f32)
    return [first, value - first]


def left_of(*values):
    return jnp.concatenate([term for value in values for term in split_left(value)], axis=0).astype(bf16)


def split_panel(value):
    high = value.astype(bf16)
    return high, (value - high.astype(f32)).astype(bf16)


def rows_dot(left, high, low):
    return jnp.dot(left, high, preferred_element_type=f32) + jnp.dot(left, low, preferred_element_type=f32)


def days_dot(left, high, low):
    dims = (((1,), (1,)), ((), ()))
    return lax.dot_general(left, high, dims, preferred_element_type=f32) + lax.dot_general(
        left, low, dims, preferred_element_type=f32
    )


def add_terms(stack, groups, place=0):
    return stack[2 * place * groups :][:groups] + stack[(2 * place + 1) * groups :][:groups]


def tree_sum(values):
    values = list(values)
    while len(values) > 1:
        values = [values[i] + values[i + 1] for i in range(0, len(values), 2)]
    return values[0]


def column(row_ref):
    count = row_ref.shape[1]
    wide = jnp.broadcast_to(row_ref[...].astype(f32), (count, count))
    row = lax.broadcasted_iota(jnp.int32, (count, count), 0)
    lane = lax.broadcasted_iota(jnp.int32, (count, count), 1)
    return jnp.sum(jnp.where(row == lane, wide, 0.0), axis=1, keepdims=True).astype(jnp.int32)


def days_of(device, shape):
    return device * shape[1] + lax.broadcasted_iota(jnp.int32, shape, 1)


def first_half_only(kernel):
    @functools.wraps(kernel)
    def guarded(half, *refs):
        @pl.when(lax.axis_index("day") < half)
        def _():
            kernel(half, *refs)

    return guarded


def fetch(sources, targets, sems):
    copies = [pltpu.make_async_copy(*pair, sems.at[i]) for i, pair in enumerate(zip(sources, targets))]
    for copy in copies:
        copy.start()
    return copies


def fetch_rows(source, target, sems, starts):
    spans = [(start, stop - start) for start, stop in zip(starts, starts[1:])]
    blocks = blocks_of(0, source.shape[0])
    copies = fetch([source.at[here] for here in blocks], [target.at[here] for here in blocks], sems)
    return [(start, rows, copies[start // block_rows : (start + rows) // block_rows]) for start, rows in spans]


def blocks_of(start, rows):
    return [pl.ds(here, block_rows) for here in range(start, start + rows, block_rows)]


def wait_all(copies):
    for copy in copies:
        copy.wait()


def repeat_start(block, out, sems):
    places = [out.at[i] for i in range(out.shape[0])]
    return fetch([block] * len(places), places, sems)


def first_kernel(all_count, half, starts, *refs):
    arguments, refs = refs[:6], refs[6:]
    out, cross, raised_days, time_norm, ends, high_ref, low_ref, *held, block, left_ref, cross_block, small_sems, panel_sems, out_sems = refs
    groups, day_cols = held[5].shape
    unit_rows, resident = held[0].shape[0], high_ref.shape[0]
    (post_copy,) = fetch(arguments[3:4], held[3:4], small_sems)
    unit_copies = fetch(arguments[1:5:3], held[1:5:3], small_sems.at[pl.ds(1, 2)])
    parts = fetch_rows(arguments[0], held[0], panel_sems, starts)
    day_copies = fetch(arguments[2:6:3], held[2:6:3], small_sems.at[pl.ds(3, 2)])
    panel, cohort, pre_row, post_row, unit_logit, time_logit = held
    post_copy.wait()
    wait_all(unit_copies)
    me = lax.axis_index("day")

    @pl.when(me < half)
    def _():
        counts = []

        def prepare(start, rows):
            here = pl.ds(start, rows)
            label = lax.broadcasted_iota(jnp.int32, (groups, rows), 0)
            treated = jnp.where(cohort[:, here] == label, 1.0, 0.0)
            control = jnp.where(cohort[:, here] > label, 1.0, 0.0)
            raised = jnp.exp(unit_logit[:, here]) * control
            left_ref[:, here] = left_of(raised, treated)
            counts.append([jnp.sum(value, axis=1, keepdims=True) for value in (raised, treated, control)])

        product = jnp.zeros((4 * groups, day_cols), f32)
        prepare(*parts[0][:2])
        for part, (start, rows, copies) in enumerate(parts):
            wait_all(copies)
            for here in blocks_of(start, rows):
                high, low = split_panel(panel[here, :])
                if here.start < resident:
                    high_ref[here, :] = high
                    low_ref[here, :] = low
                product += rows_dot(left_ref[:, here], high, low)
            if part + 1 < len(parts):
                prepare(*parts[part + 1][:2])
        lane = lax.broadcasted_iota(jnp.int32, (groups, lanes), 1)
        slot = lax.broadcasted_iota(jnp.int32, (groups, lanes), 0)
        norms = jnp.zeros((groups, lanes), f32)
        for i, count in enumerate(zip(*counts)):
            norms += jnp.where(lane == i * groups + slot, sum(count), 0.0)
        block[:, 2 * groups * day_cols :] = jnp.sum(norms, axis=0, keepdims=True)
        both_sums = jnp.concatenate([add_terms(product, groups), product[2 * groups :][:groups]], axis=0)
        for row in range(2 * groups):
            block[:, row * day_cols : (row + 1) * day_cols] = both_sums[row : row + 1, :]
        sends = repeat_start(block, out, out_sems)
        wait_all(day_copies)
        pre_end = column(pre_row)
        ends[...] = jnp.broadcast_to(pre_end.astype(f32), ends.shape)
        before = days_of(me, (groups, day_cols)) < pre_end
        raised_time = jnp.where(before, jnp.exp(time_logit[...]), 0.0)
        raised_days[...] = raised_time
        time_norm[...] = jnp.broadcast_to(jnp.sum(raised_time, axis=1, keepdims=True), time_norm.shape)
        wait_all(sends)

    @pl.when(me >= half)
    def _():
        post_start = column(post_row)
        after = jnp.where(days_of(me, (groups, day_cols)) >= post_start, 1.0, 0.0)
        left = left_of(after / (all_count - post_start).astype(f32))
        for start, rows, copies in parts:
            wait_all(copies)
            for here in blocks_of(start, rows):
                cross_block[:, here] = add_terms(days_dot(left, *split_panel(panel[here, :])), groups)
        sends = fetch([cross_block], [cross], out_sems)
        wait_all(day_copies)
        wait_all(sends)


@first_half_only
def second_kernel(half, unit_devices, panel, cohort, unit_logit, sums, raised_days, ends, high_ref, low_ref, *refs):
    pack, norms, raised_units, more_high, more_low, held, held_cohort, held_logit, sems = refs
    groups, day_cols = raised_days.shape
    unit_rows, resident = panel.shape[0], high_ref.shape[0]
    rest = pl.ds(resident, unit_rows - resident)
    copies = fetch([panel.at[rest], cohort, unit_logit], [held, held_cohort, held_logit], sems)

    @pl.when(lax.axis_index("day") < half)
    def _():
        total = tree_sum(sums[u] for u in range(unit_devices))

        def group_rows(first):
            starts = [(first + row) * day_cols for row in range(groups)]
            return jnp.concatenate([total[:, start : start + day_cols] for start in starts], axis=0)

        counts = jnp.broadcast_to(total[:, 2 * groups * day_cols :], (groups, lanes))
        slot = lax.broadcasted_iota(jnp.int32, (groups, lanes), 0)
        lane = lax.broadcasted_iota(jnp.int32, (groups, lanes), 1)
        unit_norm, treat_count, ctrl_count = [
            jnp.sum(jnp.where(lane == i * groups + slot, counts, 0.0), axis=1, keepdims=True) for i in range(3)
        ]
        norms[...] = jnp.where(lane == 0, unit_norm, ctrl_count)
        gap = group_rows(0) / unit_norm - group_rows(groups) / jnp.maximum(treat_count, 1.0)
        before = days_of(lax.axis_index("day"), (groups, day_cols)).astype(f32) < ends[:, 0:1]
        raised_time = raised_days[...]
        pack[:groups, unit_rows:] = raised_time
        pack[groups:, unit_rows:] = jnp.zeros_like(raised_time)
        left = left_of(jnp.where(before, gap, 0.0), raised_time)

        def multiply(here, high, low):
            product = days_dot(left, high, low)
            pack[:groups, here] = add_terms(product, groups)
            pack[groups:, here] = add_terms(product, groups, 1)

        late = resident - 2 * block_rows

        @pl.loop(0, late // (2 * block_rows))
        def _(block):
            here = pl.ds(pl.multiple_of(block * 2 * block_rows, 2 * block_rows), 2 * block_rows)
            multiply(here, high_ref[here, :], low_ref[here, :])

        wait_all(copies)
        label = lax.broadcasted_iota(jnp.int32, raised_units.shape, 0)
        raised_units[...] = jnp.where(held_cohort[...] > label, jnp.exp(held_logit[...]), 0.0)
        for there in blocks_of(0, unit_rows - resident):
            more_high[there, :], more_low[there, :] = split_panel(held[there, :])
        for here in blocks_of(late, resident - late):
            multiply(here, high_ref[here, :], low_ref[here, :])
        for there in blocks_of(0, unit_rows - resident):
            multiply(pl.ds(resident + there.start, block_rows), more_high[there, :], more_low[there, :])


@first_half_only
def join_kernel(half, pack, post, *refs):
    norms, out = refs[:half], refs[half]
    groups, unit_rows = post.shape
    over_time = 1.0 / tree_sum(ref[:, 0:1] for ref in norms)
    out[:groups, :unit_rows] = pack[:groups, :unit_rows]
    out[:groups, unit_rows:] = pack[:groups, unit_rows:] * over_time
    out[groups:, :unit_rows] = pack[groups:, :unit_rows] * over_time - post[...]
    out[groups:, unit_rows:] = pack[groups:, unit_rows:]


@first_half_only
def third_kernel(half, *refs):
    parts, refs = [refs[0].at[day] for day in range(half)], refs[1:]
    high_ref, low_ref, more_high, more_low, norms, raised_units, ends, scaled, lam, out = refs
    groups, unit_rows = raised_units.shape
    resident, day_cols = high_ref.shape
    unit_norm, ctrl_count = norms[:, 0:1], norms[:, 1:2]
    factor = -step_rate / jnp.sqrt(ends[:, 0:1])
    over_unit = 1.0 / unit_norm
    me = lax.rem(lax.axis_index("day"), half)
    for day in range(half):
        lam[:, day * day_cols : (day + 1) * day_cols] = parts[day][:groups, unit_rows:]
    time_grad = jnp.zeros((groups, day_cols), f32)
    new_sum = jnp.zeros((groups, 1), f32)
    for start in range(0, unit_rows, block_rows):
        here = pl.ds(start, block_rows)
        whole = tree_sum(ref[:, here] for ref in parts)
        raised = raised_units[:, here]
        new = raised * over_unit * jnp.exp(whole[:groups] * factor)
        new_sum += jnp.sum(new, axis=1, keepdims=True)
        scaled[:, here] = new * ctrl_count
        left = left_of(jnp.where(raised > 0.0, whole[groups:], 0.0))
        if start < resident:
            high, low = high_ref[here, :], low_ref[here, :]
        else:
            there = pl.ds(start - resident, block_rows)
            high, low = more_high[there, :], more_low[there, :]
        time_grad += add_terms(rows_dot(left, high, low), groups)
    lane = lax.broadcasted_iota(jnp.int32, (groups, day_cols), 1)
    spare = (lane == day_cols - 1) & (me == half - 1)
    block = jnp.where(spare, new_sum, time_grad)
    for member in range(out.shape[0]):
        out[member] = block


def time_grad_of(grads, unit_devices, half, day):
    return tree_sum(grads[unit * half + half - 1 - day] for unit in range(unit_devices))


@first_half_only
def fourth_kernel(half, unit_devices, grads, totals):
    day_cols = grads.shape[2]
    last = time_grad_of(grads, unit_devices, half, half - 1)
    totals[...] = jnp.broadcast_to(last[:, day_cols - 1 :], totals.shape)


def fifth_kernel(half, unit_devices, totals, scaled, grads, lam, norms, ends, unit_weights, time_weights):
    groups, day_cols = time_weights.shape
    me = lax.axis_index("day")

    @pl.when(me < half)
    def _():
        unit_weights[...] = scaled[...] * (1.0 / totals[:, 0:1])
        root = jnp.sqrt(jnp.maximum(norms[:, 1:2], 1.0))
        moved_total = jnp.zeros((groups, 1), f32)
        own = jnp.zeros((groups, day_cols), f32)
        for day in range(half):
            total = time_grad_of(grads, unit_devices, half, day)
            moved = lam[:, day * day_cols : (day + 1) * day_cols] * jnp.exp(total * (-step_rate / root))
            moved_total += jnp.sum(moved, axis=1, keepdims=True)
            own = jnp.where(me == day, moved, own)
        time_weights[...] = own * (ends[:, 0:1] / moved_total)

    @pl.when(me >= half)
    def _():
        time_weights[...] = jnp.zeros_like(time_weights)


def sixth_kernel(half, sent_totals, sent_scaled, _, unit_weights, block, out_sem):
    @pl.when(lax.axis_index("day") >= half)
    def _():
        block[...] = sent_scaled[...] * (1.0 / sent_totals[:, 0:1])
        wait_all(fetch([block], [unit_weights], out_sem))


def local(outcomes, cohort, pre_end, post_start, unit_logit, time_logit):
    groups = pre_end.shape[0]
    unit_rows, day_cols = outcomes.shape
    day_devices = lax.axis_size("day")
    unit_devices = lax.axis_size("unit")
    half = day_devices // 2
    assert half * 2 == day_devices and half & (half - 1) == 0
    assert unit_devices & (unit_devices - 1) == 0
    panel_starts = [0, unit_rows // 8 * 3, unit_rows // 4 * 3, unit_rows]
    resident = unit_rows * 3 // 4 // (2 * block_rows) * (2 * block_rows)
    def meeting_at(first):
        return [first] + [unit for unit in reversed(range(unit_devices)) if unit != first]

    middle = unit_devices // 2

    def to_other_half(value, day_xor=0):
        pairs = [
            (u * day_devices + d, u * day_devices + half + (d ^ day_xor)) for u in range(unit_devices) for d in range(half)
        ]
        return lax.ppermute(value, ("unit", "day"), pairs)

    def over_days(value):
        halves = [list(range(half)), list(range(half, day_devices))]
        return lax.all_gather(value, "day", axis_index_groups=halves)

    def over_first_half(value):
        members = [
            [unit * day_devices + day for unit in meeting_at(middle + 1) for day in reversed(days)]
            for days in (range(half), range(half, day_devices))
        ]
        return lax.all_to_all(
            value, ("unit", "day"), split_axis=0, concat_axis=0, axis_index_groups=members, tiled=True
        )

    def over_units(value):
        members = [
            [unit * day_devices + day for unit in meeting_at(middle - 1 if day < half else middle)]
            for day in range(day_devices)
        ]
        return lax.all_to_all(
            value, ("unit", "day"), split_axis=0, concat_axis=0, axis_index_groups=members, tiled=True
        )

    def call(kernel, shapes, name, args, in_specs=None, out_specs=None, **more):
        return pl.pallas_call(
            kernel,
            in_specs=in_specs or [vmem] * len(args),
            out_specs=out_specs or [vmem] * len(shapes),
            out_shape=[
                shape if isinstance(shape, type(in_hbm)) else jax.ShapeDtypeStruct(*shape) for shape in shapes
            ],
            compiler_params=params,
            name=name,
            **more,
        )(*args)

    arguments = (outcomes, cohort[None, :], pre_end[None, :], post_start[None, :], unit_logit, time_logit)
    fixed = [pltpu.with_memory_space_constraint(argument, pltpu.HBM) for argument in arguments]
    held = [pltpu.VMEM(argument.shape, argument.dtype) for argument in arguments]
    small_sems, panel_sems = pltpu.SemaphoreType.DMA((5,)), pltpu.SemaphoreType.DMA((unit_rows // block_rows,))
    panel_terms = [((resident, day_cols), bf16)] * 2
    other_terms = [((unit_rows - resident, day_cols), bf16)] * 2
    out_sems = pltpu.SemaphoreType.DMA((unit_devices,))
    width = 2 * groups * day_cols + lanes
    in_hbm = pltpu.HBM((unit_devices, 1, width), f32)
    sums, cross, raised_days, time_norm, ends, high, low = call(
        functools.partial(first_kernel, day_devices * day_cols, half, panel_starts),
        [
            in_hbm,
            pltpu.HBM((groups, unit_rows), f32),
            ((groups, day_cols), f32),
            ((groups, lanes), f32),
            ((groups, lanes), f32),
            *panel_terms,
        ],
        "first_product",
        fixed,
        in_specs=[hbm] * 6,
        out_specs=[hbm, hbm] + [vmem] * 5,
        scratch_shapes=held
        + [
            pltpu.VMEM((1, width), f32),
            pltpu.VMEM((4 * groups, unit_rows), bf16),
            pltpu.VMEM((groups, unit_rows), f32),
            small_sems,
            panel_sems,
            out_sems,
        ],
    )
    downward = [
        (u * day_devices + d + half, u * day_devices + d) for u in range(unit_devices) for d in range(half)
    ]
    post = lax.ppermute(cross, ("unit", "day"), downward)
    pack, norms, raised_units, more_high, more_low = call(
        functools.partial(second_kernel, half, unit_devices),
        [
            ((2 * groups, unit_rows + day_cols), f32),
            ((groups, lanes), f32),
            ((groups, unit_rows), f32),
            *other_terms,
        ],
        "unit_gradient",
        (fixed[0], fixed[1], fixed[4], over_units(sums), raised_days, ends, high, low),
        in_specs=[hbm] * 3 + [vmem] * 5,
        scratch_shapes=[
            pltpu.VMEM((unit_rows - resident, day_cols), f32),
            held[1],
            held[4],
            pltpu.SemaphoreType.DMA((3,)),
        ],
    )
    time_norms = [time_norm]
    for k in range(1, half):
        pairs = [(u * day_devices + d, u * day_devices + (d ^ k)) for u in range(unit_devices) for d in range(half)]
        time_norms.append(lax.ppermute(time_norm, ("unit", "day"), pairs))
    (pack,) = call(
        functools.partial(join_kernel, half),
        [((2 * groups, unit_rows + day_cols), f32)],
        "join_post",
        (pack, post, *time_norms),
    )
    members = unit_devices * half
    scaled, lam, grads = call(
        functools.partial(third_kernel, half),
        [
            ((groups, unit_rows), f32),
            ((groups, half * day_cols), f32),
            ((members, groups, day_cols), f32),
        ],
        "time_gradient",
        (over_days(pack), high, low, more_high, more_low, norms, raised_units, ends),
    )
    sent_scaled = to_other_half(scaled)
    all_grads = over_first_half(grads)
    (totals,) = call(
        functools.partial(fourth_kernel, half, unit_devices), [((groups, lanes), f32)], "unit_totals", (all_grads,)
    )
    unit_weights, time_weights = call(
        functools.partial(fifth_kernel, half, unit_devices),
        [((groups, unit_rows), f32), ((groups, day_cols), f32)],
        "scale_weights",
        (totals, scaled, all_grads, lam, norms, ends),
    )
    (unit_weights,) = call(
        functools.partial(sixth_kernel, half),
        [((groups, unit_rows), f32)],
        "other_half",
        (to_other_half(totals, half > 1), sent_scaled, unit_weights),
        in_specs=[vmem, vmem, hbm],
        out_specs=[hbm],
        input_output_aliases={2: 0},
        scratch_shapes=[pltpu.VMEM((groups, unit_rows), f32), pltpu.SemaphoreType.DMA((1,))],
    )
    return unit_weights, time_weights


def solution(mesh):
    return jax.shard_map(
        local,
        mesh=mesh,
        in_specs=(P("unit", "day"), P("unit"), P(), P(), P(None, "unit"), P(None, "day")),
        out_specs=(P(None, "unit"), P(None, "day")),
        check_vma=False,
    )
```

```python
import functools

import jax
import jax.numpy as jnp
from jax import lax
from jax.experimental import pallas as pl
from jax.experimental.pallas import tpu as pltpu
from jax.sharding import PartitionSpec as P

step_rate = 16.0
f32 = jnp.float32
bf16 = jnp.bfloat16
lanes = 128
block_rows = 512
params = pltpu.CompilerParams(vmem_limit_bytes=24 * 1024 * 1024)
vmem = pl.BlockSpec(memory_space=pltpu.VMEM)
hbm = pl.BlockSpec(memory_space=pltpu.HBM)


def split_left(value):
    first = value.astype(bf16).astype(f32)
    return [first, value - first]


def left_of(*values):
    return jnp.concatenate([term for value in values for term in split_left(value)], axis=0).astype(bf16)


def split_panel(value):
    high = value.astype(bf16)
    return high, (value - high.astype(f32)).astype(bf16)


def rows_dot(left, high, low):
    return jnp.dot(left, high, preferred_element_type=f32) + jnp.dot(left, low, preferred_element_type=f32)


def days_dot(left, high, low):
    dims = (((1,), (1,)), ((), ()))
    return lax.dot_general(left, high, dims, preferred_element_type=f32) + lax.dot_general(
        left, low, dims, preferred_element_type=f32
    )


def add_terms(stack, groups, place=0):
    return stack[2 * place * groups :][:groups] + stack[(2 * place + 1) * groups :][:groups]


def tree_sum(values):
    values = list(values)
    while len(values) > 1:
        values = [values[i] + values[i + 1] for i in range(0, len(values), 2)]
    return values[0]


def column(row_ref):
    count = row_ref.shape[1]
    wide = jnp.broadcast_to(row_ref[...].astype(f32), (count, count))
    row = lax.broadcasted_iota(jnp.int32, (count, count), 0)
    lane = lax.broadcasted_iota(jnp.int32, (count, count), 1)
    return jnp.sum(jnp.where(row == lane, wide, 0.0), axis=1, keepdims=True).astype(jnp.int32)


def days_of(device, shape):
    return device * shape[1] + lax.broadcasted_iota(jnp.int32, shape, 1)


def first_half_only(kernel):
    @functools.wraps(kernel)
    def guarded(half, *refs):
        @pl.when(lax.axis_index("day") < half)
        def _():
            kernel(half, *refs)

    return guarded


def describe(sources, targets, sems):
    return [pltpu.make_async_copy(*pair, sems.at[i]) for i, pair in enumerate(zip(sources, targets))]


def start_all(copies):
    for copy in copies:
        copy.start()


def fetch(sources, targets, sems):
    copies = describe(sources, targets, sems)
    start_all(copies)
    return copies


def fetch_rows(source, target, sems, starts):
    spans = [(start, stop - start) for start, stop in zip(starts, starts[1:])]
    parts = [pl.ds(*span) for span in spans]
    copies = describe([source.at[here] for here in parts], [target.at[here] for here in parts], sems)
    return [(*span, copy) for span, copy in zip(spans, copies)]


def blocks_of(start, rows):
    return [pl.ds(here, block_rows) for here in range(start, start + rows, block_rows)]


def wait_all(copies):
    for copy in copies:
        copy.wait()


def first_kernel(all_count, half, starts, *refs):
    arguments, refs = refs[:6], refs[6:]
    out, cross, raised_days, time_norm, ends, high_ref, low_ref, *held, block, left_ref, cross_block, small_sems, panel_sems, out_sem = refs
    groups, day_cols = held[5].shape
    unit_rows, resident = held[0].shape[0], high_ref.shape[0]
    me = lax.axis_index("day")
    panel, cohort, pre_row, post_row, unit_logit, time_logit = held
    post_copies = describe(arguments[3:4], held[3:4], small_sems)
    unit_copies = describe(arguments[1:5:3], held[1:5:3], small_sems.at[pl.ds(1, 2)])
    day_copies = describe(arguments[2:6:3], held[2:6:3], small_sems.at[pl.ds(3, 2)])
    parts = fetch_rows(arguments[0], held[0], panel_sems, starts)
    panel_copies = [copy for _, _, copy in parts]
    start_all(panel_copies[:1])

    @pl.when(me < half)
    def _():
        start_all(unit_copies)

    @pl.when(me >= half)
    def _():
        start_all(post_copies)

    start_all(panel_copies[1:])

    @pl.when(me < half)
    def _():
        start_all(day_copies)
        wait_all(unit_copies)
        counts = []

        def prepare(start, rows):
            here = pl.ds(start, rows)
            label = lax.broadcasted_iota(jnp.int32, (groups, rows), 0)
            treated = jnp.where(cohort[:, here] == label, 1.0, 0.0)
            control = jnp.where(cohort[:, here] > label, 1.0, 0.0)
            raised = jnp.exp(unit_logit[:, here]) * control
            left_ref[:, here] = left_of(raised, treated)
            counts.append([jnp.sum(value, axis=1, keepdims=True) for value in (raised, treated, control)])

        product = jnp.zeros((4 * groups, day_cols), f32)
        prepare(*parts[0][:2])
        for part, (start, rows, copy) in enumerate(parts):
            copy.wait()
            for here in blocks_of(start, rows):
                high, low = split_panel(panel[here, :])
                if here.start < resident:
                    high_ref[here, :] = high
                    low_ref[here, :] = low
                product += rows_dot(left_ref[:, here], high, low)
            if part + 1 < len(parts):
                prepare(*parts[part + 1][:2])
        lane = lax.broadcasted_iota(jnp.int32, (groups, lanes), 1)
        slot = lax.broadcasted_iota(jnp.int32, (groups, lanes), 0)
        norms = jnp.zeros((groups, lanes), f32)
        for i, count in enumerate(zip(*counts)):
            norms += jnp.where(lane == i * groups + slot, sum(count), 0.0)
        block[:, 2 * groups * day_cols :] = jnp.sum(norms, axis=0, keepdims=True)
        both_sums = jnp.concatenate([add_terms(product, groups), product[2 * groups :][:groups]], axis=0)
        for row in range(2 * groups):
            block[:, row * day_cols : (row + 1) * day_cols] = both_sums[row : row + 1, :]
        for member in range(out.shape[0]):
            out[member] = block[...]
        wait_all(day_copies)
        pre_end = column(pre_row)
        ends[...] = jnp.broadcast_to(pre_end.astype(f32), ends.shape)
        before = days_of(me, (groups, day_cols)) < pre_end
        raised_time = jnp.where(before, jnp.exp(time_logit[...]), 0.0)
        raised_days[...] = raised_time
        time_norm[...] = jnp.broadcast_to(jnp.sum(raised_time, axis=1, keepdims=True), time_norm.shape)

    @pl.when(me >= half)
    def _():
        wait_all(post_copies)
        post_start = column(post_row)
        after = jnp.where(days_of(me, (groups, day_cols)) >= post_start, 1.0, 0.0)
        left = left_of(after / (all_count - post_start).astype(f32))
        for start, rows, copy in parts:
            copy.wait()
            for here in blocks_of(start, rows):
                cross_block[:, here] = add_terms(days_dot(left, *split_panel(panel[here, :])), groups)
        wait_all(fetch([cross_block], [cross], out_sem))


@first_half_only
def second_kernel(half, unit_devices, panel, cohort, unit_logit, sums, raised_days, ends, high_ref, low_ref, *refs):
    pack, norms, raised_units, more_high, more_low, held, held_cohort, held_logit, sems = refs
    groups, day_cols = raised_days.shape
    unit_rows, resident = panel.shape[0], high_ref.shape[0]
    rest = pl.ds(resident, unit_rows - resident)
    copies = fetch([panel.at[rest], cohort, unit_logit], [held, held_cohort, held_logit], sems)

    @pl.when(lax.axis_index("day") < half)
    def _():
        total = tree_sum(sums[u] for u in range(unit_devices))

        def group_rows(first):
            starts = [(first + row) * day_cols for row in range(groups)]
            return jnp.concatenate([total[:, start : start + day_cols] for start in starts], axis=0)

        counts = jnp.broadcast_to(total[:, 2 * groups * day_cols :], (groups, lanes))
        slot = lax.broadcasted_iota(jnp.int32, (groups, lanes), 0)
        lane = lax.broadcasted_iota(jnp.int32, (groups, lanes), 1)
        unit_norm, treat_count, ctrl_count = [
            jnp.sum(jnp.where(lane == i * groups + slot, counts, 0.0), axis=1, keepdims=True) for i in range(3)
        ]
        norms[...] = jnp.where(lane == 0, unit_norm, ctrl_count)
        gap = group_rows(0) / unit_norm - group_rows(groups) / jnp.maximum(treat_count, 1.0)
        before = days_of(lax.axis_index("day"), (groups, day_cols)).astype(f32) < ends[:, 0:1]
        raised_time = raised_days[...]
        pack[:groups, unit_rows:] = raised_time
        pack[groups:, unit_rows:] = jnp.zeros_like(raised_time)
        left = left_of(jnp.where(before, gap, 0.0), raised_time)

        def multiply(here, high, low):
            product = days_dot(left, high, low)
            pack[:groups, here] = add_terms(product, groups)
            pack[groups:, here] = add_terms(product, groups, 1)

        late = resident - 2 * block_rows

        @pl.loop(0, late // (2 * block_rows))
        def _(block):
            here = pl.ds(pl.multiple_of(block * 2 * block_rows, 2 * block_rows), 2 * block_rows)
            multiply(here, high_ref[here, :], low_ref[here, :])

        wait_all(copies)
        label = lax.broadcasted_iota(jnp.int32, raised_units.shape, 0)
        raised_units[...] = jnp.where(held_cohort[...] > label, jnp.exp(held_logit[...]), 0.0)
        for there in blocks_of(0, unit_rows - resident):
            more_high[there, :], more_low[there, :] = split_panel(held[there, :])
        for here in blocks_of(late, resident - late):
            multiply(here, high_ref[here, :], low_ref[here, :])
        for there in blocks_of(0, unit_rows - resident):
            multiply(pl.ds(resident + there.start, block_rows), more_high[there, :], more_low[there, :])


@first_half_only
def join_kernel(half, pack, post, *refs):
    norms, out = refs[:half], refs[half]
    groups, unit_rows = post.shape
    over_time = 1.0 / tree_sum(ref[:, 0:1] for ref in norms)
    out[:groups, :unit_rows] = pack[:groups, :unit_rows]
    out[:groups, unit_rows:] = pack[:groups, unit_rows:] * over_time
    out[groups:, :unit_rows] = pack[groups:, :unit_rows] * over_time - post[...]
    out[groups:, unit_rows:] = pack[groups:, unit_rows:]


@first_half_only
def third_kernel(half, *refs):
    parts, refs = [refs[0].at[day] for day in range(half)], refs[1:]
    high_ref, low_ref, more_high, more_low, norms, raised_units, ends, scaled, lam, out = refs
    groups, unit_rows = raised_units.shape
    resident, day_cols = high_ref.shape
    unit_norm, ctrl_count = norms[:, 0:1], norms[:, 1:2]
    factor = -step_rate / jnp.sqrt(ends[:, 0:1])
    over_unit = 1.0 / unit_norm
    me = lax.rem(lax.axis_index("day"), half)
    for day in range(half):
        lam[:, day * day_cols : (day + 1) * day_cols] = parts[day][:groups, unit_rows:]
    time_grad = jnp.zeros((groups, day_cols), f32)
    new_sum = jnp.zeros((groups, 1), f32)
    for start in range(0, unit_rows, block_rows):
        here = pl.ds(start, block_rows)
        whole = tree_sum(ref[:, here] for ref in parts)
        raised = raised_units[:, here]
        new = raised * over_unit * jnp.exp(whole[:groups] * factor)
        new_sum += jnp.sum(new, axis=1, keepdims=True)
        scaled[:, here] = new * ctrl_count
        left = left_of(jnp.where(raised > 0.0, whole[groups:], 0.0))
        if start < resident:
            high, low = high_ref[here, :], low_ref[here, :]
        else:
            there = pl.ds(start - resident, block_rows)
            high, low = more_high[there, :], more_low[there, :]
        time_grad += add_terms(rows_dot(left, high, low), groups)
    lane = lax.broadcasted_iota(jnp.int32, (groups, day_cols), 1)
    spare = (lane == day_cols - 1) & (me == half - 1)
    block = jnp.where(spare, new_sum, time_grad)
    for member in range(out.shape[0]):
        out[member] = block


def time_grad_of(grads, unit_devices, half, day):
    return tree_sum(grads[unit * half + half - 1 - day] for unit in range(unit_devices))


@first_half_only
def fourth_kernel(half, unit_devices, grads, totals):
    day_cols = grads.shape[2]
    last = time_grad_of(grads, unit_devices, half, half - 1)
    totals[...] = jnp.broadcast_to(last[:, day_cols - 1 :], totals.shape)


def fifth_kernel(half, unit_devices, totals, scaled, grads, lam, norms, ends, unit_weights, time_weights):
    groups, day_cols = time_weights.shape
    me = lax.axis_index("day")

    @pl.when(me < half)
    def _():
        unit_weights[...] = scaled[...] * (1.0 / totals[:, 0:1])
        root = jnp.sqrt(jnp.maximum(norms[:, 1:2], 1.0))
        moved_total = jnp.zeros((groups, 1), f32)
        own = jnp.zeros((groups, day_cols), f32)
        for day in range(half):
            total = time_grad_of(grads, unit_devices, half, day)
            moved = lam[:, day * day_cols : (day + 1) * day_cols] * jnp.exp(total * (-step_rate / root))
            moved_total += jnp.sum(moved, axis=1, keepdims=True)
            own = jnp.where(me == day, moved, own)
        time_weights[...] = own * (ends[:, 0:1] / moved_total)

    @pl.when(me >= half)
    def _():
        time_weights[...] = jnp.zeros_like(time_weights)


def sixth_kernel(half, sent_totals, sent_scaled, _, unit_weights, block, out_sem):
    @pl.when(lax.axis_index("day") >= half)
    def _():
        block[...] = sent_scaled[...] * (1.0 / sent_totals[:, 0:1])
        wait_all(fetch([block], [unit_weights], out_sem))


def local(outcomes, cohort, pre_end, post_start, unit_logit, time_logit):
    groups = pre_end.shape[0]
    unit_rows, day_cols = outcomes.shape
    day_devices = lax.axis_size("day")
    unit_devices = lax.axis_size("unit")
    half = day_devices // 2
    assert half * 2 == day_devices and half & (half - 1) == 0
    assert unit_devices & (unit_devices - 1) == 0
    panel_starts = [0, unit_rows // 8 * 3, unit_rows // 4 * 3, unit_rows]
    resident = unit_rows * 3 // 4 // (2 * block_rows) * (2 * block_rows)
    def meeting_at(first):
        return [first] + [unit for unit in reversed(range(unit_devices)) if unit != first]

    middle = unit_devices // 2

    def to_other_half(value, day_xor=0):
        pairs = [
            (u * day_devices + d, u * day_devices + half + (d ^ day_xor)) for u in range(unit_devices) for d in range(half)
        ]
        return lax.ppermute(value, ("unit", "day"), pairs)

    def over_days(value):
        halves = [list(range(half)), list(range(half, day_devices))]
        return lax.all_gather(value, "day", axis_index_groups=halves)

    def over_first_half(value):
        members = [
            [unit * day_devices + day for unit in meeting_at(middle + 1) for day in reversed(days)]
            for days in (range(half), range(half, day_devices))
        ]
        return lax.all_to_all(
            value, ("unit", "day"), split_axis=0, concat_axis=0, axis_index_groups=members, tiled=True
        )

    def over_units(value):
        members = [
            [unit * day_devices + day for unit in meeting_at(middle - 1 if day < half else middle)]
            for day in range(day_devices)
        ]
        return lax.all_to_all(
            value, ("unit", "day"), split_axis=0, concat_axis=0, axis_index_groups=members, tiled=True
        )

    def call(kernel, shapes, name, args, in_specs=None, out_specs=None, **more):
        return pl.pallas_call(
            kernel,
            in_specs=in_specs or [vmem] * len(args),
            out_specs=out_specs or [vmem] * len(shapes),
            out_shape=[
                shape if isinstance(shape, type(cross_hbm)) else jax.ShapeDtypeStruct(*shape) for shape in shapes
            ],
            compiler_params=params,
            name=name,
            **more,
        )(*args)

    arguments = (outcomes, cohort[None, :], pre_end[None, :], post_start[None, :], unit_logit, time_logit)
    fixed = [pltpu.with_memory_space_constraint(argument, pltpu.HBM) for argument in arguments]
    held = [pltpu.VMEM(argument.shape, argument.dtype) for argument in arguments]
    small_sems, panel_sems = pltpu.SemaphoreType.DMA((5,)), pltpu.SemaphoreType.DMA((3,))
    panel_terms = [((resident, day_cols), bf16)] * 2
    other_terms = [((unit_rows - resident, day_cols), bf16)] * 2
    width = 2 * groups * day_cols + lanes
    cross_hbm = pltpu.HBM((groups, unit_rows), f32)
    sums, cross, raised_days, time_norm, ends, high, low = call(
        functools.partial(first_kernel, day_devices * day_cols, half, panel_starts),
        [
            ((unit_devices, 1, width), f32),
            cross_hbm,
            ((groups, day_cols), f32),
            ((groups, lanes), f32),
            ((groups, lanes), f32),
            *panel_terms,
        ],
        "first_product",
        fixed,
        in_specs=[hbm] * 6,
        out_specs=[vmem, hbm] + [vmem] * 5,
        scratch_shapes=held
        + [
            pltpu.VMEM((1, width), f32),
            pltpu.VMEM((4 * groups, unit_rows), bf16),
            pltpu.VMEM((groups, unit_rows), f32),
            small_sems,
            panel_sems,
            pltpu.SemaphoreType.DMA((1,)),
        ],
    )
    downward = [
        (u * day_devices + d + half, u * day_devices + d) for u in range(unit_devices) for d in range(half)
    ]
    post = lax.ppermute(cross, ("unit", "day"), downward)
    pack, norms, raised_units, more_high, more_low = call(
        functools.partial(second_kernel, half, unit_devices),
        [
            ((2 * groups, unit_rows + day_cols), f32),
            ((groups, lanes), f32),
            ((groups, unit_rows), f32),
            *other_terms,
        ],
        "unit_gradient",
        (fixed[0], fixed[1], fixed[4], over_units(sums), raised_days, ends, high, low),
        in_specs=[hbm] * 3 + [vmem] * 5,
        scratch_shapes=[
            pltpu.VMEM((unit_rows - resident, day_cols), f32),
            held[1],
            held[4],
            pltpu.SemaphoreType.DMA((3,)),
        ],
    )
    time_norms = [time_norm]
    for k in range(1, half):
        pairs = [(u * day_devices + d, u * day_devices + (d ^ k)) for u in range(unit_devices) for d in range(half)]
        time_norms.append(lax.ppermute(time_norm, ("unit", "day"), pairs))
    (pack,) = call(
        functools.partial(join_kernel, half),
        [((2 * groups, unit_rows + day_cols), f32)],
        "join_post",
        (pack, post, *time_norms),
    )
    members = unit_devices * half
    scaled, lam, grads = call(
        functools.partial(third_kernel, half),
        [
            ((groups, unit_rows), f32),
            ((groups, half * day_cols), f32),
            ((members, groups, day_cols), f32),
        ],
        "time_gradient",
        (over_days(pack), high, low, more_high, more_low, norms, raised_units, ends),
    )
    sent_scaled = to_other_half(scaled)
    all_grads = over_first_half(grads)
    (totals,) = call(
        functools.partial(fourth_kernel, half, unit_devices), [((groups, lanes), f32)], "unit_totals", (all_grads,)
    )
    unit_weights, time_weights = call(
        functools.partial(fifth_kernel, half, unit_devices),
        [((groups, unit_rows), f32), ((groups, day_cols), f32)],
        "scale_weights",
        (totals, scaled, all_grads, lam, norms, ends),
    )
    (unit_weights,) = call(
        functools.partial(sixth_kernel, half),
        [((groups, unit_rows), f32)],
        "other_half",
        (to_other_half(totals, half > 1), sent_scaled, unit_weights),
        in_specs=[vmem, vmem, hbm],
        out_specs=[hbm],
        input_output_aliases={2: 0},
        scratch_shapes=[pltpu.VMEM((groups, unit_rows), f32), pltpu.SemaphoreType.DMA((1,))],
    )
    return unit_weights, time_weights


def solution(mesh):
    return jax.shard_map(
        local,
        mesh=mesh,
        in_specs=(P("unit", "day"), P("unit"), P(), P(), P(None, "unit"), P(None, "day")),
        out_specs=(P(None, "unit"), P(None, "day")),
        check_vma=False,
    )
```

```python
import functools

import jax
import jax.numpy as jnp
from jax import lax
from jax.experimental import pallas as pl
from jax.experimental.pallas import tpu as pltpu
from jax.sharding import PartitionSpec as P

step_rate = 16.0
f32 = jnp.float32
bf16 = jnp.bfloat16
lanes = 128
block_rows = 512
params = pltpu.CompilerParams(vmem_limit_bytes=24 * 1024 * 1024)
vmem = pl.BlockSpec(memory_space=pltpu.VMEM)
hbm = pl.BlockSpec(memory_space=pltpu.HBM)


def split_left(value):
    first = value.astype(bf16).astype(f32)
    return [first, value - first]


def left_of(*values):
    return jnp.concatenate([term for value in values for term in split_left(value)], axis=0).astype(bf16)


def split_panel(value):
    high = value.astype(bf16)
    return high, (value - high.astype(f32)).astype(bf16)


def rows_dot(left, high, low):
    return jnp.dot(left, high, preferred_element_type=f32) + jnp.dot(left, low, preferred_element_type=f32)


def days_dot(left, high, low):
    dims = (((1,), (1,)), ((), ()))
    return lax.dot_general(left, high, dims, preferred_element_type=f32) + lax.dot_general(
        left, low, dims, preferred_element_type=f32
    )


def add_terms(stack, groups, place=0):
    return stack[2 * place * groups :][:groups] + stack[(2 * place + 1) * groups :][:groups]


def tree_sum(values):
    values = list(values)
    while len(values) > 1:
        values = [values[i] + values[i + 1] for i in range(0, len(values), 2)]
    return values[0]


def column(row_ref):
    count = row_ref.shape[1]
    wide = jnp.broadcast_to(row_ref[...].astype(f32), (count, count))
    row = lax.broadcasted_iota(jnp.int32, (count, count), 0)
    lane = lax.broadcasted_iota(jnp.int32, (count, count), 1)
    return jnp.sum(jnp.where(row == lane, wide, 0.0), axis=1, keepdims=True).astype(jnp.int32)


def days_of(device, shape):
    return device * shape[1] + lax.broadcasted_iota(jnp.int32, shape, 1)


def first_half_only(kernel):
    @functools.wraps(kernel)
    def guarded(half, *refs):
        @pl.when(lax.axis_index("day") < half)
        def _():
            kernel(half, *refs)

    return guarded


def fetch(sources, targets, sems):
    copies = [pltpu.make_async_copy(*pair, sems.at[i]) for i, pair in enumerate(zip(sources, targets))]
    for copy in copies:
        copy.start()
    return copies


def fetch_rows(source, target, sems, starts):
    spans = [(start, stop - start) for start, stop in zip(starts, starts[1:])]
    parts = [pl.ds(*span) for span in spans]
    copies = fetch([source.at[here] for here in parts], [target.at[here] for here in parts], sems)
    return [(*span, copy) for span, copy in zip(spans, copies)]


def blocks_of(start, rows):
    return [pl.ds(here, block_rows) for here in range(start, start + rows, block_rows)]


def wait_all(copies):
    for copy in copies:
        copy.wait()


def repeat_start(block, out, sems):
    places = [out.at[i] for i in range(out.shape[0])]
    return fetch([block] * len(places), places, sems)


def first_kernel(all_count, half, starts, *refs):
    arguments, refs = refs[:6], refs[6:]
    out, cross, raised_days, time_norm, ends, high_ref, low_ref, *held, block, left_ref, cross_block, small_sems, panel_sems, out_sems = refs
    groups, day_cols = held[5].shape
    unit_rows, resident = held[0].shape[0], high_ref.shape[0]
    (post_copy,) = fetch(arguments[3:4], held[3:4], small_sems)
    unit_copies = fetch(arguments[1:5:3], held[1:5:3], small_sems.at[pl.ds(1, 2)])
    parts = fetch_rows(arguments[0], held[0], panel_sems, starts)
    day_copies = fetch(arguments[2:6:3], held[2:6:3], small_sems.at[pl.ds(3, 2)])
    panel, cohort, pre_row, post_row, unit_logit, time_logit = held
    post_copy.wait()
    wait_all(unit_copies)
    me = lax.axis_index("day")

    @pl.when(me < half)
    def _():
        counts = []

        def prepare(start, rows):
            here = pl.ds(start, rows)
            label = lax.broadcasted_iota(jnp.int32, (groups, rows), 0)
            treated = jnp.where(cohort[:, here] == label, 1.0, 0.0)
            control = jnp.where(cohort[:, here] > label, 1.0, 0.0)
            raised = jnp.exp(unit_logit[:, here]) * control
            left_ref[:, here] = left_of(raised, treated)
            counts.append([jnp.sum(value, axis=1, keepdims=True) for value in (raised, treated, control)])

        product = jnp.zeros((4 * groups, day_cols), f32)
        prepare(*parts[0][:2])
        for part, (start, rows, copy) in enumerate(parts):
            copy.wait()
            for here in blocks_of(start, rows):
                high, low = split_panel(panel[here, :])
                if here.start < resident:
                    high_ref[here, :] = high
                    low_ref[here, :] = low
                product += rows_dot(left_ref[:, here], high, low)
            if part + 1 < len(parts):
                prepare(*parts[part + 1][:2])
        lane = lax.broadcasted_iota(jnp.int32, (groups, lanes), 1)
        slot = lax.broadcasted_iota(jnp.int32, (groups, lanes), 0)
        norms = jnp.zeros((groups, lanes), f32)
        for i, count in enumerate(zip(*counts)):
            norms += jnp.where(lane == i * groups + slot, sum(count), 0.0)
        block[:, 2 * groups * day_cols :] = jnp.sum(norms, axis=0, keepdims=True)
        both_sums = jnp.concatenate([add_terms(product, groups), product[2 * groups :][:groups]], axis=0)
        for row in range(2 * groups):
            block[:, row * day_cols : (row + 1) * day_cols] = both_sums[row : row + 1, :]
        sends = repeat_start(block, out, out_sems)
        wait_all(day_copies)
        pre_end = column(pre_row)
        ends[...] = jnp.broadcast_to(pre_end.astype(f32), ends.shape)
        before = days_of(me, (groups, day_cols)) < pre_end
        raised_time = jnp.where(before, jnp.exp(time_logit[...]), 0.0)
        raised_days[...] = raised_time
        time_norm[...] = jnp.broadcast_to(jnp.sum(raised_time, axis=1, keepdims=True), time_norm.shape)
        wait_all(sends)

    @pl.when(me >= half)
    def _():
        post_start = column(post_row)
        after = jnp.where(days_of(me, (groups, day_cols)) >= post_start, 1.0, 0.0)
        left = left_of(after / (all_count - post_start).astype(f32))
        for start, rows, copy in parts:
            copy.wait()
            for here in blocks_of(start, rows):
                cross_block[:, here] = add_terms(days_dot(left, *split_panel(panel[here, :])), groups)
        sends = fetch([cross_block], [cross], out_sems)
        wait_all(day_copies)
        wait_all(sends)


@first_half_only
def second_kernel(half, unit_devices, panel, cohort, unit_logit, sums, raised_days, ends, high_ref, low_ref, *refs):
    pack, norms, raised_units, more_high, more_low, held, held_cohort, held_logit, sems = refs
    groups, day_cols = raised_days.shape
    unit_rows, resident = panel.shape[0], high_ref.shape[0]
    rest = pl.ds(resident, unit_rows - resident)
    copies = fetch([panel.at[rest], cohort, unit_logit], [held, held_cohort, held_logit], sems)

    @pl.when(lax.axis_index("day") < half)
    def _():
        total = tree_sum(sums[u] for u in range(unit_devices))

        def group_rows(first):
            starts = [(first + row) * day_cols for row in range(groups)]
            return jnp.concatenate([total[:, start : start + day_cols] for start in starts], axis=0)

        counts = jnp.broadcast_to(total[:, 2 * groups * day_cols :], (groups, lanes))
        slot = lax.broadcasted_iota(jnp.int32, (groups, lanes), 0)
        lane = lax.broadcasted_iota(jnp.int32, (groups, lanes), 1)
        unit_norm, treat_count, ctrl_count = [
            jnp.sum(jnp.where(lane == i * groups + slot, counts, 0.0), axis=1, keepdims=True) for i in range(3)
        ]
        norms[...] = jnp.where(lane == 0, unit_norm, ctrl_count)
        gap = group_rows(0) / unit_norm - group_rows(groups) / jnp.maximum(treat_count, 1.0)
        before = days_of(lax.axis_index("day"), (groups, day_cols)).astype(f32) < ends[:, 0:1]
        raised_time = raised_days[...]
        pack[:groups, unit_rows:] = raised_time
        pack[groups:, unit_rows:] = jnp.zeros_like(raised_time)
        left = left_of(jnp.where(before, gap, 0.0), raised_time)

        def multiply(here, high, low):
            product = days_dot(left, high, low)
            pack[:groups, here] = add_terms(product, groups)
            pack[groups:, here] = add_terms(product, groups, 1)

        late = resident - 2 * block_rows

        @pl.loop(0, late // (2 * block_rows))
        def _(block):
            here = pl.ds(pl.multiple_of(block * 2 * block_rows, 2 * block_rows), 2 * block_rows)
            multiply(here, high_ref[here, :], low_ref[here, :])

        wait_all(copies)
        label = lax.broadcasted_iota(jnp.int32, raised_units.shape, 0)
        raised_units[...] = jnp.where(held_cohort[...] > label, jnp.exp(held_logit[...]), 0.0)
        for there in blocks_of(0, unit_rows - resident):
            more_high[there, :], more_low[there, :] = split_panel(held[there, :])
        for here in blocks_of(late, resident - late):
            multiply(here, high_ref[here, :], low_ref[here, :])
        for there in blocks_of(0, unit_rows - resident):
            multiply(pl.ds(resident + there.start, block_rows), more_high[there, :], more_low[there, :])


@first_half_only
def join_kernel(half, pack, post, *refs):
    norms, out = refs[:half], refs[half]
    groups, unit_rows = post.shape
    over_time = 1.0 / tree_sum(ref[:, 0:1] for ref in norms)
    out[:groups, :unit_rows] = pack[:groups, :unit_rows]
    out[groups:, :unit_rows] = pack[groups:, :unit_rows] * over_time - post[...]
    out[groups:, unit_rows:] = jnp.zeros((groups, out.shape[1] - unit_rows), f32)
    own = pack[:groups, unit_rows:] * over_time
    day_cols = own.shape[1]
    for day in range(half):
        start = unit_rows + day * day_cols
        out[:groups, start : start + day_cols] = jnp.where(lax.axis_index("day") == day, own, 0.0)


@first_half_only
def third_kernel(half, *refs):
    parts, refs = refs[:1], refs[1:]
    high_ref, low_ref, more_high, more_low, norms, raised_units, ends, scaled, lam, out = refs
    groups, unit_rows = raised_units.shape
    resident, day_cols = high_ref.shape
    unit_norm, ctrl_count = norms[:, 0:1], norms[:, 1:2]
    factor = -step_rate / jnp.sqrt(ends[:, 0:1])
    over_unit = 1.0 / unit_norm
    me = lax.rem(lax.axis_index("day"), half)
    lam[...] = parts[0][:groups, unit_rows:]
    time_grad = jnp.zeros((groups, day_cols), f32)
    new_sum = jnp.zeros((groups, 1), f32)
    for start in range(0, unit_rows, block_rows):
        here = pl.ds(start, block_rows)
        whole = tree_sum(ref[:, here] for ref in parts)
        raised = raised_units[:, here]
        new = raised * over_unit * jnp.exp(whole[:groups] * factor)
        new_sum += jnp.sum(new, axis=1, keepdims=True)
        scaled[:, here] = new * ctrl_count
        left = left_of(jnp.where(raised > 0.0, whole[groups:], 0.0))
        if start < resident:
            high, low = high_ref[here, :], low_ref[here, :]
        else:
            there = pl.ds(start - resident, block_rows)
            high, low = more_high[there, :], more_low[there, :]
        time_grad += add_terms(rows_dot(left, high, low), groups)
    lane = lax.broadcasted_iota(jnp.int32, (groups, day_cols), 1)
    spare = (lane == day_cols - 1) & (me == half - 1)
    block = jnp.where(spare, new_sum, time_grad)
    for member in range(out.shape[0]):
        out[member] = block


def time_grad_of(grads, unit_devices, half, day):
    return tree_sum(grads[unit * half + half - 1 - day] for unit in range(unit_devices))


@first_half_only
def fourth_kernel(half, unit_devices, grads, totals):
    day_cols = grads.shape[2]
    last = time_grad_of(grads, unit_devices, half, half - 1)
    totals[...] = jnp.broadcast_to(last[:, day_cols - 1 :], totals.shape)


def fifth_kernel(half, unit_devices, totals, scaled, grads, lam, norms, ends, unit_weights, time_weights):
    groups, day_cols = time_weights.shape
    me = lax.axis_index("day")

    @pl.when(me < half)
    def _():
        unit_weights[...] = scaled[...] * (1.0 / totals[:, 0:1])
        root = jnp.sqrt(jnp.maximum(norms[:, 1:2], 1.0))
        moved_total = jnp.zeros((groups, 1), f32)
        own = jnp.zeros((groups, day_cols), f32)
        for day in range(half):
            total = time_grad_of(grads, unit_devices, half, day)
            moved = lam[:, day * day_cols : (day + 1) * day_cols] * jnp.exp(total * (-step_rate / root))
            moved_total += jnp.sum(moved, axis=1, keepdims=True)
            own = jnp.where(me == day, moved, own)
        time_weights[...] = own * (ends[:, 0:1] / moved_total)

    @pl.when(me >= half)
    def _():
        time_weights[...] = jnp.zeros_like(time_weights)


def sixth_kernel(half, sent_totals, sent_scaled, _, unit_weights, block, out_sem):
    @pl.when(lax.axis_index("day") >= half)
    def _():
        block[...] = sent_scaled[...] * (1.0 / sent_totals[:, 0:1])
        wait_all(fetch([block], [unit_weights], out_sem))


def local(outcomes, cohort, pre_end, post_start, unit_logit, time_logit):
    groups = pre_end.shape[0]
    unit_rows, day_cols = outcomes.shape
    day_devices = lax.axis_size("day")
    unit_devices = lax.axis_size("unit")
    half = day_devices // 2
    assert half * 2 == day_devices and half & (half - 1) == 0
    assert unit_devices & (unit_devices - 1) == 0
    panel_starts = [0, unit_rows // 8 * 3, unit_rows // 4 * 3, unit_rows]
    resident = unit_rows * 3 // 4 // (2 * block_rows) * (2 * block_rows)
    def meeting_at(first):
        return [first] + [unit for unit in reversed(range(unit_devices)) if unit != first]

    middle = unit_devices // 2

    def to_other_half(value, day_xor=0):
        pairs = [
            (u * day_devices + d, u * day_devices + half + (d ^ day_xor)) for u in range(unit_devices) for d in range(half)
        ]
        return lax.ppermute(value, ("unit", "day"), pairs)

    def over_days(value):
        halves = [list(range(half)), list(range(half, day_devices))]
        return lax.psum(value, "day", axis_index_groups=halves)

    def over_first_half(value):
        members = [
            [unit * day_devices + day for unit in meeting_at(middle + 1) for day in reversed(days)]
            for days in (range(half), range(half, day_devices))
        ]
        return lax.all_to_all(
            value, ("unit", "day"), split_axis=0, concat_axis=0, axis_index_groups=members, tiled=True
        )

    def over_units(value):
        members = [
            [unit * day_devices + day for unit in meeting_at(middle - 1 if day < half else middle)]
            for day in range(day_devices)
        ]
        return lax.all_to_all(
            value, ("unit", "day"), split_axis=0, concat_axis=0, axis_index_groups=members, tiled=True
        )

    def call(kernel, shapes, name, args, in_specs=None, out_specs=None, **more):
        return pl.pallas_call(
            kernel,
            in_specs=in_specs or [vmem] * len(args),
            out_specs=out_specs or [vmem] * len(shapes),
            out_shape=[
                shape if isinstance(shape, type(in_hbm)) else jax.ShapeDtypeStruct(*shape) for shape in shapes
            ],
            compiler_params=params,
            name=name,
            **more,
        )(*args)

    arguments = (outcomes, cohort[None, :], pre_end[None, :], post_start[None, :], unit_logit, time_logit)
    fixed = [pltpu.with_memory_space_constraint(argument, pltpu.HBM) for argument in arguments]
    held = [pltpu.VMEM(argument.shape, argument.dtype) for argument in arguments]
    small_sems, panel_sems = pltpu.SemaphoreType.DMA((5,)), pltpu.SemaphoreType.DMA((3,))
    panel_terms = [((resident, day_cols), bf16)] * 2
    other_terms = [((unit_rows - resident, day_cols), bf16)] * 2
    out_sems = pltpu.SemaphoreType.DMA((unit_devices,))
    width = 2 * groups * day_cols + lanes
    in_hbm = pltpu.HBM((unit_devices, 1, width), f32)
    sums, cross, raised_days, time_norm, ends, high, low = call(
        functools.partial(first_kernel, day_devices * day_cols, half, panel_starts),
        [
            in_hbm,
            pltpu.HBM((groups, unit_rows), f32),
            ((groups, day_cols), f32),
            ((groups, lanes), f32),
            ((groups, lanes), f32),
            *panel_terms,
        ],
        "first_product",
        fixed,
        in_specs=[hbm] * 6,
        out_specs=[hbm, hbm] + [vmem] * 5,
        scratch_shapes=held
        + [
            pltpu.VMEM((1, width), f32),
            pltpu.VMEM((4 * groups, unit_rows), bf16),
            pltpu.VMEM((groups, unit_rows), f32),
            small_sems,
            panel_sems,
            out_sems,
        ],
    )
    downward = [
        (u * day_devices + d + half, u * day_devices + d) for u in range(unit_devices) for d in range(half)
    ]
    post = lax.ppermute(cross, ("unit", "day"), downward)
    pack, norms, raised_units, more_high, more_low = call(
        functools.partial(second_kernel, half, unit_devices),
        [
            ((2 * groups, unit_rows + day_cols), f32),
            ((groups, lanes), f32),
            ((groups, unit_rows), f32),
            *other_terms,
        ],
        "unit_gradient",
        (fixed[0], fixed[1], fixed[4], over_units(sums), raised_days, ends, high, low),
        in_specs=[hbm] * 3 + [vmem] * 5,
        scratch_shapes=[
            pltpu.VMEM((unit_rows - resident, day_cols), f32),
            held[1],
            held[4],
            pltpu.SemaphoreType.DMA((3,)),
        ],
    )
    time_norms = [time_norm]
    for k in range(1, half):
        pairs = [(u * day_devices + d, u * day_devices + (d ^ k)) for u in range(unit_devices) for d in range(half)]
        time_norms.append(lax.ppermute(time_norm, ("unit", "day"), pairs))
    (pack,) = call(
        functools.partial(join_kernel, half),
        [((2 * groups, unit_rows + half * day_cols), f32)],
        "join_post",
        (pack, post, *time_norms),
    )
    members = unit_devices * half
    scaled, lam, grads = call(
        functools.partial(third_kernel, half),
        [
            ((groups, unit_rows), f32),
            ((groups, half * day_cols), f32),
            ((members, groups, day_cols), f32),
        ],
        "time_gradient",
        (over_days(pack), high, low, more_high, more_low, norms, raised_units, ends),
    )
    sent_scaled = to_other_half(scaled)
    all_grads = over_first_half(grads)
    (totals,) = call(
        functools.partial(fourth_kernel, half, unit_devices), [((groups, lanes), f32)], "unit_totals", (all_grads,)
    )
    unit_weights, time_weights = call(
        functools.partial(fifth_kernel, half, unit_devices),
        [((groups, unit_rows), f32), ((groups, day_cols), f32)],
        "scale_weights",
        (totals, scaled, all_grads, lam, norms, ends),
    )
    (unit_weights,) = call(
        functools.partial(sixth_kernel, half),
        [((groups, unit_rows), f32)],
        "other_half",
        (to_other_half(totals, half > 1), sent_scaled, unit_weights),
        in_specs=[vmem, vmem, hbm],
        out_specs=[hbm],
        input_output_aliases={2: 0},
        scratch_shapes=[pltpu.VMEM((groups, unit_rows), f32), pltpu.SemaphoreType.DMA((1,))],
    )
    return unit_weights, time_weights


def solution(mesh):
    return jax.shard_map(
        local,
        mesh=mesh,
        in_specs=(P("unit", "day"), P("unit"), P(), P(), P(None, "unit"), P(None, "day")),
        out_specs=(P(None, "unit"), P(None, "day")),
        check_vma=False,
    )
```

```python
import functools

import jax
import jax.numpy as jnp
from jax import lax
from jax.experimental import pallas as pl
from jax.experimental.pallas import tpu as pltpu
from jax.sharding import PartitionSpec as P

step_rate = 16.0
f32 = jnp.float32
bf16 = jnp.bfloat16
lanes = 128
block_rows = 512
params = pltpu.CompilerParams(vmem_limit_bytes=24 * 1024 * 1024)
vmem = pl.BlockSpec(memory_space=pltpu.VMEM)
hbm = pl.BlockSpec(memory_space=pltpu.HBM)


def split_left(value):
    first = value.astype(bf16).astype(f32)
    return [first, value - first]


def left_of(*values):
    return jnp.concatenate([term for value in values for term in split_left(value)], axis=0).astype(bf16)


def split_panel(value):
    high = value.astype(bf16)
    return high, (value - high.astype(f32)).astype(bf16)


def rows_dot(left, high, low):
    return jnp.dot(left, high, preferred_element_type=f32) + jnp.dot(left, low, preferred_element_type=f32)


def days_dot(left, high, low):
    dims = (((1,), (1,)), ((), ()))
    return lax.dot_general(left, high, dims, preferred_element_type=f32) + lax.dot_general(
        left, low, dims, preferred_element_type=f32
    )


def add_terms(stack, groups, place=0):
    return stack[2 * place * groups :][:groups] + stack[(2 * place + 1) * groups :][:groups]


def tree_sum(values):
    values = list(values)
    while len(values) > 1:
        values = [values[i] + values[i + 1] for i in range(0, len(values), 2)]
    return values[0]


def column(row_ref):
    count = row_ref.shape[1]
    wide = jnp.broadcast_to(row_ref[...].astype(f32), (count, count))
    row = lax.broadcasted_iota(jnp.int32, (count, count), 0)
    lane = lax.broadcasted_iota(jnp.int32, (count, count), 1)
    return jnp.sum(jnp.where(row == lane, wide, 0.0), axis=1, keepdims=True).astype(jnp.int32)


def days_of(device, shape):
    return device * shape[1] + lax.broadcasted_iota(jnp.int32, shape, 1)


def first_half_only(kernel):
    @functools.wraps(kernel)
    def guarded(half, *refs):
        @pl.when(lax.axis_index("day") < half)
        def _():
            kernel(half, *refs)

    return guarded


def fetch(sources, targets, sems):
    copies = [pltpu.make_async_copy(*pair, sems.at[i]) for i, pair in enumerate(zip(sources, targets))]
    for copy in copies:
        copy.start()
    return copies


def fetch_rows(source, target, sems, starts):
    spans = [(start, stop - start) for start, stop in zip(starts, starts[1:])]
    parts = [pl.ds(*span) for span in spans]
    copies = fetch([source.at[here] for here in parts], [target.at[here] for here in parts], sems)
    return [(*span, copy) for span, copy in zip(spans, copies)]


def blocks_of(start, rows):
    return [pl.ds(here, block_rows) for here in range(start, start + rows, block_rows)]


def wait_all(copies):
    for copy in copies:
        copy.wait()


def repeat_start(block, out, sems):
    places = [out.at[i] for i in range(out.shape[0])]
    return fetch([block] * len(places), places, sems)


def first_kernel(all_count, half, starts, *refs):
    arguments, refs = refs[:6], refs[6:]
    out, cross, raised_days, time_norm, ends, high_ref, low_ref, *held, block, left_ref, cross_block, small_sems, panel_sems, out_sems = refs
    groups, day_cols = held[5].shape
    unit_rows, resident = held[0].shape[0], high_ref.shape[0]
    (post_copy,) = fetch(arguments[3:4], held[3:4], small_sems)
    unit_copies = fetch(arguments[1:5:3], held[1:5:3], small_sems.at[pl.ds(1, 2)])
    parts = fetch_rows(arguments[0], held[0], panel_sems, starts)
    day_copies = fetch(arguments[2:6:3], held[2:6:3], small_sems.at[pl.ds(3, 2)])
    panel, cohort, pre_row, post_row, unit_logit, time_logit = held
    post_copy.wait()
    wait_all(unit_copies)
    me = lax.axis_index("day")

    @pl.when(me < half)
    def _():
        counts = []

        def prepare(start, rows):
            here = pl.ds(start, rows)
            label = lax.broadcasted_iota(jnp.int32, (groups, rows), 0)
            treated = jnp.where(cohort[:, here] == label, 1.0, 0.0)
            control = jnp.where(cohort[:, here] > label, 1.0, 0.0)
            raised = jnp.exp(unit_logit[:, here]) * control
            left_ref[:, here] = left_of(raised, treated)
            counts.append([jnp.sum(value, axis=1, keepdims=True) for value in (raised, treated, control)])

        product = jnp.zeros((4 * groups, day_cols), f32)
        prepare(*parts[0][:2])
        for part, (start, rows, copy) in enumerate(parts):
            copy.wait()
            for here in blocks_of(start, rows):
                high, low = split_panel(panel[here, :])
                if here.start < resident:
                    high_ref[here, :] = high
                    low_ref[here, :] = low
                product += rows_dot(left_ref[:, here], high, low)
            if part + 1 < len(parts):
                prepare(*parts[part + 1][:2])
        lane = lax.broadcasted_iota(jnp.int32, (groups, lanes), 1)
        slot = lax.broadcasted_iota(jnp.int32, (groups, lanes), 0)
        norms = jnp.zeros((groups, lanes), f32)
        for i, count in enumerate(zip(*counts)):
            norms += jnp.where(lane == i * groups + slot, sum(count), 0.0)
        block[:, 2 * groups * day_cols :] = jnp.sum(norms, axis=0, keepdims=True)
        both_sums = jnp.concatenate([add_terms(product, groups), product[2 * groups :][:groups]], axis=0)
        for row in range(2 * groups):
            block[:, row * day_cols : (row + 1) * day_cols] = both_sums[row : row + 1, :]
        sends = repeat_start(block, out, out_sems)
        wait_all(day_copies)
        pre_end = column(pre_row)
        ends[...] = jnp.broadcast_to(pre_end.astype(f32), ends.shape)
        before = days_of(me, (groups, day_cols)) < pre_end
        raised_time = jnp.where(before, jnp.exp(time_logit[...]), 0.0)
        raised_days[...] = raised_time
        time_norm[...] = jnp.broadcast_to(jnp.sum(raised_time, axis=1, keepdims=True), time_norm.shape)
        wait_all(sends)

    @pl.when(me >= half)
    def _():
        post_start = column(post_row)
        after = jnp.where(days_of(me, (groups, day_cols)) >= post_start, 1.0, 0.0)
        left = left_of(after / (all_count - post_start).astype(f32))
        for start, rows, copy in parts:
            copy.wait()
            for here in blocks_of(start, rows):
                cross_block[:, here] = add_terms(days_dot(left, *split_panel(panel[here, :])), groups)
        sends = fetch([cross_block], [cross], out_sems)
        wait_all(day_copies)
        wait_all(sends)


@first_half_only
def second_kernel(half, unit_devices, panel, cohort, unit_logit, sums, raised_days, ends, high_ref, low_ref, *refs):
    pack, norms, raised_units, more_high, more_low, held, held_cohort, held_logit, sems = refs
    groups, day_cols = raised_days.shape
    unit_rows, resident = panel.shape[0], high_ref.shape[0]
    rest = pl.ds(resident, unit_rows - resident)
    copies = fetch([panel.at[rest], cohort, unit_logit], [held, held_cohort, held_logit], sems)

    @pl.when(lax.axis_index("day") < half)
    def _():
        total = tree_sum(sums[u] for u in range(unit_devices))

        def group_rows(first):
            starts = [(first + row) * day_cols for row in range(groups)]
            return jnp.concatenate([total[:, start : start + day_cols] for start in starts], axis=0)

        counts = jnp.broadcast_to(total[:, 2 * groups * day_cols :], (groups, lanes))
        slot = lax.broadcasted_iota(jnp.int32, (groups, lanes), 0)
        lane = lax.broadcasted_iota(jnp.int32, (groups, lanes), 1)
        unit_norm, treat_count, ctrl_count = [
            jnp.sum(jnp.where(lane == i * groups + slot, counts, 0.0), axis=1, keepdims=True) for i in range(3)
        ]
        norms[...] = jnp.where(lane == 0, unit_norm, ctrl_count)
        gap = group_rows(0) / unit_norm - group_rows(groups) / jnp.maximum(treat_count, 1.0)
        before = days_of(lax.axis_index("day"), (groups, day_cols)).astype(f32) < ends[:, 0:1]
        raised_time = raised_days[...]
        pack[:groups, unit_rows:] = raised_time
        pack[groups:, unit_rows:] = jnp.zeros_like(raised_time)
        left = left_of(jnp.where(before, gap, 0.0), raised_time)

        def multiply(here, high, low):
            product = days_dot(left, high, low)
            pack[:groups, here] = add_terms(product, groups)
            pack[groups:, here] = add_terms(product, groups, 1)

        late = resident - 2 * block_rows

        @pl.loop(0, late // (2 * block_rows))
        def _(block):
            here = pl.ds(pl.multiple_of(block * 2 * block_rows, 2 * block_rows), 2 * block_rows)
            multiply(here, high_ref[here, :], low_ref[here, :])

        wait_all(copies)
        label = lax.broadcasted_iota(jnp.int32, raised_units.shape, 0)
        raised_units[...] = jnp.where(held_cohort[...] > label, jnp.exp(held_logit[...]), 0.0)
        for there in blocks_of(0, unit_rows - resident):
            more_high[there, :], more_low[there, :] = split_panel(held[there, :])
        for here in blocks_of(late, resident - late):
            multiply(here, high_ref[here, :], low_ref[here, :])
        for there in blocks_of(0, unit_rows - resident):
            multiply(pl.ds(resident + there.start, block_rows), more_high[there, :], more_low[there, :])


@first_half_only
def join_kernel(half, pack, post, *refs):
    norms, out = refs[:half], refs[half]
    groups, unit_rows = post.shape
    over_time = 1.0 / tree_sum(ref[:, 0:1] for ref in norms)
    out[:groups, :unit_rows] = pack[:groups, :unit_rows]
    out[:groups, unit_rows:] = pack[:groups, unit_rows:] * over_time
    out[groups:, :unit_rows] = pack[groups:, :unit_rows] * over_time - post[...]
    out[groups:, unit_rows:] = pack[groups:, unit_rows:]


@first_half_only
def third_kernel(half, *refs):
    parts, refs = [refs[0].at[day] for day in range(half)], refs[1:]
    high_ref, low_ref, more_high, more_low, norms, raised_units, ends, scaled, lam, out = refs
    groups, unit_rows = raised_units.shape
    resident, day_cols = high_ref.shape
    unit_norm, ctrl_count = norms[:, 0:1], norms[:, 1:2]
    factor = -step_rate / jnp.sqrt(ends[:, 0:1])
    over_unit = 1.0 / unit_norm
    me = lax.rem(lax.axis_index("day"), half)
    for day in range(half):
        lam[:, day * day_cols : (day + 1) * day_cols] = parts[day][:groups, unit_rows:]
    time_grad = jnp.zeros((groups, day_cols), f32)
    new_sum = jnp.zeros((groups, 1), f32)
    for start in range(0, unit_rows, block_rows):
        here = pl.ds(start, block_rows)
        whole = tree_sum(ref[:, here] for ref in parts)
        raised = raised_units[:, here]
        new = raised * over_unit * jnp.exp(whole[:groups] * factor)
        new_sum += jnp.sum(new, axis=1, keepdims=True)
        scaled[:, here] = new * ctrl_count
        left = left_of(jnp.where(raised > 0.0, whole[groups:], 0.0))
        if start < resident:
            high, low = high_ref[here, :], low_ref[here, :]
        else:
            there = pl.ds(start - resident, block_rows)
            high, low = more_high[there, :], more_low[there, :]
        time_grad += add_terms(rows_dot(left, high, low), groups)
    lane = lax.broadcasted_iota(jnp.int32, (groups, day_cols), 1)
    spare = (lane == day_cols - 1) & (me == half - 1)
    block = jnp.where(spare, new_sum, time_grad)
    for member in range(out.shape[0]):
        out[member] = block


def time_grad_of(grads, unit_devices, half, day):
    return tree_sum(grads[unit * half + half - 1 - day] for unit in range(unit_devices))


@first_half_only
def fourth_kernel(half, unit_devices, grads, totals):
    day_cols = grads.shape[2]
    last = time_grad_of(grads, unit_devices, half, half - 1)
    totals[...] = jnp.broadcast_to(last[:, day_cols - 1 :], totals.shape)


def fifth_kernel(half, unit_devices, totals, scaled, grads, lam, norms, ends, unit_weights, time_weights):
    groups, day_cols = time_weights.shape
    me = lax.axis_index("day")

    @pl.when(me < half)
    def _():
        unit_weights[...] = scaled[...] * (1.0 / totals[:, 0:1])
        root = jnp.sqrt(jnp.maximum(norms[:, 1:2], 1.0))
        moved_total = jnp.zeros((groups, 1), f32)
        own = jnp.zeros((groups, day_cols), f32)
        for day in range(half):
            total = time_grad_of(grads, unit_devices, half, day)
            moved = lam[:, day * day_cols : (day + 1) * day_cols] * jnp.exp(total * (-step_rate / root))
            moved_total += jnp.sum(moved, axis=1, keepdims=True)
            own = jnp.where(me == day, moved, own)
        time_weights[...] = own * (ends[:, 0:1] / moved_total)

    @pl.when(me >= half)
    def _():
        time_weights[...] = jnp.zeros_like(time_weights)


def sixth_kernel(half, sent_totals, sent_scaled, _, unit_weights, block, out_sem):
    @pl.when(lax.axis_index("day") >= half)
    def _():
        block[...] = sent_scaled[...] * (1.0 / sent_totals[:, 0:1])
        wait_all(fetch([block], [unit_weights], out_sem))


def local(outcomes, cohort, pre_end, post_start, unit_logit, time_logit):
    groups = pre_end.shape[0]
    unit_rows, day_cols = outcomes.shape
    day_devices = lax.axis_size("day")
    unit_devices = lax.axis_size("unit")
    half = day_devices // 2
    assert half * 2 == day_devices and half & (half - 1) == 0
    assert unit_devices & (unit_devices - 1) == 0
    panel_starts = [0, unit_rows // 8 * 3, unit_rows // 4 * 3, unit_rows]
    resident = unit_rows * 3 // 4 // (2 * block_rows) * (2 * block_rows)
    def meeting_at(first):
        return [first] + [unit for unit in reversed(range(unit_devices)) if unit != first]

    middle = unit_devices // 2

    def to_other_half(value, day_xor=0):
        pairs = [
            (u * day_devices + d, u * day_devices + half + (d ^ day_xor)) for u in range(unit_devices) for d in range(half)
        ]
        return lax.ppermute(value, ("unit", "day"), pairs)

    def over_days(value):
        halves = [list(range(half)), list(range(half, day_devices))]
        return lax.all_gather(value, "day", axis_index_groups=halves)

    def over_first_half(value):
        members = [
            [unit * day_devices + day for unit in meeting_at(unit_devices - 1) for day in reversed(days)]
            for days in (range(half), range(half, day_devices))
        ]
        return lax.all_to_all(
            value, ("unit", "day"), split_axis=0, concat_axis=0, axis_index_groups=members, tiled=True
        )

    def over_units(value):
        members = [
            [unit * day_devices + day for unit in meeting_at(middle - 1 if day < half else middle)]
            for day in range(day_devices)
        ]
        return lax.all_to_all(
            value, ("unit", "day"), split_axis=0, concat_axis=0, axis_index_groups=members, tiled=True
        )

    def call(kernel, shapes, name, args, in_specs=None, out_specs=None, **more):
        return pl.pallas_call(
            kernel,
            in_specs=in_specs or [vmem] * len(args),
            out_specs=out_specs or [vmem] * len(shapes),
            out_shape=[
                shape if isinstance(shape, type(in_hbm)) else jax.ShapeDtypeStruct(*shape) for shape in shapes
            ],
            compiler_params=params,
            name=name,
            **more,
        )(*args)

    arguments = (outcomes, cohort[None, :], pre_end[None, :], post_start[None, :], unit_logit, time_logit)
    fixed = [pltpu.with_memory_space_constraint(argument, pltpu.HBM) for argument in arguments]
    held = [pltpu.VMEM(argument.shape, argument.dtype) for argument in arguments]
    small_sems, panel_sems = pltpu.SemaphoreType.DMA((5,)), pltpu.SemaphoreType.DMA((3,))
    panel_terms = [((resident, day_cols), bf16)] * 2
    other_terms = [((unit_rows - resident, day_cols), bf16)] * 2
    out_sems = pltpu.SemaphoreType.DMA((unit_devices,))
    width = 2 * groups * day_cols + lanes
    in_hbm = pltpu.HBM((unit_devices, 1, width), f32)
    sums, cross, raised_days, time_norm, ends, high, low = call(
        functools.partial(first_kernel, day_devices * day_cols, half, panel_starts),
        [
            in_hbm,
            pltpu.HBM((groups, unit_rows), f32),
            ((groups, day_cols), f32),
            ((groups, lanes), f32),
            ((groups, lanes), f32),
            *panel_terms,
        ],
        "first_product",
        fixed,
        in_specs=[hbm] * 6,
        out_specs=[hbm, hbm] + [vmem] * 5,
        scratch_shapes=held
        + [
            pltpu.VMEM((1, width), f32),
            pltpu.VMEM((4 * groups, unit_rows), bf16),
            pltpu.VMEM((groups, unit_rows), f32),
            small_sems,
            panel_sems,
            out_sems,
        ],
    )
    downward = [
        (u * day_devices + d + half, u * day_devices + d) for u in range(unit_devices) for d in range(half)
    ]
    post = lax.ppermute(cross, ("unit", "day"), downward)
    pack, norms, raised_units, more_high, more_low = call(
        functools.partial(second_kernel, half, unit_devices),
        [
            ((2 * groups, unit_rows + day_cols), f32),
            ((groups, lanes), f32),
            ((groups, unit_rows), f32),
            *other_terms,
        ],
        "unit_gradient",
        (fixed[0], fixed[1], fixed[4], over_units(sums), raised_days, ends, high, low),
        in_specs=[hbm] * 3 + [vmem] * 5,
        scratch_shapes=[
            pltpu.VMEM((unit_rows - resident, day_cols), f32),
            held[1],
            held[4],
            pltpu.SemaphoreType.DMA((3,)),
        ],
    )
    time_norms = [time_norm]
    for k in range(1, half):
        pairs = [(u * day_devices + d, u * day_devices + (d ^ k)) for u in range(unit_devices) for d in range(half)]
        time_norms.append(lax.ppermute(time_norm, ("unit", "day"), pairs))
    (pack,) = call(
        functools.partial(join_kernel, half),
        [((2 * groups, unit_rows + day_cols), f32)],
        "join_post",
        (pack, post, *time_norms),
    )
    members = unit_devices * half
    scaled, lam, grads = call(
        functools.partial(third_kernel, half),
        [
            ((groups, unit_rows), f32),
            ((groups, half * day_cols), f32),
            ((members, groups, day_cols), f32),
        ],
        "time_gradient",
        (over_days(pack), high, low, more_high, more_low, norms, raised_units, ends),
    )
    sent_scaled = to_other_half(scaled)
    all_grads = over_first_half(grads)
    (totals,) = call(
        functools.partial(fourth_kernel, half, unit_devices), [((groups, lanes), f32)], "unit_totals", (all_grads,)
    )
    unit_weights, time_weights = call(
        functools.partial(fifth_kernel, half, unit_devices),
        [((groups, unit_rows), f32), ((groups, day_cols), f32)],
        "scale_weights",
        (totals, scaled, all_grads, lam, norms, ends),
    )
    (unit_weights,) = call(
        functools.partial(sixth_kernel, half),
        [((groups, unit_rows), f32)],
        "other_half",
        (to_other_half(totals, half > 1), sent_scaled, unit_weights),
        in_specs=[vmem, vmem, hbm],
        out_specs=[hbm],
        input_output_aliases={2: 0},
        scratch_shapes=[pltpu.VMEM((groups, unit_rows), f32), pltpu.SemaphoreType.DMA((1,))],
    )
    return unit_weights, time_weights


def solution(mesh):
    return jax.shard_map(
        local,
        mesh=mesh,
        in_specs=(P("unit", "day"), P("unit"), P(), P(), P(None, "unit"), P(None, "day")),
        out_specs=(P(None, "unit"), P(None, "day")),
        check_vma=False,
    )
```

```python
import functools

import jax
import jax.numpy as jnp
from jax import lax
from jax.experimental import pallas as pl
from jax.experimental.pallas import tpu as pltpu
from jax.sharding import PartitionSpec as P

step_rate = 16.0
f32 = jnp.float32
bf16 = jnp.bfloat16
lanes = 128
block_rows = 512
params = pltpu.CompilerParams(vmem_limit_bytes=24 * 1024 * 1024)
vmem = pl.BlockSpec(memory_space=pltpu.VMEM)
hbm = pl.BlockSpec(memory_space=pltpu.HBM)


def split_left(value):
    first = value.astype(bf16).astype(f32)
    return [first, value - first]


def left_of(*values):
    return jnp.concatenate([term for value in values for term in split_left(value)], axis=0).astype(bf16)


def split_panel(value):
    high = value.astype(bf16)
    return high, (value - high.astype(f32)).astype(bf16)


def rows_dot(left, high, low):
    return jnp.dot(left, high, preferred_element_type=f32) + jnp.dot(left, low, preferred_element_type=f32)


def days_dot(left, high, low):
    dims = (((1,), (1,)), ((), ()))
    return lax.dot_general(left, high, dims, preferred_element_type=f32) + lax.dot_general(
        left, low, dims, preferred_element_type=f32
    )


def add_terms(stack, groups, place=0):
    return stack[2 * place * groups :][:groups] + stack[(2 * place + 1) * groups :][:groups]


def tree_sum(values):
    values = list(values)
    while len(values) > 1:
        values = [values[i] + values[i + 1] for i in range(0, len(values), 2)]
    return values[0]


def column(row_ref):
    count = row_ref.shape[1]
    wide = jnp.broadcast_to(row_ref[...].astype(f32), (count, count))
    row = lax.broadcasted_iota(jnp.int32, (count, count), 0)
    lane = lax.broadcasted_iota(jnp.int32, (count, count), 1)
    return jnp.sum(jnp.where(row == lane, wide, 0.0), axis=1, keepdims=True).astype(jnp.int32)


def days_of(device, shape):
    return device * shape[1] + lax.broadcasted_iota(jnp.int32, shape, 1)


def first_half_only(kernel):
    @functools.wraps(kernel)
    def guarded(half, *refs):
        @pl.when(lax.axis_index("day") < half)
        def _():
            kernel(half, *refs)

    return guarded


def fetch(sources, targets, sems):
    copies = [pltpu.make_async_copy(*pair, sems.at[i]) for i, pair in enumerate(zip(sources, targets))]
    for copy in copies:
        copy.start()
    return copies


def fetch_rows(source, target, sems, starts):
    spans = [(start, stop - start) for start, stop in zip(starts, starts[1:])]
    parts = [pl.ds(*span) for span in spans]
    copies = fetch([source.at[here] for here in parts], [target.at[here] for here in parts], sems)
    return [(*span, copy) for span, copy in zip(spans, copies)]


def blocks_of(start, rows):
    return [pl.ds(here, block_rows) for here in range(start, start + rows, block_rows)]


def wait_all(copies):
    for copy in copies:
        copy.wait()


def repeat_start(block, out, sems):
    places = [out.at[i] for i in range(out.shape[0])]
    return fetch([block] * len(places), places, sems)


def first_kernel(all_count, half, starts, *refs):
    arguments, refs = refs[:6], refs[6:]
    out, cross, raised_days, time_norm, ends, high_ref, low_ref, *held, block, left_ref, cross_block, small_sems, panel_sems, out_sems = refs
    groups, day_cols = held[5].shape
    unit_rows, resident = held[0].shape[0], high_ref.shape[0]
    (post_copy,) = fetch(arguments[3:4], held[3:4], small_sems)
    unit_copies = fetch(arguments[1:5:3], held[1:5:3], small_sems.at[pl.ds(1, 2)])
    parts = fetch_rows(arguments[0], held[0], panel_sems, starts)
    day_copies = fetch(arguments[2:6:3], held[2:6:3], small_sems.at[pl.ds(3, 2)])
    panel, cohort, pre_row, post_row, unit_logit, time_logit = held
    post_copy.wait()
    wait_all(unit_copies)
    me = lax.axis_index("day")

    @pl.when(me < half)
    def _():
        counts = []

        def prepare(start, rows):
            here = pl.ds(start, rows)
            label = lax.broadcasted_iota(jnp.int32, (groups, rows), 0)
            treated = jnp.where(cohort[:, here] == label, 1.0, 0.0)
            control = jnp.where(cohort[:, here] > label, 1.0, 0.0)
            raised = jnp.exp(unit_logit[:, here]) * control
            left_ref[:, here] = left_of(raised, treated)
            counts.append([jnp.sum(value, axis=1, keepdims=True) for value in (raised, treated, control)])

        product = jnp.zeros((4 * groups, day_cols), f32)
        prepare(*parts[0][:2])
        for part, (start, rows, copy) in enumerate(parts):
            copy.wait()
            for here in blocks_of(start, rows):
                high, low = split_panel(panel[here, :])
                if here.start < resident:
                    high_ref[here, :] = high
                    low_ref[here, :] = low
                product += rows_dot(left_ref[:, here], high, low)
            if part + 1 < len(parts):
                prepare(*parts[part + 1][:2])
        lane = lax.broadcasted_iota(jnp.int32, (groups, lanes), 1)
        slot = lax.broadcasted_iota(jnp.int32, (groups, lanes), 0)
        norms = jnp.zeros((groups, lanes), f32)
        for i, count in enumerate(zip(*counts)):
            norms += jnp.where(lane == i * groups + slot, sum(count), 0.0)
        block[:, 2 * groups * day_cols :] = jnp.sum(norms, axis=0, keepdims=True)
        both_sums = jnp.concatenate([add_terms(product, groups), product[2 * groups :][:groups]], axis=0)
        for row in range(2 * groups):
            block[:, row * day_cols : (row + 1) * day_cols] = both_sums[row : row + 1, :]
        sends = repeat_start(block, out, out_sems)
        wait_all(day_copies)
        pre_end = column(pre_row)
        ends[...] = jnp.broadcast_to(pre_end.astype(f32), ends.shape)
        before = days_of(me, (groups, day_cols)) < pre_end
        raised_time = jnp.where(before, jnp.exp(time_logit[...]), 0.0)
        raised_days[...] = raised_time
        time_norm[...] = jnp.broadcast_to(jnp.sum(raised_time, axis=1, keepdims=True), time_norm.shape)
        wait_all(sends)

    @pl.when(me >= half)
    def _():
        post_start = column(post_row)
        after = jnp.where(days_of(me, (groups, day_cols)) >= post_start, 1.0, 0.0)
        left = left_of(after / (all_count - post_start).astype(f32))
        for start, rows, copy in parts:
            copy.wait()
            for here in blocks_of(start, rows):
                cross_block[:, here] = add_terms(days_dot(left, *split_panel(panel[here, :])), groups)
        sends = fetch([cross_block], [cross], out_sems)
        wait_all(day_copies)
        wait_all(sends)


@first_half_only
def second_kernel(half, unit_devices, panel, cohort, unit_logit, sums, raised_days, ends, high_ref, low_ref, *refs):
    pack, norms, raised_units, more_high, more_low, held, held_cohort, held_logit, sems = refs
    groups, day_cols = raised_days.shape
    unit_rows, resident = panel.shape[0], high_ref.shape[0]
    rest = pl.ds(resident, unit_rows - resident)
    copies = fetch([panel.at[rest], cohort, unit_logit], [held, held_cohort, held_logit], sems)

    @pl.when(lax.axis_index("day") < half)
    def _():
        total = tree_sum(sums[u] for u in range(unit_devices))

        def group_rows(first):
            starts = [(first + row) * day_cols for row in range(groups)]
            return jnp.concatenate([total[:, start : start + day_cols] for start in starts], axis=0)

        counts = jnp.broadcast_to(total[:, 2 * groups * day_cols :], (groups, lanes))
        slot = lax.broadcasted_iota(jnp.int32, (groups, lanes), 0)
        lane = lax.broadcasted_iota(jnp.int32, (groups, lanes), 1)
        unit_norm, treat_count, ctrl_count = [
            jnp.sum(jnp.where(lane == i * groups + slot, counts, 0.0), axis=1, keepdims=True) for i in range(3)
        ]
        norms[...] = jnp.where(lane == 0, unit_norm, ctrl_count)
        gap = group_rows(0) / unit_norm - group_rows(groups) / jnp.maximum(treat_count, 1.0)
        before = days_of(lax.axis_index("day"), (groups, day_cols)).astype(f32) < ends[:, 0:1]
        raised_time = raised_days[...]
        pack[:groups, unit_rows:] = raised_time
        pack[groups:, unit_rows:] = jnp.zeros_like(raised_time)
        left = left_of(jnp.where(before, gap, 0.0), raised_time)

        def multiply(here, high, low):
            product = days_dot(left, high, low)
            pack[:groups, here] = add_terms(product, groups)
            pack[groups:, here] = add_terms(product, groups, 1)

        late = resident - 4 * block_rows

        @pl.loop(0, late // (2 * block_rows))
        def _(block):
            here = pl.ds(pl.multiple_of(block * 2 * block_rows, 2 * block_rows), 2 * block_rows)
            multiply(here, high_ref[here, :], low_ref[here, :])

        wait_all(copies)
        label = lax.broadcasted_iota(jnp.int32, raised_units.shape, 0)
        raised_units[...] = jnp.where(held_cohort[...] > label, jnp.exp(held_logit[...]), 0.0)
        for there in blocks_of(0, unit_rows - resident):
            more_high[there, :], more_low[there, :] = split_panel(held[there, :])
        for here in blocks_of(late, resident - late):
            multiply(here, high_ref[here, :], low_ref[here, :])
        for there in blocks_of(0, unit_rows - resident):
            multiply(pl.ds(resident + there.start, block_rows), more_high[there, :], more_low[there, :])


@first_half_only
def join_kernel(half, pack, post, *refs):
    norms, out = refs[:half], refs[half]
    groups, unit_rows = post.shape
    over_time = 1.0 / tree_sum(ref[:, 0:1] for ref in norms)
    out[:groups, :unit_rows] = pack[:groups, :unit_rows]
    out[:groups, unit_rows:] = pack[:groups, unit_rows:] * over_time
    out[groups:, :unit_rows] = pack[groups:, :unit_rows] * over_time - post[...]
    out[groups:, unit_rows:] = pack[groups:, unit_rows:]


@first_half_only
def third_kernel(half, *refs):
    parts, refs = [refs[0].at[day] for day in range(half)], refs[1:]
    high_ref, low_ref, more_high, more_low, norms, raised_units, ends, scaled, lam, out = refs
    groups, unit_rows = raised_units.shape
    resident, day_cols = high_ref.shape
    unit_norm, ctrl_count = norms[:, 0:1], norms[:, 1:2]
    factor = -step_rate / jnp.sqrt(ends[:, 0:1])
    over_unit = 1.0 / unit_norm
    me = lax.rem(lax.axis_index("day"), half)
    for day in range(half):
        lam[:, day * day_cols : (day + 1) * day_cols] = parts[day][:groups, unit_rows:]
    time_grad = jnp.zeros((groups, day_cols), f32)
    new_sum = jnp.zeros((groups, 1), f32)
    for start in range(0, unit_rows, block_rows):
        here = pl.ds(start, block_rows)
        whole = tree_sum(ref[:, here] for ref in parts)
        raised = raised_units[:, here]
        new = raised * over_unit * jnp.exp(whole[:groups] * factor)
        new_sum += jnp.sum(new, axis=1, keepdims=True)
        scaled[:, here] = new * ctrl_count
        left = left_of(jnp.where(raised > 0.0, whole[groups:], 0.0))
        if start < resident:
            high, low = high_ref[here, :], low_ref[here, :]
        else:
            there = pl.ds(start - resident, block_rows)
            high, low = more_high[there, :], more_low[there, :]
        time_grad += add_terms(rows_dot(left, high, low), groups)
    lane = lax.broadcasted_iota(jnp.int32, (groups, day_cols), 1)
    spare = (lane == day_cols - 1) & (me == half - 1)
    block = jnp.where(spare, new_sum, time_grad)
    for member in range(out.shape[0]):
        out[member] = block


def time_grad_of(grads, unit_devices, half, day):
    return tree_sum(grads[unit * half + half - 1 - day] for unit in range(unit_devices))


@first_half_only
def fourth_kernel(half, unit_devices, grads, totals):
    day_cols = grads.shape[2]
    last = time_grad_of(grads, unit_devices, half, half - 1)
    totals[...] = jnp.broadcast_to(last[:, day_cols - 1 :], totals.shape)


def fifth_kernel(half, unit_devices, totals, scaled, grads, lam, norms, ends, unit_weights, time_weights):
    groups, day_cols = time_weights.shape
    me = lax.axis_index("day")

    @pl.when(me < half)
    def _():
        unit_weights[...] = scaled[...] * (1.0 / totals[:, 0:1])
        root = jnp.sqrt(jnp.maximum(norms[:, 1:2], 1.0))
        moved_total = jnp.zeros((groups, 1), f32)
        own = jnp.zeros((groups, day_cols), f32)
        for day in range(half):
            total = time_grad_of(grads, unit_devices, half, day)
            moved = lam[:, day * day_cols : (day + 1) * day_cols] * jnp.exp(total * (-step_rate / root))
            moved_total += jnp.sum(moved, axis=1, keepdims=True)
            own = jnp.where(me == day, moved, own)
        time_weights[...] = own * (ends[:, 0:1] / moved_total)

    @pl.when(me >= half)
    def _():
        time_weights[...] = jnp.zeros_like(time_weights)


def sixth_kernel(half, sent_totals, sent_scaled, _, unit_weights, block, out_sem):
    @pl.when(lax.axis_index("day") >= half)
    def _():
        block[...] = sent_scaled[...] * (1.0 / sent_totals[:, 0:1])
        wait_all(fetch([block], [unit_weights], out_sem))


def local(outcomes, cohort, pre_end, post_start, unit_logit, time_logit):
    groups = pre_end.shape[0]
    unit_rows, day_cols = outcomes.shape
    day_devices = lax.axis_size("day")
    unit_devices = lax.axis_size("unit")
    half = day_devices // 2
    assert half * 2 == day_devices and half & (half - 1) == 0
    assert unit_devices & (unit_devices - 1) == 0
    panel_starts = [0, unit_rows // 8 * 3, unit_rows // 4 * 3, unit_rows]
    resident = unit_rows * 3 // 4 // (2 * block_rows) * (2 * block_rows)
    def meeting_at(first):
        return [first] + [unit for unit in reversed(range(unit_devices)) if unit != first]

    middle = unit_devices // 2

    def to_other_half(value, day_xor=0):
        pairs = [
            (u * day_devices + d, u * day_devices + half + (d ^ day_xor)) for u in range(unit_devices) for d in range(half)
        ]
        return lax.ppermute(value, ("unit", "day"), pairs)

    def over_days(value):
        halves = [list(range(half)), list(range(half, day_devices))]
        return lax.all_gather(value, "day", axis_index_groups=halves)

    def over_first_half(value):
        members = [
            [unit * day_devices + day for unit in meeting_at(middle + 1) for day in reversed(days)]
            for days in (range(half), range(half, day_devices))
        ]
        return lax.all_to_all(
            value, ("unit", "day"), split_axis=0, concat_axis=0, axis_index_groups=members, tiled=True
        )

    def over_units(value):
        members = [
            [unit * day_devices + day for unit in meeting_at(middle - 1 if day < half else middle)]
            for day in range(day_devices)
        ]
        return lax.all_to_all(
            value, ("unit", "day"), split_axis=0, concat_axis=0, axis_index_groups=members, tiled=True
        )

    def call(kernel, shapes, name, args, in_specs=None, out_specs=None, **more):
        return pl.pallas_call(
            kernel,
            in_specs=in_specs or [vmem] * len(args),
            out_specs=out_specs or [vmem] * len(shapes),
            out_shape=[
                shape if isinstance(shape, type(in_hbm)) else jax.ShapeDtypeStruct(*shape) for shape in shapes
            ],
            compiler_params=params,
            name=name,
            **more,
        )(*args)

    arguments = (outcomes, cohort[None, :], pre_end[None, :], post_start[None, :], unit_logit, time_logit)
    fixed = [pltpu.with_memory_space_constraint(argument, pltpu.HBM) for argument in arguments]
    held = [pltpu.VMEM(argument.shape, argument.dtype) for argument in arguments]
    small_sems, panel_sems = pltpu.SemaphoreType.DMA((5,)), pltpu.SemaphoreType.DMA((3,))
    panel_terms = [((resident, day_cols), bf16)] * 2
    other_terms = [((unit_rows - resident, day_cols), bf16)] * 2
    out_sems = pltpu.SemaphoreType.DMA((unit_devices,))
    width = 2 * groups * day_cols + lanes
    in_hbm = pltpu.HBM((unit_devices, 1, width), f32)
    sums, cross, raised_days, time_norm, ends, high, low = call(
        functools.partial(first_kernel, day_devices * day_cols, half, panel_starts),
        [
            in_hbm,
            pltpu.HBM((groups, unit_rows), f32),
            ((groups, day_cols), f32),
            ((groups, lanes), f32),
            ((groups, lanes), f32),
            *panel_terms,
        ],
        "first_product",
        fixed,
        in_specs=[hbm] * 6,
        out_specs=[hbm, hbm] + [vmem] * 5,
        scratch_shapes=held
        + [
            pltpu.VMEM((1, width), f32),
            pltpu.VMEM((4 * groups, unit_rows), bf16),
            pltpu.VMEM((groups, unit_rows), f32),
            small_sems,
            panel_sems,
            out_sems,
        ],
    )
    downward = [
        (u * day_devices + d + half, u * day_devices + d) for u in range(unit_devices) for d in range(half)
    ]
    post = lax.ppermute(cross, ("unit", "day"), downward)
    pack, norms, raised_units, more_high, more_low = call(
        functools.partial(second_kernel, half, unit_devices),
        [
            ((2 * groups, unit_rows + day_cols), f32),
            ((groups, lanes), f32),
            ((groups, unit_rows), f32),
            *other_terms,
        ],
        "unit_gradient",
        (fixed[0], fixed[1], fixed[4], over_units(sums), raised_days, ends, high, low),
        in_specs=[hbm] * 3 + [vmem] * 5,
        scratch_shapes=[
            pltpu.VMEM((unit_rows - resident, day_cols), f32),
            held[1],
            held[4],
            pltpu.SemaphoreType.DMA((3,)),
        ],
    )
    time_norms = [time_norm]
    for k in range(1, half):
        pairs = [(u * day_devices + d, u * day_devices + (d ^ k)) for u in range(unit_devices) for d in range(half)]
        time_norms.append(lax.ppermute(time_norm, ("unit", "day"), pairs))
    (pack,) = call(
        functools.partial(join_kernel, half),
        [((2 * groups, unit_rows + day_cols), f32)],
        "join_post",
        (pack, post, *time_norms),
    )
    members = unit_devices * half
    scaled, lam, grads = call(
        functools.partial(third_kernel, half),
        [
            ((groups, unit_rows), f32),
            ((groups, half * day_cols), f32),
            ((members, groups, day_cols), f32),
        ],
        "time_gradient",
        (over_days(pack), high, low, more_high, more_low, norms, raised_units, ends),
    )
    sent_scaled = to_other_half(scaled)
    all_grads = over_first_half(grads)
    (totals,) = call(
        functools.partial(fourth_kernel, half, unit_devices), [((groups, lanes), f32)], "unit_totals", (all_grads,)
    )
    unit_weights, time_weights = call(
        functools.partial(fifth_kernel, half, unit_devices),
        [((groups, unit_rows), f32), ((groups, day_cols), f32)],
        "scale_weights",
        (totals, scaled, all_grads, lam, norms, ends),
    )
    (unit_weights,) = call(
        functools.partial(sixth_kernel, half),
        [((groups, unit_rows), f32)],
        "other_half",
        (to_other_half(totals, half > 1), sent_scaled, unit_weights),
        in_specs=[vmem, vmem, hbm],
        out_specs=[hbm],
        input_output_aliases={2: 0},
        scratch_shapes=[pltpu.VMEM((groups, unit_rows), f32), pltpu.SemaphoreType.DMA((1,))],
    )
    return unit_weights, time_weights


def solution(mesh):
    return jax.shard_map(
        local,
        mesh=mesh,
        in_specs=(P("unit", "day"), P("unit"), P(), P(), P(None, "unit"), P(None, "day")),
        out_specs=(P(None, "unit"), P(None, "day")),
        check_vma=False,
    )
```

```python
import functools

import jax
import jax.numpy as jnp
from jax import lax
from jax.experimental import pallas as pl
from jax.experimental.pallas import tpu as pltpu
from jax.sharding import PartitionSpec as P

step_rate = 16.0
f32 = jnp.float32
bf16 = jnp.bfloat16
lanes = 128
block_rows = 512
params = pltpu.CompilerParams(vmem_limit_bytes=24 * 1024 * 1024)
vmem = pl.BlockSpec(memory_space=pltpu.VMEM)
hbm = pl.BlockSpec(memory_space=pltpu.HBM)


def split_left(value):
    first = value.astype(bf16).astype(f32)
    return [first, value - first]


def left_of(*values):
    return jnp.concatenate([term for value in values for term in split_left(value)], axis=0).astype(bf16)


def split_panel(value):
    high = value.astype(bf16)
    return high, (value - high.astype(f32)).astype(bf16)


def rows_dot(left, high, low):
    return jnp.dot(left, high, preferred_element_type=f32) + jnp.dot(left, low, preferred_element_type=f32)


def days_dot(left, high, low):
    dims = (((1,), (1,)), ((), ()))
    return lax.dot_general(left, high, dims, preferred_element_type=f32) + lax.dot_general(
        left, low, dims, preferred_element_type=f32
    )


def add_terms(stack, groups, place=0):
    return stack[2 * place * groups :][:groups] + stack[(2 * place + 1) * groups :][:groups]


def tree_sum(values):
    values = list(values)
    while len(values) > 1:
        values = [values[i] + values[i + 1] for i in range(0, len(values), 2)]
    return values[0]


def column(row_ref):
    count = row_ref.shape[1]
    wide = jnp.broadcast_to(row_ref[...].astype(f32), (count, count))
    row = lax.broadcasted_iota(jnp.int32, (count, count), 0)
    lane = lax.broadcasted_iota(jnp.int32, (count, count), 1)
    return jnp.sum(jnp.where(row == lane, wide, 0.0), axis=1, keepdims=True).astype(jnp.int32)


def days_of(device, shape):
    return device * shape[1] + lax.broadcasted_iota(jnp.int32, shape, 1)


def first_half_only(kernel):
    @functools.wraps(kernel)
    def guarded(half, *refs):
        @pl.when(lax.axis_index("day") < half)
        def _():
            kernel(half, *refs)

    return guarded


def fetch(sources, targets, sems):
    copies = [pltpu.make_async_copy(*pair, sems.at[i]) for i, pair in enumerate(zip(sources, targets))]
    for copy in copies:
        copy.start()
    return copies


def fetch_rows(source, target, sems, starts):
    spans = [(start, stop - start) for start, stop in zip(starts, starts[1:])]
    parts = [pl.ds(*span) for span in spans]
    copies = fetch([source.at[here] for here in parts], [target.at[here] for here in parts], sems)
    return [(*span, copy) for span, copy in zip(spans, copies)]


def blocks_of(start, rows):
    return [pl.ds(here, block_rows) for here in range(start, start + rows, block_rows)]


def wait_all(copies):
    for copy in copies:
        copy.wait()


def repeat_start(block, out, sems):
    places = [out.at[i] for i in range(out.shape[0])]
    return fetch([block] * len(places), places, sems)


def first_kernel(all_count, half, starts, *refs):
    arguments, refs = refs[:6], refs[6:]
    out, cross, raised_days, time_norm, ends, high_ref, low_ref, *held, block, left_ref, cross_block, small_sems, panel_sems, out_sems = refs
    groups, day_cols = held[5].shape
    unit_rows, resident = held[0].shape[0], high_ref.shape[0]
    (post_copy,) = fetch(arguments[3:4], held[3:4], small_sems)
    unit_copies = fetch(arguments[1:5:3], held[1:5:3], small_sems.at[pl.ds(1, 2)])
    parts = fetch_rows(arguments[0], held[0], panel_sems, starts)
    day_copies = fetch(arguments[2:6:3], held[2:6:3], small_sems.at[pl.ds(3, 2)])
    panel, cohort, pre_row, post_row, unit_logit, time_logit = held
    post_copy.wait()
    wait_all(unit_copies)
    me = lax.axis_index("day")

    @pl.when(me < half)
    def _():
        counts = []

        def prepare(start, rows):
            here = pl.ds(start, rows)
            label = lax.broadcasted_iota(jnp.int32, (groups, rows), 0)
            treated = jnp.where(cohort[:, here] == label, 1.0, 0.0)
            control = jnp.where(cohort[:, here] > label, 1.0, 0.0)
            raised = jnp.exp(unit_logit[:, here]) * control
            left_ref[:, here] = left_of(raised, treated)
            counts.append([jnp.sum(value, axis=1, keepdims=True) for value in (raised, treated, control)])

        product = jnp.zeros((4 * groups, day_cols), f32)
        prepare(*parts[0][:2])
        for part, (start, rows, copy) in enumerate(parts):
            copy.wait()
            for here in blocks_of(start, rows):
                high, low = split_panel(panel[here, :])
                if here.start < resident:
                    high_ref[here, :] = high
                    low_ref[here, :] = low
                product += rows_dot(left_ref[:, here], high, low)
            if part + 1 < len(parts):
                prepare(*parts[part + 1][:2])
        lane = lax.broadcasted_iota(jnp.int32, (groups, lanes), 1)
        slot = lax.broadcasted_iota(jnp.int32, (groups, lanes), 0)
        norms = jnp.zeros((groups, lanes), f32)
        for i, count in enumerate(zip(*counts)):
            norms += jnp.where(lane == i * groups + slot, sum(count), 0.0)
        block[:, 2 * groups * day_cols :] = jnp.sum(norms, axis=0, keepdims=True)
        both_sums = jnp.concatenate([add_terms(product, groups), product[2 * groups :][:groups]], axis=0)
        for row in range(2 * groups):
            block[:, row * day_cols : (row + 1) * day_cols] = both_sums[row : row + 1, :]
        sends = repeat_start(block, out, out_sems)
        wait_all(day_copies)
        pre_end = column(pre_row)
        ends[...] = jnp.broadcast_to(pre_end.astype(f32), ends.shape)
        before = days_of(me, (groups, day_cols)) < pre_end
        raised_time = jnp.where(before, jnp.exp(time_logit[...]), 0.0)
        raised_days[...] = raised_time
        time_norm[...] = jnp.broadcast_to(jnp.sum(raised_time, axis=1, keepdims=True), time_norm.shape)
        wait_all(sends)

    @pl.when(me >= half)
    def _():
        post_start = column(post_row)
        after = jnp.where(days_of(me, (groups, day_cols)) >= post_start, 1.0, 0.0)
        left = left_of(after / (all_count - post_start).astype(f32))
        for start, rows, copy in parts:
            copy.wait()
            for here in blocks_of(start, rows):
                cross_block[:, here] = add_terms(days_dot(left, *split_panel(panel[here, :])), groups)
        sends = fetch([cross_block], [cross], out_sems)
        wait_all(day_copies)
        wait_all(sends)


@first_half_only
def second_kernel(half, unit_devices, panel, cohort, unit_logit, sums, raised_days, ends, high_ref, low_ref, *refs):
    pack, norms, raised_units, more_high, more_low, held, held_cohort, held_logit, sems = refs
    groups, day_cols = raised_days.shape
    unit_rows, resident = panel.shape[0], high_ref.shape[0]
    rest = pl.ds(resident, unit_rows - resident)
    copies = fetch([panel.at[rest], cohort, unit_logit], [held, held_cohort, held_logit], sems)

    @pl.when(lax.axis_index("day") < half)
    def _():
        total = tree_sum(sums[u] for u in range(unit_devices))

        def group_rows(first):
            starts = [(first + row) * day_cols for row in range(groups)]
            return jnp.concatenate([total[:, start : start + day_cols] for start in starts], axis=0)

        counts = jnp.broadcast_to(total[:, 2 * groups * day_cols :], (groups, lanes))
        slot = lax.broadcasted_iota(jnp.int32, (groups, lanes), 0)
        lane = lax.broadcasted_iota(jnp.int32, (groups, lanes), 1)
        unit_norm, treat_count, ctrl_count = [
            jnp.sum(jnp.where(lane == i * groups + slot, counts, 0.0), axis=1, keepdims=True) for i in range(3)
        ]
        norms[...] = jnp.where(lane == 0, unit_norm, ctrl_count)
        gap = group_rows(0) / unit_norm - group_rows(groups) / jnp.maximum(treat_count, 1.0)
        before = days_of(lax.axis_index("day"), (groups, day_cols)).astype(f32) < ends[:, 0:1]
        raised_time = raised_days[...]
        pack[:groups, unit_rows:] = raised_time
        pack[groups:, unit_rows:] = jnp.zeros_like(raised_time)
        left = left_of(jnp.where(before, gap, 0.0), raised_time)

        def multiply(here, high, low):
            product = days_dot(left, high, low)
            pack[:groups, here] = add_terms(product, groups)
            pack[groups:, here] = add_terms(product, groups, 1)

        late = resident - block_rows

        @pl.loop(0, late // block_rows)
        def _(block):
            here = pl.ds(pl.multiple_of(block * block_rows, block_rows), block_rows)
            multiply(here, high_ref[here, :], low_ref[here, :])

        wait_all(copies)
        label = lax.broadcasted_iota(jnp.int32, raised_units.shape, 0)
        raised_units[...] = jnp.where(held_cohort[...] > label, jnp.exp(held_logit[...]), 0.0)
        for there in blocks_of(0, unit_rows - resident):
            more_high[there, :], more_low[there, :] = split_panel(held[there, :])
        for here in blocks_of(late, resident - late):
            multiply(here, high_ref[here, :], low_ref[here, :])
        for there in blocks_of(0, unit_rows - resident):
            multiply(pl.ds(resident + there.start, block_rows), more_high[there, :], more_low[there, :])


@first_half_only
def join_kernel(half, pack, post, *refs):
    norms, out = refs[:half], refs[half]
    groups, unit_rows = post.shape
    over_time = 1.0 / tree_sum(ref[:, 0:1] for ref in norms)
    out[:groups, :unit_rows] = pack[:groups, :unit_rows]
    out[:groups, unit_rows:] = pack[:groups, unit_rows:] * over_time
    out[groups:, :unit_rows] = pack[groups:, :unit_rows] * over_time - post[...]
    out[groups:, unit_rows:] = pack[groups:, unit_rows:]


@first_half_only
def third_kernel(half, *refs):
    parts, refs = [refs[0].at[day] for day in range(half)], refs[1:]
    high_ref, low_ref, more_high, more_low, norms, raised_units, ends, scaled, lam, out = refs
    groups, unit_rows = raised_units.shape
    resident, day_cols = high_ref.shape
    unit_norm, ctrl_count = norms[:, 0:1], norms[:, 1:2]
    factor = -step_rate / jnp.sqrt(ends[:, 0:1])
    over_unit = 1.0 / unit_norm
    me = lax.rem(lax.axis_index("day"), half)
    for day in range(half):
        lam[:, day * day_cols : (day + 1) * day_cols] = parts[day][:groups, unit_rows:]
    time_grad = jnp.zeros((groups, day_cols), f32)
    new_sum = jnp.zeros((groups, 1), f32)
    for start in range(0, unit_rows, block_rows):
        here = pl.ds(start, block_rows)
        whole = tree_sum(ref[:, here] for ref in parts)
        raised = raised_units[:, here]
        new = raised * over_unit * jnp.exp(whole[:groups] * factor)
        new_sum += jnp.sum(new, axis=1, keepdims=True)
        scaled[:, here] = new * ctrl_count
        left = left_of(jnp.where(raised > 0.0, whole[groups:], 0.0))
        if start < resident:
            high, low = high_ref[here, :], low_ref[here, :]
        else:
            there = pl.ds(start - resident, block_rows)
            high, low = more_high[there, :], more_low[there, :]
        time_grad += add_terms(rows_dot(left, high, low), groups)
    lane = lax.broadcasted_iota(jnp.int32, (groups, day_cols), 1)
    spare = (lane == day_cols - 1) & (me == half - 1)
    block = jnp.where(spare, new_sum, time_grad)
    for member in range(out.shape[0]):
        out[member] = block


def time_grad_of(grads, unit_devices, half, day):
    return tree_sum(grads[unit * half + half - 1 - day] for unit in range(unit_devices))


@first_half_only
def fourth_kernel(half, unit_devices, grads, totals):
    day_cols = grads.shape[2]
    last = time_grad_of(grads, unit_devices, half, half - 1)
    totals[...] = jnp.broadcast_to(last[:, day_cols - 1 :], totals.shape)


def fifth_kernel(half, unit_devices, totals, scaled, grads, lam, norms, ends, unit_weights, time_weights):
    groups, day_cols = time_weights.shape
    me = lax.axis_index("day")

    @pl.when(me < half)
    def _():
        unit_weights[...] = scaled[...] * (1.0 / totals[:, 0:1])
        root = jnp.sqrt(jnp.maximum(norms[:, 1:2], 1.0))
        moved_total = jnp.zeros((groups, 1), f32)
        own = jnp.zeros((groups, day_cols), f32)
        for day in range(half):
            total = time_grad_of(grads, unit_devices, half, day)
            moved = lam[:, day * day_cols : (day + 1) * day_cols] * jnp.exp(total * (-step_rate / root))
            moved_total += jnp.sum(moved, axis=1, keepdims=True)
            own = jnp.where(me == day, moved, own)
        time_weights[...] = own * (ends[:, 0:1] / moved_total)

    @pl.when(me >= half)
    def _():
        time_weights[...] = jnp.zeros_like(time_weights)


def sixth_kernel(half, sent_totals, sent_scaled, _, unit_weights, block, out_sem):
    @pl.when(lax.axis_index("day") >= half)
    def _():
        block[...] = sent_scaled[...] * (1.0 / sent_totals[:, 0:1])
        wait_all(fetch([block], [unit_weights], out_sem))


def local(outcomes, cohort, pre_end, post_start, unit_logit, time_logit):
    groups = pre_end.shape[0]
    unit_rows, day_cols = outcomes.shape
    day_devices = lax.axis_size("day")
    unit_devices = lax.axis_size("unit")
    half = day_devices // 2
    assert half * 2 == day_devices and half & (half - 1) == 0
    assert unit_devices & (unit_devices - 1) == 0
    panel_starts = [0, unit_rows // 8 * 3, unit_rows // 4 * 3, unit_rows]
    resident = unit_rows * 3 // 4 // (2 * block_rows) * (2 * block_rows)
    def meeting_at(first):
        return [first] + [unit for unit in reversed(range(unit_devices)) if unit != first]

    middle = unit_devices // 2

    def to_other_half(value, day_xor=0):
        pairs = [
            (u * day_devices + d, u * day_devices + half + (d ^ day_xor)) for u in range(unit_devices) for d in range(half)
        ]
        return lax.ppermute(value, ("unit", "day"), pairs)

    def over_days(value):
        halves = [list(range(half)), list(range(half, day_devices))]
        return lax.all_gather(value, "day", axis_index_groups=halves)

    def over_first_half(value):
        members = [
            [unit * day_devices + day for unit in meeting_at(middle + 1) for day in reversed(days)]
            for days in (range(half), range(half, day_devices))
        ]
        return lax.all_to_all(
            value, ("unit", "day"), split_axis=0, concat_axis=0, axis_index_groups=members, tiled=True
        )

    def over_units(value):
        members = [
            [unit * day_devices + day for unit in meeting_at(middle - 1 if day < half else middle)]
            for day in range(day_devices)
        ]
        return lax.all_to_all(
            value, ("unit", "day"), split_axis=0, concat_axis=0, axis_index_groups=members, tiled=True
        )

    def call(kernel, shapes, name, args, in_specs=None, out_specs=None, **more):
        return pl.pallas_call(
            kernel,
            in_specs=in_specs or [vmem] * len(args),
            out_specs=out_specs or [vmem] * len(shapes),
            out_shape=[
                shape if isinstance(shape, type(in_hbm)) else jax.ShapeDtypeStruct(*shape) for shape in shapes
            ],
            compiler_params=params,
            name=name,
            **more,
        )(*args)

    arguments = (outcomes, cohort[None, :], pre_end[None, :], post_start[None, :], unit_logit, time_logit)
    fixed = [pltpu.with_memory_space_constraint(argument, pltpu.HBM) for argument in arguments]
    held = [pltpu.VMEM(argument.shape, argument.dtype) for argument in arguments]
    small_sems, panel_sems = pltpu.SemaphoreType.DMA((5,)), pltpu.SemaphoreType.DMA((3,))
    panel_terms = [((resident, day_cols), bf16)] * 2
    other_terms = [((unit_rows - resident, day_cols), bf16)] * 2
    out_sems = pltpu.SemaphoreType.DMA((unit_devices,))
    width = 2 * groups * day_cols + lanes
    in_hbm = pltpu.HBM((unit_devices, 1, width), f32)
    sums, cross, raised_days, time_norm, ends, high, low = call(
        functools.partial(first_kernel, day_devices * day_cols, half, panel_starts),
        [
            in_hbm,
            pltpu.HBM((groups, unit_rows), f32),
            ((groups, day_cols), f32),
            ((groups, lanes), f32),
            ((groups, lanes), f32),
            *panel_terms,
        ],
        "first_product",
        fixed,
        in_specs=[hbm] * 6,
        out_specs=[hbm, hbm] + [vmem] * 5,
        scratch_shapes=held
        + [
            pltpu.VMEM((1, width), f32),
            pltpu.VMEM((4 * groups, unit_rows), bf16),
            pltpu.VMEM((groups, unit_rows), f32),
            small_sems,
            panel_sems,
            out_sems,
        ],
    )
    downward = [
        (u * day_devices + d + half, u * day_devices + d) for u in range(unit_devices) for d in range(half)
    ]
    post = lax.ppermute(cross, ("unit", "day"), downward)
    pack, norms, raised_units, more_high, more_low = call(
        functools.partial(second_kernel, half, unit_devices),
        [
            ((2 * groups, unit_rows + day_cols), f32),
            ((groups, lanes), f32),
            ((groups, unit_rows), f32),
            *other_terms,
        ],
        "unit_gradient",
        (fixed[0], fixed[1], fixed[4], over_units(sums), raised_days, ends, high, low),
        in_specs=[hbm] * 3 + [vmem] * 5,
        scratch_shapes=[
            pltpu.VMEM((unit_rows - resident, day_cols), f32),
            held[1],
            held[4],
            pltpu.SemaphoreType.DMA((3,)),
        ],
    )
    time_norms = [time_norm]
    for k in range(1, half):
        pairs = [(u * day_devices + d, u * day_devices + (d ^ k)) for u in range(unit_devices) for d in range(half)]
        time_norms.append(lax.ppermute(time_norm, ("unit", "day"), pairs))
    (pack,) = call(
        functools.partial(join_kernel, half),
        [((2 * groups, unit_rows + day_cols), f32)],
        "join_post",
        (pack, post, *time_norms),
    )
    members = unit_devices * half
    scaled, lam, grads = call(
        functools.partial(third_kernel, half),
        [
            ((groups, unit_rows), f32),
            ((groups, half * day_cols), f32),
            ((members, groups, day_cols), f32),
        ],
        "time_gradient",
        (over_days(pack), high, low, more_high, more_low, norms, raised_units, ends),
    )
    sent_scaled = to_other_half(scaled)
    all_grads = over_first_half(grads)
    (totals,) = call(
        functools.partial(fourth_kernel, half, unit_devices), [((groups, lanes), f32)], "unit_totals", (all_grads,)
    )
    unit_weights, time_weights = call(
        functools.partial(fifth_kernel, half, unit_devices),
        [((groups, unit_rows), f32), ((groups, day_cols), f32)],
        "scale_weights",
        (totals, scaled, all_grads, lam, norms, ends),
    )
    (unit_weights,) = call(
        functools.partial(sixth_kernel, half),
        [((groups, unit_rows), f32)],
        "other_half",
        (to_other_half(totals, half > 1), sent_scaled, unit_weights),
        in_specs=[vmem, vmem, hbm],
        out_specs=[hbm],
        input_output_aliases={2: 0},
        scratch_shapes=[pltpu.VMEM((groups, unit_rows), f32), pltpu.SemaphoreType.DMA((1,))],
    )
    return unit_weights, time_weights


def solution(mesh):
    return jax.shard_map(
        local,
        mesh=mesh,
        in_specs=(P("unit", "day"), P("unit"), P(), P(), P(None, "unit"), P(None, "day")),
        out_specs=(P(None, "unit"), P(None, "day")),
        check_vma=False,
    )
```

```python
import functools

import jax
import jax.numpy as jnp
from jax import lax
from jax.experimental import pallas as pl
from jax.experimental.pallas import tpu as pltpu
from jax.sharding import PartitionSpec as P

step_rate = 16.0
f32 = jnp.float32
bf16 = jnp.bfloat16
lanes = 128
block_rows = 512
params = pltpu.CompilerParams(vmem_limit_bytes=24 * 1024 * 1024)
vmem = pl.BlockSpec(memory_space=pltpu.VMEM)
hbm = pl.BlockSpec(memory_space=pltpu.HBM)


def split_left(value):
    first = value.astype(bf16).astype(f32)
    return [first, value - first]


def left_of(*values):
    return jnp.concatenate([term for value in values for term in split_left(value)], axis=0).astype(bf16)


def split_panel(value):
    high = value.astype(bf16)
    return high, (value - high.astype(f32)).astype(bf16)


def rows_dot(left, high, low):
    return jnp.dot(left, high, preferred_element_type=f32) + jnp.dot(left, low, preferred_element_type=f32)


def days_dot(left, high, low):
    dims = (((1,), (1,)), ((), ()))
    return lax.dot_general(left, high, dims, preferred_element_type=f32) + lax.dot_general(
        left, low, dims, preferred_element_type=f32
    )


def add_terms(stack, groups, place=0):
    return stack[2 * place * groups :][:groups] + stack[(2 * place + 1) * groups :][:groups]


def tree_sum(values):
    values = list(values)
    while len(values) > 1:
        values = [values[i] + values[i + 1] for i in range(0, len(values), 2)]
    return values[0]


def column(row_ref):
    count = row_ref.shape[1]
    wide = jnp.broadcast_to(row_ref[...].astype(f32), (count, count))
    row = lax.broadcasted_iota(jnp.int32, (count, count), 0)
    lane = lax.broadcasted_iota(jnp.int32, (count, count), 1)
    return jnp.sum(jnp.where(row == lane, wide, 0.0), axis=1, keepdims=True).astype(jnp.int32)


def days_of(device, shape):
    return device * shape[1] + lax.broadcasted_iota(jnp.int32, shape, 1)


def first_half_only(kernel):
    @functools.wraps(kernel)
    def guarded(half, *refs):
        @pl.when(lax.axis_index("day") < half)
        def _():
            kernel(half, *refs)

    return guarded


def fetch(sources, targets, sems):
    copies = [pltpu.make_async_copy(*pair, sems.at[i]) for i, pair in enumerate(zip(sources, targets))]
    for copy in copies:
        copy.start()
    return copies


def fetch_rows(source, target, sems, starts):
    spans = [(start, stop - start) for start, stop in zip(starts, starts[1:])]
    parts = [pl.ds(*span) for span in spans]
    copies = fetch([source.at[here] for here in parts], [target.at[here] for here in parts], sems)
    return [(*span, copy) for span, copy in zip(spans, copies)]


def blocks_of(start, rows):
    return [pl.ds(here, block_rows) for here in range(start, start + rows, block_rows)]


def wait_all(copies):
    for copy in copies:
        copy.wait()


def repeat_start(block, out, sems):
    places = [out.at[i] for i in range(out.shape[0])]
    return fetch([block] * len(places), places, sems)


def first_kernel(all_count, half, starts, *refs):
    arguments, refs = refs[:6], refs[6:]
    out, cross, raised_days, time_norm, ends, high_ref, low_ref, *held, block, left_ref, cross_block, small_sems, panel_sems, out_sems = refs
    groups, day_cols = held[5].shape
    unit_rows, resident = held[0].shape[0], high_ref.shape[0]
    (post_copy,) = fetch(arguments[3:4], held[3:4], small_sems)
    unit_copies = fetch(arguments[1:5:3], held[1:5:3], small_sems.at[pl.ds(1, 2)])
    parts = fetch_rows(arguments[0], held[0], panel_sems, starts)
    day_copies = fetch(arguments[2:6:3], held[2:6:3], small_sems.at[pl.ds(3, 2)])
    panel, cohort, pre_row, post_row, unit_logit, time_logit = held
    post_copy.wait()
    wait_all(unit_copies)
    me = lax.axis_index("day")

    @pl.when(me < half)
    def _():
        counts = []

        def prepare(start, rows):
            here = pl.ds(start, rows)
            label = lax.broadcasted_iota(jnp.int32, (groups, rows), 0)
            treated = jnp.where(cohort[:, here] == label, 1.0, 0.0)
            control = jnp.where(cohort[:, here] > label, 1.0, 0.0)
            raised = jnp.exp(unit_logit[:, here]) * control
            left_ref[:, here] = left_of(raised, treated)
            counts.append([jnp.sum(value, axis=1, keepdims=True) for value in (raised, treated, control)])

        product = jnp.zeros((4 * groups, day_cols), f32)
        prepare(*parts[0][:2])
        for part, (start, rows, copy) in enumerate(parts):
            copy.wait()
            for here in blocks_of(start, rows):
                high, low = split_panel(panel[here, :])
                if here.start < resident:
                    high_ref[here, :] = high
                    low_ref[here, :] = low
                product += rows_dot(left_ref[:, here], high, low)
            if part + 1 < len(parts):
                prepare(*parts[part + 1][:2])
        lane = lax.broadcasted_iota(jnp.int32, (groups, lanes), 1)
        slot = lax.broadcasted_iota(jnp.int32, (groups, lanes), 0)
        norms = jnp.zeros((groups, lanes), f32)
        for i, count in enumerate(zip(*counts)):
            norms += jnp.where(lane == i * groups + slot, sum(count), 0.0)
        block[:, 2 * groups * day_cols :] = jnp.sum(norms, axis=0, keepdims=True)
        both_sums = jnp.concatenate([add_terms(product, groups), product[2 * groups :][:groups]], axis=0)
        for row in range(2 * groups):
            block[:, row * day_cols : (row + 1) * day_cols] = both_sums[row : row + 1, :]
        sends = repeat_start(block, out, out_sems)
        wait_all(day_copies)
        pre_end = column(pre_row)
        ends[...] = jnp.broadcast_to(pre_end.astype(f32), ends.shape)
        before = days_of(me, (groups, day_cols)) < pre_end
        raised_time = jnp.where(before, jnp.exp(time_logit[...]), 0.0)
        raised_days[...] = raised_time
        time_norm[...] = jnp.broadcast_to(jnp.sum(raised_time, axis=1, keepdims=True), time_norm.shape)
        wait_all(sends)

    @pl.when(me >= half)
    def _():
        post_start = column(post_row)
        after = jnp.where(days_of(me, (groups, day_cols)) >= post_start, 1.0, 0.0)
        left = left_of(after / (all_count - post_start).astype(f32))
        for start, rows, copy in parts:
            copy.wait()
            for here in blocks_of(start, rows):
                cross_block[:, here] = add_terms(days_dot(left, *split_panel(panel[here, :])), groups)
        sends = fetch([cross_block], [cross], out_sems)
        wait_all(day_copies)
        wait_all(sends)


@first_half_only
def second_kernel(half, unit_devices, panel, cohort, unit_logit, sums, raised_days, ends, high_ref, low_ref, *refs):
    pack, norms, raised_units, more_high, more_low, held, held_cohort, held_logit, sems = refs
    groups, day_cols = raised_days.shape
    unit_rows, resident = panel.shape[0], high_ref.shape[0]
    rest = pl.ds(resident, unit_rows - resident)
    copies = fetch([panel.at[rest], cohort, unit_logit], [held, held_cohort, held_logit], sems)

    @pl.when(lax.axis_index("day") < half)
    def _():
        total = tree_sum(sums[u] for u in range(unit_devices))

        def group_rows(first):
            starts = [(first + row) * day_cols for row in range(groups)]
            return jnp.concatenate([total[:, start : start + day_cols] for start in starts], axis=0)

        counts = jnp.broadcast_to(total[:, 2 * groups * day_cols :], (groups, lanes))
        slot = lax.broadcasted_iota(jnp.int32, (groups, lanes), 0)
        lane = lax.broadcasted_iota(jnp.int32, (groups, lanes), 1)
        unit_norm, treat_count, ctrl_count = [
            jnp.sum(jnp.where(lane == i * groups + slot, counts, 0.0), axis=1, keepdims=True) for i in range(3)
        ]
        norms[...] = jnp.where(lane == 0, unit_norm, ctrl_count)
        gap = group_rows(0) / unit_norm - group_rows(groups) / jnp.maximum(treat_count, 1.0)
        before = days_of(lax.axis_index("day"), (groups, day_cols)).astype(f32) < ends[:, 0:1]
        raised_time = raised_days[...]
        pack[:groups, unit_rows:] = raised_time
        pack[groups:, unit_rows:] = jnp.zeros_like(raised_time)
        left = left_of(jnp.where(before, gap, 0.0), raised_time)

        def multiply(here, high, low):
            product = days_dot(left, high, low)
            pack[:groups, here] = add_terms(product, groups)
            pack[groups:, here] = add_terms(product, groups, 1)

        late = resident - 2 * block_rows

        @pl.loop(0, late // (2 * block_rows))
        def _(block):
            here = pl.ds(pl.multiple_of(block * 2 * block_rows, 2 * block_rows), 2 * block_rows)
            multiply(here, high_ref[here, :], low_ref[here, :])

        wait_all(copies)
        label = lax.broadcasted_iota(jnp.int32, raised_units.shape, 0)
        raised_units[...] = jnp.where(held_cohort[...] > label, jnp.exp(held_logit[...]), 0.0)
        for there in blocks_of(0, unit_rows - resident):
            more_high[there, :], more_low[there, :] = split_panel(held[there, :])
        for here in blocks_of(late, resident - late):
            multiply(here, high_ref[here, :], low_ref[here, :])
        for there in blocks_of(0, unit_rows - resident):
            multiply(pl.ds(resident + there.start, block_rows), more_high[there, :], more_low[there, :])


@first_half_only
def join_kernel(half, pack, post, *refs):
    norms, out = refs[:half], refs[half]
    groups, unit_rows = post.shape
    over_time = 1.0 / tree_sum(ref[:, 0:1] for ref in norms)
    out[:groups, :unit_rows] = pack[:groups, :unit_rows]
    out[:groups, unit_rows:] = pack[:groups, unit_rows:] * over_time
    out[groups:, :unit_rows] = pack[groups:, :unit_rows] * over_time - post[...]
    out[groups:, unit_rows:] = pack[groups:, unit_rows:]


@first_half_only
def third_kernel(half, *refs):
    parts, refs = [refs[0].at[day] for day in range(half)], refs[1:]
    high_ref, low_ref, more_high, more_low, norms, raised_units, ends, scaled, lam, out = refs
    groups, unit_rows = raised_units.shape
    resident, day_cols = high_ref.shape
    unit_norm, ctrl_count = norms[:, 0:1], norms[:, 1:2]
    factor = -step_rate / jnp.sqrt(ends[:, 0:1])
    over_unit = 1.0 / unit_norm
    me = lax.rem(lax.axis_index("day"), half)
    for day in range(half):
        lam[:, day * day_cols : (day + 1) * day_cols] = parts[day][:groups, unit_rows:]
    time_grad = jnp.zeros((groups, day_cols), f32)
    new_sum = jnp.zeros((groups, 1), f32)
    for start in range(0, unit_rows, block_rows):
        here = pl.ds(start, block_rows)
        whole = tree_sum(ref[:, here] for ref in parts)
        raised = raised_units[:, here]
        new = raised * over_unit * jnp.exp(whole[:groups] * factor)
        new_sum += jnp.sum(new, axis=1, keepdims=True)
        scaled[:, here] = new * ctrl_count
        left = left_of(jnp.where(raised > 0.0, whole[groups:], 0.0))
        if start < resident:
            high, low = high_ref[here, :], low_ref[here, :]
        else:
            there = pl.ds(start - resident, block_rows)
            high, low = more_high[there, :], more_low[there, :]
        time_grad += add_terms(rows_dot(left, high, low), groups)
    lane = lax.broadcasted_iota(jnp.int32, (groups, day_cols), 1)
    spare = (lane == day_cols - 1) & (me == half - 1)
    block = jnp.where(spare, new_sum, time_grad)
    for member in range(out.shape[0]):
        out[member] = block


def time_grad_of(grads, unit_devices, half, day):
    return tree_sum(grads[unit * half + half - 1 - day] for unit in range(unit_devices))


@first_half_only
def fourth_kernel(half, unit_devices, grads, totals):
    day_cols = grads.shape[2]
    last = time_grad_of(grads, unit_devices, half, half - 1)
    totals[...] = jnp.broadcast_to(last[:, day_cols - 1 :], totals.shape)


def fifth_kernel(half, unit_devices, totals, scaled, grads, lam, norms, ends, unit_weights, time_weights):
    groups, day_cols = time_weights.shape
    me = lax.axis_index("day")

    @pl.when(me < half)
    def _():
        unit_weights[...] = scaled[...] * (1.0 / totals[:, 0:1])
        root = jnp.sqrt(jnp.maximum(norms[:, 1:2], 1.0))
        moved_total = jnp.zeros((groups, 1), f32)
        own = jnp.zeros((groups, day_cols), f32)
        for day in range(half):
            total = time_grad_of(grads, unit_devices, half, day)
            moved = lam[:, day * day_cols : (day + 1) * day_cols] * jnp.exp(total * (-step_rate / root))
            moved_total += jnp.sum(moved, axis=1, keepdims=True)
            own = jnp.where(me == day, moved, own)
        time_weights[...] = own * (ends[:, 0:1] / moved_total)

    @pl.when(me >= half)
    def _():
        time_weights[...] = jnp.zeros_like(time_weights)


def sixth_kernel(half, sent_totals, sent_scaled, _, unit_weights, block, out_sem):
    @pl.when(lax.axis_index("day") >= half)
    def _():
        block[...] = sent_scaled[...] * (1.0 / sent_totals[:, 0:1])
        wait_all(fetch([block], [unit_weights], out_sem))


def local(outcomes, cohort, pre_end, post_start, unit_logit, time_logit):
    groups = pre_end.shape[0]
    unit_rows, day_cols = outcomes.shape
    day_devices = lax.axis_size("day")
    unit_devices = lax.axis_size("unit")
    half = day_devices // 2
    assert half * 2 == day_devices and half & (half - 1) == 0
    assert unit_devices & (unit_devices - 1) == 0
    panel_starts = [0, unit_rows // 2, unit_rows // 8 * 7, unit_rows]
    resident = unit_rows * 3 // 4 // (2 * block_rows) * (2 * block_rows)
    def meeting_at(first):
        return [first] + [unit for unit in reversed(range(unit_devices)) if unit != first]

    middle = unit_devices // 2

    def to_other_half(value, day_xor=0):
        pairs = [
            (u * day_devices + d, u * day_devices + half + (d ^ day_xor)) for u in range(unit_devices) for d in range(half)
        ]
        return lax.ppermute(value, ("unit", "day"), pairs)

    def over_days(value):
        halves = [list(range(half)), list(range(half, day_devices))]
        return lax.all_gather(value, "day", axis_index_groups=halves)

    def over_first_half(value):
        members = [
            [unit * day_devices + day for unit in meeting_at(middle + 1) for day in reversed(days)]
            for days in (range(half), range(half, day_devices))
        ]
        return lax.all_to_all(
            value, ("unit", "day"), split_axis=0, concat_axis=0, axis_index_groups=members, tiled=True
        )

    def over_units(value):
        members = [
            [unit * day_devices + day for unit in meeting_at(middle - 1 if day < half else middle)]
            for day in range(day_devices)
        ]
        return lax.all_to_all(
            value, ("unit", "day"), split_axis=0, concat_axis=0, axis_index_groups=members, tiled=True
        )

    def call(kernel, shapes, name, args, in_specs=None, out_specs=None, **more):
        return pl.pallas_call(
            kernel,
            in_specs=in_specs or [vmem] * len(args),
            out_specs=out_specs or [vmem] * len(shapes),
            out_shape=[
                shape if isinstance(shape, type(in_hbm)) else jax.ShapeDtypeStruct(*shape) for shape in shapes
            ],
            compiler_params=params,
            name=name,
            **more,
        )(*args)

    arguments = (outcomes, cohort[None, :], pre_end[None, :], post_start[None, :], unit_logit, time_logit)
    fixed = [pltpu.with_memory_space_constraint(argument, pltpu.HBM) for argument in arguments]
    held = [pltpu.VMEM(argument.shape, argument.dtype) for argument in arguments]
    small_sems, panel_sems = pltpu.SemaphoreType.DMA((5,)), pltpu.SemaphoreType.DMA((3,))
    panel_terms = [((resident, day_cols), bf16)] * 2
    other_terms = [((unit_rows - resident, day_cols), bf16)] * 2
    out_sems = pltpu.SemaphoreType.DMA((unit_devices,))
    width = 2 * groups * day_cols + lanes
    in_hbm = pltpu.HBM((unit_devices, 1, width), f32)
    sums, cross, raised_days, time_norm, ends, high, low = call(
        functools.partial(first_kernel, day_devices * day_cols, half, panel_starts),
        [
            in_hbm,
            pltpu.HBM((groups, unit_rows), f32),
            ((groups, day_cols), f32),
            ((groups, lanes), f32),
            ((groups, lanes), f32),
            *panel_terms,
        ],
        "first_product",
        fixed,
        in_specs=[hbm] * 6,
        out_specs=[hbm, hbm] + [vmem] * 5,
        scratch_shapes=held
        + [
            pltpu.VMEM((1, width), f32),
            pltpu.VMEM((4 * groups, unit_rows), bf16),
            pltpu.VMEM((groups, unit_rows), f32),
            small_sems,
            panel_sems,
            out_sems,
        ],
    )
    downward = [
        (u * day_devices + d + half, u * day_devices + d) for u in range(unit_devices) for d in range(half)
    ]
    post = lax.ppermute(cross, ("unit", "day"), downward)
    pack, norms, raised_units, more_high, more_low = call(
        functools.partial(second_kernel, half, unit_devices),
        [
            ((2 * groups, unit_rows + day_cols), f32),
            ((groups, lanes), f32),
            ((groups, unit_rows), f32),
            *other_terms,
        ],
        "unit_gradient",
        (fixed[0], fixed[1], fixed[4], over_units(sums), raised_days, ends, high, low),
        in_specs=[hbm] * 3 + [vmem] * 5,
        scratch_shapes=[
            pltpu.VMEM((unit_rows - resident, day_cols), f32),
            held[1],
            held[4],
            pltpu.SemaphoreType.DMA((3,)),
        ],
    )
    time_norms = [time_norm]
    for k in range(1, half):
        pairs = [(u * day_devices + d, u * day_devices + (d ^ k)) for u in range(unit_devices) for d in range(half)]
        time_norms.append(lax.ppermute(time_norm, ("unit", "day"), pairs))
    (pack,) = call(
        functools.partial(join_kernel, half),
        [((2 * groups, unit_rows + day_cols), f32)],
        "join_post",
        (pack, post, *time_norms),
    )
    members = unit_devices * half
    scaled, lam, grads = call(
        functools.partial(third_kernel, half),
        [
            ((groups, unit_rows), f32),
            ((groups, half * day_cols), f32),
            ((members, groups, day_cols), f32),
        ],
        "time_gradient",
        (over_days(pack), high, low, more_high, more_low, norms, raised_units, ends),
    )
    sent_scaled = to_other_half(scaled)
    all_grads = over_first_half(grads)
    (totals,) = call(
        functools.partial(fourth_kernel, half, unit_devices), [((groups, lanes), f32)], "unit_totals", (all_grads,)
    )
    unit_weights, time_weights = call(
        functools.partial(fifth_kernel, half, unit_devices),
        [((groups, unit_rows), f32), ((groups, day_cols), f32)],
        "scale_weights",
        (totals, scaled, all_grads, lam, norms, ends),
    )
    (unit_weights,) = call(
        functools.partial(sixth_kernel, half),
        [((groups, unit_rows), f32)],
        "other_half",
        (to_other_half(totals, half > 1), sent_scaled, unit_weights),
        in_specs=[vmem, vmem, hbm],
        out_specs=[hbm],
        input_output_aliases={2: 0},
        scratch_shapes=[pltpu.VMEM((groups, unit_rows), f32), pltpu.SemaphoreType.DMA((1,))],
    )
    return unit_weights, time_weights


def solution(mesh):
    return jax.shard_map(
        local,
        mesh=mesh,
        in_specs=(P("unit", "day"), P("unit"), P(), P(), P(None, "unit"), P(None, "day")),
        out_specs=(P(None, "unit"), P(None, "day")),
        check_vma=False,
    )
```
